32 devices in a mesh: batch: 16 (over z, y, core), blk: 2 (over x).
Axes of the slice: x: 2, y: 2, z: 4, core: 2. Of those that a mesh axis runs over, the one named last changes fastest.
Arguments:
- tokens: bfloat16 [128, 512, 768], P('batch', 'blk'), may hold values from -6 to 6
- span_mask: int32 [128, 512], P('batch', 'blk'), may hold values from 0 to 1, as said below
- cotangent: bfloat16 [128, 512, 768], P('batch', 'blk'), may hold values from -6 to 6
- w_query: bfloat16 [768, 768], P('batch'), may hold values from -0.21875 to 0.21875
- b_query: bfloat16 [768], P('batch'), may hold values from -3 to 3
- w_key: bfloat16 [768, 768], P('batch'), may hold values from -0.21875 to 0.21875
- w_value: bfloat16 [768, 768], P('batch'), may hold values from -0.21875 to 0.21875
- b_value: bfloat16 [768], P('batch'), may hold values from -0.19921875 to 0.19921875
- w_out: bfloat16 [768, 768], P('batch'), may hold values from -2.5 to 2.5
- b_out: bfloat16 [768], P('batch'), may hold values from -2 to 2
- gain_first: bfloat16 [768], P('batch'), may hold values from 0.25 to 1.75
- bias_first: bfloat16 [768], P('batch'), may hold values from -2 to 2
- w_inner: bfloat16 [768, 3072], P('batch'), may hold values from -0.21875 to 0.21875
- b_inner: bfloat16 [3072], P('batch'), may hold values from -2 to 2
- w_outer: bfloat16 [3072, 768], P('batch'), may hold values from -0.109375 to 0.109375
- b_outer: bfloat16 [768], P('batch'), may hold values from -2 to 2
- gain_second: bfloat16 [768], P('batch'), may hold values from 0.25 to 1.75
- bias_second: bfloat16 [768], P('batch'), may hold values from -2 to 2
Outputs:
- output: bfloat16 [128, 512, 768], P('batch', 'blk')
- grad_tokens: bfloat16 [128, 512, 768], P('batch', 'blk')
- grad_w_query: float32 [768, 768], P('batch')
- grad_b_query: float32 [768], P('batch')
- grad_w_key: float32 [768, 768], P('batch')
- grad_w_value: float32 [768, 768], P('batch')
- grad_b_value: float32 [768], P('batch')
- grad_w_out: float32 [768, 768], P('batch')
- grad_b_out: float32 [768], P('batch')
- grad_gain_first: float32 [768], P('batch')
- grad_bias_first: float32 [768], P('batch')
- grad_w_inner: float32 [768, 3072], P('batch')
- grad_b_inner: float32 [3072], P('batch')
- grad_w_outer: float32 [3072, 768], P('batch')
- grad_b_outer: float32 [768], P('batch')
- grad_gain_second: float32 [768], P('batch')
- grad_bias_second: float32 [768], P('batch')
The draws below stay inside these ranges and needn't reach their ends.
Inputs may be any that keep to these rules, and one draw needn't show every extreme that they name: `span_mask`: masked positions come in runs of 6 or more consecutive tokens, except where a run is cut by the end of the sequence; the masked share differs from sequence to sequence.
All inputs are finite; a program needn't handle non-finite values.
Results may differ from the reference program's by a relative error of at most 0.04.
Values may be sent and summed in bfloat16 or wider, within the bound.
A program may use at most 512 MiB of HBM per device.

```python
import jax
import jax.numpy as jnp
from jax import lax

D = 768
HEADS = 12
HEAD_DIM = 64
FF = 3072
SEQ = 512
ROWS_DEV = 8
BATCH = 128
N_BATCH = 16


def draw_span_mask(key, part):
    key = jax.random.fold_in(key, 11)
    rate_key, start_key = jax.random.split(key)
    rates = jax.random.randint(rate_key, (BATCH, 1), 1, 6)
    starts = (jax.random.randint(start_key, (BATCH, SEQ), 0, 96) < rates).astype(jnp.int32)
    padded = jnp.pad(starts, ((0, 0), (5, 0)))
    covered = jnp.zeros((BATCH, SEQ), jnp.int32)
    for offset in range(6):
        covered = covered + padded[:, 5 - offset:5 - offset + SEQ]
    return (covered > 0).astype(jnp.int32)


def block_levels(own_key, dims, cuts, least, largest):
    level, own = 1.0, jax.random.fold_in(own_key, 6)
    for axis_at, parts in cuts:
        heights = jnp.exp(jax.random.uniform(jax.random.fold_in(own, axis_at), (parts,), jnp.float32, least / len(cuts), largest / len(cuts)))
        level = level * jnp.repeat(heights, dims[axis_at] // parts).reshape([-1 if axis == axis_at else 1 for axis in range(len(dims))])
    return level


def centred(own_key, shape, deviation, bound, cuts=(), kind=jnp.bfloat16):
    entries = deviation * jax.random.normal(own_key, shape, jnp.float32)
    if cuts:
        entries = entries * block_levels(own_key, shape, cuts, -0.22, 0.18)
    return jnp.clip(entries, -bound, bound).astype(kind)


def setup_inputs(seed: int = 0) -> dict:
    splits = jax.random.split(jax.random.key(seed), 19)
    return {
        "tokens": centred(splits[0], (BATCH, SEQ, D), 1.0, 6.0, ((0, 16), (1, 2))),
        "span_mask": draw_span_mask(jax.random.fold_in(splits[18], 71), 0),
        "cotangent": centred(splits[2], (BATCH, SEQ, D), 1.0, 6.0, ((0, 16), (1, 2))),
        "w_query": centred(splits[3], (D, D), D ** -0.5, 0.21875, ((0, 16),)),
        "b_query": centred(splits[4], (D,), 0.5, 3.0, ((0, 16),)),
        "w_key": centred(splits[5], (D, D), D ** -0.5, 0.21875, ((0, 16),)),
        "w_value": centred(splits[6], (D, D), D ** -0.5, 0.21875, ((0, 16),)),
        "b_value": centred(splits[7], (D,), 0.03, 0.19921875, ((0, 16),)),
        "w_out": centred(splits[8], (D, D), (D // 128) ** -0.5, 2.5, ((0, 16),)),
        "b_out": centred(splits[9], (D,), 0.3, 2.0, ((0, 16),)),
        "gain_first": jnp.clip(1.0 + 0.15 * jax.random.normal(splits[10], (D,), jnp.float32), 0.25, 1.75).astype(jnp.bfloat16),
        "bias_first": centred(splits[11], (D,), 0.3, 2.0, ((0, 16),)),
        "w_inner": centred(splits[12], (D, FF), D ** -0.5, 0.21875, ((0, 16),)),
        "b_inner": centred(splits[13], (FF,), 0.3, 2.0, ((0, 16),)),
        "w_outer": centred(splits[14], (FF, D), FF ** -0.5, 0.109375, ((0, 16),)),
        "b_outer": centred(splits[15], (D,), 0.3, 2.0, ((0, 16),)),
        "gain_second": jnp.clip(1.0 + 0.15 * jax.random.normal(splits[16], (D,), jnp.float32), 0.25, 1.75).astype(jnp.bfloat16),
        "bias_second": centred(splits[17], (D,), 0.3, 2.0, ((0, 16),)),
    }


@jax.custom_vjp
def low(v):
    return lax.optimization_barrier(v.astype(jnp.bfloat16)).astype(jnp.float32)

@jax.custom_vjp
def low_back(v):
    return v

def low_keep(v):
    return (low(v), None)

def low_pass(kept, grad):
    return (grad,)

def back_keep(v):
    return (v, None)

def back_low(kept, grad):
    return (low(grad),)
low.defvjp(low_keep, low_pass)
low_back.defvjp(back_keep, back_low)
epsilon = 1e-06
highest = lax.Precision.HIGHEST

def both_ways(values):
    return low_back(low(values))

def normalize(values, gain, bias):
    center = values - lax.optimization_barrier(jnp.mean(values, -1, keepdims=True))
    spread = lax.optimization_barrier(jnp.mean(center * center, -1, keepdims=True))
    return center * lax.rsqrt(spread + epsilon) * gain + bias

def matmul(left, right):
    return jnp.einsum('gsd,de->gse', left, right, precision=highest)

def forward(inputs, w_query, b_query, w_key, w_value, b_value, w_out, b_out, gain_first, bias_first, w_inner, b_inner, w_outer, b_outer, gain_second, bias_second):
    group, length, width = inputs.shape
    depth = width // HEADS
    queries = both_ways(matmul(inputs, w_query) + b_query).reshape(group, length, HEADS, depth)
    keys = both_ways(matmul(inputs, w_key)).reshape(group, length, HEADS, depth)
    values = both_ways(matmul(inputs, w_value) + b_value).reshape(group, length, HEADS, depth)
    scores = low_back(jnp.einsum('gqhd,gkhd->ghqk', queries, keys, precision=highest) * HEAD_DIM ** (-0.5))
    probs = jax.nn.softmax(scores, -1)
    context = jnp.einsum('ghqk,gkhd->gqhd', low(probs), values, precision=highest).reshape(group, length, width)
    context = both_ways(context)
    branch = low_back(matmul(context, w_out) + b_out)
    middle = normalize(inputs + branch, gain_first, bias_first)
    inner = low_back(matmul(low(middle), w_inner) + b_inner)
    hidden = low(jax.nn.gelu(inner, approximate=False))
    outer = low_back(matmul(hidden, w_outer) + b_outer)
    return normalize(middle + outer, gain_second, bias_second)

def reference(tokens, span_mask, cotangent, w_query, b_query, w_key, w_value, b_value, w_out, b_out, gain_first, bias_first, w_inner, b_inner, w_outer, b_outer, gain_second, bias_second):
    weights = (w_query, b_query, w_key, w_value, b_value, w_out, b_out, gain_first, bias_first, w_inner, b_inner, w_outer, b_outer, gain_second, bias_second)
    weights = tuple((w.astype(jnp.float32) for w in weights))
    inputs = tokens.astype(jnp.float32).reshape(N_BATCH, ROWS_DEV, SEQ, D)
    masks = span_mask.astype(jnp.float32).reshape(N_BATCH, ROWS_DEV, SEQ)
    cotans = cotangent.astype(jnp.float32).reshape(N_BATCH, ROWS_DEV, SEQ, D)

    def step(totals, batch_in):
        group_in, group_mask, group_cot = batch_in
        result, backward = jax.vjp(forward, group_in, *weights)
        grads = backward(group_cot * group_mask[..., None])
        newer = tuple((total + grad for total, grad in zip(totals, grads[1:])))
        return (newer, (result.astype(jnp.bfloat16), grads[0].astype(jnp.bfloat16)))
    start = tuple((jnp.zeros(w.shape, jnp.float32) for w in weights))
    totals, (results, grad_in) = lax.scan(step, start, (inputs, masks, cotans))
    output = results.reshape(BATCH, SEQ, D)
    grad_tokens = grad_in.reshape(BATCH, SEQ, D)
    return (output, grad_tokens, totals[0], totals[1], totals[2], totals[3], totals[4], totals[5], totals[6], totals[7], totals[8], totals[9], totals[10], totals[11], totals[12], totals[13], totals[14])
```

```python
import functools

import jax
import jax.numpy as jnp
from jax import lax
from jax.experimental import pallas as pl
from jax.experimental.pallas import tpu as pltpu
from jax.sharding import PartitionSpec as P

HEADS = 12
HEAD_DIM = 64
PAIR = 2 * HEAD_DIM
STAT_ROWS = 16
VMEM_BYTES = 60 * 2**20

epsilon = 1e-06
bf16 = jnp.bfloat16
f32 = jnp.float32

NN = (((1,), (0,)), ((), ()))
NT = (((1,), (1,)), ((), ()))
TN = (((0,), (0,)), ((), ()))

B_QUERY, B_VALUE, B_OUT, GAIN_1, BIAS_1, B_OUTER, GAIN_2, BIAS_2, B_INNER = range(9)


def mul(left, right, dims=NN):
    return lax.dot_general(left, right, dims, preferred_element_type=f32)


def row(ref, index):
    return ref[index : index + 1, :]


def halves(block):
    lane = lax.broadcasted_iota(jnp.int32, block.shape, 1)
    zero = jnp.zeros_like(block)
    return jnp.where(lane < HEAD_DIM, block, zero), jnp.where(lane < HEAD_DIM, zero, block)


def pair_at(p):
    return pl.ds(pl.multiple_of(p * PAIR, PAIR), PAIR)


def normalize(values):
    center = values - jnp.mean(values, -1, keepdims=True)
    inverse = lax.rsqrt(jnp.mean(center * center, -1, keepdims=True) + epsilon)
    return center * inverse, inverse


def norm_back(grad, normed, inverse, gain):
    scaled = grad * gain
    return inverse * (
        scaled
        - jnp.mean(scaled, -1, keepdims=True)
        - normed * jnp.mean(scaled * normed, -1, keepdims=True)
    )


def column_sum(values):
    return jnp.sum(values.astype(f32), 0, keepdims=True)


def project(x, w_ref, vec_ref, q_ref, k_ref, v_ref):
    width = x.shape[-1]
    q = (mul(x, w_ref[:, :width]) + row(vec_ref, B_QUERY)).astype(bf16)
    q_ref[...] = q * bf16(HEAD_DIM**-0.5)
    k_ref[...] = mul(x, w_ref[:, width : 2 * width]).astype(bf16)
    v_ref[...] = (mul(x, w_ref[:, 2 * width :]) + row(vec_ref, B_VALUE)).astype(bf16)


def attend(q_ref, k_ref, v_ref, c_ref, l_ref, stat):
    length = q_ref.shape[0]
    lane = lax.broadcasted_iota(jnp.int32, (length, 128), 1)

    def pair(p, carry):
        at = pair_at(p)
        q2, k2, v2 = q_ref[:, at], k_ref[:, at], v_ref[:, at]
        context = None
        for h, (k_one, v_one) in enumerate(zip(halves(k2), halves(v2))):
            scores = mul(q2, k_one, NT)
            best = jnp.max(scores, 1, keepdims=True)
            weights = jnp.exp(scores - best)
            total = jnp.sum(weights, 1, keepdims=True)
            part = mul(weights.astype(bf16), v_one) * (1.0 / total)
            context = part if context is None else context + part
            stat[...] = jnp.where(lane == 2 * p + h, best + jnp.log(total), stat[...])
        c_ref[:, at] = context.astype(bf16)
        return carry

    stat[...] = jnp.zeros_like(stat)
    lax.fori_loop(0, HEADS // 2, pair, 0, unroll=2)
    l_ref[...] = stat[...].T[:STAT_ROWS]


def attend_back(q_ref, k_ref, v_ref, g_ref, l_ref, d_ref, gq_ref, gk_ref, gv_ref, kt, gqt):
    kt[...] = (k_ref[...] * bf16(HEAD_DIM**-0.5)).T

    def pair(p, carry):
        at = pair_at(p)
        q2, g2 = q_ref[:, at], g_ref[:, at]
        ks, vs = halves(k_ref[:, at]), halves(v_ref[:, at])
        qs, gs = halves(q2), halves(g2)
        gk = gv = None
        for h in range(2):
            probs = jnp.exp(mul(ks[h], q2, NT) - l_ref[pl.ds(2 * p + h, 1), :])
            grad_probs = mul(vs[h], g2, NT)
            grad_scores = (probs * (grad_probs - d_ref[pl.ds(2 * p + h, 1), :])).astype(bf16)
            gk_one = mul(grad_scores, qs[h])
            gv_one = mul(probs.astype(bf16), gs[h])
            gk = gk_one if gk is None else gk + gk_one
            gv = gv_one if gv is None else gv + gv_one
            rows = pl.ds(pl.multiple_of((2 * p + h) * HEAD_DIM, HEAD_DIM), HEAD_DIM)
            gqt[rows, :] = mul(kt[rows, :], grad_scores).astype(bf16)
        gk_ref[:, at] = gk.astype(bf16)
        gv_ref[:, at] = gv.astype(bf16)
        return carry

    lax.fori_loop(0, HEADS // 2, pair, 0, unroll=2)
    gq_ref[...] = gqt[...].T


def feed_forward(
    x, cb, cot, wo_ref, wi_ref, wu_ref, vec_ref, out_ref, mid_ref, gf_ref, ga_ref, gc_ref, d_ref, h_ref, gu_ref, sums_ref
):
    width = x.shape[-1]
    chunks = wi_ref.shape[1] // width
    gain_1, gain_2 = row(vec_ref, GAIN_1), row(vec_ref, GAIN_2)
    normed_1, inverse_1 = normalize(x.astype(f32) + (mul(cb, wo_ref[...]) + row(vec_ref, B_OUT)))
    middle = normed_1 * gain_1 + row(vec_ref, BIAS_1)
    mid = middle.astype(bf16)
    mid_ref[...] = mid
    total = middle + row(vec_ref, B_OUTER)
    for c in range(chunks):
        at = slice(c * width, (c + 1) * width)
        inner = mul(mid, wi_ref[:, at]) + row(vec_ref, B_INNER + c)
        cdf = 0.5 + 0.5 * lax.erf(inner * (0.5**0.5))
        hidden = (inner * cdf).astype(bf16)
        h_ref[:, at] = hidden
        slope = cdf + inner * (jnp.exp(inner * inner * -0.5) * ((0.5 / jnp.pi) ** 0.5))
        gu_ref[:, at] = slope.astype(bf16)
        total = total + mul(hidden, wu_ref[at, :])
    normed_2, inverse_2 = normalize(total)
    out_ref[...] = (normed_2 * gain_2 + row(vec_ref, BIAS_2)).astype(bf16)
    grad = cot.astype(f32)
    sums_ref[GAIN_2 : GAIN_2 + 1, :] += column_sum(grad * normed_2)
    sums_ref[BIAS_2 : BIAS_2 + 1, :] += column_sum(grad)
    grad_2 = norm_back(grad, normed_2, inverse_2, gain_2)
    gf = grad_2.astype(bf16)
    gf_ref[...] = gf
    sums_ref[B_OUTER : B_OUTER + 1, :] += column_sum(gf)
    grad_mid = grad_2
    for c in range(chunks):
        at = slice(c * width, (c + 1) * width)
        gu = (mul(gf, wu_ref[at, :], NT) * gu_ref[:, at].astype(f32)).astype(bf16)
        gu_ref[:, at] = gu
        sums_ref[B_INNER + c : B_INNER + c + 1, :] += column_sum(gu)
        grad_mid = grad_mid + mul(gu, wi_ref[:, at], NT)
    sums_ref[GAIN_1 : GAIN_1 + 1, :] += column_sum(grad_mid * normed_1)
    sums_ref[BIAS_1 : BIAS_1 + 1, :] += column_sum(grad_mid)
    ga = norm_back(grad_mid, normed_1, inverse_1, gain_1).astype(bf16)
    ga_ref[...] = ga
    sums_ref[B_OUT : B_OUT + 1, :] += column_sum(ga)
    gc = mul(ga, wo_ref[...], NT).astype(bf16)
    gc_ref[...] = gc
    product = gc.astype(f32) * cb.astype(f32)
    high = product.astype(bf16)
    low = (product - high.astype(f32)).astype(bf16)
    head = lax.broadcasted_iota(jnp.int32, (STAT_ROWS, width), 0)
    column = lax.broadcasted_iota(jnp.int32, (STAT_ROWS, width), 1)
    pick = jnp.where(column // HEAD_DIM == head, 1.0, 0.0).astype(bf16)
    d_ref[...] = mul(pick, high, NT) + mul(pick, low, NT)


def spec(shape, pipelined=True):
    zeros = (0,) * (len(shape) - 1)
    if pipelined:
        return pl.BlockSpec(shape, lambda i: (i,) + zeros)
    return pl.BlockSpec(shape, lambda i: (0,) + zeros)


def whole_vmem():
    return pl.BlockSpec(memory_space=pltpu.VMEM)


def params():
    return pltpu.CompilerParams(vmem_limit_bytes=VMEM_BYTES, dimension_semantics=("arbitrary",))


def attention_call(x, w_qkv, vec):
    count, length, width = x.shape
    block = (None, length, width)

    def kernel(x_ref, w_ref, vec_ref, q_ref, k_ref, v_ref, c_ref, l_ref, stat):
        project(x_ref[...], w_ref, vec_ref, q_ref, k_ref, v_ref)
        attend(q_ref, k_ref, v_ref, c_ref, l_ref, stat)

    seq = jax.ShapeDtypeStruct(x.shape, bf16)
    return pl.pallas_call(
        kernel,
        grid=(count,),
        in_specs=[spec(block), whole_vmem(), whole_vmem()],
        out_specs=[spec(block)] * 4 + [spec((None, STAT_ROWS, length))],
        out_shape=[seq] * 4 + [jax.ShapeDtypeStruct((count, STAT_ROWS, length), f32)],
        scratch_shapes=[pltpu.VMEM((length, 128), f32)],
        compiler_params=params(),
        name="attention",
    )(x, w_qkv, vec)


def feed_forward_call(x, cb, cot, w_out, w_inner, w_outer, vec):
    count, length, width = x.shape
    inner = w_inner.shape[1]
    block, wide = (None, length, width), (None, length, inner)

    def kernel(x_ref, cb_ref, cot_ref, wo, wi, wu, vec_ref, out, mid, gf, ga, gc, d, h, gu, sums):
        @pl.when(pl.program_id(0) == 0)
        def _():
            sums[...] = jnp.zeros_like(sums)

        feed_forward(
            x_ref[...], cb_ref[...], cot_ref[...], wo, wi, wu, vec_ref, out, mid, gf, ga, gc, d, h, gu, sums
        )

    seq = jax.ShapeDtypeStruct(x.shape, bf16)
    seq_wide = jax.ShapeDtypeStruct((count, length, inner), bf16)
    return pl.pallas_call(
        kernel,
        grid=(count,),
        in_specs=[spec(block)] * 3 + [whole_vmem()] * 4,
        out_specs=[spec(block)] * 5
        + [spec((None, STAT_ROWS, length)), spec(wide), spec(wide), spec((16, width), False)],
        out_shape=[seq] * 5
        + [
            jax.ShapeDtypeStruct((count, STAT_ROWS, length), f32),
            seq_wide,
            seq_wide,
            jax.ShapeDtypeStruct((16, width), f32),
        ],
        compiler_params=params(),
        name="feed_forward",
    )(x, cb, cot, w_out, w_inner, w_outer, vec)


def weight_grad_call(left, right, over_left):
    tokens, rows = left.shape
    columns = right.shape[1]
    step = min(rows, columns)

    def kernel(left_ref, right_ref, out_ref):
        out_ref[...] = mul(left_ref[...], right_ref[...], TN).astype(bf16)

    if over_left:
        grid, left_map, right_map, out_map = rows // step, lambda i: (0, i), lambda i: (0, 0), lambda i: (i, 0)
    else:
        grid, left_map, right_map, out_map = columns // step, lambda i: (0, 0), lambda i: (0, i), lambda i: (0, i)
    return pl.pallas_call(
        kernel,
        grid=(grid,),
        in_specs=[pl.BlockSpec((tokens, step), left_map), pl.BlockSpec((tokens, step), right_map)],
        out_specs=pl.BlockSpec((step, step), out_map),
        out_shape=jax.ShapeDtypeStruct((rows, columns), bf16),
        compiler_params=params(),
        name="weight_grad",
    )(left, right)


def attention_back_call(x, q, k, v, gc, ga, stat_l, stat_d, w_qkv):
    count, length, width = x.shape
    block = (None, length, width)

    def kernel(x_ref, q_ref, k_ref, v_ref, gc_ref, ga_ref, l_ref, d_ref, w_ref, gx_ref, gw_ref, sums_ref, kt, gqt, gq, gk, gv, total):
        step = pl.program_id(0)

        @pl.when(step == 0)
        def _():
            sums_ref[...] = jnp.zeros_like(sums_ref)
            total[...] = jnp.zeros_like(total)

        attend_back(q_ref, k_ref, v_ref, gc_ref, l_ref, d_ref, gq, gk, gv, kt, gqt)
        sums_ref[B_QUERY : B_QUERY + 1, :] += column_sum(gq[...])
        sums_ref[B_VALUE : B_VALUE + 1, :] += column_sum(gv[...])
        grad = ga_ref[...].astype(f32)
        x = x_ref[...]
        for i, ref in enumerate((gq, gk, gv)):
            at = slice(i * width, (i + 1) * width)
            grad = grad + mul(ref[...], w_ref[:, at], NT)
            total[:, at] += mul(x, ref[...], TN)
        gx_ref[...] = grad.astype(bf16)

        @pl.when(step == count - 1)
        def _():
            gw_ref[...] = total[...].astype(bf16)

    seq_scratch = pltpu.VMEM((length, width), bf16)
    return pl.pallas_call(
        kernel,
        grid=(count,),
        in_specs=[spec(block)] * 6 + [spec((None, STAT_ROWS, length))] * 2 + [whole_vmem()],
        out_specs=[spec(block), spec((width, 3 * width), False), spec((16, width), False)],
        out_shape=[
            jax.ShapeDtypeStruct(x.shape, bf16),
            jax.ShapeDtypeStruct((width, 3 * width), bf16),
            jax.ShapeDtypeStruct((16, width), f32),
        ],
        scratch_shapes=[pltpu.VMEM((width, length), bf16)] * 2 + [seq_scratch] * 3 + [pltpu.VMEM((width, 3 * width), f32)],
        compiler_params=params(),
        name="attention_back",
    )(x, q, k, v, gc, ga, stat_l, stat_d, w_qkv)


def pack_shard(w_query, w_key, w_value, w_out, w_inner, w_outer, vectors):
    width = w_query.shape[1]
    inner_parts = [w_inner[:, i : i + width] for i in range(0, w_inner.shape[1], width)]
    small = jnp.concatenate(vectors)
    body_rows = sum(part.shape[0] for part in (w_query, w_key, w_value, w_out, w_outer, *inner_parts))
    rows = -(-(body_rows + 1) // 16) * 16
    tail = jnp.zeros(((rows - body_rows) * width,), small.dtype).at[: small.shape[0]].set(small)
    return jnp.concatenate(
        [w_query, w_key, w_value, w_out, *inner_parts, w_outer, tail.reshape(-1, width)]
    )


def vec_table(small, vec_names_sizes):
    rows, at = [], 0
    for size in vec_names_sizes:
        rows.append(small[:, at : at + size].reshape(-1))
        at += size
    return rows


def body(
    tokens,
    span_mask,
    cotangent,
    w_query,
    b_query,
    w_key,
    w_value,
    b_value,
    w_out,
    b_out,
    gain_first,
    bias_first,
    w_inner,
    b_inner,
    w_outer,
    b_outer,
    gain_second,
    bias_second,
):
    rows, stretch, width = tokens.shape
    inner = w_inner.shape[1]
    part = w_query.shape[0]
    outer_part = w_outer.shape[0]
    vectors = (b_query, b_value, b_out, gain_first, bias_first, b_outer, gain_second, bias_second, b_inner)
    sizes = [vector.shape[0] for vector in vectors]

    packed = pack_shard(w_query, w_key, w_value, w_out, w_inner, w_outer, vectors)
    shard_rows = packed.shape[0]
    gathered = lax.all_gather(packed, "batch", axis=0)
    chunks = inner // width

    def weight(at, count):
        return gathered[:, at : at + count].reshape(-1, width)

    squares = [weight(i * part, part) for i in range(4 + chunks)]
    w_qkv = jnp.concatenate(squares[:3], 1)
    w_out_all = squares[3]
    w_inner_all = jnp.concatenate(squares[4:], 1)
    outer_at = (4 + chunks) * part
    w_outer_all = weight(outer_at, outer_part)
    small = gathered[:, outer_at + outer_part :].reshape(gathered.shape[0], -1)
    vec = jnp.concatenate(vec_table(small, sizes)).reshape(-1, width).astype(f32)
    vec = jnp.concatenate([vec, jnp.zeros((16 - vec.shape[0], width), f32)])

    masked = cotangent * span_mask[..., None].astype(bf16)
    swap = functools.partial(lax.all_to_all, axis_name="blk", tiled=True)
    x = swap(tokens, split_axis=0, concat_axis=1)
    cot = swap(masked, split_axis=0, concat_axis=1)

    q, k, v, cb, stat_l = attention_call(x, w_qkv, vec)
    out, mid, gf, ga, gc, stat_d, hidden, gu, sums_ffn = feed_forward_call(
        x, cb, cot, w_out_all, w_inner_all, w_outer_all, vec
    )
    gx, gw_qkv, sums_att = attention_back_call(x, q, k, v, gc, ga, stat_l, stat_d, w_qkv)
    output = swap(out, split_axis=1, concat_axis=0)
    grad_tokens = swap(gx, split_axis=1, concat_axis=0)

    def flat(values):
        return values.reshape(-1, values.shape[-1])

    gw_out = weight_grad_call(flat(cb), flat(ga), False)
    gw_inner = weight_grad_call(flat(mid), flat(gu), False)
    gw_outer = weight_grad_call(flat(hidden), flat(gf), True)

    devices = gathered.shape[0]
    sums = sums_ffn + sums_att
    small_sums = [sums[i].reshape(devices, -1) for i in range(B_INNER)]
    small_sums.append(sums[B_INNER : B_INNER + chunks].reshape(devices, -1))
    tail = jnp.concatenate(small_sums, 1).astype(bf16)
    tail = jnp.pad(tail, ((0, 0), (0, (shard_rows - outer_at - outer_part) * width - tail.shape[1])))
    pieces = [gw_qkv[:, i * width : (i + 1) * width].reshape(devices, part, width) for i in range(3)]
    pieces.append(gw_out.reshape(devices, part, width))
    pieces += [gw_inner[:, i * width : (i + 1) * width].reshape(devices, part, width) for i in range(chunks)]
    pieces.append(gw_outer.reshape(devices, outer_part, width))
    pieces.append(tail.reshape(devices, -1, width))
    grads = jnp.concatenate(pieces, 1)
    share = lax.psum_scatter(grads, "batch", scatter_dimension=0, tiled=False)
    share = lax.psum(share, "blk").astype(f32)
    square = [share[i * part : (i + 1) * part] for i in range(4 + chunks)]
    share_small = share[outer_at + outer_part :].reshape(-1)
    small_out, at = [], 0
    for size in sizes:
        small_out.append(share_small[at : at + size])
        at += size
    (g_b_query, g_b_value, g_b_out, g_gain_1, g_bias_1, g_b_outer, g_gain_2, g_bias_2, g_b_inner) = small_out
    return (
        output,
        grad_tokens,
        square[0],
        g_b_query,
        square[1],
        square[2],
        g_b_value,
        square[3],
        g_b_out,
        g_gain_1,
        g_bias_1,
        jnp.concatenate(square[4:], 1),
        g_b_inner,
        share[outer_at : outer_at + outer_part],
        g_b_outer,
        g_gain_2,
        g_bias_2,
    )


def solution(mesh):
    block = P("batch", "blk", None)
    matrix, vector = P("batch", None), P("batch")
    weights = (
        matrix, vector, matrix, matrix, vector, matrix, vector, vector, vector, matrix, vector, matrix, vector, vector, vector,
    )
    return jax.shard_map(
        body,
        mesh=mesh,
        in_specs=(block, P("batch", "blk"), block) + weights,
        out_specs=(block, block) + weights,
        check_vma=False,
    )
```

```python
import functools

import jax
import jax.numpy as jnp
from jax import lax
from jax.experimental import pallas as pl
from jax.experimental.pallas import tpu as pltpu
from jax.sharding import PartitionSpec as P

HEADS = 12
HEAD_DIM = 64
PAIR = 2 * HEAD_DIM
STAT_ROWS = 16
VMEM_BYTES = 60 * 2**20

epsilon = 1e-06
bf16 = jnp.bfloat16
f32 = jnp.float32

NN = (((1,), (0,)), ((), ()))
NT = (((1,), (1,)), ((), ()))
TN = (((0,), (0,)), ((), ()))

B_QUERY, B_VALUE, B_OUT, GAIN_1, BIAS_1, B_OUTER, GAIN_2, BIAS_2, B_INNER = range(9)


def mul(left, right, dims=NN):
    return lax.dot_general(left, right, dims, preferred_element_type=f32)


def row(ref, index):
    return ref[index : index + 1, :]


def halves(block):
    lane = lax.broadcasted_iota(jnp.int32, block.shape, 1)
    zero = jnp.zeros_like(block)
    return jnp.where(lane < HEAD_DIM, block, zero), jnp.where(lane < HEAD_DIM, zero, block)


def pair_at(p):
    return pl.ds(pl.multiple_of(p * PAIR, PAIR), PAIR)


def normalize(values):
    center = values - jnp.mean(values, -1, keepdims=True)
    inverse = lax.rsqrt(jnp.mean(center * center, -1, keepdims=True) + epsilon)
    return center * inverse, inverse


def norm_back(grad, normed, inverse, gain):
    scaled = grad * gain
    return inverse * (
        scaled
        - jnp.mean(scaled, -1, keepdims=True)
        - normed * jnp.mean(scaled * normed, -1, keepdims=True)
    )


def column_sum(values):
    return jnp.sum(values.astype(f32), 0, keepdims=True)


def project(x, w_ref, vec_ref, q_ref, k_ref, v_ref):
    width = x.shape[-1]
    q = (mul(x, w_ref[:, :width]) + row(vec_ref, B_QUERY)).astype(bf16)
    q_ref[...] = q * bf16(HEAD_DIM**-0.5)
    k_ref[...] = mul(x, w_ref[:, width : 2 * width]).astype(bf16)
    v_ref[...] = (mul(x, w_ref[:, 2 * width :]) + row(vec_ref, B_VALUE)).astype(bf16)


def attend_pairs(q_ref, k_ref, v_ref, c_ref, stat, first, end):
    lane = lax.broadcasted_iota(jnp.int32, stat.shape, 1)

    def pair(p, carry):
        at = pair_at(p)
        q2, k2, v2 = q_ref[:, at], k_ref[:, at], v_ref[:, at]
        context = None
        for h, (k_one, v_one) in enumerate(zip(halves(k2), halves(v2))):
            scores = mul(q2, k_one, NT)
            best = jnp.max(scores, 1, keepdims=True)
            weights = jnp.exp(scores - best)
            total = jnp.sum(weights, 1, keepdims=True)
            part = mul(weights.astype(bf16), v_one) * (1.0 / total)
            context = part if context is None else context + part
            stat[...] = jnp.where(lane == 2 * p + h, best + jnp.log(total), stat[...])
        c_ref[:, at] = context.astype(bf16)
        return carry

    lax.fori_loop(first, end, pair, 0, unroll=3)


def attend(q_ref, k_ref, v_ref, c_ref, l_ref, stat):
    stat[...] = jnp.zeros_like(stat)
    attend_pairs(q_ref, k_ref, v_ref, c_ref, stat, 0, HEADS // 2)
    l_ref[...] = stat[...].T[:STAT_ROWS]


def attend_back(q_ref, k_ref, v_ref, g_ref, l_ref, d_ref, gq_ref, gk_ref, gv_ref, kt, gqt):
    kt[...] = (k_ref[...] * bf16(HEAD_DIM**-0.5)).T

    def pair(p, carry):
        at = pair_at(p)
        q2, g2 = q_ref[:, at], g_ref[:, at]
        ks, vs = halves(k_ref[:, at]), halves(v_ref[:, at])
        qs, gs = halves(q2), halves(g2)
        gk = gv = None
        for h in range(2):
            probs = jnp.exp(mul(ks[h], q2, NT) - l_ref[pl.ds(2 * p + h, 1), :])
            grad_probs = mul(vs[h], g2, NT)
            grad_scores = (probs * (grad_probs - d_ref[pl.ds(2 * p + h, 1), :])).astype(bf16)
            gk_one = mul(grad_scores, qs[h])
            gv_one = mul(probs.astype(bf16), gs[h])
            gk = gk_one if gk is None else gk + gk_one
            gv = gv_one if gv is None else gv + gv_one
            rows = pl.ds(pl.multiple_of((2 * p + h) * HEAD_DIM, HEAD_DIM), HEAD_DIM)
            gqt[rows, :] = mul(kt[rows, :], grad_scores).astype(bf16)
        gk_ref[:, at] = gk.astype(bf16)
        gv_ref[:, at] = gv.astype(bf16)
        return carry

    lax.fori_loop(0, HEADS // 2, pair, 0, unroll=2)
    gq_ref[...] = gqt[...].T


def feed_forward(
    x, cb, cot, wo_ref, wi_ref, wu_ref, vec_ref, out_ref, mid_ref, gf_ref, ga_ref, gc_ref, d_ref, h_ref, gu_ref, sums_ref
):
    width = x.shape[-1]
    chunks = wi_ref.shape[1] // width
    gain_1, gain_2 = row(vec_ref, GAIN_1), row(vec_ref, GAIN_2)
    normed_1, inverse_1 = normalize(x.astype(f32) + (mul(cb, wo_ref[...]) + row(vec_ref, B_OUT)))
    middle = normed_1 * gain_1 + row(vec_ref, BIAS_1)
    mid = middle.astype(bf16)
    mid_ref[...] = mid
    total = middle + row(vec_ref, B_OUTER)
    for c in range(chunks):
        at = slice(c * width, (c + 1) * width)
        inner = mul(mid, wi_ref[:, at]) + row(vec_ref, B_INNER + c)
        cdf = 0.5 + 0.5 * lax.erf(inner * (0.5**0.5))
        hidden = (inner * cdf).astype(bf16)
        h_ref[:, at] = hidden
        slope = cdf + inner * (jnp.exp(inner * inner * -0.5) * ((0.5 / jnp.pi) ** 0.5))
        gu_ref[:, at] = slope.astype(bf16)
        total = total + mul(hidden, wu_ref[at, :])
    normed_2, inverse_2 = normalize(total)
    out_ref[...] = (normed_2 * gain_2 + row(vec_ref, BIAS_2)).astype(bf16)
    grad = cot.astype(f32)
    sums_ref[GAIN_2 : GAIN_2 + 1, :] += column_sum(grad * normed_2)
    sums_ref[BIAS_2 : BIAS_2 + 1, :] += column_sum(grad)
    grad_2 = norm_back(grad, normed_2, inverse_2, gain_2)
    gf = grad_2.astype(bf16)
    gf_ref[...] = gf
    sums_ref[B_OUTER : B_OUTER + 1, :] += column_sum(gf)
    grad_mid = grad_2
    for c in range(chunks):
        at = slice(c * width, (c + 1) * width)
        gu = (mul(gf, wu_ref[at, :], NT) * gu_ref[:, at].astype(f32)).astype(bf16)
        gu_ref[:, at] = gu
        sums_ref[B_INNER + c : B_INNER + c + 1, :] += column_sum(gu)
        grad_mid = grad_mid + mul(gu, wi_ref[:, at], NT)
    sums_ref[GAIN_1 : GAIN_1 + 1, :] += column_sum(grad_mid * normed_1)
    sums_ref[BIAS_1 : BIAS_1 + 1, :] += column_sum(grad_mid)
    ga = norm_back(grad_mid, normed_1, inverse_1, gain_1).astype(bf16)
    ga_ref[...] = ga
    sums_ref[B_OUT : B_OUT + 1, :] += column_sum(ga)
    gc = mul(ga, wo_ref[...], NT).astype(bf16)
    gc_ref[...] = gc
    product = gc.astype(f32) * cb.astype(f32)
    high = product.astype(bf16)
    low = (product - high.astype(f32)).astype(bf16)
    head = lax.broadcasted_iota(jnp.int32, (STAT_ROWS, width), 0)
    column = lax.broadcasted_iota(jnp.int32, (STAT_ROWS, width), 1)
    pick = jnp.where(column // HEAD_DIM == head, 1.0, 0.0).astype(bf16)
    d_ref[...] = mul(pick, high, NT) + mul(pick, low, NT)


def spec(shape, pipelined=True):
    zeros = (0,) * (len(shape) - 1)
    if pipelined:
        return pl.BlockSpec(shape, lambda i: (i,) + zeros)
    return pl.BlockSpec(shape, lambda i: (0,) + zeros)


def whole_vmem():
    return pl.BlockSpec(memory_space=pltpu.VMEM)


def params():
    return pltpu.CompilerParams(vmem_limit_bytes=VMEM_BYTES, dimension_semantics=("arbitrary",))


def attention_call(x, w_qkv, vec):
    count, length, width = x.shape
    block = (None, length, width)

    def kernel(x_ref, w_ref, vec_ref, q_ref, k_ref, v_ref, c_ref, l_ref, stat):
        project(x_ref[...], w_ref, vec_ref, q_ref, k_ref, v_ref)
        attend(q_ref, k_ref, v_ref, c_ref, l_ref, stat)

    seq = jax.ShapeDtypeStruct(x.shape, bf16)
    return pl.pallas_call(
        kernel,
        grid=(count,),
        in_specs=[spec(block), whole_vmem(), whole_vmem()],
        out_specs=[spec(block)] * 4 + [spec((None, STAT_ROWS, length))],
        out_shape=[seq] * 4 + [jax.ShapeDtypeStruct((count, STAT_ROWS, length), f32)],
        scratch_shapes=[pltpu.VMEM((length, 128), f32)],
        compiler_params=params(),
        name="attention",
    )(x, w_qkv, vec)


def feed_forward_call(x, cb, cot, w_out, w_inner, w_outer, vec):
    count, length, width = x.shape
    inner = w_inner.shape[1]
    block, wide = (None, length, width), (None, length, inner)

    def kernel(x_ref, cb_ref, cot_ref, wo, wi, wu, vec_ref, out, mid, gf, ga, gc, d, h, gu, sums):
        @pl.when(pl.program_id(0) == 0)
        def _():
            sums[...] = jnp.zeros_like(sums)

        feed_forward(
            x_ref[...], cb_ref[...], cot_ref[...], wo, wi, wu, vec_ref, out, mid, gf, ga, gc, d, h, gu, sums
        )

    seq = jax.ShapeDtypeStruct(x.shape, bf16)
    seq_wide = jax.ShapeDtypeStruct((count, length, inner), bf16)
    return pl.pallas_call(
        kernel,
        grid=(count,),
        in_specs=[spec(block)] * 3 + [whole_vmem()] * 4,
        out_specs=[spec(block)] * 5
        + [spec((None, STAT_ROWS, length)), spec(wide), spec(wide), spec((16, width), False)],
        out_shape=[seq] * 5
        + [
            jax.ShapeDtypeStruct((count, STAT_ROWS, length), f32),
            seq_wide,
            seq_wide,
            jax.ShapeDtypeStruct((16, width), f32),
        ],
        compiler_params=params(),
        name="feed_forward",
    )(x, cb, cot, w_out, w_inner, w_outer, vec)


def weight_grad_call(left, right, over_left):
    tokens, rows = left.shape
    columns = right.shape[1]
    step = min(rows, columns)

    def kernel(left_ref, right_ref, out_ref):
        out_ref[...] = mul(left_ref[...], right_ref[...], TN).astype(bf16)

    if over_left:
        grid, left_map, right_map, out_map = rows // step, lambda i: (0, i), lambda i: (0, 0), lambda i: (i, 0)
    else:
        grid, left_map, right_map, out_map = columns // step, lambda i: (0, 0), lambda i: (0, i), lambda i: (0, i)
    return pl.pallas_call(
        kernel,
        grid=(grid,),
        in_specs=[pl.BlockSpec((tokens, step), left_map), pl.BlockSpec((tokens, step), right_map)],
        out_specs=pl.BlockSpec((step, step), out_map),
        out_shape=jax.ShapeDtypeStruct((rows, columns), bf16),
        compiler_params=params(),
        name="weight_grad",
    )(left, right)


def attention_back_call(x, q, k, v, gc, ga, stat_l, stat_d, w_qkv):
    count, length, width = x.shape
    block = (None, length, width)

    def kernel(x_ref, q_ref, k_ref, v_ref, gc_ref, ga_ref, l_ref, d_ref, w_ref, gx_ref, gw_ref, sums_ref, kt, gqt, gq, gk, gv, total):
        step = pl.program_id(0)

        @pl.when(step == 0)
        def _():
            sums_ref[...] = jnp.zeros_like(sums_ref)
            total[...] = jnp.zeros_like(total)

        attend_back(q_ref, k_ref, v_ref, gc_ref, l_ref, d_ref, gq, gk, gv, kt, gqt)
        sums_ref[B_QUERY : B_QUERY + 1, :] += column_sum(gq[...])
        sums_ref[B_VALUE : B_VALUE + 1, :] += column_sum(gv[...])
        grad = ga_ref[...].astype(f32)
        x = x_ref[...]
        for i, ref in enumerate((gq, gk, gv)):
            at = slice(i * width, (i + 1) * width)
            grad = grad + mul(ref[...], w_ref[:, at], NT)
            total[:, at] += mul(x, ref[...], TN)
        gx_ref[...] = grad.astype(bf16)

        @pl.when(step == count - 1)
        def _():
            gw_ref[...] = total[...].astype(bf16)

    seq_scratch = pltpu.VMEM((length, width), bf16)
    return pl.pallas_call(
        kernel,
        grid=(count,),
        in_specs=[spec(block)] * 6 + [spec((None, STAT_ROWS, length))] * 2 + [whole_vmem()],
        out_specs=[spec(block), spec((width, 3 * width), False), spec((16, width), False)],
        out_shape=[
            jax.ShapeDtypeStruct(x.shape, bf16),
            jax.ShapeDtypeStruct((width, 3 * width), bf16),
            jax.ShapeDtypeStruct((16, width), f32),
        ],
        scratch_shapes=[pltpu.VMEM((width, length), bf16)] * 2 + [seq_scratch] * 3 + [pltpu.VMEM((width, 3 * width), f32)],
        compiler_params=params(),
        name="attention_back",
    )(x, q, k, v, gc, ga, stat_l, stat_d, w_qkv)


def forward_call(tokens, span_mask, cotangent, w_query, w_key, w_value, w_out, w_inner, w_outer, table, sizes):
    depth_z, depth_y, cores = sizes
    rows, stretch, width = tokens.shape
    inner = w_inner.shape[1]
    part, outer_part = w_query.shape[0], w_outer.shape[0]
    devices = depth_z * depth_y * cores
    count, length = rows // 2, 2 * stretch
    chunks = inner // width
    qkv_width, mid_width = 3 * width, width + inner
    last = depth_z - 1
    ARRAYS = 4

    def kernel(
        tokens_ref, mask_ref, cot_ref, wq_in, wk_in, wv_in, wo_in, wi_in, wu_in, table_in,
        x_out, q_out, k_out, v_out, cb_out, l_out, o_out, mid_out, gf_out, ga_out, gc_out, d_out, h_out, gu_out,
        sums_out, w_qkv_out,
        w_qkv, w_mid, w_up, tables, vec, x_all, cot_all, cot_away, cb_all, q_s, k_s, v_s, l_s, stat, o_s, mid_s, gf_s,
        ga_s, gc_s, d_s, h_s, gu_s,
        up_send, down_send, z_recv, y_send, y_recv, c_send, c_recv, t_send, t_recv, g_send, g_recv, in_sem, out_sem,
    ):
        b, k = lax.axis_index("batch"), lax.axis_index("blk")
        z, y, c = b // (depth_y * cores), (b // cores) % depth_y, b % cores

        def at(z_, y_, c_):
            return (z_ * depth_y + y_) * cores + c_

        barrier = pltpu.get_barrier_semaphore()

        def greet(device):
            pl.semaphore_signal(barrier, inc=1, device_id=device, device_id_type=pl.DeviceIdType.MESH)

        greet((b, 1 - k))
        greet((at(z, 1 - y, c), k))
        greet((at(z, y, 1 - c), k))

        @pl.when(z < last)
        def _():
            greet((at(z + 1, y, c), k))

        @pl.when(z > 0)
        def _():
            greet((at(z - 1, y, c), k))

        shard = pl.ds(b * part, part)
        mine = pl.ds(pl.multiple_of(k * stretch, stretch), stretch)
        loads = [
            pltpu.make_async_copy(wq_in, w_qkv.at[shard, 0:width], in_sem.at[0]),
            pltpu.make_async_copy(wk_in, w_qkv.at[shard, width : 2 * width], in_sem.at[1]),
            pltpu.make_async_copy(wv_in, w_qkv.at[shard, 2 * width : 3 * width], in_sem.at[2]),
            pltpu.make_async_copy(wo_in, w_mid.at[shard, 0:width], in_sem.at[3]),
            pltpu.make_async_copy(wi_in, w_mid.at[shard, width:mid_width], in_sem.at[4]),
            pltpu.make_async_copy(wu_in, w_up.at[pl.ds(b * outer_part, outer_part)], in_sem.at[5]),
            pltpu.make_async_copy(cot_ref.at[pl.ds(k * count, count)], cot_all.at[:, mine], in_sem.at[6]),
            pltpu.make_async_copy(cot_ref.at[pl.ds((1 - k) * count, count)], cot_away, in_sem.at[7]),
            pltpu.make_async_copy(tokens_ref.at[pl.ds(k * count, count)], x_all.at[:, mine], in_sem.at[8]),
        ]
        for load in loads:
            load.start()

        raw = table_in[...]
        rolled = pltpu.roll(raw, b * part, 1)
        wide = pltpu.roll(raw[B_INNER : B_INNER + 1, :], (b % (devices // chunks)) * outer_part, 1)
        line = lax.broadcasted_iota(jnp.int32, raw.shape, 0)
        own_table = jnp.where(line < B_INNER, rolled, 0.0)
        own_table = jnp.where(line == B_INNER + b // (devices // chunks), wide, own_table)
        tables[b] = own_table.astype(bf16)

        def piece(array, z_, y_, c_):
            d = at(z_, y_, c_)
            if array == 0:
                return w_qkv.at[pl.ds(d * part, part)]
            if array == 1:
                return tables.at[d]
            if array == 2:
                return w_mid.at[pl.ds(d * part, part)]
            return w_up.at[pl.ds(d * outer_part, outer_part)]

        def remote(ref, device, send, recv):
            return pltpu.make_async_remote_copy(
                src_ref=ref, dst_ref=ref, send_sem=send, recv_sem=recv, device_id=device, device_id_type=pl.DeviceIdType.MESH
            )

        def up(a, zs):
            return remote(piece(a, zs, y, c), (at(z + 1, y, c), k), up_send.at[a, zs], z_recv.at[a, zs])

        def down(a, zs):
            return remote(piece(a, zs, y, c), (at(z - 1, y, c), k), down_send.at[a, zs], z_recv.at[a, zs])

        def across(a, zs):
            return remote(piece(a, zs, y, c), (at(z, 1 - y, c), k), y_send.at[a, zs], y_recv.at[a, zs])

        def core(a, zs, ys):
            i = zs * depth_y + ys
            return remote(piece(a, zs, ys, c), (at(z, y, 1 - c), k), c_send.at[a, i], c_recv.at[a, i])

        def arrived(ref, sem):
            remote(ref, (b, 1 - k), sem, sem).wait_recv()

        def begin(a):
            @pl.when(z < last)
            def _():
                up(a, z).start()

            @pl.when(z > 0)
            def _():
                down(a, z).start()

            across(a, z).start()
            core(a, z, y).start()

        def hop(a, step):
            @pl.when(z >= step)
            def _():
                zs = z - step
                arrived(piece(a, zs, y, c), z_recv.at[a, zs])

                @pl.when(z < last)
                def _():
                    up(a, zs).start()

                across(a, zs).start()
                core(a, zs, y).start()

            @pl.when(z + step <= last)
            def _():
                zs = z + step
                arrived(piece(a, zs, y, c), z_recv.at[a, zs])

                @pl.when(z > 0)
                def _():
                    down(a, zs).start()

                across(a, zs).start()
                core(a, zs, y).start()

        def relay(a, step):
            def one(zs):
                arrived(piece(a, zs, 1 - y, c), y_recv.at[a, zs])
                core(a, zs, 1 - y).start()

            if step == 0:
                one(z)
                return

            @pl.when(z >= step)
            def _():
                one(z - step)

            @pl.when(z + step <= last)
            def _():
                one(z + step)

        def complete(a):
            for zs in range(depth_z):
                for ys in range(depth_y):
                    arrived(piece(a, zs, ys, 1 - c), c_recv.at[a, zs * depth_y + ys])

        def sent(a):
            for zs in range(depth_z):
                @pl.when((z < last) & (zs <= z))
                def _():
                    up(a, zs).wait_send()

                @pl.when((z > 0) & (zs >= z))
                def _():
                    down(a, zs).wait_send()

                across(a, zs).wait_send()
                for ys in range(depth_y):
                    core(a, zs, ys).wait_send()

        def token_copy(s):
            return pltpu.make_async_remote_copy(
                src_ref=tokens_ref.at[(1 - k) * count + s],
                dst_ref=x_all.at[s, mine],
                send_sem=t_send.at[s],
                recv_sem=t_recv.at[s],
                device_id=(b, 1 - k),
                device_id_type=pl.DeviceIdType.MESH,
            )

        def grad_copy(s):
            return pltpu.make_async_remote_copy(
                src_ref=cot_away.at[s],
                dst_ref=cot_all.at[s, mine],
                send_sem=g_send.at[s],
                recv_sem=g_recv.at[s],
                device_id=(b, 1 - k),
                device_id_type=pl.DeviceIdType.MESH,
            )

        def put(i, src, dst):
            return pltpu.make_async_copy(src, dst, out_sem.at[i])

        partners = 3 + (z < last).astype(jnp.int32) + (z > 0).astype(jnp.int32)
        pl.semaphore_wait(barrier, partners)
        token_copy(0).start()
        begin(1)
        for i in range(3):
            loads[i].wait()
        begin(0)
        token_copy(1).start()

        for i in (6, 7):
            loads[i].wait()
        mask = mask_ref[...].astype(f32)
        own, away = jnp.where(k == 0, mask[:count], mask[count:]), jnp.where(k == 0, mask[count:], mask[:count])
        columns = jnp.concatenate([own, away], 0).T
        for s in range(count):
            cot_all[s, mine, :] = (cot_all[s, mine, :].astype(f32) * columns[:, s : s + 1]).astype(bf16)
            cot_away[s] = (cot_away[s].astype(f32) * columns[:, count + s : count + s + 1]).astype(bf16)

        for i in (3, 4, 5, 8):
            loads[i].wait()
        relay(0, 0)
        relay(1, 0)
        for step in range(1, depth_z):
            for a in (0, 1):
                hop(a, step)
        begin(2)
        for step in range(1, depth_z):
            for a in (0, 1):
                relay(a, step)
        complete(0)
        complete(1)
        vec[...] = jnp.sum(tables[...].astype(f32), 0)
        save_w = put(0, w_qkv, w_qkv_out)
        save_w.start()

        plan = {
            (0, 0): [],
            (0, 1): [lambda: hop(2, 1)],
            (0, 2): [lambda: relay(2, 0)],
            (1, 0): [lambda: hop(2, 2)],
            (1, 1): [lambda: relay(2, 1)],
            (1, 2): [lambda: hop(2, 3), lambda: begin(3)],
            (2, 0): [lambda: relay(2, 2)],
            (2, 1): [lambda: hop(3, 1)],
            (2, 2): [],
            (3, 0): [lambda: hop(3, 2), lambda: relay(2, 3)],
            (3, 1): [lambda: relay(3, 0)],
            (3, 2): [lambda: hop(3, 3)],
        }

        def pump(s, slot):
            for (when, where), steps in plan.items():
                if where == slot and steps:
                    @pl.when(s == when)
                    def _():
                        for step in steps:
                            step()

        def first(s, carry):
            arrived(x_all.at[s, pl.ds(pl.multiple_of((1 - k) * stretch, stretch), stretch)], t_recv.at[s])

            @pl.when(s + 2 < count)
            def _():
                token_copy(s + 2).start()

            @pl.when(s + 2 >= count)
            def _():
                grad_copy(s + 2 - count).start()

            saves = [
                put(1, x_all.at[s], x_out.at[s]),
                put(2, q_s, q_out.at[s]),
                put(3, k_s, k_out.at[s]),
                put(4, v_s, v_out.at[s]),
                put(5, cb_all.at[s], cb_out.at[s]),
                put(6, l_s, l_out.at[s]),
            ]

            @pl.when(s > 0)
            def _():
                for save in saves:
                    save.wait()

            project(x_all[s], w_qkv, vec, q_s, k_s, v_s)
            for save in saves[:4]:
                save.start()
            pump(s, 0)
            stat[...] = jnp.zeros_like(stat)
            attend_pairs(q_s, k_s, v_s, cb_all.at[s], stat, 0, HEADS // 4)
            pump(s, 1)
            attend_pairs(q_s, k_s, v_s, cb_all.at[s], stat, HEADS // 4, HEADS // 2)
            l_s[...] = stat[...].T[:STAT_ROWS]
            for save in saves[4:]:
                save.start()
            pump(s, 2)
            return carry

        lax.fori_loop(0, count, first, 0)
        for i, (src, dst) in enumerate(((x_all.at[0], x_out.at[0]), (q_s, q_out.at[0]), (k_s, k_out.at[0]), (v_s, v_out.at[0]), (cb_all.at[0], cb_out.at[0]), (l_s, l_out.at[0]))):
            put(i + 1, src, dst).wait()
        save_w.wait()
        for step in range(1, depth_z):
            relay(3, step)
        complete(2)
        complete(3)

        sums_out[...] = jnp.zeros_like(sums_out)

        def second(s, carry):
            arrived(cot_all.at[s, pl.ds(pl.multiple_of((1 - k) * stretch, stretch), stretch)], g_recv.at[s])

            @pl.when(s + 2 < count)
            def _():
                grad_copy(s + 2).start()

            saves = [
                put(i + 1, src, dst.at[s])
                for i, (src, dst) in enumerate(
                    (
                        (o_s, o_out), (mid_s, mid_out), (gf_s, gf_out), (ga_s, ga_out), (gc_s, gc_out), (d_s, d_out),
                        (h_s, h_out), (gu_s, gu_out),
                    )
                )
            ]

            @pl.when(s > 0)
            def _():
                for save in saves:
                    save.wait()

            feed_forward(
                x_all[s], cb_all[s], cot_all[s], w_mid.at[:, 0:width], w_mid.at[:, width:mid_width], w_up, vec,
                o_s, mid_s, gf_s, ga_s, gc_s, d_s, h_s, gu_s, sums_out,
            )
            for save in saves:
                save.start()
            return carry

        lax.fori_loop(0, count, second, 0)
        for i, (src, dst) in enumerate(
            (
                (o_s, o_out), (mid_s, mid_out), (gf_s, gf_out), (ga_s, ga_out), (gc_s, gc_out), (d_s, d_out),
                (h_s, h_out), (gu_s, gu_out),
            )
        ):
            put(i + 1, src, dst.at[0]).wait()
        for s in range(count):
            token_copy(s).wait_send()
            grad_copy(s).wait_send()
        for a in range(ARRAYS):
            sent(a)

    seq = jax.ShapeDtypeStruct((count, length, width), bf16)
    seq_wide = jax.ShapeDtypeStruct((count, length, inner), bf16)
    stat_shape = jax.ShapeDtypeStruct((count, STAT_ROWS, length), f32)
    hbm = pl.BlockSpec(memory_space=pl.ANY)
    one = pltpu.VMEM((length, width), bf16)
    one_wide = pltpu.VMEM((length, inner), bf16)
    all_seq = pltpu.VMEM((count, length, width), bf16)
    stat_one = pltpu.VMEM((STAT_ROWS, length), f32)
    dma = pltpu.SemaphoreType.DMA
    return pl.pallas_call(
        kernel,
        in_specs=[hbm, whole_vmem()] + [hbm] * 7 + [whole_vmem()],
        out_specs=[hbm] * 14 + [whole_vmem(), hbm],
        out_shape=[seq] * 5 + [stat_shape] + [seq] * 5 + [stat_shape, seq_wide, seq_wide]
        + [jax.ShapeDtypeStruct((16, width), f32), jax.ShapeDtypeStruct((width, qkv_width), bf16)],
        scratch_shapes=[
            pltpu.VMEM((width, qkv_width), bf16),
            pltpu.VMEM((width, mid_width), bf16),
            pltpu.VMEM((inner, width), bf16),
            pltpu.VMEM((devices, 16, width), bf16),
            pltpu.VMEM((16, width), f32),
            all_seq, all_seq,
            pltpu.VMEM((count, stretch, width), bf16),
            all_seq,
            one, one, one, stat_one, pltpu.VMEM((length, 128), f32),
            one, one, one, one, one, stat_one, one_wide, one_wide,
            dma((ARRAYS, depth_z)), dma((ARRAYS, depth_z)), dma((ARRAYS, depth_z)),
            dma((ARRAYS, depth_z)), dma((ARRAYS, depth_z)),
            dma((ARRAYS, depth_z * depth_y)), dma((ARRAYS, depth_z * depth_y)),
            dma((count,)), dma((count,)), dma((count,)), dma((count,)), dma((9,)), dma((9,)),
        ],
        compiler_params=pltpu.CompilerParams(collective_id=1, has_side_effects=True, vmem_limit_bytes=VMEM_BYTES),
        name="forward",
    )(tokens, span_mask, cotangent, w_query, w_key, w_value, w_out, w_inner, w_outer, table)


def pack_shard(w_query, w_key, w_value, w_out, w_inner, w_outer, vectors):
    width = w_query.shape[1]
    inner_parts = [w_inner[:, i : i + width] for i in range(0, w_inner.shape[1], width)]
    small = jnp.concatenate(vectors)
    body_rows = sum(part.shape[0] for part in (w_query, w_key, w_value, w_out, w_outer, *inner_parts))
    rows = -(-(body_rows + 1) // 16) * 16
    tail = jnp.zeros(((rows - body_rows) * width,), small.dtype).at[: small.shape[0]].set(small)
    return jnp.concatenate(
        [w_query, w_key, w_value, w_out, *inner_parts, w_outer, tail.reshape(-1, width)]
    )


def vec_table(small, vec_names_sizes):
    rows, at = [], 0
    for size in vec_names_sizes:
        rows.append(small[:, at : at + size].reshape(-1))
        at += size
    return rows


def gather_weights(w_query, w_key, w_value, w_out, w_inner, w_outer, vectors):
    part, width = w_query.shape
    outer_part = w_outer.shape[0]
    chunks = w_inner.shape[1] // width
    sizes = [vector.shape[0] for vector in vectors]
    packed = pack_shard(w_query, w_key, w_value, w_out, w_inner, w_outer, vectors)
    gathered = lax.all_gather(packed, "batch", axis=0)

    def weight(at, count):
        return gathered[:, at : at + count].reshape(-1, width)

    squares = [weight(i * part, part) for i in range(4 + chunks)]
    outer_at = (4 + chunks) * part
    w_outer_all = weight(outer_at, outer_part)
    small = gathered[:, outer_at + outer_part :].reshape(gathered.shape[0], -1)
    vec = jnp.concatenate(vec_table(small, sizes)).reshape(-1, width).astype(f32)
    vec = jnp.concatenate([vec, jnp.zeros((16 - vec.shape[0], width), f32)])
    return jnp.concatenate(squares[:3], 1), squares[3], jnp.concatenate(squares[4:], 1), w_outer_all, vec


def body(
    tokens,
    span_mask,
    cotangent,
    w_query,
    b_query,
    w_key,
    w_value,
    b_value,
    w_out,
    b_out,
    gain_first,
    bias_first,
    w_inner,
    b_inner,
    w_outer,
    b_outer,
    gain_second,
    bias_second,
):
    rows, stretch, width = tokens.shape
    inner = w_inner.shape[1]
    part = w_query.shape[0]
    outer_part = w_outer.shape[0]
    vectors = (b_query, b_value, b_out, gain_first, bias_first, b_outer, gain_second, bias_second, b_inner)
    sizes = [vector.shape[0] for vector in vectors]

    devices = lax.axis_size("batch")
    chunks = inner // width
    swap = functools.partial(lax.all_to_all, axis_name="blk", tiled=True)
    outer_at = (4 + chunks) * part
    shard_rows = -(-(outer_at + outer_part + 1) // 16) * 16
    if (devices, lax.axis_size("blk")) == (16, 2):
        table = sum(
            lax.pad(
                vector.astype(f32).reshape(1, -1), f32(0), ((i, 15 - i, 0), (0, width - vector.shape[0], 0))
            )
            for i, vector in enumerate(vectors)
        )
        x, q, k, v, cb, stat_l, out, mid, gf, ga, gc, stat_d, hidden, gu, sums_ffn, w_qkv = forward_call(
            tokens, span_mask, cotangent, w_query, w_key, w_value, w_out, w_inner, w_outer, table, (4, 2, 2)
        )
    else:
        w_qkv, w_out_all, w_inner_all, w_outer_all, vec = gather_weights(
            w_query, w_key, w_value, w_out, w_inner, w_outer, vectors
        )
        masked = cotangent * span_mask[..., None].astype(bf16)
        x = swap(tokens, split_axis=0, concat_axis=1)
        cot = swap(masked, split_axis=0, concat_axis=1)
        q, k, v, cb, stat_l = attention_call(x, w_qkv, vec)
        out, mid, gf, ga, gc, stat_d, hidden, gu, sums_ffn = feed_forward_call(
            x, cb, cot, w_out_all, w_inner_all, w_outer_all, vec
        )
    gx, gw_qkv, sums_att = attention_back_call(x, q, k, v, gc, ga, stat_l, stat_d, w_qkv)
    output = swap(out, split_axis=1, concat_axis=0)
    grad_tokens = swap(gx, split_axis=1, concat_axis=0)

    def flat(values):
        return values.reshape(-1, values.shape[-1])

    gw_out = weight_grad_call(flat(cb), flat(ga), False)
    gw_inner = weight_grad_call(flat(mid), flat(gu), False)
    gw_outer = weight_grad_call(flat(hidden), flat(gf), True)

    sums = sums_ffn + sums_att
    small_sums = [sums[i].reshape(devices, -1) for i in range(B_INNER)]
    small_sums.append(sums[B_INNER : B_INNER + chunks].reshape(devices, -1))
    tail = jnp.concatenate(small_sums, 1).astype(bf16)
    tail = jnp.pad(tail, ((0, 0), (0, (shard_rows - outer_at - outer_part) * width - tail.shape[1])))
    pieces = [gw_qkv[:, i * width : (i + 1) * width].reshape(devices, part, width) for i in range(3)]
    pieces.append(gw_out.reshape(devices, part, width))
    pieces += [gw_inner[:, i * width : (i + 1) * width].reshape(devices, part, width) for i in range(chunks)]
    pieces.append(gw_outer.reshape(devices, outer_part, width))
    pieces.append(tail.reshape(devices, -1, width))
    grads = jnp.concatenate(pieces, 1)
    share = lax.psum_scatter(grads, "batch", scatter_dimension=0, tiled=False)
    share = lax.psum(share, "blk").astype(f32)
    square = [share[i * part : (i + 1) * part] for i in range(4 + chunks)]
    share_small = share[outer_at + outer_part :].reshape(-1)
    small_out, at = [], 0
    for size in sizes:
        small_out.append(share_small[at : at + size])
        at += size
    (g_b_query, g_b_value, g_b_out, g_gain_1, g_bias_1, g_b_outer, g_gain_2, g_bias_2, g_b_inner) = small_out
    return (
        output,
        grad_tokens,
        square[0],
        g_b_query,
        square[1],
        square[2],
        g_b_value,
        square[3],
        g_b_out,
        g_gain_1,
        g_bias_1,
        jnp.concatenate(square[4:], 1),
        g_b_inner,
        share[outer_at : outer_at + outer_part],
        g_b_outer,
        g_gain_2,
        g_bias_2,
    )


def solution(mesh):
    block = P("batch", "blk", None)
    matrix, vector = P("batch", None), P("batch")
    weights = (
        matrix, vector, matrix, matrix, vector, matrix, vector, vector, vector, matrix, vector, matrix, vector, vector, vector,
    )
    return jax.shard_map(
        body,
        mesh=mesh,
        in_specs=(block, P("batch", "blk"), block) + weights,
        out_specs=(block, block) + weights,
        check_vma=False,
    )
```

```python
import functools

import jax
import jax.numpy as jnp
from jax import lax
from jax.experimental import pallas as pl
from jax.experimental.pallas import tpu as pltpu
from jax.sharding import PartitionSpec as P

HEADS = 12
HEAD_DIM = 64
PAIR = 2 * HEAD_DIM
STAT_ROWS = 16
VMEM_BYTES = 60 * 2**20

epsilon = 1e-06
bf16 = jnp.bfloat16
f32 = jnp.float32

NN = (((1,), (0,)), ((), ()))
NT = (((1,), (1,)), ((), ()))
TN = (((0,), (0,)), ((), ()))

B_QUERY, B_VALUE, B_OUT, GAIN_1, BIAS_1, B_OUTER, GAIN_2, BIAS_2, B_INNER = range(9)


def mul(left, right, dims=NN):
    return lax.dot_general(left, right, dims, preferred_element_type=f32)


def row(ref, index):
    return ref[index : index + 1, :]


def halves(block):
    lane = lax.broadcasted_iota(jnp.int32, block.shape, 1)
    zero = jnp.zeros_like(block)
    return jnp.where(lane < HEAD_DIM, block, zero), jnp.where(lane < HEAD_DIM, zero, block)


def pair_at(p):
    return pl.ds(pl.multiple_of(p * PAIR, PAIR), PAIR)


def normalize(values):
    center = values - jnp.mean(values, -1, keepdims=True)
    inverse = lax.rsqrt(jnp.mean(center * center, -1, keepdims=True) + epsilon)
    return center * inverse, inverse


def norm_back(grad, normed, inverse, gain):
    scaled = grad * gain
    return inverse * (
        scaled
        - jnp.mean(scaled, -1, keepdims=True)
        - normed * jnp.mean(scaled * normed, -1, keepdims=True)
    )


def column_sum(values):
    return jnp.sum(values.astype(f32), 0, keepdims=True)


def project(x, w_ref, vec_ref, q_ref, k_ref, v_ref):
    width = x.shape[-1]
    q = (mul(x, w_ref[:, :width]) + row(vec_ref, B_QUERY)).astype(bf16)
    q_ref[...] = q * bf16(HEAD_DIM**-0.5)
    k_ref[...] = mul(x, w_ref[:, width : 2 * width]).astype(bf16)
    v_ref[...] = (mul(x, w_ref[:, 2 * width :]) + row(vec_ref, B_VALUE)).astype(bf16)


def attend_pairs(q_ref, k_ref, v_ref, c_ref, stat, first, end):
    lane = lax.broadcasted_iota(jnp.int32, stat.shape, 1)

    def pair(p, carry):
        at = pair_at(p)
        q2, k2, v2 = q_ref[:, at], k_ref[:, at], v_ref[:, at]
        context = None
        for h, (k_one, v_one) in enumerate(zip(halves(k2), halves(v2))):
            scores = mul(q2, k_one, NT)
            best = jnp.max(scores, 1, keepdims=True)
            weights = jnp.exp(scores - best)
            total = jnp.sum(weights, 1, keepdims=True)
            part = mul(weights.astype(bf16), v_one) * (1.0 / total)
            context = part if context is None else context + part
            stat[...] = jnp.where(lane == 2 * p + h, best + jnp.log(total), stat[...])
        c_ref[:, at] = context.astype(bf16)
        return carry

    lax.fori_loop(first, end, pair, 0, unroll=3)


def attend(q_ref, k_ref, v_ref, c_ref, l_ref, stat):
    stat[...] = jnp.zeros_like(stat)
    attend_pairs(q_ref, k_ref, v_ref, c_ref, stat, 0, HEADS // 2)
    l_ref[...] = stat[...].T[:STAT_ROWS]


def attend_back(q_ref, k_ref, v_ref, g_ref, l_ref, d_ref, out_ref, kt, gqt, first, pairs):
    part = pairs * PAIR
    columns = pl.ds(pl.multiple_of(first * PAIR, PAIR), part)
    kt[...] = (k_ref[:, columns] * bf16(HEAD_DIM**-0.5)).T
    for p in range(pairs):
        at = pair_at(first + p)
        q2, g2 = q_ref[:, at], g_ref[:, at]
        ks, vs = halves(k_ref[:, at]), halves(v_ref[:, at])
        qs, gs = halves(q2), halves(g2)
        gk = gv = None
        for h in range(2):
            head = 2 * (first + p) + h
            probs = jnp.exp(mul(ks[h], q2, NT) - l_ref[pl.ds(head, 1), :])
            grad_probs = mul(vs[h], g2, NT)
            grad_scores = (probs * (grad_probs - d_ref[pl.ds(head, 1), :])).astype(bf16)
            gk_one = mul(grad_scores, qs[h])
            gv_one = mul(probs.astype(bf16), gs[h])
            gk = gk_one if gk is None else gk + gk_one
            gv = gv_one if gv is None else gv + gv_one
            rows = slice((2 * p + h) * HEAD_DIM, (2 * p + h + 1) * HEAD_DIM)
            gqt[rows, :] = mul(kt[rows, :], grad_scores).astype(bf16)
        out_ref[:, part + p * PAIR : part + (p + 1) * PAIR] = gk.astype(bf16)
        out_ref[:, 2 * part + p * PAIR : 2 * part + (p + 1) * PAIR] = gv.astype(bf16)
    out_ref[:, :part] = gqt[...].T


def feed_forward(
    x, cb, cot, wo_ref, wi_ref, wu_ref, vec_ref, out_ref, mid_ref, gf_ref, ga_ref, gc_ref, d_ref, h_ref, gu_ref, sums_ref
):
    width = x.shape[-1]
    chunks = wi_ref.shape[1] // width
    gain_1, gain_2 = row(vec_ref, GAIN_1), row(vec_ref, GAIN_2)
    normed_1, inverse_1 = normalize(x.astype(f32) + (mul(cb, wo_ref[...]) + row(vec_ref, B_OUT)))
    middle = normed_1 * gain_1 + row(vec_ref, BIAS_1)
    mid = middle.astype(bf16)
    mid_ref[...] = mid
    total = middle + row(vec_ref, B_OUTER)
    for c in range(chunks):
        at = slice(c * width, (c + 1) * width)
        inner = mul(mid, wi_ref[:, at]) + row(vec_ref, B_INNER + c)
        cdf = 0.5 + 0.5 * lax.erf(inner * (0.5**0.5))
        hidden = (inner * cdf).astype(bf16)
        h_ref[:, at] = hidden
        slope = cdf + inner * (jnp.exp(inner * inner * -0.5) * ((0.5 / jnp.pi) ** 0.5))
        gu_ref[:, at] = slope.astype(bf16)
        total = total + mul(hidden, wu_ref[at, :])
    normed_2, inverse_2 = normalize(total)
    out_ref[...] = (normed_2 * gain_2 + row(vec_ref, BIAS_2)).astype(bf16)
    grad = cot.astype(f32)
    sums_ref[GAIN_2 : GAIN_2 + 1, :] += column_sum(grad * normed_2)
    sums_ref[BIAS_2 : BIAS_2 + 1, :] += column_sum(grad)
    grad_2 = norm_back(grad, normed_2, inverse_2, gain_2)
    gf = grad_2.astype(bf16)
    gf_ref[...] = gf
    sums_ref[B_OUTER : B_OUTER + 1, :] += column_sum(gf)
    grad_mid = grad_2
    for c in range(chunks):
        at = slice(c * width, (c + 1) * width)
        gu = (mul(gf, wu_ref[at, :], NT) * gu_ref[:, at].astype(f32)).astype(bf16)
        gu_ref[:, at] = gu
        sums_ref[B_INNER + c : B_INNER + c + 1, :] += column_sum(gu)
        grad_mid = grad_mid + mul(gu, wi_ref[:, at], NT)
    sums_ref[GAIN_1 : GAIN_1 + 1, :] += column_sum(grad_mid * normed_1)
    sums_ref[BIAS_1 : BIAS_1 + 1, :] += column_sum(grad_mid)
    ga = norm_back(grad_mid, normed_1, inverse_1, gain_1).astype(bf16)
    ga_ref[...] = ga
    sums_ref[B_OUT : B_OUT + 1, :] += column_sum(ga)
    gc = mul(ga, wo_ref[...], NT).astype(bf16)
    gc_ref[...] = gc
    product = gc.astype(f32) * cb.astype(f32)
    high = product.astype(bf16)
    low = (product - high.astype(f32)).astype(bf16)
    head = lax.broadcasted_iota(jnp.int32, (STAT_ROWS, width), 0)
    column = lax.broadcasted_iota(jnp.int32, (STAT_ROWS, width), 1)
    pick = jnp.where(column // HEAD_DIM == head, 1.0, 0.0).astype(bf16)
    d_ref[...] = mul(pick, high, NT) + mul(pick, low, NT)


def spec(shape, pipelined=True):
    zeros = (0,) * (len(shape) - 1)
    if pipelined:
        return pl.BlockSpec(shape, lambda i: (i,) + zeros)
    return pl.BlockSpec(shape, lambda i: (0,) + zeros)


def whole_vmem():
    return pl.BlockSpec(memory_space=pltpu.VMEM)


def params():
    return pltpu.CompilerParams(vmem_limit_bytes=VMEM_BYTES, dimension_semantics=("arbitrary",))


def attention_call(x, w_qkv, vec):
    count, length, width = x.shape
    block = (None, length, width)

    def kernel(x_ref, w_ref, vec_ref, q_ref, k_ref, v_ref, c_ref, l_ref, stat):
        project(x_ref[...], w_ref, vec_ref, q_ref, k_ref, v_ref)
        attend(q_ref, k_ref, v_ref, c_ref, l_ref, stat)

    seq = jax.ShapeDtypeStruct(x.shape, bf16)
    return pl.pallas_call(
        kernel,
        grid=(count,),
        in_specs=[spec(block), whole_vmem(), whole_vmem()],
        out_specs=[spec(block)] * 4 + [spec((None, STAT_ROWS, length))],
        out_shape=[seq] * 4 + [jax.ShapeDtypeStruct((count, STAT_ROWS, length), f32)],
        scratch_shapes=[pltpu.VMEM((length, 128), f32)],
        compiler_params=params(),
        name="attention",
    )(x, w_qkv, vec)


def feed_forward_call(x, cb, cot, w_out, w_inner, w_outer, vec):
    count, length, width = x.shape
    inner = w_inner.shape[1]
    block, wide = (None, length, width), (None, length, inner)

    def kernel(x_ref, cb_ref, cot_ref, wo, wi, wu, vec_ref, out, mid, gf, ga, gc, d, h, gu, sums):
        @pl.when(pl.program_id(0) == 0)
        def _():
            sums[...] = jnp.zeros_like(sums)

        feed_forward(
            x_ref[...], cb_ref[...], cot_ref[...], wo, wi, wu, vec_ref, out, mid, gf, ga, gc, d, h, gu, sums
        )

    seq = jax.ShapeDtypeStruct(x.shape, bf16)
    seq_wide = jax.ShapeDtypeStruct((count, length, inner), bf16)
    return pl.pallas_call(
        kernel,
        grid=(count,),
        in_specs=[spec(block)] * 3 + [whole_vmem()] * 4,
        out_specs=[spec(block)] * 5
        + [spec((None, STAT_ROWS, length)), spec(wide), spec(wide), spec((16, width), False)],
        out_shape=[seq] * 5
        + [
            jax.ShapeDtypeStruct((count, STAT_ROWS, length), f32),
            seq_wide,
            seq_wide,
            jax.ShapeDtypeStruct((16, width), f32),
        ],
        compiler_params=params(),
        name="feed_forward",
    )(x, cb, cot, w_out, w_inner, w_outer, vec)


def weight_grad_call(left, right, over_left):
    tokens, rows = left.shape
    columns = right.shape[1]
    step = min(rows, columns)

    def kernel(left_ref, right_ref, out_ref):
        out_ref[...] = mul(left_ref[...], right_ref[...], TN).astype(bf16)

    if over_left:
        grid, left_map, right_map, out_map = rows // step, lambda i: (0, i), lambda i: (0, 0), lambda i: (i, 0)
    else:
        grid, left_map, right_map, out_map = columns // step, lambda i: (0, 0), lambda i: (0, i), lambda i: (0, i)
    return pl.pallas_call(
        kernel,
        grid=(grid,),
        in_specs=[pl.BlockSpec((tokens, step), left_map), pl.BlockSpec((tokens, step), right_map)],
        out_specs=pl.BlockSpec((step, step), out_map),
        out_shape=jax.ShapeDtypeStruct((rows, columns), bf16),
        compiler_params=params(),
        name="weight_grad",
    )(left, right)


def attention_back_call(x, q, k, v, gc, ga, stat_l, stat_d, w_qkv):
    count, length, width = x.shape
    block = (None, length, width)
    pairs = HEADS // 2

    def kernel(x_ref, q_ref, k_ref, v_ref, gc_ref, ga_ref, l_ref, d_ref, w_ref, gx_ref, gw_ref, sums_ref, kt, gqt, g, total):
        step = pl.program_id(0)

        @pl.when(step == 0)
        def _():
            sums_ref[...] = jnp.zeros_like(sums_ref)
            total[...] = jnp.zeros_like(total)

        attend_back(q_ref, k_ref, v_ref, gc_ref, l_ref, d_ref, g, kt, gqt, 0, pairs)
        sums_ref[B_QUERY : B_QUERY + 1, :] += column_sum(g[:, :width])
        sums_ref[B_VALUE : B_VALUE + 1, :] += column_sum(g[:, 2 * width :])
        grad = ga_ref[...].astype(f32)
        x = x_ref[...]
        for i in range(3):
            at = slice(i * width, (i + 1) * width)
            grad = grad + mul(g[:, at], w_ref[:, at], NT)
            total[:, at] += mul(x, g[:, at], TN)
        gx_ref[...] = grad.astype(bf16)

        @pl.when(step == count - 1)
        def _():
            gw_ref[...] = total[...].astype(bf16)

    return pl.pallas_call(
        kernel,
        grid=(count,),
        in_specs=[spec(block)] * 6 + [spec((None, STAT_ROWS, length))] * 2 + [whole_vmem()],
        out_specs=[spec(block), spec((width, 3 * width), False), spec((16, width), False)],
        out_shape=[
            jax.ShapeDtypeStruct(x.shape, bf16),
            jax.ShapeDtypeStruct((width, 3 * width), bf16),
            jax.ShapeDtypeStruct((16, width), f32),
        ],
        scratch_shapes=[pltpu.VMEM((width, length), bf16)] * 2
        + [pltpu.VMEM((length, 3 * width), bf16), pltpu.VMEM((width, 3 * width), f32)],
        compiler_params=params(),
        name="attention_back",
    )(x, q, k, v, gc, ga, stat_l, stat_d, w_qkv)


def forward_call(tokens, span_mask, cotangent, w_query, w_key, w_value, w_out, w_inner, w_outer, table, sizes):
    depth_z, depth_y, cores = sizes
    rows, stretch, width = tokens.shape
    inner = w_inner.shape[1]
    part, outer_part = w_query.shape[0], w_outer.shape[0]
    devices = depth_z * depth_y * cores
    count, length = rows // 2, 2 * stretch
    chunks = inner // width
    qkv_width, mid_width = 3 * width, width + inner
    last = depth_z - 1
    ARRAYS = 4

    def kernel(
        tokens_ref, mask_ref, cot_ref, wq_in, wk_in, wv_in, wo_in, wi_in, wu_in, table_in,
        x_out, q_out, k_out, v_out, cb_out, l_out, o_out, mid_out, gf_out, ga_out, gc_out, d_out, h_out, gu_out,
        sums_out, w_qkv_out,
        w_qkv, w_mid, w_up, tables, vec, x_all, cot_all, cot_away, cb_all, q_s, k_s, v_s, l_s, stat, o_s, mid_s, gf_s,
        ga_s, gc_s, d_s, h_s, gu_s,
        up_send, down_send, z_recv, y_send, y_recv, c_send, c_recv, t_send, t_recv, g_send, g_recv, in_sem, out_sem,
    ):
        b, k = lax.axis_index("batch"), lax.axis_index("blk")
        z, y, c = b // (depth_y * cores), (b // cores) % depth_y, b % cores

        def at(z_, y_, c_):
            return (z_ * depth_y + y_) * cores + c_

        barrier = pltpu.get_barrier_semaphore()

        def greet(device):
            pl.semaphore_signal(barrier, inc=1, device_id=device, device_id_type=pl.DeviceIdType.MESH)

        greet((b, 1 - k))
        greet((at(z, 1 - y, c), k))
        greet((at(z, y, 1 - c), k))

        @pl.when(z < last)
        def _():
            greet((at(z + 1, y, c), k))

        @pl.when(z > 0)
        def _():
            greet((at(z - 1, y, c), k))

        shard = pl.ds(b * part, part)
        mine = pl.ds(pl.multiple_of(k * stretch, stretch), stretch)
        loads = [
            pltpu.make_async_copy(wq_in, w_qkv.at[shard, 0:width], in_sem.at[0]),
            pltpu.make_async_copy(wk_in, w_qkv.at[shard, width : 2 * width], in_sem.at[1]),
            pltpu.make_async_copy(wv_in, w_qkv.at[shard, 2 * width : 3 * width], in_sem.at[2]),
            pltpu.make_async_copy(wo_in, w_mid.at[shard, 0:width], in_sem.at[3]),
            pltpu.make_async_copy(wi_in, w_mid.at[shard, width:mid_width], in_sem.at[4]),
            pltpu.make_async_copy(wu_in, w_up.at[pl.ds(b * outer_part, outer_part)], in_sem.at[5]),
            pltpu.make_async_copy(cot_ref.at[pl.ds(k * count, count)], cot_all.at[:, mine], in_sem.at[6]),
            pltpu.make_async_copy(cot_ref.at[pl.ds((1 - k) * count, count)], cot_away, in_sem.at[7]),
            pltpu.make_async_copy(tokens_ref.at[pl.ds(k * count, count)], x_all.at[:, mine], in_sem.at[8]),
        ]
        for load in loads:
            load.start()

        raw = table_in[...]
        rolled = pltpu.roll(raw, b * part, 1)
        wide = pltpu.roll(raw[B_INNER : B_INNER + 1, :], (b % (devices // chunks)) * outer_part, 1)
        line = lax.broadcasted_iota(jnp.int32, raw.shape, 0)
        own_table = jnp.where(line < B_INNER, rolled, 0.0)
        own_table = jnp.where(line == B_INNER + b // (devices // chunks), wide, own_table)
        tables[b] = own_table.astype(bf16)

        def piece(array, z_, y_, c_):
            d = at(z_, y_, c_)
            if array == 0:
                return w_qkv.at[pl.ds(d * part, part)]
            if array == 1:
                return tables.at[d]
            if array == 2:
                return w_mid.at[pl.ds(d * part, part)]
            return w_up.at[pl.ds(d * outer_part, outer_part)]

        def remote(ref, device, send, recv):
            return pltpu.make_async_remote_copy(
                src_ref=ref, dst_ref=ref, send_sem=send, recv_sem=recv, device_id=device, device_id_type=pl.DeviceIdType.MESH
            )

        def up(a, zs):
            return remote(piece(a, zs, y, c), (at(z + 1, y, c), k), up_send.at[a, zs], z_recv.at[a, zs])

        def down(a, zs):
            return remote(piece(a, zs, y, c), (at(z - 1, y, c), k), down_send.at[a, zs], z_recv.at[a, zs])

        def across(a, zs):
            return remote(piece(a, zs, y, c), (at(z, 1 - y, c), k), y_send.at[a, zs], y_recv.at[a, zs])

        def core(a, zs, ys):
            i = zs * depth_y + ys
            return remote(piece(a, zs, ys, c), (at(z, y, 1 - c), k), c_send.at[a, i], c_recv.at[a, i])

        def arrived(ref, sem):
            remote(ref, (b, 1 - k), sem, sem).wait_recv()

        def begin(a):
            @pl.when(z < last)
            def _():
                up(a, z).start()

            @pl.when(z > 0)
            def _():
                down(a, z).start()

            across(a, z).start()
            core(a, z, y).start()

        def hop(a, step):
            @pl.when(z >= step)
            def _():
                zs = z - step
                arrived(piece(a, zs, y, c), z_recv.at[a, zs])

                @pl.when(z < last)
                def _():
                    up(a, zs).start()

                across(a, zs).start()
                core(a, zs, y).start()

            @pl.when(z + step <= last)
            def _():
                zs = z + step
                arrived(piece(a, zs, y, c), z_recv.at[a, zs])

                @pl.when(z > 0)
                def _():
                    down(a, zs).start()

                across(a, zs).start()
                core(a, zs, y).start()

        def relay(a, step):
            def one(zs):
                arrived(piece(a, zs, 1 - y, c), y_recv.at[a, zs])
                core(a, zs, 1 - y).start()

            if step == 0:
                one(z)
                return

            @pl.when(z >= step)
            def _():
                one(z - step)

            @pl.when(z + step <= last)
            def _():
                one(z + step)

        def complete(a):
            for zs in range(depth_z):
                for ys in range(depth_y):
                    arrived(piece(a, zs, ys, 1 - c), c_recv.at[a, zs * depth_y + ys])

        def sent(a):
            for zs in range(depth_z):
                @pl.when((z < last) & (zs <= z))
                def _():
                    up(a, zs).wait_send()

                @pl.when((z > 0) & (zs >= z))
                def _():
                    down(a, zs).wait_send()

                across(a, zs).wait_send()
                for ys in range(depth_y):
                    core(a, zs, ys).wait_send()

        def token_copy(s):
            return pltpu.make_async_remote_copy(
                src_ref=tokens_ref.at[(1 - k) * count + s],
                dst_ref=x_all.at[s, mine],
                send_sem=t_send.at[s],
                recv_sem=t_recv.at[s],
                device_id=(b, 1 - k),
                device_id_type=pl.DeviceIdType.MESH,
            )

        def grad_copy(s):
            return pltpu.make_async_remote_copy(
                src_ref=cot_away.at[s],
                dst_ref=cot_all.at[s, mine],
                send_sem=g_send.at[s],
                recv_sem=g_recv.at[s],
                device_id=(b, 1 - k),
                device_id_type=pl.DeviceIdType.MESH,
            )

        def put(i, src, dst):
            return pltpu.make_async_copy(src, dst, out_sem.at[i])

        partners = 3 + (z < last).astype(jnp.int32) + (z > 0).astype(jnp.int32)
        pl.semaphore_wait(barrier, partners)
        token_copy(0).start()
        begin(1)
        for i in range(3):
            loads[i].wait()
        begin(0)
        token_copy(1).start()

        for i in (6, 7):
            loads[i].wait()
        mask = mask_ref[...].astype(f32)
        own, away = jnp.where(k == 0, mask[:count], mask[count:]), jnp.where(k == 0, mask[count:], mask[:count])
        columns = jnp.concatenate([own, away], 0).T
        for s in range(count):
            cot_all[s, mine, :] = (cot_all[s, mine, :].astype(f32) * columns[:, s : s + 1]).astype(bf16)
            cot_away[s] = (cot_away[s].astype(f32) * columns[:, count + s : count + s + 1]).astype(bf16)

        for i in (3, 4, 5, 8):
            loads[i].wait()
        relay(0, 0)
        relay(1, 0)
        for step in range(1, depth_z):
            for a in (0, 1):
                hop(a, step)
        begin(2)
        for step in range(1, depth_z):
            for a in (0, 1):
                relay(a, step)
        complete(0)
        complete(1)
        vec[...] = jnp.sum(tables[...].astype(f32), 0)
        save_w = put(0, w_qkv, w_qkv_out)
        save_w.start()

        plan = {
            (0, 0): [],
            (0, 1): [lambda: hop(2, 1)],
            (0, 2): [lambda: relay(2, 0)],
            (1, 0): [lambda: hop(2, 2)],
            (1, 1): [lambda: relay(2, 1)],
            (1, 2): [lambda: hop(2, 3), lambda: begin(3)],
            (2, 0): [lambda: relay(2, 2)],
            (2, 1): [lambda: hop(3, 1)],
            (2, 2): [],
            (3, 0): [lambda: hop(3, 2), lambda: relay(2, 3)],
            (3, 1): [lambda: relay(3, 0)],
            (3, 2): [lambda: hop(3, 3)],
        }

        def pump(s, slot):
            for (when, where), steps in plan.items():
                if where == slot and steps:
                    @pl.when(s == when)
                    def _():
                        for step in steps:
                            step()

        def first(s, carry):
            arrived(x_all.at[s, pl.ds(pl.multiple_of((1 - k) * stretch, stretch), stretch)], t_recv.at[s])

            @pl.when(s + 2 < count)
            def _():
                token_copy(s + 2).start()

            @pl.when(s + 2 >= count)
            def _():
                grad_copy(s + 2 - count).start()

            saves = [
                put(1, x_all.at[s], x_out.at[s]),
                put(2, q_s, q_out.at[s]),
                put(3, k_s, k_out.at[s]),
                put(4, v_s, v_out.at[s]),
                put(5, cb_all.at[s], cb_out.at[s]),
                put(6, l_s, l_out.at[s]),
            ]

            @pl.when(s > 0)
            def _():
                for save in saves:
                    save.wait()

            project(x_all[s], w_qkv, vec, q_s, k_s, v_s)
            for save in saves[:4]:
                save.start()
            pump(s, 0)
            stat[...] = jnp.zeros_like(stat)
            attend_pairs(q_s, k_s, v_s, cb_all.at[s], stat, 0, HEADS // 4)
            pump(s, 1)
            attend_pairs(q_s, k_s, v_s, cb_all.at[s], stat, HEADS // 4, HEADS // 2)
            l_s[...] = stat[...].T[:STAT_ROWS]
            for save in saves[4:]:
                save.start()
            pump(s, 2)
            return carry

        lax.fori_loop(0, count, first, 0)
        for i, (src, dst) in enumerate(((x_all.at[0], x_out.at[0]), (q_s, q_out.at[0]), (k_s, k_out.at[0]), (v_s, v_out.at[0]), (cb_all.at[0], cb_out.at[0]), (l_s, l_out.at[0]))):
            put(i + 1, src, dst).wait()
        save_w.wait()
        for step in range(1, depth_z):
            relay(3, step)
        complete(2)
        complete(3)

        sums_out[...] = jnp.zeros_like(sums_out)

        def second(s, carry):
            arrived(cot_all.at[s, pl.ds(pl.multiple_of((1 - k) * stretch, stretch), stretch)], g_recv.at[s])

            @pl.when(s + 2 < count)
            def _():
                grad_copy(s + 2).start()

            saves = [
                put(i + 1, src, dst.at[s])
                for i, (src, dst) in enumerate(
                    (
                        (o_s, o_out), (mid_s, mid_out), (gf_s, gf_out), (ga_s, ga_out), (gc_s, gc_out), (d_s, d_out),
                        (h_s, h_out), (gu_s, gu_out),
                    )
                )
            ]

            @pl.when(s > 0)
            def _():
                for save in saves:
                    save.wait()

            feed_forward(
                x_all[s], cb_all[s], cot_all[s], w_mid.at[:, 0:width], w_mid.at[:, width:mid_width], w_up, vec,
                o_s, mid_s, gf_s, ga_s, gc_s, d_s, h_s, gu_s, sums_out,
            )
            for save in saves:
                save.start()
            return carry

        lax.fori_loop(0, count, second, 0)
        for i, (src, dst) in enumerate(
            (
                (o_s, o_out), (mid_s, mid_out), (gf_s, gf_out), (ga_s, ga_out), (gc_s, gc_out), (d_s, d_out),
                (h_s, h_out), (gu_s, gu_out),
            )
        ):
            put(i + 1, src, dst.at[0]).wait()
        for s in range(count):
            token_copy(s).wait_send()
            grad_copy(s).wait_send()
        for a in range(ARRAYS):
            sent(a)

    seq = jax.ShapeDtypeStruct((count, length, width), bf16)
    seq_wide = jax.ShapeDtypeStruct((count, length, inner), bf16)
    stat_shape = jax.ShapeDtypeStruct((count, STAT_ROWS, length), f32)
    hbm = pl.BlockSpec(memory_space=pl.ANY)
    one = pltpu.VMEM((length, width), bf16)
    one_wide = pltpu.VMEM((length, inner), bf16)
    all_seq = pltpu.VMEM((count, length, width), bf16)
    stat_one = pltpu.VMEM((STAT_ROWS, length), f32)
    dma = pltpu.SemaphoreType.DMA
    return pl.pallas_call(
        kernel,
        in_specs=[hbm, whole_vmem()] + [hbm] * 7 + [whole_vmem()],
        out_specs=[hbm] * 14 + [whole_vmem(), hbm],
        out_shape=[seq] * 5 + [stat_shape] + [seq] * 5 + [stat_shape, seq_wide, seq_wide]
        + [jax.ShapeDtypeStruct((16, width), f32), jax.ShapeDtypeStruct((width, qkv_width), bf16)],
        scratch_shapes=[
            pltpu.VMEM((width, qkv_width), bf16),
            pltpu.VMEM((width, mid_width), bf16),
            pltpu.VMEM((inner, width), bf16),
            pltpu.VMEM((devices, 16, width), bf16),
            pltpu.VMEM((16, width), f32),
            all_seq, all_seq,
            pltpu.VMEM((count, stretch, width), bf16),
            all_seq,
            one, one, one, stat_one, pltpu.VMEM((length, 128), f32),
            one, one, one, one, one, stat_one, one_wide, one_wide,
            dma((ARRAYS, depth_z)), dma((ARRAYS, depth_z)), dma((ARRAYS, depth_z)),
            dma((ARRAYS, depth_z)), dma((ARRAYS, depth_z)),
            dma((ARRAYS, depth_z * depth_y)), dma((ARRAYS, depth_z * depth_y)),
            dma((count,)), dma((count,)), dma((count,)), dma((count,)), dma((9,)), dma((9,)),
        ],
        compiler_params=pltpu.CompilerParams(collective_id=1, has_side_effects=True, vmem_limit_bytes=VMEM_BYTES),
        name="forward",
    )(tokens, span_mask, cotangent, w_query, w_key, w_value, w_out, w_inner, w_outer, table)


def backward_call(x, q, k, v, cb, mid, gf, ga, gc, hidden, gu, out, stat_l, stat_d, w_qkv, sums, sizes):
    depth_z, depth_y, cores = sizes
    count, length, width = x.shape
    inner = hidden.shape[2]
    devices = depth_z * depth_y * cores
    part, outer_part = width // devices, inner // devices
    stretch, rows = length // 2, 2 * count
    chunks = inner // width
    GROUPS = 3
    pairs = HEADS // 2 // GROUPS
    column = pairs * PAIR
    narrow = width // GROUPS
    OUT = chunks
    QKV = chunks + 1
    N = QKV + GROUPS
    SLOTS = 2
    STEPS = 5
    tokens_all = count * length

    def kernel(
        x_in, q_in, k_in, v_in, cb_in, mid_in, gf_in, ga_in, gc_in, h_in, gu_in, out_in, w_in, l_ref, d_ref, sums_ref,
        output, grad_tokens, g_query, g_key, g_value, g_out, g_inner, g_outer, vectors,
        big, pool, w_cat, ga_s, gx_s, kt, gqt, own_s, own_o, r1, r2, r3, s4, r4, r1o, r2o, r3o, s4o, r4o, v_own, v_got,
        s1_send, s1_recv, s2_send, s2_recv, s3_send, s3_recv, s4_send, s4_recv,
        v_send, v_recv, o_send, o_recv, g_send, g_recv, big_sem, pool_sem, w_sem, ga_sem, keep_sem,
    ):
        b, k = lax.axis_index("batch"), lax.axis_index("blk")
        z, y, c = b // (depth_y * cores), (b // cores) % depth_y, b % cores

        def at(z_, y_, c_):
            return (z_ * depth_y + y_) * cores + c_

        beside = (b, 1 - k)
        other_core = (at(z, y, 1 - c), k)
        other_y = (at(z, 1 - y, c), k)

        def level(j):
            return (z + j) % depth_z

        barrier = pltpu.get_barrier_semaphore()
        partners = [beside, other_core, other_y] + [(at(level(j), y, c), k) for j in range(1, depth_z)]
        for device in partners:
            pl.semaphore_signal(barrier, inc=1, device_id=device, device_id_type=pl.DeviceIdType.MESH)

        def remote(src, dst, device, send, recv):
            return pltpu.make_async_remote_copy(
                src_ref=src, dst_ref=dst, send_sem=send, recv_sem=recv, device_id=device, device_id_type=pl.DeviceIdType.MESH
            )

        def load(i, src):
            return pltpu.make_async_copy(src, big.at[i], big_sem.at[i])

        def wide_load(i, src, j):
            return pltpu.make_async_copy(src.at[:, :, j * width : (j + 1) * width], big.at[i], big_sem.at[i])

        def pool_load(s, slot):
            return [
                pltpu.make_async_copy(src.at[s], pool.at[slot, i], pool_sem.at[slot, i])
                for i, src in enumerate((q_in, k_in, v_in, gc_in))
            ]

        def w_load(i, g):
            return pltpu.make_async_copy(
                w_in.at[:, i * width + g * column : i * width + (g + 1) * column],
                w_cat.at[g, :, i * column : (i + 1) * column],
                w_sem.at[i, g],
            )

        first_loads = [load(0, mid_in), wide_load(2, gu_in, 0), load(1, gf_in), wide_load(3, gu_in, 1)]
        for copy in first_loads:
            copy.start()
        mine = pl.ds(pl.multiple_of(k * stretch, stretch), stretch)
        theirs = pl.ds(pl.multiple_of((1 - k) * stretch, stretch), stretch)

        def buffers(g, outer):
            if outer:
                return own_o.at[g], r1o.at[g], r2o.at[g], r3o.at[g], s4o.at[g], r4o.at[g], N + g
            return own_s.at[g % SLOTS], r1.at[g], r2.at[g], r3.at[g], s4.at[g], r4.at[g], g

        def step_1(g, outer=False):
            own, a1, _, _, _, _, i = buffers(g, outer)
            return remote(own.at[:, :, 1 - c], a1, other_core, s1_send.at[i], s1_recv.at[i])

        def step_2(g, outer=False):
            _, a1, a2, _, _, _, i = buffers(g, outer)
            return remote(a1.at[:, 1 - y], a2, other_y, s2_send.at[i], s2_recv.at[i])

        def step_3(g, j, outer=False):
            _, _, a2, a3, _, _, i = buffers(g, outer)
            return remote(
                a2.at[level(j)], a3.at[j - 1], (at(level(j), y, c), k), s3_send.at[i, j - 1], s3_recv.at[i, j - 1]
            )

        def step_4(g, outer=False):
            _, _, _, _, a4, b4, i = buffers(g, outer)
            return remote(a4, b4, beside, s4_send.at[i], s4_recv.at[i])

        def move_1(g, outer=False):
            own, a1, _, _, _, _, _ = buffers(g, outer)
            step_1(g, outer).wait()

            def add(i, carry):
                zi, yi = i // depth_y, i % depth_y
                a1[zi, yi] = a1[zi, yi] + own[zi, yi, c]
                return carry

            lax.fori_loop(0, depth_z * depth_y, add, 0)
            step_2(g, outer).start()

        def move_2(g, outer=False):
            _, a1, a2, _, _, _, _ = buffers(g, outer)
            step_2(g, outer).wait()

            def add(zi, carry):
                a2[zi] = a2[zi] + a1[zi, y]
                return carry

            lax.fori_loop(0, depth_z, add, 0)
            for j in range(1, depth_z):
                step_3(g, j, outer).start()

        def move_3(g, outer=False):
            _, _, a2, a3, a4, _, _ = buffers(g, outer)
            for j in range(1, depth_z):
                step_3(g, j, outer).wait()
            total = a2[z].astype(f32)
            for j in range(1, depth_z):
                total = total + a3[j - 1].astype(f32)
            a4[...] = total.astype(bf16)
            step_4(g, outer).start()

        def move_4(g, outer=False):
            _, _, _, _, a4, b4, _ = buffers(g, outer)
            step_4(g, outer).wait()
            total = a4[...].astype(f32) + b4[...].astype(f32)
            if outer:
                g_outer[:, g * narrow : (g + 1) * narrow] = total
            elif g < OUT:
                g_inner[:, g * width : (g + 1) * width] = total
            elif g == OUT:
                g_out[...] = total
            else:
                for i, ref in enumerate((g_query, g_key, g_value)):
                    ref[:, (g - QKV) * column : (g - QKV + 1) * column] = total[:, i * column : (i + 1) * column]

        def whole(i):
            return big[i].reshape(tokens_all, width)

        def begin(g, value):
            own_s[g % SLOTS] = value.astype(bf16).reshape(depth_z, depth_y, cores, part, width)
            step_1(g).start()

        pl.semaphore_wait(barrier, len(partners))
        output_copies = [
            remote(out_in.at[s, theirs], output.at[k * count + s], beside, o_send.at[s], o_recv.at[s]) for s in range(count)
        ]
        keep_output = pltpu.make_async_copy(out_in.at[:, mine], output.at[pl.ds(k * count, count)], keep_sem.at[0])
        for copy in output_copies:
            copy.start()

        first_loads[0].wait()
        for j in range(chunks):
            wide_load(2 + j % 2, gu_in, j).wait()
            if j >= SLOTS:
                move_1(j - SLOTS)
            begin(j, mul(whole(0), whole(2 + j % 2), TN))
            following = j + 2 - chunks
            if following < 0:
                wide_load(2 + j % 2, gu_in, j + 2).start()
            else:
                wide_load(2 + j % 2, h_in, following).start()
            if j == 0:
                for s in range(2):
                    for copy in pool_load(s, s):
                        copy.start()
            if j == 1:
                keep_output.start()
                for g in range(GROUPS):
                    for i in range(3):
                        w_load(i, g).start()
        load(0, ga_in).start()
        first_loads[2].wait()
        for j in range(chunks):
            wide_load(2 + j % 2, h_in, j).wait()
            product = mul(whole(2 + j % 2), whole(1), TN).astype(bf16)
            for g in range(GROUPS):
                own_o[g, j] = product[:, g * narrow : (g + 1) * narrow].reshape(depth_y, cores, outer_part, narrow)
            if j + 2 < chunks:
                wide_load(2 + j % 2, h_in, j + 2).start()
            elif j + 2 == chunks:
                load(2 + j % 2, cb_in).start()
            else:
                load(2 + j % 2, x_in).start()
            if j < SLOTS:
                move_1(chunks - SLOTS + j)
            if j == 2:
                move_2(0)
        for g in range(GROUPS):
            step_1(g, True).start()
        move_2(1)
        load(0, ga_in).wait()
        load(2 + chunks % 2, cb_in).wait()
        begin(OUT, mul(whole(2 + chunks % 2), whole(0), TN))
        for copy in pool_load(2, 2):
            copy.start()
        move_3(0)
        for g in range(GROUPS):
            for i in range(3):
                w_load(i, g).wait()
        load(2 + (chunks + 1) % 2, x_in).wait()
        x_at = 2 + (chunks + 1) % 2
        v_own[0] = sums_ref[...]

        half = count // 2
        cells = GROUPS * count
        plan = {
            0: [lambda: [move_1(g, True) for g in range(GROUPS)], lambda: move_2(2)],
            1: [lambda: move_1(OUT), lambda: move_3(1), lambda: move_4(0)],
            2: [lambda: move_2(3)],
            3: [lambda: move_3(2), lambda: move_4(1)],
            4: [lambda: move_2(0, True), lambda: move_3(3), lambda: move_4(2)],
            5: [lambda: move_4(3)],
            6: [lambda: move_2(1, True), lambda: move_3(0, True)],
            7: [lambda: move_4(0, True)],
            8: [lambda: move_2(2, True), lambda: move_3(1, True), lambda: move_1(QKV)],
            9: [lambda: move_2(OUT), lambda: move_4(1, True)],
            10: [lambda: move_3(2, True), lambda: move_2(QKV), lambda: move_1(QKV + 1)],
            11: [lambda: move_4(2, True), lambda: move_3(OUT)],
        }

        def pick(i):
            late = i // (GROUPS * half)
            j = i % (GROUPS * half)
            s = (1 - late) * (j // GROUPS) + late * (half + j % half)
            g = (1 - late) * (j % GROUPS) + late * (j // half)
            return s, g

        def gx_copies(s):
            away = remote(gx_s.at[theirs], grad_tokens.at[k * count + s], beside, g_send.at[s], g_recv.at[s])
            keep = pltpu.make_async_copy(gx_s.at[mine], grad_tokens.at[k * count + s], keep_sem.at[1])
            return away, keep

        ga_load = [pltpu.make_async_copy(ga_in.at[s], ga_s, ga_sem.at[0]) for s in range(count)]
        ga_load[0].start()

        def cell(i, carry):
            s, g = pick(i)
            slot = s % 3

            @pl.when(g == 0)
            def _():
                for copy in pool_load(s, slot):
                    copy.wait()

            attend_back(
                pool.at[slot, 0], pool.at[slot, 1], pool.at[slot, 2], pool.at[slot, 3], l_ref.at[s], d_ref.at[s],
                big.at[g, s], kt, gqt, g * pairs, pairs,
            )
            span = pl.ds(pl.multiple_of(g * column, column), column)
            v_own[0, B_QUERY : B_QUERY + 1, span] += column_sum(big[g, s, :, :column])
            v_own[0, B_VALUE : B_VALUE + 1, span] += column_sum(big[g, s, :, 2 * column :])

            @pl.when(i == GROUPS - 1)
            def _():
                for copy in pool_load(3, 0):
                    copy.start()

            for when, steps in plan.items():
                @pl.when(i == when)
                def _():
                    for step in steps:
                        step()

            late = i // (GROUPS * half)

            @pl.when((late == 1) & (i % half == half - 1))
            def _():
                begin(QKV + g, mul(whole(x_at), big[g].reshape(tokens_all, width), TN))

            @pl.when(g == GROUPS - 1)
            def _():
                ga_load[0].wait()

                @pl.when(s > 0)
                def _():
                    away, keep = gx_copies(s - 1)
                    away.wait_send()
                    keep.wait()

                grad = ga_s[...].astype(f32)
                for group in range(GROUPS):
                    grad = grad + mul(big[group, s], w_cat[group], NT)
                gx_s[...] = grad.astype(bf16)
                away, keep = gx_copies(s)
                away.start()
                keep.start()

                @pl.when(s < count - 1)
                def _():
                    pltpu.make_async_copy(ga_in.at[s + 1], ga_s, ga_sem.at[0]).start()

            return carry

        lax.fori_loop(0, cells, cell, 0)

        towards = [other_core, other_y, (at(z + 1 - 2 * (z % 2), y, c), k), (at((z + 2) % 4, y, c), k), beside]

        def v_copy(i):
            return remote(v_own.at[i], v_got.at[i], towards[i], v_send.at[i], v_recv.at[i])

        def v_move(i):
            v_copy(i).wait()
            v_own[i + 1] = v_own[i] + v_got[i]
            if i + 1 < STEPS:
                v_copy(i + 1).start()

        v_copy(0).start()
        last_group = N - 1
        move_4(OUT)
        move_1(last_group)
        v_move(0)
        v_move(1)
        move_3(QKV)
        v_move(2)
        move_2(QKV + 1)
        v_move(3)
        move_2(last_group)
        v_move(4)
        total = v_own[STEPS]
        inner_row = v_own[STEPS, pl.ds(B_INNER + b // (devices // chunks), 1), :]
        rolled = pltpu.roll(total, (width - b * part) % width, 1)
        wide = pltpu.roll(inner_row, (width - (b % (devices // chunks)) * outer_part) % width, 1)
        line = lax.broadcasted_iota(jnp.int32, total.shape, 0)
        vectors[...] = jnp.where(line == B_INNER, wide, rolled)
        move_4(QKV)
        move_3(QKV + 1)
        move_3(last_group)
        move_4(QKV + 1)
        move_4(last_group)
        away, keep = gx_copies(count - 1)
        away.wait_send()
        keep.wait()
        keep_output.wait()
        for s in range(count):
            output_copies[s].wait_send()
            remote(out_in.at[s, theirs], output.at[(1 - k) * count + s], beside, o_send.at[s], o_recv.at[s]).wait_recv()
            remote(gx_s.at[theirs], grad_tokens.at[(1 - k) * count + s], beside, g_send.at[s], g_recv.at[s]).wait_recv()

    hbm = pl.BlockSpec(memory_space=pl.ANY)
    dma = pltpu.SemaphoreType.DMA
    every = N + GROUPS

    def vmem(*shape):
        return pltpu.VMEM(shape, bf16)

    def result(*shape):
        return jax.ShapeDtypeStruct(shape, f32)

    back = jax.ShapeDtypeStruct((rows, stretch, width), bf16)
    return pl.pallas_call(
        kernel,
        in_specs=[hbm] * 13 + [whole_vmem()] * 3,
        out_specs=[hbm] * 2 + [whole_vmem()] * 7,
        out_shape=[
            back, back, result(part, width), result(part, width), result(part, width), result(part, width),
            result(part, inner), result(outer_part, width), result(16, width),
        ],
        scratch_shapes=[
            vmem(4, count, length, width),
            vmem(3, 4, length, width),
            vmem(GROUPS, width, 3 * column),
            vmem(length, width), vmem(length, width),
            vmem(column, length), vmem(column, length),
            vmem(SLOTS, depth_z, depth_y, cores, part, width),
            vmem(GROUPS, depth_z, depth_y, cores, outer_part, narrow),
            vmem(N, depth_z, depth_y, part, width), vmem(N, depth_z, part, width), vmem(N, depth_z - 1, part, width),
            vmem(N, part, width), vmem(N, part, width),
            vmem(GROUPS, depth_z, depth_y, outer_part, narrow), vmem(GROUPS, depth_z, outer_part, narrow),
            vmem(GROUPS, depth_z - 1, outer_part, narrow), vmem(GROUPS, outer_part, narrow), vmem(GROUPS, outer_part, narrow),
            pltpu.VMEM((STEPS + 1, 16, width), f32), pltpu.VMEM((STEPS, 16, width), f32),
            dma((every,)), dma((every,)), dma((every,)), dma((every,)),
            dma((every, depth_z - 1)), dma((every, depth_z - 1)), dma((every,)), dma((every,)),
            dma((STEPS,)), dma((STEPS,)), dma((count,)), dma((count,)), dma((count,)), dma((count,)),
            dma((4,)), dma((3, 4)), dma((3, GROUPS)), dma((1,)), dma((2,)),
        ],
        compiler_params=pltpu.CompilerParams(collective_id=2, has_side_effects=True, vmem_limit_bytes=63 * 2**20),
        name="backward",
    )(x, q, k, v, cb, mid, gf, ga, gc, hidden, gu, out, w_qkv, stat_l, stat_d, sums)


def pack_shard(w_query, w_key, w_value, w_out, w_inner, w_outer, vectors):
    width = w_query.shape[1]
    inner_parts = [w_inner[:, i : i + width] for i in range(0, w_inner.shape[1], width)]
    small = jnp.concatenate(vectors)
    body_rows = sum(part.shape[0] for part in (w_query, w_key, w_value, w_out, w_outer, *inner_parts))
    rows = -(-(body_rows + 1) // 16) * 16
    tail = jnp.zeros(((rows - body_rows) * width,), small.dtype).at[: small.shape[0]].set(small)
    return jnp.concatenate(
        [w_query, w_key, w_value, w_out, *inner_parts, w_outer, tail.reshape(-1, width)]
    )


def vec_table(small, vec_names_sizes):
    rows, at = [], 0
    for size in vec_names_sizes:
        rows.append(small[:, at : at + size].reshape(-1))
        at += size
    return rows


def gather_weights(w_query, w_key, w_value, w_out, w_inner, w_outer, vectors):
    part, width = w_query.shape
    outer_part = w_outer.shape[0]
    chunks = w_inner.shape[1] // width
    sizes = [vector.shape[0] for vector in vectors]
    packed = pack_shard(w_query, w_key, w_value, w_out, w_inner, w_outer, vectors)
    gathered = lax.all_gather(packed, "batch", axis=0)

    def weight(at, count):
        return gathered[:, at : at + count].reshape(-1, width)

    squares = [weight(i * part, part) for i in range(4 + chunks)]
    outer_at = (4 + chunks) * part
    w_outer_all = weight(outer_at, outer_part)
    small = gathered[:, outer_at + outer_part :].reshape(gathered.shape[0], -1)
    vec = jnp.concatenate(vec_table(small, sizes)).reshape(-1, width).astype(f32)
    vec = jnp.concatenate([vec, jnp.zeros((16 - vec.shape[0], width), f32)])
    return jnp.concatenate(squares[:3], 1), squares[3], jnp.concatenate(squares[4:], 1), w_outer_all, vec


def body(
    tokens,
    span_mask,
    cotangent,
    w_query,
    b_query,
    w_key,
    w_value,
    b_value,
    w_out,
    b_out,
    gain_first,
    bias_first,
    w_inner,
    b_inner,
    w_outer,
    b_outer,
    gain_second,
    bias_second,
):
    rows, stretch, width = tokens.shape
    inner = w_inner.shape[1]
    part = w_query.shape[0]
    outer_part = w_outer.shape[0]
    vectors = (b_query, b_value, b_out, gain_first, bias_first, b_outer, gain_second, bias_second, b_inner)
    sizes = [vector.shape[0] for vector in vectors]

    devices = lax.axis_size("batch")
    chunks = inner // width
    swap = functools.partial(lax.all_to_all, axis_name="blk", tiled=True)
    outer_at = (4 + chunks) * part
    shard_rows = -(-(outer_at + outer_part + 1) // 16) * 16
    if (devices, lax.axis_size("blk")) == (16, 2):
        table = sum(
            lax.pad(
                vector.astype(f32).reshape(1, -1), f32(0), ((i, 15 - i, 0), (0, width - vector.shape[0], 0))
            )
            for i, vector in enumerate(vectors)
        )
        x, q, k, v, cb, stat_l, out, mid, gf, ga, gc, stat_d, hidden, gu, sums_ffn, w_qkv = forward_call(
            tokens, span_mask, cotangent, w_query, w_key, w_value, w_out, w_inner, w_outer, table, (4, 2, 2)
        )
        results = backward_call(
            x, q, k, v, cb, mid, gf, ga, gc, hidden, gu, out, stat_l, stat_d, w_qkv, sums_ffn, (4, 2, 2)
        )
        output, grad_tokens, g_query, g_key, g_value, g_out, g_inner, g_outer, totals = results
        small = [totals[i, :size] for i, size in enumerate(sizes)]
        return (
            output, grad_tokens, g_query, small[0], g_key, g_value, small[1], g_out, small[2], small[3], small[4], g_inner,
            small[8], g_outer, small[5], small[6], small[7],
        )
    w_qkv, w_out_all, w_inner_all, w_outer_all, vec = gather_weights(
        w_query, w_key, w_value, w_out, w_inner, w_outer, vectors
    )
    masked = cotangent * span_mask[..., None].astype(bf16)
    x = swap(tokens, split_axis=0, concat_axis=1)
    cot = swap(masked, split_axis=0, concat_axis=1)
    q, k, v, cb, stat_l = attention_call(x, w_qkv, vec)
    out, mid, gf, ga, gc, stat_d, hidden, gu, sums_ffn = feed_forward_call(
        x, cb, cot, w_out_all, w_inner_all, w_outer_all, vec
    )
    gx, gw_qkv, sums_att = attention_back_call(x, q, k, v, gc, ga, stat_l, stat_d, w_qkv)
    output = swap(out, split_axis=1, concat_axis=0)
    grad_tokens = swap(gx, split_axis=1, concat_axis=0)

    def flat(values):
        return values.reshape(-1, values.shape[-1])

    gw_out = weight_grad_call(flat(cb), flat(ga), False)
    gw_inner = weight_grad_call(flat(mid), flat(gu), False)
    gw_outer = weight_grad_call(flat(hidden), flat(gf), True)

    sums = sums_ffn + sums_att
    small_sums = [sums[i].reshape(devices, -1) for i in range(B_INNER)]
    small_sums.append(sums[B_INNER : B_INNER + chunks].reshape(devices, -1))
    tail = jnp.concatenate(small_sums, 1).astype(bf16)
    tail = jnp.pad(tail, ((0, 0), (0, (shard_rows - outer_at - outer_part) * width - tail.shape[1])))
    pieces = [gw_qkv[:, i * width : (i + 1) * width].reshape(devices, part, width) for i in range(3)]
    pieces.append(gw_out.reshape(devices, part, width))
    pieces += [gw_inner[:, i * width : (i + 1) * width].reshape(devices, part, width) for i in range(chunks)]
    pieces.append(gw_outer.reshape(devices, outer_part, width))
    pieces.append(tail.reshape(devices, -1, width))
    grads = jnp.concatenate(pieces, 1)
    share = lax.psum_scatter(grads, "batch", scatter_dimension=0, tiled=False)
    share = lax.psum(share, "blk").astype(f32)
    square = [share[i * part : (i + 1) * part] for i in range(4 + chunks)]
    share_small = share[outer_at + outer_part :].reshape(-1)
    small_out, at = [], 0
    for size in sizes:
        small_out.append(share_small[at : at + size])
        at += size
    (g_b_query, g_b_value, g_b_out, g_gain_1, g_bias_1, g_b_outer, g_gain_2, g_bias_2, g_b_inner) = small_out
    return (
        output,
        grad_tokens,
        square[0],
        g_b_query,
        square[1],
        square[2],
        g_b_value,
        square[3],
        g_b_out,
        g_gain_1,
        g_bias_1,
        jnp.concatenate(square[4:], 1),
        g_b_inner,
        share[outer_at : outer_at + outer_part],
        g_b_outer,
        g_gain_2,
        g_bias_2,
    )


def solution(mesh):
    block = P("batch", "blk", None)
    matrix, vector = P("batch", None), P("batch")
    weights = (
        matrix, vector, matrix, matrix, vector, matrix, vector, vector, vector, matrix, vector, matrix, vector, vector, vector,
    )
    return jax.shard_map(
        body,
        mesh=mesh,
        in_specs=(block, P("batch", "blk"), block) + weights,
        out_specs=(block, block) + weights,
        check_vma=False,
    )
```

```python
import functools

import jax
import jax.numpy as jnp
from jax import lax
from jax.experimental import pallas as pl
from jax.experimental.pallas import tpu as pltpu
from jax.sharding import PartitionSpec as P

HEADS = 12
HEAD_DIM = 64
PAIR = 2 * HEAD_DIM
STAT_ROWS = 16
VMEM_BYTES = 60 * 2**20

epsilon = 1e-06
bf16 = jnp.bfloat16
f32 = jnp.float32

NN = (((1,), (0,)), ((), ()))
NT = (((1,), (1,)), ((), ()))
TN = (((0,), (0,)), ((), ()))

B_QUERY, B_VALUE, B_OUT, GAIN_1, BIAS_1, B_OUTER, GAIN_2, BIAS_2, B_INNER = range(9)


def mul(left, right, dims=NN):
    return lax.dot_general(left, right, dims, preferred_element_type=f32)


def row(ref, index):
    return ref[index : index + 1, :]


def halves(block):
    lane = lax.broadcasted_iota(jnp.int32, block.shape, 1)
    zero = jnp.zeros_like(block)
    return jnp.where(lane < HEAD_DIM, block, zero), jnp.where(lane < HEAD_DIM, zero, block)


def pair_at(p):
    return pl.ds(pl.multiple_of(p * PAIR, PAIR), PAIR)


def normalize(values):
    center = values - jnp.mean(values, -1, keepdims=True)
    inverse = lax.rsqrt(jnp.mean(center * center, -1, keepdims=True) + epsilon)
    return center * inverse, inverse


def norm_back(grad, normed, inverse, gain):
    scaled = grad * gain
    return inverse * (
        scaled
        - jnp.mean(scaled, -1, keepdims=True)
        - normed * jnp.mean(scaled * normed, -1, keepdims=True)
    )


def column_sum(values):
    return jnp.sum(values.astype(f32), 0, keepdims=True)


def project(x, w_ref, vec_ref, q_ref, k_ref, v_ref):
    width = x.shape[-1]
    q = (mul(x, w_ref[:, :width]) + row(vec_ref, B_QUERY)).astype(bf16)
    q_ref[...] = q * bf16(HEAD_DIM**-0.5)
    k_ref[...] = mul(x, w_ref[:, width : 2 * width]).astype(bf16)
    v_ref[...] = (mul(x, w_ref[:, 2 * width :]) + row(vec_ref, B_VALUE)).astype(bf16)


def attend_pairs(q_ref, k_ref, v_ref, c_ref, stat, first, end):
    lane = lax.broadcasted_iota(jnp.int32, stat.shape, 1)

    def pair(p, carry):
        at = pair_at(p)
        q2, k2, v2 = q_ref[:, at], k_ref[:, at], v_ref[:, at]
        context = None
        for h, (k_one, v_one) in enumerate(zip(halves(k2), halves(v2))):
            scores = mul(q2, k_one, NT)
            best = jnp.max(scores, 1, keepdims=True)
            weights = jnp.exp(scores - best)
            total = jnp.sum(weights, 1, keepdims=True)
            part = mul(weights.astype(bf16), v_one) * (1.0 / total)
            context = part if context is None else context + part
            stat[...] = jnp.where(lane == 2 * p + h, best + jnp.log(total), stat[...])
        c_ref[:, at] = context.astype(bf16)
        return carry

    lax.fori_loop(first, end, pair, 0, unroll=3)


def attend(q_ref, k_ref, v_ref, c_ref, l_ref, stat):
    stat[...] = jnp.zeros_like(stat)
    attend_pairs(q_ref, k_ref, v_ref, c_ref, stat, 0, HEADS // 2)
    l_ref[...] = stat[...].T[:STAT_ROWS]


def attend_back(q_ref, k_ref, v_ref, g_ref, l_ref, d_ref, out_ref, kt, gqt, first, pairs):
    part = pairs * PAIR
    columns = pl.ds(pl.multiple_of(first * PAIR, PAIR), part)
    kt[...] = (k_ref[:, columns] * bf16(HEAD_DIM**-0.5)).T
    for p in range(pairs):
        at = pair_at(first + p)
        q2, g2 = q_ref[:, at], g_ref[:, at]
        ks, vs = halves(k_ref[:, at]), halves(v_ref[:, at])
        qs, gs = halves(q2), halves(g2)
        gk = gv = None
        for h in range(2):
            head = 2 * (first + p) + h
            probs = jnp.exp(mul(ks[h], q2, NT) - l_ref[pl.ds(head, 1), :])
            grad_probs = mul(vs[h], g2, NT)
            grad_scores = (probs * (grad_probs - d_ref[pl.ds(head, 1), :])).astype(bf16)
            gk_one = mul(grad_scores, qs[h])
            gv_one = mul(probs.astype(bf16), gs[h])
            gk = gk_one if gk is None else gk + gk_one
            gv = gv_one if gv is None else gv + gv_one
            rows = slice((2 * p + h) * HEAD_DIM, (2 * p + h + 1) * HEAD_DIM)
            gqt[rows, :] = mul(kt[rows, :], grad_scores).astype(bf16)
        out_ref[:, part + p * PAIR : part + (p + 1) * PAIR] = gk.astype(bf16)
        out_ref[:, 2 * part + p * PAIR : 2 * part + (p + 1) * PAIR] = gv.astype(bf16)
    out_ref[:, :part] = gqt[...].T


def to_hidden(x, cb, wo_ref, wi_ref, vec_ref, mid_ref, h_ref, slope_ref):
    width = x.shape[-1]
    normed, inverse = normalize(x.astype(f32) + (mul(cb, wo_ref[...]) + row(vec_ref, B_OUT)))
    mid = (normed * row(vec_ref, GAIN_1) + row(vec_ref, BIAS_1)).astype(bf16)
    mid_ref[...] = mid
    for c in range(wi_ref.shape[1] // width):
        at = slice(c * width, (c + 1) * width)
        inner = mul(mid, wi_ref[:, at]) + row(vec_ref, B_INNER + c)
        cdf = 0.5 + 0.5 * lax.erf(inner * (0.5**0.5))
        h_ref[:, at] = (inner * cdf).astype(bf16)
        slope = cdf + inner * (jnp.exp(inner * inner * -0.5) * ((0.5 / jnp.pi) ** 0.5))
        slope_ref[:, at] = slope.astype(bf16)
    return normed, inverse


def to_output(normed_1, cot, wu_ref, vec_ref, h_ref, out_ref, gf_ref, sums_ref):
    width = normed_1.shape[-1]
    total = normed_1 * row(vec_ref, GAIN_1) + (row(vec_ref, BIAS_1) + row(vec_ref, B_OUTER))
    for c in range(h_ref.shape[1] // width):
        at = slice(c * width, (c + 1) * width)
        total = total + mul(h_ref[:, at], wu_ref[at, :])
    normed, inverse = normalize(total)
    gain = row(vec_ref, GAIN_2)
    out_ref[...] = (normed * gain + row(vec_ref, BIAS_2)).astype(bf16)
    grad = cot.astype(f32)
    sums_ref[GAIN_2 : GAIN_2 + 1, :] += column_sum(grad * normed)
    sums_ref[BIAS_2 : BIAS_2 + 1, :] += column_sum(grad)
    grad_2 = norm_back(grad, normed, inverse, gain)
    gf = grad_2.astype(bf16)
    gf_ref[...] = gf
    sums_ref[B_OUTER : B_OUTER + 1, :] += column_sum(gf)
    return grad_2


def to_context_grad(
    grad_2, normed_1, inverse_1, cb, wo_ref, wi_ref, wu_ref, vec_ref, gf_ref, ga_ref, gc_ref, d_ref, gu_ref, sums_ref
):
    width = grad_2.shape[-1]
    gf = gf_ref[...]
    grad_mid = grad_2
    for c in range(wi_ref.shape[1] // width):
        at = slice(c * width, (c + 1) * width)
        gu = (mul(gf, wu_ref[at, :], NT) * gu_ref[:, at].astype(f32)).astype(bf16)
        gu_ref[:, at] = gu
        sums_ref[B_INNER + c : B_INNER + c + 1, :] += column_sum(gu)
        grad_mid = grad_mid + mul(gu, wi_ref[:, at], NT)
    sums_ref[GAIN_1 : GAIN_1 + 1, :] += column_sum(grad_mid * normed_1)
    sums_ref[BIAS_1 : BIAS_1 + 1, :] += column_sum(grad_mid)
    ga = norm_back(grad_mid, normed_1, inverse_1, row(vec_ref, GAIN_1)).astype(bf16)
    ga_ref[...] = ga
    sums_ref[B_OUT : B_OUT + 1, :] += column_sum(ga)
    gc = mul(ga, wo_ref[...], NT).astype(bf16)
    gc_ref[...] = gc
    product = gc.astype(f32) * cb.astype(f32)
    high = product.astype(bf16)
    low = (product - high.astype(f32)).astype(bf16)
    head = lax.broadcasted_iota(jnp.int32, (STAT_ROWS, width), 0)
    column = lax.broadcasted_iota(jnp.int32, (STAT_ROWS, width), 1)
    pick = jnp.where(column // HEAD_DIM == head, 1.0, 0.0).astype(bf16)
    d_ref[...] = mul(pick, high, NT) + mul(pick, low, NT)


def spec(shape, pipelined=True):
    zeros = (0,) * (len(shape) - 1)
    if pipelined:
        return pl.BlockSpec(shape, lambda i: (i,) + zeros)
    return pl.BlockSpec(shape, lambda i: (0,) + zeros)


def whole_vmem():
    return pl.BlockSpec(memory_space=pltpu.VMEM)


def params():
    return pltpu.CompilerParams(vmem_limit_bytes=VMEM_BYTES, dimension_semantics=("arbitrary",))


def attention_call(x, w_qkv, vec):
    count, length, width = x.shape
    block = (None, length, width)

    def kernel(x_ref, w_ref, vec_ref, q_ref, k_ref, v_ref, c_ref, l_ref, stat):
        project(x_ref[...], w_ref, vec_ref, q_ref, k_ref, v_ref)
        attend(q_ref, k_ref, v_ref, c_ref, l_ref, stat)

    seq = jax.ShapeDtypeStruct(x.shape, bf16)
    return pl.pallas_call(
        kernel,
        grid=(count,),
        in_specs=[spec(block), whole_vmem(), whole_vmem()],
        out_specs=[spec(block)] * 4 + [spec((None, STAT_ROWS, length))],
        out_shape=[seq] * 4 + [jax.ShapeDtypeStruct((count, STAT_ROWS, length), f32)],
        scratch_shapes=[pltpu.VMEM((length, 128), f32)],
        compiler_params=params(),
        name="attention",
    )(x, w_qkv, vec)


def feed_forward_call(x, cb, cot, w_out, w_inner, w_outer, vec):
    count, length, width = x.shape
    inner = w_inner.shape[1]
    block, wide = (None, length, width), (None, length, inner)

    def kernel(x_ref, cb_ref, cot_ref, wo, wi, wu, vec_ref, out, mid, gf, ga, gc, d, h, gu, sums):
        @pl.when(pl.program_id(0) == 0)
        def _():
            sums[...] = jnp.zeros_like(sums)

        cb = cb_ref[...]
        normed, inverse = to_hidden(x_ref[...], cb, wo, wi, vec_ref, mid, h, gu)
        grad_2 = to_output(normed, cot_ref[...], wu, vec_ref, h, out, gf, sums)
        to_context_grad(grad_2, normed, inverse, cb, wo, wi, wu, vec_ref, gf, ga, gc, d, gu, sums)

    seq = jax.ShapeDtypeStruct(x.shape, bf16)
    seq_wide = jax.ShapeDtypeStruct((count, length, inner), bf16)
    return pl.pallas_call(
        kernel,
        grid=(count,),
        in_specs=[spec(block)] * 3 + [whole_vmem()] * 4,
        out_specs=[spec(block)] * 5
        + [spec((None, STAT_ROWS, length)), spec(wide), spec(wide), spec((16, width), False)],
        out_shape=[seq] * 5
        + [
            jax.ShapeDtypeStruct((count, STAT_ROWS, length), f32),
            seq_wide,
            seq_wide,
            jax.ShapeDtypeStruct((16, width), f32),
        ],
        compiler_params=params(),
        name="feed_forward",
    )(x, cb, cot, w_out, w_inner, w_outer, vec)


def weight_grad_call(left, right, over_left):
    tokens, rows = left.shape
    columns = right.shape[1]
    step = min(rows, columns)

    def kernel(left_ref, right_ref, out_ref):
        out_ref[...] = mul(left_ref[...], right_ref[...], TN).astype(bf16)

    if over_left:
        grid, left_map, right_map, out_map = rows // step, lambda i: (0, i), lambda i: (0, 0), lambda i: (i, 0)
    else:
        grid, left_map, right_map, out_map = columns // step, lambda i: (0, 0), lambda i: (0, i), lambda i: (0, i)
    return pl.pallas_call(
        kernel,
        grid=(grid,),
        in_specs=[pl.BlockSpec((tokens, step), left_map), pl.BlockSpec((tokens, step), right_map)],
        out_specs=pl.BlockSpec((step, step), out_map),
        out_shape=jax.ShapeDtypeStruct((rows, columns), bf16),
        compiler_params=params(),
        name="weight_grad",
    )(left, right)


def attention_back_call(x, q, k, v, gc, ga, stat_l, stat_d, w_qkv):
    count, length, width = x.shape
    block = (None, length, width)
    pairs = HEADS // 2

    def kernel(x_ref, q_ref, k_ref, v_ref, gc_ref, ga_ref, l_ref, d_ref, w_ref, gx_ref, gw_ref, sums_ref, kt, gqt, g, total):
        step = pl.program_id(0)

        @pl.when(step == 0)
        def _():
            sums_ref[...] = jnp.zeros_like(sums_ref)
            total[...] = jnp.zeros_like(total)

        attend_back(q_ref, k_ref, v_ref, gc_ref, l_ref, d_ref, g, kt, gqt, 0, pairs)
        sums_ref[B_QUERY : B_QUERY + 1, :] += column_sum(g[:, :width])
        sums_ref[B_VALUE : B_VALUE + 1, :] += column_sum(g[:, 2 * width :])
        grad = ga_ref[...].astype(f32)
        x = x_ref[...]
        for i in range(3):
            at = slice(i * width, (i + 1) * width)
            grad = grad + mul(g[:, at], w_ref[:, at], NT)
            total[:, at] += mul(x, g[:, at], TN)
        gx_ref[...] = grad.astype(bf16)

        @pl.when(step == count - 1)
        def _():
            gw_ref[...] = total[...].astype(bf16)

    return pl.pallas_call(
        kernel,
        grid=(count,),
        in_specs=[spec(block)] * 6 + [spec((None, STAT_ROWS, length))] * 2 + [whole_vmem()],
        out_specs=[spec(block), spec((width, 3 * width), False), spec((16, width), False)],
        out_shape=[
            jax.ShapeDtypeStruct(x.shape, bf16),
            jax.ShapeDtypeStruct((width, 3 * width), bf16),
            jax.ShapeDtypeStruct((16, width), f32),
        ],
        scratch_shapes=[pltpu.VMEM((width, length), bf16)] * 2
        + [pltpu.VMEM((length, 3 * width), bf16), pltpu.VMEM((width, 3 * width), f32)],
        compiler_params=params(),
        name="attention_back",
    )(x, q, k, v, gc, ga, stat_l, stat_d, w_qkv)


W1, W2, TABLE, M1, M2, UP = range(6)
GATHER_PLAN = {
    1: (("tokens", 1), ("own_z", M2),),
    2: (("own", M2), ("own_z", UP), ("tokens", 2),),
    3: (("hop", UP, 1),),
    4: (("hop", UP, 2), ("own_z", M1),),
    5: (("hop", UP, 3),),
    6: (("hop", M2, 1),),
    7: (("own", M1), ("hop", M2, 2), ("relay", M2, 0),),
    8: (("hop", M2, 3),),
    9: (("tokens", 3), ("hop", M1, 1), ("relay", M2, 1),),
    11: (("hop", M1, 2), ("relay", M2, 2), ("relay", M2, 3), ("swap", M2, 2, 0),),
    12: (("relay", UP, 2), ("own", UP),),
    13: (("swap", UP, 3, 0), ("swap", M2, 3, 0), ("relay", M1, 1), ("hop", M1, 3), ("swap", M2, 0, 1),),
    14: (("relay", M1, 0),),
    15: (("relay", M1, 2), ("relay", UP, 1), ("swap", M2, 1, 1), ("swap", M2, 2, 1),),
    16: (("swap", UP, 1, 0), ("swap", M2, 3, 1),),
    17: (("swap", M2, 1, 0), ("relay", M1, 3), ("relay", UP, 3), ("relay", UP, 0),),
    18: (("cotangent", 2),),
    19: (("swap", UP, 3, 1), ("cotangent", 3),),
    20: (("swap", UP, 2, 1), ("swap", UP, 2, 0), ("swap", UP, 1, 1), ("swap", UP, 0, 1),),
    21: (("cotangent", 0), ("cotangent", 1),),
}


def forward_call(tokens, span_mask, cotangent, w_query, w_key, w_value, w_out, w_inner, w_outer, table, sizes):
    depth_z, depth_y, cores = sizes
    rows, stretch, width = tokens.shape
    inner = w_inner.shape[1]
    part, outer_part = w_query.shape[0], w_outer.shape[0]
    devices = depth_z * depth_y * cores
    count, length = rows // 2, 2 * stretch
    chunks = inner // width
    qkv_width, mid_width = 3 * width, width + inner
    last = depth_z - 1
    ARRAYS = 6
    early = (TABLE, W1, W2)
    shared = (M2, UP)
    places = depth_z * depth_y
    half = width // 2
    m2_half = mid_width // 512 * 128
    m1_width = mid_width - 2 * m2_half

    def kernel(
        tokens_ref, mask_ref, cot_ref, wq_in, wk_in, wv_in, wo_in, wi_in, wu_in, table_in,
        x_out, q_out, k_out, v_out, cb_out, l_out, o_out, mid_out, gf_out, ga_out, gc_out, d_out, h_out, gu_out,
        sums_out, w_qkv_out,
        w_qkv, w_mid, w_up, tables, vec, x_all, cot_all, cot_away, cb_all, t_mid, t_3, t_4, t_5, l_s, stat, inv, d_s,
        normed_all, h_s, gu_s,
        up_send, down_send, z_recv, y_send, y_recv, c_send, c_recv, x_send, x_recv, t_send, t_recv, g_send, g_recv,
        in_sem, out_sem,
    ):
        b, k = lax.axis_index("batch"), lax.axis_index("blk")
        z, y, c = b // (depth_y * cores), (b // cores) % depth_y, b % cores

        def at(z_, y_, c_):
            return (z_ * depth_y + y_) * cores + c_

        barrier = pltpu.get_barrier_semaphore()

        def greet(device):
            pl.semaphore_signal(barrier, inc=1, device_id=device, device_id_type=pl.DeviceIdType.MESH)

        greet((b, 1 - k))
        greet((at(z, 1 - y, c), k))
        greet((at(z, y, 1 - c), k))

        @pl.when(z < last)
        def _():
            greet((at(z + 1, y, c), k))

        @pl.when(z > 0)
        def _():
            greet((at(z - 1, y, c), k))

        shard = pl.ds(b * part, part)
        mine = pl.ds(pl.multiple_of(k * stretch, stretch), stretch)
        theirs = pl.ds(pl.multiple_of((1 - k) * stretch, stretch), stretch)
        loads = [
            pltpu.make_async_copy(wq_in, w_qkv.at[shard, 0:width], in_sem.at[0]),
            pltpu.make_async_copy(wk_in, w_qkv.at[shard, width : 2 * width], in_sem.at[1]),
            pltpu.make_async_copy(wv_in, w_qkv.at[shard, 2 * width : 3 * width], in_sem.at[2]),
            pltpu.make_async_copy(wu_in, w_up.at[pl.ds(b * outer_part, outer_part)], in_sem.at[5]),
            pltpu.make_async_copy(wo_in, w_mid.at[shard, 0:width], in_sem.at[3]),
            pltpu.make_async_copy(wi_in, w_mid.at[shard, width:mid_width], in_sem.at[4]),
            pltpu.make_async_copy(cot_ref.at[pl.ds(k * count, count)], cot_all.at[:, mine], in_sem.at[6]),
            pltpu.make_async_copy(cot_ref.at[pl.ds((1 - k) * count, count)], cot_away, in_sem.at[7]),
            pltpu.make_async_copy(tokens_ref.at[pl.ds(k * count, count)], x_all.at[:, mine], in_sem.at[8]),
        ]
        for copy in loads:
            copy.start()

        raw = table_in[...]
        rolled = pltpu.roll(raw, b * part, 1)
        wide = pltpu.roll(raw[B_INNER : B_INNER + 1, :], (b % (devices // chunks)) * outer_part, 1)
        line = lax.broadcasted_iota(jnp.int32, raw.shape, 0)
        own_table = jnp.where(line < B_INNER, rolled, 0.0)
        own_table = jnp.where(line == B_INNER + b // (devices // chunks), wide, own_table)
        tables[b] = own_table.astype(bf16)

        t_1, t_2 = t_mid.at[0], t_mid.at[1]

        def piece(a, z_, y_, c_, side):
            d = at(z_, y_, c_)
            rows = pl.ds(d * part, part)
            if a == W1:
                return w_qkv.at[rows, : qkv_width // 2]
            if a == W2:
                return w_qkv.at[rows, qkv_width // 2 :]
            if a == TABLE:
                return tables.at[d]
            if a == M1:
                return w_mid.at[rows, :m1_width]
            if a == M2:
                return w_mid.at[rows, pl.ds(pl.multiple_of(m1_width + side * m2_half, 128), m2_half)]
            return w_up.at[pl.ds(d * outer_part, outer_part), pl.ds(pl.multiple_of(side * half, half), half)]

        def remote(ref, device, send, recv):
            return pltpu.make_async_remote_copy(
                src_ref=ref, dst_ref=ref, send_sem=send, recv_sem=recv, device_id=device, device_id_type=pl.DeviceIdType.MESH
            )

        def up(a, zs):
            return remote(piece(a, zs, y, c, k), (at(z + 1, y, c), k), up_send.at[a, zs], z_recv.at[a, zs])

        def down(a, zs):
            return remote(piece(a, zs, y, c, k), (at(z - 1, y, c), k), down_send.at[a, zs], z_recv.at[a, zs])

        def across(a, zs):
            return remote(piece(a, zs, y, c, k), (at(z, 1 - y, c), k), y_send.at[a, zs], y_recv.at[a, zs])

        def core(a, zs, ys, side):
            i = (zs * depth_y + ys) * 2 + (side if a in shared else 0)
            return remote(piece(a, zs, ys, c, side), (at(z, y, 1 - c), k), c_send.at[a, i], c_recv.at[a, i])

        def plane(a, zs, ys):
            i = zs * depth_y + ys
            return remote(piece(a, zs, ys, c, k), (b, 1 - k), x_send.at[a, i], x_recv.at[a, i])

        def arrived(ref, sem):
            remote(ref, (b, 1 - k), sem, sem).wait_recv()

        def begin_z(a):
            @pl.when(z < last)
            def _():
                up(a, z).start()

            @pl.when(z > 0)
            def _():
                down(a, z).start()

        def begin_y(a):
            across(a, z).start()

        def begin_core(a):
            core(a, z, y, k).start()
            if a in shared:
                core(a, z, y, 1 - k).start()

        def levels(step, do):
            if step == 0:
                do(z, 0)
                return

            @pl.when(z >= step)
            def _():
                do(z - step, 1)

            @pl.when(z + step <= last)
            def _():
                do(z + step, -1)

        def hop(a, step):
            def one(zs, way):
                arrived(piece(a, zs, y, c, k), z_recv.at[a, zs])
                if way > 0:
                    @pl.when(z < last)
                    def _():
                        up(a, zs).start()
                else:
                    @pl.when(z > 0)
                    def _():
                        down(a, zs).start()
                across(a, zs).start()
                if a in shared:
                    plane(a, zs, y).start()
                core(a, zs, y, k).start()

            levels(step, one)

        def relay(a, step):
            def one(zs, way):
                arrived(piece(a, zs, 1 - y, c, k), y_recv.at[a, zs])
                if a in shared:
                    plane(a, zs, 1 - y).start()
                core(a, zs, 1 - y, k).start()

            levels(step, one)

        def swap(a, step, ys):
            def one(zs, way):
                arrived(piece(a, zs, ys, c, 1 - k), x_recv.at[a, zs * depth_y + ys])
                core(a, zs, ys, 1 - k).start()

            levels(step, one)

        def complete(a):
            for zs in range(depth_z):
                for ys in range(depth_y):
                    for side in range(2 if a in shared else 1):
                        arrived(piece(a, zs, ys, 1 - c, side), c_recv.at[a, (zs * depth_y + ys) * 2 + side])

        def sent(a):
            for zs in range(depth_z):
                @pl.when((z < last) & (zs <= z))
                def _():
                    up(a, zs).wait_send()

                @pl.when((z > 0) & (zs >= z))
                def _():
                    down(a, zs).wait_send()

                across(a, zs).wait_send()
                for ys in range(depth_y):
                    for side in range(2 if a in shared else 1):
                        core(a, zs, ys, side).wait_send()
                    if a in shared:
                        @pl.when((zs != z) | (ys != y))
                        def _():
                            plane(a, zs, ys).wait_send()

        def token_copy(s):
            return pltpu.make_async_remote_copy(
                src_ref=tokens_ref.at[(1 - k) * count + s],
                dst_ref=x_all.at[s, mine],
                send_sem=t_send.at[s],
                recv_sem=t_recv.at[s],
                device_id=(b, 1 - k),
                device_id_type=pl.DeviceIdType.MESH,
            )

        def grad_copy(s):
            return pltpu.make_async_remote_copy(
                src_ref=cot_away.at[s],
                dst_ref=cot_all.at[s, mine],
                send_sem=g_send.at[s],
                recv_sem=g_recv.at[s],
                device_id=(b, 1 - k),
                device_id_type=pl.DeviceIdType.MESH,
            )

        def put(i, src, dst):
            return pltpu.make_async_copy(src, dst, out_sem.at[i])

        partners = 3 + (z < last).astype(jnp.int32) + (z > 0).astype(jnp.int32)
        pl.semaphore_wait(barrier, partners)
        for a in early:
            if a == W1:
                for i in range(3):
                    loads[i].wait()
            begin_z(a)
            begin_y(a)
            begin_core(a)
        token_copy(0).start()
        for i in (3, 4, 5):
            loads[i].wait()

        def begin_own(a):
            begin_y(a)
            begin_core(a)

        actions = {
            "hop": hop, "relay": relay, "swap": lambda a, step, far: swap(a, step, (1 - y) if far else y),
            "own": begin_own, "own_z": begin_z,
            "tokens": lambda s: token_copy(s).start(), "cotangent": lambda s: grad_copy(s).start(),
        }

        def at_slot(slot):
            for name, *what in GATHER_PLAN.get(slot, ()):
                actions[name](*what)

        def at_slots(first_slot, stride, index, bound):
            for value in range(bound):
                if first_slot + stride * value in GATHER_PLAN:
                    @pl.when(index == value)
                    def _():
                        at_slot(first_slot + stride * value)

        at_slot(0)

        for i in (6, 7):
            loads[i].wait()
        mask = mask_ref[...].astype(f32)
        own, away = jnp.where(k == 0, mask[:count], mask[count:]), jnp.where(k == 0, mask[count:], mask[:count])
        columns = jnp.concatenate([own, away], 0).T
        for s in range(count):
            cot_all[s, mine, :] = (cot_all[s, mine, :].astype(f32) * columns[:, s : s + 1]).astype(bf16)
            cot_away[s] = (cot_away[s].astype(f32) * columns[:, count + s : count + s + 1]).astype(bf16)

        loads[8].wait()
        for step in range(1, depth_z):
            for a in early:
                hop(a, step)
            at_slot(step)
            for a in early:
                relay(a, step - 1)
        for a in early:
            relay(a, last)
        at_slot(4)
        for a in early:
            complete(a)
        vec[...] = jnp.sum(tables[...].astype(f32), 0)
        save_w = put(0, w_qkv, w_qkv_out)
        save_w.start()

        def first(s, carry):
            arrived(x_all.at[s, theirs], t_recv.at[s])
            saves = [
                put(1, x_all.at[s], x_out.at[s]),
                put(2, t_1, q_out.at[s]),
                put(3, t_2, k_out.at[s]),
                put(4, t_3, v_out.at[s]),
                put(5, cb_all.at[s], cb_out.at[s]),
                put(6, l_s, l_out.at[s]),
            ]

            @pl.when(s > 0)
            def _():
                for save in saves[:4]:
                    save.wait()

            project(x_all[s], w_qkv, vec, t_1, t_2, t_3)
            for save in saves[:4]:
                save.start()
            at_slots(5, 3, s, count)
            stat[...] = jnp.zeros_like(stat)
            attend_pairs(t_1, t_2, t_3, cb_all.at[s], stat, 0, HEADS // 4)
            at_slots(6, 3, s, count)
            attend_pairs(t_1, t_2, t_3, cb_all.at[s], stat, HEADS // 4, HEADS // 2)

            @pl.when(s > 0)
            def _():
                for save in saves[4:]:
                    save.wait()

            l_s[...] = stat[...].T[:STAT_ROWS]
            for save in saves[4:]:
                save.start()
            at_slots(7, 3, s, count)
            return carry

        lax.fori_loop(0, count, first, 0)
        at_slot(17)
        for a in (M1, M2):
            complete(a)
        for i, (src, dst) in enumerate(((x_all.at[0], x_out.at[0]), (t_1, q_out.at[0]), (t_2, k_out.at[0]), (t_3, v_out.at[0]), (cb_all.at[0], cb_out.at[0]), (l_s, l_out.at[0]))):
            put(i + 1, src, dst).wait()
        save_w.wait()
        sums_out[...] = jnp.zeros_like(sums_out)
        w_o, w_i = w_mid.at[:, 0:width], w_mid.at[:, width:mid_width]
        O, GF, GA, GC, DELTA, H, GU, H_IN, GU_IN, MID = 8, 9, 10, 11, 12, 13, 15, 17, 19, 21

        lane = lax.broadcasted_iota(jnp.int32, inv.shape, 1)
        inv[...] = jnp.zeros_like(inv)

        def second(s, carry):
            slot = s % 2

            mid_s = t_mid.at[slot]

            @pl.when(s >= 2)
            def _():
                put(MID + slot, mid_s, mid_out.at[s]).wait()
                put(H + slot, h_s.at[slot], h_out.at[s]).wait()
                put(GU + slot, gu_s.at[slot], gu_out.at[s]).wait()

            normed, inverse = to_hidden(x_all[s], cb_all[s], w_o, w_i, vec, mid_s, h_s.at[slot], gu_s.at[slot])
            normed_all[s] = normed
            inv[...] = jnp.where(lane == s, inverse, inv[...])
            put(MID + slot, mid_s, mid_out.at[s]).start()
            put(H + slot, h_s.at[slot], h_out.at[s]).start()

            @pl.when(s < 2)
            def _():
                put(GU + slot, gu_s.at[slot], gu_out.at[s]).start()

            at_slots(18, 1, s, count)
            return carry

        lax.fori_loop(0, count, second, 0)
        for slot in range(2):
            put(MID + slot, t_mid.at[slot], mid_out.at[0]).wait()
        complete(UP)

        def third(i, carry):
            s = (i + count // 2) % count
            slot = i % 2
            at_slots(22, 1, i, count)
            arrived(cot_all.at[s, theirs], g_recv.at[s])
            saves = [
                put(O, t_1, o_out.at[s]),
                put(GF, t_3, gf_out.at[s]),
                put(GA, t_4, ga_out.at[s]),
                put(GC, t_5, gc_out.at[s]),
                put(DELTA, d_s, d_out.at[s]),
            ]

            @pl.when(i >= 2)
            def _():
                put(H_IN + slot, h_out.at[s], h_s.at[slot]).wait()
                put(GU_IN + slot, gu_out.at[s], gu_s.at[slot]).wait()

            @pl.when(i > 0)
            def _():
                for save in saves[:2]:
                    save.wait()

            grad_2 = to_output(normed_all[s], cot_all[s], w_up, vec, h_s.at[slot], t_1, t_3, sums_out)
            for save in saves[:2]:
                save.start()

            @pl.when(i > 0)
            def _():
                for save in saves[2:]:
                    save.wait()

            @pl.when((i > 0) & (i + 1 < count))
            def _():
                put(GU + 1 - slot, gu_s.at[1 - slot], gu_out.at[s]).wait()
                put(GU_IN + 1 - slot, gu_out.at[(s + 1) % count], gu_s.at[1 - slot]).start()

            inverse = jnp.sum(jnp.where(lane == s, inv[...], 0.0), 1, keepdims=True)
            to_context_grad(
                grad_2, normed_all[s], inverse, cb_all[s], w_o, w_i, w_up, vec, t_3, t_4, t_5, d_s, gu_s.at[slot], sums_out
            )
            for save in saves[2:]:
                save.start()
            put(GU + slot, gu_s.at[slot], gu_out.at[s]).start()

            @pl.when(i + 2 < count)
            def _():
                put(H + slot, h_s.at[slot], h_out.at[s]).wait()
                put(H_IN + slot, h_out.at[(s + 2) % count], h_s.at[slot]).start()

            return carry

        lax.fori_loop(0, count, third, 0)
        for i, src, dst in ((O, t_1, o_out), (GF, t_3, gf_out), (GA, t_4, ga_out), (GC, t_5, gc_out), (DELTA, d_s, d_out)):
            put(i, src, dst.at[0]).wait()
        for slot in range(2):
            put(GU + slot, gu_s.at[slot], gu_out.at[0]).wait()
        for s in range(count):
            token_copy(s).wait_send()
            grad_copy(s).wait_send()
        for a in range(ARRAYS):
            sent(a)

    seq = jax.ShapeDtypeStruct((count, length, width), bf16)
    seq_wide = jax.ShapeDtypeStruct((count, length, inner), bf16)
    stat_shape = jax.ShapeDtypeStruct((count, STAT_ROWS, length), f32)
    hbm = pl.BlockSpec(memory_space=pl.ANY)
    one = pltpu.VMEM((length, width), bf16)
    two_wide = pltpu.VMEM((2, length, inner), bf16)
    all_seq = pltpu.VMEM((count, length, width), bf16)
    stat_one = pltpu.VMEM((STAT_ROWS, length), f32)
    lanes = pltpu.VMEM((length, 128), f32)
    dma = pltpu.SemaphoreType.DMA
    return pl.pallas_call(
        kernel,
        in_specs=[hbm, whole_vmem()] + [hbm] * 7 + [whole_vmem()],
        out_specs=[hbm] * 14 + [whole_vmem(), hbm],
        out_shape=[seq] * 5 + [stat_shape] + [seq] * 5 + [stat_shape, seq_wide, seq_wide]
        + [jax.ShapeDtypeStruct((16, width), f32), jax.ShapeDtypeStruct((width, qkv_width), bf16)],
        scratch_shapes=[
            pltpu.VMEM((width, qkv_width), bf16),
            pltpu.VMEM((width, mid_width), bf16),
            pltpu.VMEM((inner, width), bf16),
            pltpu.VMEM((devices, 16, width), bf16),
            pltpu.VMEM((16, width), f32),
            all_seq, all_seq,
            pltpu.VMEM((count, stretch, width), bf16),
            all_seq,
            pltpu.VMEM((2, length, width), bf16), one, one, one, stat_one, lanes, lanes, stat_one,
            pltpu.VMEM((count, length, width), f32),
            two_wide, two_wide,
            dma((ARRAYS, depth_z)), dma((ARRAYS, depth_z)), dma((ARRAYS, depth_z)),
            dma((ARRAYS, depth_z)), dma((ARRAYS, depth_z)),
            dma((ARRAYS, 2 * places)), dma((ARRAYS, 2 * places)), dma((ARRAYS, places)), dma((ARRAYS, places)),
            dma((count,)), dma((count,)), dma((count,)), dma((count,)), dma((9,)), dma((23,)),
        ],
        compiler_params=pltpu.CompilerParams(collective_id=1, has_side_effects=True, vmem_limit_bytes=63 * 2**20),
        name="forward",
    )(tokens, span_mask, cotangent, w_query, w_key, w_value, w_out, w_inner, w_outer, table)


def backward_call(x, q, k, v, cb, mid, gf, ga, gc, hidden, gu, out, stat_l, stat_d, w_qkv, sums, sizes):
    depth_z, depth_y, cores = sizes
    count, length, width = x.shape
    inner = hidden.shape[2]
    devices = depth_z * depth_y * cores
    part, outer_part = width // devices, inner // devices
    stretch, rows = length // 2, 2 * count
    chunks = inner // width
    GROUPS = 3
    pairs = HEADS // 2 // GROUPS
    column = pairs * PAIR
    narrow = width // GROUPS
    OUT = chunks
    QKV = chunks + 1
    N = QKV + GROUPS
    SLOTS = 2
    STEPS = 5
    tokens_all = count * length

    def kernel(
        x_in, q_in, k_in, v_in, cb_in, mid_in, gf_in, ga_in, gc_in, h_in, gu_in, out_in, w_in, l_ref, d_ref, sums_ref,
        output, grad_tokens, g_query, g_key, g_value, g_out, g_inner, g_outer, vectors,
        big, pool, w_cat, ga_s, gx_s, kt, gqt, own_s, own_o, r1, r2, r3, s4, r4, r1o, r2o, r3o, s4o, r4o, v_own, v_got,
        s1_send, s1_recv, s2_send, s2_recv, s3_send, s3_recv, s4_send, s4_recv,
        v_send, v_recv, o_send, o_recv, g_send, g_recv, big_sem, pool_sem, w_sem, ga_sem, keep_sem,
    ):
        b, k = lax.axis_index("batch"), lax.axis_index("blk")
        z, y, c = b // (depth_y * cores), (b // cores) % depth_y, b % cores

        def at(z_, y_, c_):
            return (z_ * depth_y + y_) * cores + c_

        beside = (b, 1 - k)
        other_core = (at(z, y, 1 - c), k)
        other_y = (at(z, 1 - y, c), k)

        def level(j):
            return (z + j) % depth_z

        barrier = pltpu.get_barrier_semaphore()
        partners = [beside, other_core, other_y] + [(at(level(j), y, c), k) for j in range(1, depth_z)]
        for device in partners:
            pl.semaphore_signal(barrier, inc=1, device_id=device, device_id_type=pl.DeviceIdType.MESH)

        def remote(src, dst, device, send, recv):
            return pltpu.make_async_remote_copy(
                src_ref=src, dst_ref=dst, send_sem=send, recv_sem=recv, device_id=device, device_id_type=pl.DeviceIdType.MESH
            )

        def load(i, src):
            return pltpu.make_async_copy(src, big.at[i], big_sem.at[i])

        def wide_load(i, src, j):
            return pltpu.make_async_copy(src.at[:, :, j * width : (j + 1) * width], big.at[i], big_sem.at[i])

        def pool_load(s, slot):
            return [
                pltpu.make_async_copy(src.at[s], pool.at[slot, i], pool_sem.at[slot, i])
                for i, src in enumerate((q_in, k_in, v_in, gc_in))
            ]

        def w_load(i, g):
            return pltpu.make_async_copy(
                w_in.at[:, i * width + g * column : i * width + (g + 1) * column],
                w_cat.at[g, :, i * column : (i + 1) * column],
                w_sem.at[i, g],
            )

        first_loads = [load(0, mid_in), wide_load(2, gu_in, 0), load(1, gf_in), wide_load(3, gu_in, 1)]
        for copy in first_loads:
            copy.start()
        mine = pl.ds(pl.multiple_of(k * stretch, stretch), stretch)
        theirs = pl.ds(pl.multiple_of((1 - k) * stretch, stretch), stretch)

        def buffers(g, outer):
            if outer:
                return own_o.at[g], r1o.at[g], r2o.at[g], r3o.at[g], s4o.at[g], r4o.at[g], N + g
            return own_s.at[g % SLOTS], r1.at[g], r2.at[g], r3.at[g], s4.at[g], r4.at[g], g

        def step_1(g, outer=False):
            own, a1, _, _, _, _, i = buffers(g, outer)
            return remote(own.at[:, :, 1 - c], a1, other_core, s1_send.at[i], s1_recv.at[i])

        def step_2(g, outer=False):
            _, a1, a2, _, _, _, i = buffers(g, outer)
            return remote(a1.at[:, 1 - y], a2, other_y, s2_send.at[i], s2_recv.at[i])

        def step_3(g, j, outer=False):
            _, _, a2, a3, _, _, i = buffers(g, outer)
            return remote(
                a2.at[level(j)], a3.at[j - 1], (at(level(j), y, c), k), s3_send.at[i, j - 1], s3_recv.at[i, j - 1]
            )

        def step_4(g, outer=False):
            _, _, _, _, a4, b4, i = buffers(g, outer)
            return remote(a4, b4, beside, s4_send.at[i], s4_recv.at[i])

        def move_1(g, outer=False):
            own, a1, _, _, _, _, _ = buffers(g, outer)
            step_1(g, outer).wait()

            def add(i, carry):
                zi, yi = i // depth_y, i % depth_y
                a1[zi, yi] = a1[zi, yi] + own[zi, yi, c]
                return carry

            lax.fori_loop(0, depth_z * depth_y, add, 0)
            step_2(g, outer).start()

        def move_2(g, outer=False):
            _, a1, a2, _, _, _, _ = buffers(g, outer)
            step_2(g, outer).wait()

            def add(zi, carry):
                a2[zi] = a2[zi] + a1[zi, y]
                return carry

            lax.fori_loop(0, depth_z, add, 0)
            for j in range(1, depth_z):
                step_3(g, j, outer).start()

        def move_3(g, outer=False):
            _, _, a2, a3, a4, _, _ = buffers(g, outer)
            for j in range(1, depth_z):
                step_3(g, j, outer).wait()
            total = a2[z].astype(f32)
            for j in range(1, depth_z):
                total = total + a3[j - 1].astype(f32)
            a4[...] = total.astype(bf16)
            step_4(g, outer).start()

        def move_4(g, outer=False):
            _, _, _, _, a4, b4, _ = buffers(g, outer)
            step_4(g, outer).wait()
            total = a4[...].astype(f32) + b4[...].astype(f32)
            if outer:
                g_outer[:, g * narrow : (g + 1) * narrow] = total
            elif g < OUT:
                g_inner[:, g * width : (g + 1) * width] = total
            elif g == OUT:
                g_out[...] = total
            else:
                for i, ref in enumerate((g_query, g_key, g_value)):
                    ref[:, (g - QKV) * column : (g - QKV + 1) * column] = total[:, i * column : (i + 1) * column]

        def whole(i):
            return big[i].reshape(tokens_all, width)

        def begin(g, value):
            own_s[g % SLOTS] = value.astype(bf16).reshape(depth_z, depth_y, cores, part, width)
            step_1(g).start()

        pl.semaphore_wait(barrier, len(partners))
        output_copies = [
            remote(out_in.at[s, theirs], output.at[k * count + s], beside, o_send.at[s], o_recv.at[s]) for s in range(count)
        ]
        keep_output = pltpu.make_async_copy(out_in.at[:, mine], output.at[pl.ds(k * count, count)], keep_sem.at[0])
        for copy in output_copies:
            copy.start()

        first_loads[0].wait()
        for j in range(chunks):
            wide_load(2 + j % 2, gu_in, j).wait()
            if j >= SLOTS:
                move_1(j - SLOTS)
            begin(j, mul(whole(0), whole(2 + j % 2), TN))
            following = j + 2 - chunks
            if following < 0:
                wide_load(2 + j % 2, gu_in, j + 2).start()
            else:
                wide_load(2 + j % 2, h_in, following).start()
            if j == 0:
                for s in range(2):
                    for copy in pool_load(s, s):
                        copy.start()
            if j == 1:
                keep_output.start()
                for g in range(GROUPS):
                    for i in range(3):
                        w_load(i, g).start()
        load(0, ga_in).start()
        first_loads[2].wait()
        for j in range(chunks):
            wide_load(2 + j % 2, h_in, j).wait()
            product = mul(whole(2 + j % 2), whole(1), TN).astype(bf16)
            for g in range(GROUPS):
                own_o[g, j] = product[:, g * narrow : (g + 1) * narrow].reshape(depth_y, cores, outer_part, narrow)
            if j + 2 < chunks:
                wide_load(2 + j % 2, h_in, j + 2).start()
            elif j + 2 == chunks:
                load(2 + j % 2, cb_in).start()
            else:
                load(2 + j % 2, x_in).start()
            if j < SLOTS:
                move_1(chunks - SLOTS + j)
            if j == 2:
                move_2(0)
        for g in range(GROUPS):
            step_1(g, True).start()
        move_2(1)
        load(0, ga_in).wait()
        load(2 + chunks % 2, cb_in).wait()
        begin(OUT, mul(whole(2 + chunks % 2), whole(0), TN))
        for copy in pool_load(2, 2):
            copy.start()
        for g in range(GROUPS):
            for i in range(3):
                w_load(i, g).wait()
        load(2 + (chunks + 1) % 2, x_in).wait()
        x_at = 2 + (chunks + 1) % 2
        v_own[0] = sums_ref[...]

        cells = GROUPS * count
        plan = {
            0: [lambda: [move_1(g, True) for g in range(GROUPS)]],
            1: [lambda: move_1(OUT), lambda: move_2(2), lambda: move_3(0)],
            2: [lambda: move_3(1)],
            3: [lambda: move_2(3)],
            4: [lambda: move_3(2)],
            5: [lambda: move_2(0, True), lambda: move_4(0)],
            6: [lambda: move_3(3), lambda: move_4(1)],
            7: [lambda: move_2(1, True), lambda: move_4(2)],
            8: [lambda: move_3(0, True)],
            9: [lambda: move_2(2, True), lambda: move_4(3)],
            10: [lambda: move_1(QKV), lambda: move_2(OUT), lambda: move_3(1, True), lambda: move_4(0, True)],
            11: [lambda: move_1(QKV + 1), lambda: move_3(2, True)],
        }

        def gx_copies(s):
            away = remote(gx_s.at[theirs], grad_tokens.at[k * count + s], beside, g_send.at[s], g_recv.at[s])
            keep = pltpu.make_async_copy(gx_s.at[mine], grad_tokens.at[k * count + s], keep_sem.at[1])
            return away, keep

        ga_load = [pltpu.make_async_copy(ga_in.at[s], ga_s, ga_sem.at[0]) for s in range(count)]
        ga_load[0].start()

        def cell(i, carry):
            s, g = i // GROUPS, i % GROUPS
            slot = s % 3

            @pl.when(g == 0)
            def _():
                for copy in pool_load(s, slot):
                    copy.wait()

            attend_back(
                pool.at[slot, 0], pool.at[slot, 1], pool.at[slot, 2], pool.at[slot, 3], l_ref.at[s], d_ref.at[s],
                big.at[g, s], kt, gqt, g * pairs, pairs,
            )
            span = pl.ds(pl.multiple_of(g * column, column), column)
            v_own[0, B_QUERY : B_QUERY + 1, span] += column_sum(big[g, s, :, :column])
            v_own[0, B_VALUE : B_VALUE + 1, span] += column_sum(big[g, s, :, 2 * column :])

            @pl.when(i == GROUPS - 1)
            def _():
                for copy in pool_load(3, 0):
                    copy.start()

            for when, steps in plan.items():
                @pl.when(i == when)
                def _():
                    for step in steps:
                        step()

            @pl.when(s == count - 1)
            def _():
                begin(QKV + g, mul(whole(x_at), big[g].reshape(tokens_all, width), TN))

            @pl.when(g == GROUPS - 1)
            def _():
                ga_load[0].wait()

                @pl.when(s > 0)
                def _():
                    away, keep = gx_copies(s - 1)
                    away.wait_send()
                    keep.wait()

                grad = ga_s[...].astype(f32)
                for group in range(GROUPS):
                    grad = grad + mul(big[group, s], w_cat[group], NT)
                gx_s[...] = grad.astype(bf16)
                away, keep = gx_copies(s)
                away.start()
                keep.start()

                @pl.when(s < count - 1)
                def _():
                    pltpu.make_async_copy(ga_in.at[s + 1], ga_s, ga_sem.at[0]).start()

            return carry

        lax.fori_loop(0, cells, cell, 0)

        towards = [other_core, other_y, (at(z + 1 - 2 * (z % 2), y, c), k), (at((z + 2) % 4, y, c), k), beside]

        def v_copy(i):
            return remote(v_own.at[i], v_got.at[i], towards[i], v_send.at[i], v_recv.at[i])

        def v_move(i):
            v_copy(i).wait()
            v_own[i + 1] = v_own[i] + v_got[i]
            if i + 1 < STEPS:
                v_copy(i + 1).start()

        v_copy(0).start()
        last_group = N - 1
        move_1(last_group)
        v_move(0)
        move_2(QKV)
        v_move(1)
        move_4(1, True)
        move_3(OUT)
        v_move(2)
        move_2(QKV + 1)
        v_move(3)
        move_3(QKV)
        move_2(last_group)
        move_4(2, True)
        v_move(4)
        total = v_own[STEPS]
        inner_row = v_own[STEPS, pl.ds(B_INNER + b // (devices // chunks), 1), :]
        rolled = pltpu.roll(total, (width - b * part) % width, 1)
        wide = pltpu.roll(inner_row, (width - (b % (devices // chunks)) * outer_part) % width, 1)
        line = lax.broadcasted_iota(jnp.int32, total.shape, 0)
        vectors[...] = jnp.where(line == B_INNER, wide, rolled)
        move_4(OUT)
        move_3(QKV + 1)
        move_4(QKV)
        move_3(last_group)
        move_4(QKV + 1)
        move_4(last_group)
        away, keep = gx_copies(count - 1)
        away.wait_send()
        keep.wait()
        keep_output.wait()
        for s in range(count):
            output_copies[s].wait_send()
            remote(out_in.at[s, theirs], output.at[(1 - k) * count + s], beside, o_send.at[s], o_recv.at[s]).wait_recv()
            remote(gx_s.at[theirs], grad_tokens.at[(1 - k) * count + s], beside, g_send.at[s], g_recv.at[s]).wait_recv()

    hbm = pl.BlockSpec(memory_space=pl.ANY)
    dma = pltpu.SemaphoreType.DMA
    every = N + GROUPS

    def vmem(*shape):
        return pltpu.VMEM(shape, bf16)

    def result(*shape):
        return jax.ShapeDtypeStruct(shape, f32)

    back = jax.ShapeDtypeStruct((rows, stretch, width), bf16)
    return pl.pallas_call(
        kernel,
        in_specs=[hbm] * 13 + [whole_vmem()] * 3,
        out_specs=[hbm] * 2 + [whole_vmem()] * 7,
        out_shape=[
            back, back, result(part, width), result(part, width), result(part, width), result(part, width),
            result(part, inner), result(outer_part, width), result(16, width),
        ],
        scratch_shapes=[
            vmem(4, count, length, width),
            vmem(3, 4, length, width),
            vmem(GROUPS, width, 3 * column),
            vmem(length, width), vmem(length, width),
            vmem(column, length), vmem(column, length),
            vmem(SLOTS, depth_z, depth_y, cores, part, width),
            vmem(GROUPS, depth_z, depth_y, cores, outer_part, narrow),
            vmem(N, depth_z, depth_y, part, width), vmem(N, depth_z, part, width), vmem(N, depth_z - 1, part, width),
            vmem(N, part, width), vmem(N, part, width),
            vmem(GROUPS, depth_z, depth_y, outer_part, narrow), vmem(GROUPS, depth_z, outer_part, narrow),
            vmem(GROUPS, depth_z - 1, outer_part, narrow), vmem(GROUPS, outer_part, narrow), vmem(GROUPS, outer_part, narrow),
            pltpu.VMEM((STEPS + 1, 16, width), f32), pltpu.VMEM((STEPS, 16, width), f32),
            dma((every,)), dma((every,)), dma((every,)), dma((every,)),
            dma((every, depth_z - 1)), dma((every, depth_z - 1)), dma((every,)), dma((every,)),
            dma((STEPS,)), dma((STEPS,)), dma((count,)), dma((count,)), dma((count,)), dma((count,)),
            dma((4,)), dma((3, 4)), dma((3, GROUPS)), dma((1,)), dma((2,)),
        ],
        compiler_params=pltpu.CompilerParams(collective_id=2, has_side_effects=True, vmem_limit_bytes=63 * 2**20),
        name="backward",
    )(x, q, k, v, cb, mid, gf, ga, gc, hidden, gu, out, w_qkv, stat_l, stat_d, sums)


def pack_shard(w_query, w_key, w_value, w_out, w_inner, w_outer, vectors):
    width = w_query.shape[1]
    inner_parts = [w_inner[:, i : i + width] for i in range(0, w_inner.shape[1], width)]
    small = jnp.concatenate(vectors)
    body_rows = sum(part.shape[0] for part in (w_query, w_key, w_value, w_out, w_outer, *inner_parts))
    rows = -(-(body_rows + 1) // 16) * 16
    tail = jnp.zeros(((rows - body_rows) * width,), small.dtype).at[: small.shape[0]].set(small)
    return jnp.concatenate(
        [w_query, w_key, w_value, w_out, *inner_parts, w_outer, tail.reshape(-1, width)]
    )


def vec_table(small, vec_names_sizes):
    rows, at = [], 0
    for size in vec_names_sizes:
        rows.append(small[:, at : at + size].reshape(-1))
        at += size
    return rows


def gather_weights(w_query, w_key, w_value, w_out, w_inner, w_outer, vectors):
    part, width = w_query.shape
    outer_part = w_outer.shape[0]
    chunks = w_inner.shape[1] // width
    sizes = [vector.shape[0] for vector in vectors]
    packed = pack_shard(w_query, w_key, w_value, w_out, w_inner, w_outer, vectors)
    gathered = lax.all_gather(packed, "batch", axis=0)

    def weight(at, count):
        return gathered[:, at : at + count].reshape(-1, width)

    squares = [weight(i * part, part) for i in range(4 + chunks)]
    outer_at = (4 + chunks) * part
    w_outer_all = weight(outer_at, outer_part)
    small = gathered[:, outer_at + outer_part :].reshape(gathered.shape[0], -1)
    vec = jnp.concatenate(vec_table(small, sizes)).reshape(-1, width).astype(f32)
    vec = jnp.concatenate([vec, jnp.zeros((16 - vec.shape[0], width), f32)])
    return jnp.concatenate(squares[:3], 1), squares[3], jnp.concatenate(squares[4:], 1), w_outer_all, vec


def body(
    tokens,
    span_mask,
    cotangent,
    w_query,
    b_query,
    w_key,
    w_value,
    b_value,
    w_out,
    b_out,
    gain_first,
    bias_first,
    w_inner,
    b_inner,
    w_outer,
    b_outer,
    gain_second,
    bias_second,
):
    rows, stretch, width = tokens.shape
    inner = w_inner.shape[1]
    part = w_query.shape[0]
    outer_part = w_outer.shape[0]
    vectors = (b_query, b_value, b_out, gain_first, bias_first, b_outer, gain_second, bias_second, b_inner)
    sizes = [vector.shape[0] for vector in vectors]

    devices = lax.axis_size("batch")
    chunks = inner // width
    swap = functools.partial(lax.all_to_all, axis_name="blk", tiled=True)
    outer_at = (4 + chunks) * part
    shard_rows = -(-(outer_at + outer_part + 1) // 16) * 16
    if (devices, lax.axis_size("blk")) == (16, 2):
        table = sum(
            lax.pad(
                vector.astype(f32).reshape(1, -1), f32(0), ((i, 15 - i, 0), (0, width - vector.shape[0], 0))
            )
            for i, vector in enumerate(vectors)
        )
        x, q, k, v, cb, stat_l, out, mid, gf, ga, gc, stat_d, hidden, gu, sums_ffn, w_qkv = forward_call(
            tokens, span_mask, cotangent, w_query, w_key, w_value, w_out, w_inner, w_outer, table, (4, 2, 2)
        )
        results = backward_call(
            x, q, k, v, cb, mid, gf, ga, gc, hidden, gu, out, stat_l, stat_d, w_qkv, sums_ffn, (4, 2, 2)
        )
        output, grad_tokens, g_query, g_key, g_value, g_out, g_inner, g_outer, totals = results
        small = [totals[i, :size] for i, size in enumerate(sizes)]
        return (
            output, grad_tokens, g_query, small[0], g_key, g_value, small[1], g_out, small[2], small[3], small[4], g_inner,
            small[8], g_outer, small[5], small[6], small[7],
        )
    w_qkv, w_out_all, w_inner_all, w_outer_all, vec = gather_weights(
        w_query, w_key, w_value, w_out, w_inner, w_outer, vectors
    )
    masked = cotangent * span_mask[..., None].astype(bf16)
    x = swap(tokens, split_axis=0, concat_axis=1)
    cot = swap(masked, split_axis=0, concat_axis=1)
    q, k, v, cb, stat_l = attention_call(x, w_qkv, vec)
    out, mid, gf, ga, gc, stat_d, hidden, gu, sums_ffn = feed_forward_call(
        x, cb, cot, w_out_all, w_inner_all, w_outer_all, vec
    )
    gx, gw_qkv, sums_att = attention_back_call(x, q, k, v, gc, ga, stat_l, stat_d, w_qkv)
    output = swap(out, split_axis=1, concat_axis=0)
    grad_tokens = swap(gx, split_axis=1, concat_axis=0)

    def flat(values):
        return values.reshape(-1, values.shape[-1])

    gw_out = weight_grad_call(flat(cb), flat(ga), False)
    gw_inner = weight_grad_call(flat(mid), flat(gu), False)
    gw_outer = weight_grad_call(flat(hidden), flat(gf), True)

    sums = sums_ffn + sums_att
    small_sums = [sums[i].reshape(devices, -1) for i in range(B_INNER)]
    small_sums.append(sums[B_INNER : B_INNER + chunks].reshape(devices, -1))
    tail = jnp.concatenate(small_sums, 1).astype(bf16)
    tail = jnp.pad(tail, ((0, 0), (0, (shard_rows - outer_at - outer_part) * width - tail.shape[1])))
    pieces = [gw_qkv[:, i * width : (i + 1) * width].reshape(devices, part, width) for i in range(3)]
    pieces.append(gw_out.reshape(devices, part, width))
    pieces += [gw_inner[:, i * width : (i + 1) * width].reshape(devices, part, width) for i in range(chunks)]
    pieces.append(gw_outer.reshape(devices, outer_part, width))
    pieces.append(tail.reshape(devices, -1, width))
    grads = jnp.concatenate(pieces, 1)
    share = lax.psum_scatter(grads, "batch", scatter_dimension=0, tiled=False)
    share = lax.psum(share, "blk").astype(f32)
    square = [share[i * part : (i + 1) * part] for i in range(4 + chunks)]
    share_small = share[outer_at + outer_part :].reshape(-1)
    small_out, at = [], 0
    for size in sizes:
        small_out.append(share_small[at : at + size])
        at += size
    (g_b_query, g_b_value, g_b_out, g_gain_1, g_bias_1, g_b_outer, g_gain_2, g_bias_2, g_b_inner) = small_out
    return (
        output,
        grad_tokens,
        square[0],
        g_b_query,
        square[1],
        square[2],
        g_b_value,
        square[3],
        g_b_out,
        g_gain_1,
        g_bias_1,
        jnp.concatenate(square[4:], 1),
        g_b_inner,
        share[outer_at : outer_at + outer_part],
        g_b_outer,
        g_gain_2,
        g_bias_2,
    )


def solution(mesh):
    block = P("batch", "blk", None)
    matrix, vector = P("batch", None), P("batch")
    weights = (
        matrix, vector, matrix, matrix, vector, matrix, vector, vector, vector, matrix, vector, matrix, vector, vector, vector,
    )
    return jax.shard_map(
        body,
        mesh=mesh,
        in_specs=(block, P("batch", "blk"), block) + weights,
        out_specs=(block, block) + weights,
        check_vma=False,
    )
```

```python
import functools

import jax
import jax.numpy as jnp
from jax import lax
from jax.experimental import pallas as pl
from jax.experimental.pallas import tpu as pltpu
from jax.sharding import PartitionSpec as P

HEADS = 12
HEAD_DIM = 64
PAIR = 2 * HEAD_DIM
STAT_ROWS = 16
VMEM_BYTES = 60 * 2**20

epsilon = 1e-06
bf16 = jnp.bfloat16
f32 = jnp.float32

NN = (((1,), (0,)), ((), ()))
NT = (((1,), (1,)), ((), ()))
TN = (((0,), (0,)), ((), ()))

B_QUERY, B_VALUE, B_OUT, GAIN_1, BIAS_1, B_OUTER, GAIN_2, BIAS_2, B_INNER = range(9)


def mul(left, right, dims=NN):
    return lax.dot_general(left, right, dims, preferred_element_type=f32)


def row(ref, index):
    return ref[index : index + 1, :]


def halves(block):
    lane = lax.broadcasted_iota(jnp.int32, block.shape, 1)
    zero = jnp.zeros_like(block)
    return jnp.where(lane < HEAD_DIM, block, zero), jnp.where(lane < HEAD_DIM, zero, block)


def pair_at(p):
    return pl.ds(pl.multiple_of(p * PAIR, PAIR), PAIR)


def normalize(values):
    center = values - jnp.mean(values, -1, keepdims=True)
    inverse = lax.rsqrt(jnp.mean(center * center, -1, keepdims=True) + epsilon)
    return center * inverse, inverse


def norm_back(grad, normed, inverse, gain):
    scaled = grad * gain
    return inverse * (
        scaled
        - jnp.mean(scaled, -1, keepdims=True)
        - normed * jnp.mean(scaled * normed, -1, keepdims=True)
    )


def column_sum(values):
    return jnp.sum(values.astype(f32), 0, keepdims=True)


def project(x, w_ref, vec_ref, q_ref, k_ref, v_ref):
    width = x.shape[-1]
    q = (mul(x, w_ref[:, :width]) + row(vec_ref, B_QUERY)).astype(bf16)
    q_ref[...] = q * bf16(HEAD_DIM**-0.5)
    k_ref[...] = mul(x, w_ref[:, width : 2 * width]).astype(bf16)
    v_ref[...] = (mul(x, w_ref[:, 2 * width :]) + row(vec_ref, B_VALUE)).astype(bf16)


def attend_pairs(q_ref, k_ref, v_ref, c_ref, stat, first, end):
    lane = lax.broadcasted_iota(jnp.int32, stat.shape, 1)

    def pair(p, carry):
        at = pair_at(p)
        q2, k2, v2 = q_ref[:, at], k_ref[:, at], v_ref[:, at]
        context = None
        for h, (k_one, v_one) in enumerate(zip(halves(k2), halves(v2))):
            scores = mul(q2, k_one, NT)
            best = jnp.max(scores, 1, keepdims=True)
            weights = jnp.exp(scores - best)
            total = jnp.sum(weights, 1, keepdims=True)
            part = mul(weights.astype(bf16), v_one) * (1.0 / total)
            context = part if context is None else context + part
            stat[...] = jnp.where(lane == 2 * p + h, best + jnp.log(total), stat[...])
        c_ref[:, at] = context.astype(bf16)
        return carry

    lax.fori_loop(first, end, pair, 0, unroll=3)


def attend(q_ref, k_ref, v_ref, c_ref, l_ref, stat):
    stat[...] = jnp.zeros_like(stat)
    attend_pairs(q_ref, k_ref, v_ref, c_ref, stat, 0, HEADS // 2)
    l_ref[...] = stat[...].T[:STAT_ROWS]


def attend_back(q_ref, k_ref, v_ref, g_ref, l_ref, d_ref, out_ref, kt, gqt, first, pairs):
    part = pairs * PAIR
    columns = pl.ds(pl.multiple_of(first * PAIR, PAIR), part)
    kt[...] = (k_ref[:, columns] * bf16(HEAD_DIM**-0.5)).T
    for p in range(pairs):
        at = pair_at(first + p)
        q2, g2 = q_ref[:, at], g_ref[:, at]
        ks, vs = halves(k_ref[:, at]), halves(v_ref[:, at])
        qs, gs = halves(q2), halves(g2)
        gk = gv = None
        for h in range(2):
            head = 2 * (first + p) + h
            probs = jnp.exp(mul(ks[h], q2, NT) - l_ref[pl.ds(head, 1), :])
            grad_probs = mul(vs[h], g2, NT)
            grad_scores = (probs * (grad_probs - d_ref[pl.ds(head, 1), :])).astype(bf16)
            gk_one = mul(grad_scores, qs[h])
            gv_one = mul(probs.astype(bf16), gs[h])
            gk = gk_one if gk is None else gk + gk_one
            gv = gv_one if gv is None else gv + gv_one
            rows = slice((2 * p + h) * HEAD_DIM, (2 * p + h + 1) * HEAD_DIM)
            gqt[rows, :] = mul(kt[rows, :], grad_scores).astype(bf16)
        out_ref[:, part + p * PAIR : part + (p + 1) * PAIR] = gk.astype(bf16)
        out_ref[:, 2 * part + p * PAIR : 2 * part + (p + 1) * PAIR] = gv.astype(bf16)
    out_ref[:, :part] = gqt[...].T


def to_hidden(x, cb, wo_ref, wi_ref, vec_ref, mid_ref, h_ref, slope_ref):
    width = x.shape[-1]
    normed, inverse = normalize(x.astype(f32) + (mul(cb, wo_ref[...]) + row(vec_ref, B_OUT)))
    mid = (normed * row(vec_ref, GAIN_1) + row(vec_ref, BIAS_1)).astype(bf16)
    mid_ref[...] = mid
    for c in range(wi_ref.shape[1] // width):
        at = slice(c * width, (c + 1) * width)
        inner = mul(mid, wi_ref[:, at]) + row(vec_ref, B_INNER + c)
        cdf = 0.5 + 0.5 * lax.erf(inner * (0.5**0.5))
        h_ref[:, at] = (inner * cdf).astype(bf16)
        slope = cdf + inner * (jnp.exp(inner * inner * -0.5) * ((0.5 / jnp.pi) ** 0.5))
        slope_ref[:, at] = slope.astype(bf16)
    return normed, inverse


def to_output(normed_1, cot, wu_ref, vec_ref, h_ref, out_ref, gf_ref, sums_ref):
    width = normed_1.shape[-1]
    total = normed_1 * row(vec_ref, GAIN_1) + (row(vec_ref, BIAS_1) + row(vec_ref, B_OUTER))
    for c in range(h_ref.shape[1] // width):
        at = slice(c * width, (c + 1) * width)
        total = total + mul(h_ref[:, at], wu_ref[at, :])
    normed, inverse = normalize(total)
    gain = row(vec_ref, GAIN_2)
    out_ref[...] = (normed * gain + row(vec_ref, BIAS_2)).astype(bf16)
    grad = cot.astype(f32)
    sums_ref[GAIN_2 : GAIN_2 + 1, :] += column_sum(grad * normed)
    sums_ref[BIAS_2 : BIAS_2 + 1, :] += column_sum(grad)
    grad_2 = norm_back(grad, normed, inverse, gain)
    gf = grad_2.astype(bf16)
    gf_ref[...] = gf
    sums_ref[B_OUTER : B_OUTER + 1, :] += column_sum(gf)
    return grad_2


def to_context_grad(
    grad_2, normed_1, inverse_1, cb, wo_ref, wi_ref, wu_ref, vec_ref, gf_ref, ga_ref, gc_ref, d_ref, gu_ref, sums_ref
):
    width = grad_2.shape[-1]
    gf = gf_ref[...]
    grad_mid = grad_2
    for c in range(wi_ref.shape[1] // width):
        at = slice(c * width, (c + 1) * width)
        gu = (mul(gf, wu_ref[at, :], NT) * gu_ref[:, at].astype(f32)).astype(bf16)
        gu_ref[:, at] = gu
        sums_ref[B_INNER + c : B_INNER + c + 1, :] += column_sum(gu)
        grad_mid = grad_mid + mul(gu, wi_ref[:, at], NT)
    sums_ref[GAIN_1 : GAIN_1 + 1, :] += column_sum(grad_mid * normed_1)
    sums_ref[BIAS_1 : BIAS_1 + 1, :] += column_sum(grad_mid)
    ga = norm_back(grad_mid, normed_1, inverse_1, row(vec_ref, GAIN_1)).astype(bf16)
    ga_ref[...] = ga
    sums_ref[B_OUT : B_OUT + 1, :] += column_sum(ga)
    gc = mul(ga, wo_ref[...], NT).astype(bf16)
    gc_ref[...] = gc
    product = gc.astype(f32) * cb.astype(f32)
    high = product.astype(bf16)
    low = (product - high.astype(f32)).astype(bf16)
    head = lax.broadcasted_iota(jnp.int32, (STAT_ROWS, width), 0)
    column = lax.broadcasted_iota(jnp.int32, (STAT_ROWS, width), 1)
    pick = jnp.where(column // HEAD_DIM == head, 1.0, 0.0).astype(bf16)
    d_ref[...] = mul(pick, high, NT) + mul(pick, low, NT)


def spec(shape, pipelined=True):
    zeros = (0,) * (len(shape) - 1)
    if pipelined:
        return pl.BlockSpec(shape, lambda i: (i,) + zeros)
    return pl.BlockSpec(shape, lambda i: (0,) + zeros)


def whole_vmem():
    return pl.BlockSpec(memory_space=pltpu.VMEM)


def params():
    return pltpu.CompilerParams(vmem_limit_bytes=VMEM_BYTES, dimension_semantics=("arbitrary",))


def attention_call(x, w_qkv, vec):
    count, length, width = x.shape
    block = (None, length, width)

    def kernel(x_ref, w_ref, vec_ref, q_ref, k_ref, v_ref, c_ref, l_ref, stat):
        project(x_ref[...], w_ref, vec_ref, q_ref, k_ref, v_ref)
        attend(q_ref, k_ref, v_ref, c_ref, l_ref, stat)

    seq = jax.ShapeDtypeStruct(x.shape, bf16)
    return pl.pallas_call(
        kernel,
        grid=(count,),
        in_specs=[spec(block), whole_vmem(), whole_vmem()],
        out_specs=[spec(block)] * 4 + [spec((None, STAT_ROWS, length))],
        out_shape=[seq] * 4 + [jax.ShapeDtypeStruct((count, STAT_ROWS, length), f32)],
        scratch_shapes=[pltpu.VMEM((length, 128), f32)],
        compiler_params=params(),
        name="attention",
    )(x, w_qkv, vec)


def feed_forward_call(x, cb, cot, w_out, w_inner, w_outer, vec):
    count, length, width = x.shape
    inner = w_inner.shape[1]
    block, wide = (None, length, width), (None, length, inner)

    def kernel(x_ref, cb_ref, cot_ref, wo, wi, wu, vec_ref, out, mid, gf, ga, gc, d, h, gu, sums):
        @pl.when(pl.program_id(0) == 0)
        def _():
            sums[...] = jnp.zeros_like(sums)

        cb = cb_ref[...]
        normed, inverse = to_hidden(x_ref[...], cb, wo, wi, vec_ref, mid, h, gu)
        grad_2 = to_output(normed, cot_ref[...], wu, vec_ref, h, out, gf, sums)
        to_context_grad(grad_2, normed, inverse, cb, wo, wi, wu, vec_ref, gf, ga, gc, d, gu, sums)

    seq = jax.ShapeDtypeStruct(x.shape, bf16)
    seq_wide = jax.ShapeDtypeStruct((count, length, inner), bf16)
    return pl.pallas_call(
        kernel,
        grid=(count,),
        in_specs=[spec(block)] * 3 + [whole_vmem()] * 4,
        out_specs=[spec(block)] * 5
        + [spec((None, STAT_ROWS, length)), spec(wide), spec(wide), spec((16, width), False)],
        out_shape=[seq] * 5
        + [
            jax.ShapeDtypeStruct((count, STAT_ROWS, length), f32),
            seq_wide,
            seq_wide,
            jax.ShapeDtypeStruct((16, width), f32),
        ],
        compiler_params=params(),
        name="feed_forward",
    )(x, cb, cot, w_out, w_inner, w_outer, vec)


def weight_grad_call(left, right, over_left):
    tokens, rows = left.shape
    columns = right.shape[1]
    step = min(rows, columns)

    def kernel(left_ref, right_ref, out_ref):
        out_ref[...] = mul(left_ref[...], right_ref[...], TN).astype(bf16)

    if over_left:
        grid, left_map, right_map, out_map = rows // step, lambda i: (0, i), lambda i: (0, 0), lambda i: (i, 0)
    else:
        grid, left_map, right_map, out_map = columns // step, lambda i: (0, 0), lambda i: (0, i), lambda i: (0, i)
    return pl.pallas_call(
        kernel,
        grid=(grid,),
        in_specs=[pl.BlockSpec((tokens, step), left_map), pl.BlockSpec((tokens, step), right_map)],
        out_specs=pl.BlockSpec((step, step), out_map),
        out_shape=jax.ShapeDtypeStruct((rows, columns), bf16),
        compiler_params=params(),
        name="weight_grad",
    )(left, right)


def attention_back_call(x, q, k, v, gc, ga, stat_l, stat_d, w_qkv):
    count, length, width = x.shape
    block = (None, length, width)
    pairs = HEADS // 2

    def kernel(x_ref, q_ref, k_ref, v_ref, gc_ref, ga_ref, l_ref, d_ref, w_ref, gx_ref, gw_ref, sums_ref, kt, gqt, g, total):
        step = pl.program_id(0)

        @pl.when(step == 0)
        def _():
            sums_ref[...] = jnp.zeros_like(sums_ref)
            total[...] = jnp.zeros_like(total)

        attend_back(q_ref, k_ref, v_ref, gc_ref, l_ref, d_ref, g, kt, gqt, 0, pairs)
        sums_ref[B_QUERY : B_QUERY + 1, :] += column_sum(g[:, :width])
        sums_ref[B_VALUE : B_VALUE + 1, :] += column_sum(g[:, 2 * width :])
        grad = ga_ref[...].astype(f32)
        x = x_ref[...]
        for i in range(3):
            at = slice(i * width, (i + 1) * width)
            grad = grad + mul(g[:, at], w_ref[:, at], NT)
            total[:, at] += mul(x, g[:, at], TN)
        gx_ref[...] = grad.astype(bf16)

        @pl.when(step == count - 1)
        def _():
            gw_ref[...] = total[...].astype(bf16)

    return pl.pallas_call(
        kernel,
        grid=(count,),
        in_specs=[spec(block)] * 6 + [spec((None, STAT_ROWS, length))] * 2 + [whole_vmem()],
        out_specs=[spec(block), spec((width, 3 * width), False), spec((16, width), False)],
        out_shape=[
            jax.ShapeDtypeStruct(x.shape, bf16),
            jax.ShapeDtypeStruct((width, 3 * width), bf16),
            jax.ShapeDtypeStruct((16, width), f32),
        ],
        scratch_shapes=[pltpu.VMEM((width, length), bf16)] * 2
        + [pltpu.VMEM((length, 3 * width), bf16), pltpu.VMEM((width, 3 * width), f32)],
        compiler_params=params(),
        name="attention_back",
    )(x, q, k, v, gc, ga, stat_l, stat_d, w_qkv)


W1, W2, TABLE, M1, M2, UP = range(6)
GATHER_PLAN = {
    1: (("tokens", 1), ("own_z", M2),),
    2: (("own", M2), ("own_z", UP), ("tokens", 2),),
    3: (("hop", UP, 1),),
    4: (("hop", UP, 2), ("own_z", M1),),
    5: (("hop", UP, 3),),
    6: (("hop", M2, 1),),
    7: (("own", M1), ("hop", M2, 2), ("relay", M2, 0),),
    8: (("hop", M2, 3),),
    9: (("tokens", 3), ("hop", M1, 1), ("relay", M2, 1),),
    11: (("hop", M1, 2), ("relay", M2, 2), ("relay", M2, 3), ("swap", M2, 2, 0),),
    12: (("relay", UP, 2), ("own", UP),),
    13: (("swap", UP, 3, 0), ("swap", M2, 3, 0), ("relay", M1, 1), ("hop", M1, 3), ("swap", M2, 0, 1),),
    14: (("relay", M1, 0),),
    15: (("relay", M1, 2), ("relay", UP, 1), ("swap", M2, 1, 1), ("swap", M2, 2, 1),),
    16: (("swap", UP, 1, 0), ("swap", M2, 3, 1),),
    17: (("swap", M2, 1, 0), ("relay", M1, 3), ("relay", UP, 3), ("relay", UP, 0),),
    18: (("cotangent", 2),),
    19: (("swap", UP, 3, 1), ("cotangent", 3),),
    20: (("swap", UP, 2, 1), ("swap", UP, 2, 0), ("swap", UP, 1, 1), ("swap", UP, 0, 1),),
    21: (("cotangent", 0), ("cotangent", 1),),
}


def forward_call(tokens, span_mask, cotangent, w_query, w_key, w_value, w_out, w_inner, w_outer, table, sizes):
    depth_z, depth_y, cores = sizes
    rows, stretch, width = tokens.shape
    inner = w_inner.shape[1]
    part, outer_part = w_query.shape[0], w_outer.shape[0]
    devices = depth_z * depth_y * cores
    count, length = rows // 2, 2 * stretch
    chunks = inner // width
    qkv_width, mid_width = 3 * width, width + inner
    last = depth_z - 1
    ARRAYS = 6
    early = (TABLE, W1, W2)
    shared = (M2, UP)
    places = depth_z * depth_y
    half = width // 2
    m2_half = mid_width // 512 * 128
    m1_width = mid_width - 2 * m2_half

    def kernel(
        tokens_ref, mask_ref, cot_ref, wq_in, wk_in, wv_in, wo_in, wi_in, wu_in, table_in,
        x_out, q_out, k_out, v_out, cb_out, l_out, o_out, mid_out, gf_out, ga_out, gc_out, d_out, h_out, gu_out,
        sums_out, w_qkv_out,
        w_qkv, w_mid, w_up, tables, vec, x_all, cot_all, cot_away, cb_all, t_mid, t_3, t_4, t_5, l_s, stat, inv, d_s,
        normed_all, h_s, gu_s,
        up_send, down_send, z_recv, y_send, y_recv, c_send, c_recv, x_send, x_recv, t_send, t_recv, g_send, g_recv,
        in_sem, out_sem,
    ):
        b, k = lax.axis_index("batch"), lax.axis_index("blk")
        z, y, c = b // (depth_y * cores), (b // cores) % depth_y, b % cores

        def at(z_, y_, c_):
            return (z_ * depth_y + y_) * cores + c_

        barrier = pltpu.get_barrier_semaphore()

        def greet(device):
            pl.semaphore_signal(barrier, inc=1, device_id=device, device_id_type=pl.DeviceIdType.MESH)

        greet((b, 1 - k))
        greet((at(z, 1 - y, c), k))
        greet((at(z, y, 1 - c), k))

        @pl.when(z < last)
        def _():
            greet((at(z + 1, y, c), k))

        @pl.when(z > 0)
        def _():
            greet((at(z - 1, y, c), k))

        shard = pl.ds(b * part, part)
        mine = pl.ds(pl.multiple_of(k * stretch, stretch), stretch)
        theirs = pl.ds(pl.multiple_of((1 - k) * stretch, stretch), stretch)
        loads = [
            pltpu.make_async_copy(wq_in, w_qkv.at[shard, 0:width], in_sem.at[0]),
            pltpu.make_async_copy(wk_in, w_qkv.at[shard, width : 2 * width], in_sem.at[1]),
            pltpu.make_async_copy(wv_in, w_qkv.at[shard, 2 * width : 3 * width], in_sem.at[2]),
            pltpu.make_async_copy(wu_in, w_up.at[pl.ds(b * outer_part, outer_part)], in_sem.at[5]),
            pltpu.make_async_copy(wo_in, w_mid.at[shard, 0:width], in_sem.at[3]),
            pltpu.make_async_copy(wi_in, w_mid.at[shard, width:mid_width], in_sem.at[4]),
            pltpu.make_async_copy(cot_ref.at[pl.ds(k * count, count)], cot_all.at[:, mine], in_sem.at[6]),
            pltpu.make_async_copy(cot_ref.at[pl.ds((1 - k) * count, count)], cot_away, in_sem.at[7]),
            pltpu.make_async_copy(tokens_ref.at[pl.ds(k * count, count)], x_all.at[:, mine], in_sem.at[8]),
        ]
        for copy in loads:
            copy.start()

        raw = table_in[...]
        rolled = pltpu.roll(raw, b * part, 1)
        wide = pltpu.roll(raw[B_INNER : B_INNER + 1, :], (b % (devices // chunks)) * outer_part, 1)
        line = lax.broadcasted_iota(jnp.int32, raw.shape, 0)
        own_table = jnp.where(line < B_INNER, rolled, 0.0)
        own_table = jnp.where(line == B_INNER + b // (devices // chunks), wide, own_table)
        tables[b] = own_table.astype(bf16)

        t_1, t_2 = t_mid.at[0], t_mid.at[1]

        def piece(a, z_, y_, c_, side):
            d = at(z_, y_, c_)
            rows = pl.ds(d * part, part)
            if a == W1:
                return w_qkv.at[rows, : qkv_width // 2]
            if a == W2:
                return w_qkv.at[rows, qkv_width // 2 :]
            if a == TABLE:
                return tables.at[d]
            if a == M1:
                return w_mid.at[rows, :m1_width]
            if a == M2:
                return w_mid.at[rows, pl.ds(pl.multiple_of(m1_width + side * m2_half, 128), m2_half)]
            return w_up.at[pl.ds(d * outer_part, outer_part), pl.ds(pl.multiple_of(side * half, half), half)]

        def remote(ref, device, send, recv):
            return pltpu.make_async_remote_copy(
                src_ref=ref, dst_ref=ref, send_sem=send, recv_sem=recv, device_id=device, device_id_type=pl.DeviceIdType.MESH
            )

        def up(a, zs):
            return remote(piece(a, zs, y, c, k), (at(z + 1, y, c), k), up_send.at[a, zs], z_recv.at[a, zs])

        def down(a, zs):
            return remote(piece(a, zs, y, c, k), (at(z - 1, y, c), k), down_send.at[a, zs], z_recv.at[a, zs])

        def across(a, zs):
            return remote(piece(a, zs, y, c, k), (at(z, 1 - y, c), k), y_send.at[a, zs], y_recv.at[a, zs])

        def core(a, zs, ys, side):
            i = (zs * depth_y + ys) * 2 + (side if a in shared else 0)
            return remote(piece(a, zs, ys, c, side), (at(z, y, 1 - c), k), c_send.at[a, i], c_recv.at[a, i])

        def plane(a, zs, ys):
            i = zs * depth_y + ys
            return remote(piece(a, zs, ys, c, k), (b, 1 - k), x_send.at[a, i], x_recv.at[a, i])

        def arrived(ref, sem):
            remote(ref, (b, 1 - k), sem, sem).wait_recv()

        def begin_z(a):
            @pl.when(z < last)
            def _():
                up(a, z).start()

            @pl.when(z > 0)
            def _():
                down(a, z).start()

        def begin_y(a):
            across(a, z).start()

        def begin_core(a):
            core(a, z, y, k).start()
            if a in shared:
                core(a, z, y, 1 - k).start()

        def levels(step, do):
            if step == 0:
                do(z, 0)
                return

            @pl.when(z >= step)
            def _():
                do(z - step, 1)

            @pl.when(z + step <= last)
            def _():
                do(z + step, -1)

        def hop(a, step):
            def one(zs, way):
                arrived(piece(a, zs, y, c, k), z_recv.at[a, zs])
                if way > 0:
                    @pl.when(z < last)
                    def _():
                        up(a, zs).start()
                else:
                    @pl.when(z > 0)
                    def _():
                        down(a, zs).start()
                across(a, zs).start()
                if a in shared:
                    plane(a, zs, y).start()
                core(a, zs, y, k).start()

            levels(step, one)

        def relay(a, step):
            def one(zs, way):
                arrived(piece(a, zs, 1 - y, c, k), y_recv.at[a, zs])
                if a in shared:
                    plane(a, zs, 1 - y).start()
                core(a, zs, 1 - y, k).start()

            levels(step, one)

        def swap(a, step, ys):
            def one(zs, way):
                arrived(piece(a, zs, ys, c, 1 - k), x_recv.at[a, zs * depth_y + ys])
                core(a, zs, ys, 1 - k).start()

            levels(step, one)

        def complete(a):
            for zs in range(depth_z):
                for ys in range(depth_y):
                    for side in range(2 if a in shared else 1):
                        arrived(piece(a, zs, ys, 1 - c, side), c_recv.at[a, (zs * depth_y + ys) * 2 + side])

        def sent(a):
            for zs in range(depth_z):
                @pl.when((z < last) & (zs <= z))
                def _():
                    up(a, zs).wait_send()

                @pl.when((z > 0) & (zs >= z))
                def _():
                    down(a, zs).wait_send()

                across(a, zs).wait_send()
                for ys in range(depth_y):
                    for side in range(2 if a in shared else 1):
                        core(a, zs, ys, side).wait_send()
                    if a in shared:
                        @pl.when((zs != z) | (ys != y))
                        def _():
                            plane(a, zs, ys).wait_send()

        def token_copy(s):
            return pltpu.make_async_remote_copy(
                src_ref=tokens_ref.at[(1 - k) * count + s],
                dst_ref=x_all.at[s, mine],
                send_sem=t_send.at[s],
                recv_sem=t_recv.at[s],
                device_id=(b, 1 - k),
                device_id_type=pl.DeviceIdType.MESH,
            )

        def grad_copy(s):
            return pltpu.make_async_remote_copy(
                src_ref=cot_away.at[s],
                dst_ref=cot_all.at[s, mine],
                send_sem=g_send.at[s],
                recv_sem=g_recv.at[s],
                device_id=(b, 1 - k),
                device_id_type=pl.DeviceIdType.MESH,
            )

        def put(i, src, dst):
            return pltpu.make_async_copy(src, dst, out_sem.at[i])

        partners = 3 + (z < last).astype(jnp.int32) + (z > 0).astype(jnp.int32)
        pl.semaphore_wait(barrier, partners)
        for a in early:
            if a == W1:
                for i in range(3):
                    loads[i].wait()
            begin_z(a)
            begin_y(a)
            begin_core(a)
        token_copy(0).start()
        for i in (3, 4, 5):
            loads[i].wait()

        def begin_own(a):
            begin_y(a)
            begin_core(a)

        actions = {
            "hop": hop, "relay": relay, "swap": lambda a, step, far: swap(a, step, (1 - y) if far else y),
            "own": begin_own, "own_z": begin_z,
            "tokens": lambda s: token_copy(s).start(), "cotangent": lambda s: grad_copy(s).start(),
        }

        def at_slot(slot):
            for name, *what in GATHER_PLAN.get(slot, ()):
                actions[name](*what)

        def at_slots(first_slot, stride, index, bound):
            for value in range(bound):
                if first_slot + stride * value in GATHER_PLAN:
                    @pl.when(index == value)
                    def _():
                        at_slot(first_slot + stride * value)

        at_slot(0)

        for i in (6, 7):
            loads[i].wait()
        mask = mask_ref[...].astype(f32)
        own, away = jnp.where(k == 0, mask[:count], mask[count:]), jnp.where(k == 0, mask[count:], mask[:count])
        columns = jnp.concatenate([own, away], 0).T
        for s in range(count):
            cot_all[s, mine, :] = (cot_all[s, mine, :].astype(f32) * columns[:, s : s + 1]).astype(bf16)
            cot_away[s] = (cot_away[s].astype(f32) * columns[:, count + s : count + s + 1]).astype(bf16)

        loads[8].wait()
        for step in range(1, depth_z):
            for a in early:
                hop(a, step)
            at_slot(step)
            for a in early:
                relay(a, step - 1)
        for a in early:
            relay(a, last)
        at_slot(4)
        for a in early:
            complete(a)
        vec[...] = jnp.sum(tables[...].astype(f32), 0)
        save_w = put(0, w_qkv, w_qkv_out)
        save_w.start()

        def first(s, carry):
            arrived(x_all.at[s, theirs], t_recv.at[s])
            saves = [
                put(1, x_all.at[s], x_out.at[s]),
                put(2, t_1, q_out.at[s]),
                put(3, t_2, k_out.at[s]),
                put(4, t_3, v_out.at[s]),
                put(5, cb_all.at[s], cb_out.at[s]),
                put(6, l_s, l_out.at[s]),
            ]

            @pl.when(s > 0)
            def _():
                for save in saves[:4]:
                    save.wait()

            project(x_all[s], w_qkv, vec, t_1, t_2, t_3)
            for save in saves[:4]:
                save.start()
            at_slots(5, 3, s, count)
            stat[...] = jnp.zeros_like(stat)
            attend_pairs(t_1, t_2, t_3, cb_all.at[s], stat, 0, HEADS // 4)
            at_slots(6, 3, s, count)
            attend_pairs(t_1, t_2, t_3, cb_all.at[s], stat, HEADS // 4, HEADS // 2)

            @pl.when(s > 0)
            def _():
                for save in saves[4:]:
                    save.wait()

            l_s[...] = stat[...].T[:STAT_ROWS]
            for save in saves[4:]:
                save.start()
            at_slots(7, 3, s, count)
            return carry

        lax.fori_loop(0, count, first, 0)
        at_slot(17)
        for a in (M1, M2):
            complete(a)
        for i, (src, dst) in enumerate(((x_all.at[0], x_out.at[0]), (t_1, q_out.at[0]), (t_2, k_out.at[0]), (t_3, v_out.at[0]), (cb_all.at[0], cb_out.at[0]), (l_s, l_out.at[0]))):
            put(i + 1, src, dst).wait()
        save_w.wait()
        sums_out[...] = jnp.zeros_like(sums_out)
        w_o, w_i = w_mid.at[:, 0:width], w_mid.at[:, width:mid_width]
        O, GF, GA, GC, DELTA, H, GU, H_IN, GU_IN, MID = 8, 9, 10, 11, 12, 13, 15, 17, 19, 21

        lane = lax.broadcasted_iota(jnp.int32, inv.shape, 1)
        inv[...] = jnp.zeros_like(inv)

        def second(s, carry):
            slot = s % 2

            mid_s = t_mid.at[slot]

            @pl.when(s >= 2)
            def _():
                put(MID + slot, mid_s, mid_out.at[s]).wait()
                put(H + slot, h_s.at[slot], h_out.at[s]).wait()
                put(GU + slot, gu_s.at[slot], gu_out.at[s]).wait()

            normed, inverse = to_hidden(x_all[s], cb_all[s], w_o, w_i, vec, mid_s, h_s.at[slot], gu_s.at[slot])
            normed_all[s] = normed
            inv[...] = jnp.where(lane == s, inverse, inv[...])
            put(MID + slot, mid_s, mid_out.at[s]).start()
            put(H + slot, h_s.at[slot], h_out.at[s]).start()

            @pl.when(s < 2)
            def _():
                put(GU + slot, gu_s.at[slot], gu_out.at[s]).start()

            at_slots(18, 1, s, count)
            return carry

        lax.fori_loop(0, count, second, 0)
        for slot in range(2):
            put(MID + slot, t_mid.at[slot], mid_out.at[0]).wait()
        complete(UP)

        def third(i, carry):
            s = (i + count // 2) % count
            slot = i % 2
            at_slots(22, 1, i, count)
            arrived(cot_all.at[s, theirs], g_recv.at[s])
            saves = [
                put(O, t_1, o_out.at[s]),
                put(GF, t_3, gf_out.at[s]),
                put(GA, t_4, ga_out.at[s]),
                put(GC, t_5, gc_out.at[s]),
                put(DELTA, d_s, d_out.at[s]),
            ]

            @pl.when(i >= 2)
            def _():
                put(H_IN + slot, h_out.at[s], h_s.at[slot]).wait()
                put(GU_IN + slot, gu_out.at[s], gu_s.at[slot]).wait()

            @pl.when(i > 0)
            def _():
                for save in saves[:2]:
                    save.wait()

            grad_2 = to_output(normed_all[s], cot_all[s], w_up, vec, h_s.at[slot], t_1, t_3, sums_out)
            for save in saves[:2]:
                save.start()

            @pl.when(i > 0)
            def _():
                for save in saves[2:]:
                    save.wait()

            @pl.when((i > 0) & (i + 1 < count))
            def _():
                put(GU + 1 - slot, gu_s.at[1 - slot], gu_out.at[s]).wait()
                put(GU_IN + 1 - slot, gu_out.at[(s + 1) % count], gu_s.at[1 - slot]).start()

            inverse = jnp.sum(jnp.where(lane == s, inv[...], 0.0), 1, keepdims=True)
            to_context_grad(
                grad_2, normed_all[s], inverse, cb_all[s], w_o, w_i, w_up, vec, t_3, t_4, t_5, d_s, gu_s.at[slot], sums_out
            )
            for save in saves[2:]:
                save.start()
            put(GU + slot, gu_s.at[slot], gu_out.at[s]).start()

            @pl.when(i + 2 < count)
            def _():
                put(H + slot, h_s.at[slot], h_out.at[s]).wait()
                put(H_IN + slot, h_out.at[(s + 2) % count], h_s.at[slot]).start()

            return carry

        lax.fori_loop(0, count, third, 0)
        for i, src, dst in ((O, t_1, o_out), (GF, t_3, gf_out), (GA, t_4, ga_out), (GC, t_5, gc_out), (DELTA, d_s, d_out)):
            put(i, src, dst.at[0]).wait()
        for slot in range(2):
            put(GU + slot, gu_s.at[slot], gu_out.at[0]).wait()
        for s in range(count):
            token_copy(s).wait_send()
            grad_copy(s).wait_send()
        for a in range(ARRAYS):
            sent(a)

    seq = jax.ShapeDtypeStruct((count, length, width), bf16)
    seq_wide = jax.ShapeDtypeStruct((count, length, inner), bf16)
    stat_shape = jax.ShapeDtypeStruct((count, STAT_ROWS, length), f32)
    hbm = pl.BlockSpec(memory_space=pl.ANY)
    one = pltpu.VMEM((length, width), bf16)
    two_wide = pltpu.VMEM((2, length, inner), bf16)
    all_seq = pltpu.VMEM((count, length, width), bf16)
    stat_one = pltpu.VMEM((STAT_ROWS, length), f32)
    lanes = pltpu.VMEM((length, 128), f32)
    dma = pltpu.SemaphoreType.DMA
    return pl.pallas_call(
        kernel,
        in_specs=[hbm, whole_vmem()] + [hbm] * 7 + [whole_vmem()],
        out_specs=[hbm] * 14 + [whole_vmem(), hbm],
        out_shape=[seq] * 5 + [stat_shape] + [seq] * 5 + [stat_shape, seq_wide, seq_wide]
        + [jax.ShapeDtypeStruct((16, width), f32), jax.ShapeDtypeStruct((width, qkv_width), bf16)],
        scratch_shapes=[
            pltpu.VMEM((width, qkv_width), bf16),
            pltpu.VMEM((width, mid_width), bf16),
            pltpu.VMEM((inner, width), bf16),
            pltpu.VMEM((devices, 16, width), bf16),
            pltpu.VMEM((16, width), f32),
            all_seq, all_seq,
            pltpu.VMEM((count, stretch, width), bf16),
            all_seq,
            pltpu.VMEM((2, length, width), bf16), one, one, one, stat_one, lanes, lanes, stat_one,
            pltpu.VMEM((count, length, width), f32),
            two_wide, two_wide,
            dma((ARRAYS, depth_z)), dma((ARRAYS, depth_z)), dma((ARRAYS, depth_z)),
            dma((ARRAYS, depth_z)), dma((ARRAYS, depth_z)),
            dma((ARRAYS, 2 * places)), dma((ARRAYS, 2 * places)), dma((ARRAYS, places)), dma((ARRAYS, places)),
            dma((count,)), dma((count,)), dma((count,)), dma((count,)), dma((9,)), dma((23,)),
        ],
        compiler_params=pltpu.CompilerParams(collective_id=1, has_side_effects=True, vmem_limit_bytes=63 * 2**20),
        name="forward",
    )(tokens, span_mask, cotangent, w_query, w_key, w_value, w_out, w_inner, w_outer, table)


SCATTER_PLAN = {
    2: (("out", 2), (1, "s", 0),),
    3: ((1, "s", 1),),
    4: (("out", 1), ("out", 3),),
    6: ((1, "s", 3), (2, "s", 0), ("out", 0),),
    7: ((1, "s", 2),),
    8: ((2, "s", 1),),
    9: ((1, "o", 0), (2, "s", 3),),
    10: ((1, "s", 4),),
    11: ((2, "s", 2),),
    14: ((2, "o", 0), (1, "o", 1),),
    16: ((3, "s", 0),),
    17: ((2, "s", 4),),
    18: ((1, "o", 2), (3, "o", 0),),
    19: ((2, "o", 1),),
    21: ((3, "s", 1),),
    22: ((2, "o", 2),),
    23: ((1, "p", 0), (1, "p", 1),),
    25: ((1, "p", 3), (3, "s", 4), (2, "p", 0), (3, "o", 1),),
    26: ((2, "p", 1), (1, "p", 2), (3, "o", 2),),
    27: ((2, "p", 3), (1, "p", 5), (4, "s", 4),),
    28: (
        (3, "p", 0),
        (4, "s", 0),
        (1, "p", 4),
        (3, "s", 3),
        (2, "p", 2),
        (4, "o", 2),
        (2, "p", 5),
        (4, "o", 0),
        (3, "p", 3),
        (3, "s", 2),
        (4, "o", 1),
        (4, "s", 1),
        (2, "p", 4),
        (4, "p", 0),
        (3, "p", 2),
        (3, "p", 1),
        (3, "p", 5),
        (3, "p", 4),
        (4, "s", 2),
        (4, "p", 5),
        (4, "p", 2),
        (4, "p", 1),
        (4, "s", 3),
        (4, "p", 3),
        (4, "p", 4),
    ),
}


def backward_call(x, q, k, v, cb, mid, gf, ga, gc, hidden, gu, out, stat_l, stat_d, w_qkv, sums, sizes):
    depth_z, depth_y, cores = sizes
    count, length, width = x.shape
    inner = hidden.shape[2]
    devices = depth_z * depth_y * cores
    part, outer_part = width // devices, inner // devices
    stretch, rows = length // 2, 2 * count
    chunks = inner // width
    GROUPS = 3
    pairs = HEADS // 2 // GROUPS
    column = pairs * PAIR
    narrow = width // GROUPS
    OUT = chunks
    QKV = chunks + 1
    SQUARES, PARTS = QKV, 2 * GROUPS
    first_of = {"s": 0, "o": SQUARES, "p": SQUARES + GROUPS}
    every = SQUARES + GROUPS + PARTS
    half = width // 2
    SLOTS = 2
    STEPS = 5
    tokens_all = count * length

    def kernel(
        x_in, q_in, k_in, v_in, cb_in, mid_in, gf_in, ga_in, gc_in, h_in, gu_in, out_in, w_in, l_ref, d_ref, sums_ref,
        received, grad_tokens, g_query, g_key, g_value, g_out, g_inner, g_outer, vectors,
        big, pool, w_cat, ga_s, gx_s, kt, gqt, own_s, own_o, r1, r2, r3, s4, r4, r1o, r2o, r3o, s4o, r4o, r1p, r2p, r3p, s4p, r4p, v_own, v_got,
        s1_send, s1_recv, s2_send, s2_recv, s3_send, s3_recv, s4_send, s4_recv,
        v_send, v_recv, o_send, o_recv, g_send, g_recv, big_sem, pool_sem, w_sem, ga_sem, keep_sem,
    ):
        b, k = lax.axis_index("batch"), lax.axis_index("blk")
        z, y, c = b // (depth_y * cores), (b // cores) % depth_y, b % cores

        def at(z_, y_, c_):
            return (z_ * depth_y + y_) * cores + c_

        beside = (b, 1 - k)
        other_core = (at(z, y, 1 - c), k)
        other_y = (at(z, 1 - y, c), k)

        def level(j):
            return (z + j) % depth_z

        barrier = pltpu.get_barrier_semaphore()
        partners = [beside, other_core, other_y] + [(at(level(j), y, c), k) for j in range(1, depth_z)]
        for device in partners:
            pl.semaphore_signal(barrier, inc=1, device_id=device, device_id_type=pl.DeviceIdType.MESH)

        def remote(src, dst, device, send, recv):
            return pltpu.make_async_remote_copy(
                src_ref=src, dst_ref=dst, send_sem=send, recv_sem=recv, device_id=device, device_id_type=pl.DeviceIdType.MESH
            )

        def load(i, src):
            return pltpu.make_async_copy(src, big.at[i], big_sem.at[i])

        def wide_load(i, src, j):
            return pltpu.make_async_copy(src.at[:, :, j * width : (j + 1) * width], big.at[i], big_sem.at[i])

        def pool_load(s, slot):
            return [
                pltpu.make_async_copy(src.at[s], pool.at[slot, i], pool_sem.at[slot, i])
                for i, src in enumerate((q_in, k_in, v_in, gc_in))
            ]

        def w_load(i, g):
            return pltpu.make_async_copy(
                w_in.at[:, i * width + g * column : i * width + (g + 1) * column],
                w_cat.at[g, :, i * column : (i + 1) * column],
                w_sem.at[i, g],
            )

        first_loads = [load(0, mid_in), wide_load(2, gu_in, 0), load(1, gf_in), wide_load(3, gu_in, 1)]
        for copy in first_loads:
            copy.start()
        mine = pl.ds(pl.multiple_of(k * stretch, stretch), stretch)
        theirs = pl.ds(pl.multiple_of((1 - k) * stretch, stretch), stretch)

        sums_of = {"s": (r1, r2, r3, s4, r4), "o": (r1o, r2o, r3o, s4o, r4o), "p": (r1p, r2p, r3p, s4p, r4p)}

        def buffers(kind, g):
            return [ref.at[g] for ref in sums_of[kind]] + [first_of[kind] + g]

        def own_part(kind, g, half_of, z_, y_, c_):
            if kind == "o":
                return own_o.at[g, z_, y_, c_]
            if kind == "s":
                return own_s.at[g % SLOTS, z_, y_, c_]
            return own_s.at[(QKV + g) % SLOTS, z_, y_, c_, :, half_of * half : (half_of + 1) * half]

        def step_1(kind, g, half_of=0):
            a1, _, _, _, _, i = buffers(kind, 2 * g + half_of if kind == "p" else g)
            own = own_part(kind, g, half_of, slice(None), slice(None), 1 - c)
            return remote(own, a1, other_core, s1_send.at[i], s1_recv.at[i])

        def step_2(kind, g):
            a1, a2, _, _, _, i = buffers(kind, g)
            return remote(a1.at[:, 1 - y], a2, other_y, s2_send.at[i], s2_recv.at[i])

        def step_3(kind, g, j):
            _, a2, a3, _, _, i = buffers(kind, g)
            return remote(
                a2.at[level(j)], a3.at[j - 1], (at(level(j), y, c), k), s3_send.at[i, j - 1], s3_recv.at[i, j - 1]
            )

        def step_4(kind, g):
            _, _, _, a4, b4, i = buffers(kind, g)
            return remote(a4, b4, beside, s4_send.at[i], s4_recv.at[i])

        def move_1(kind, g):
            a1, _, _, _, _, _ = buffers(kind, g)
            source = (g // 2, g % 2) if kind == "p" else (g, 0)
            step_1(kind, *source).wait()

            def add(i, carry):
                zi, yi = i // depth_y, i % depth_y
                a1[zi, yi] = a1[zi, yi] + own_part(kind, *source, zi, yi, c)[...]
                return carry

            lax.fori_loop(0, depth_z * depth_y, add, 0)
            step_2(kind, g).start()

        def move_2(kind, g):
            a1, a2, _, _, _, _ = buffers(kind, g)
            step_2(kind, g).wait()

            def add(zi, carry):
                a2[zi] = a2[zi] + a1[zi, y]
                return carry

            lax.fori_loop(0, depth_z, add, 0)
            for j in range(1, depth_z):
                step_3(kind, g, j).start()

        def move_3(kind, g):
            _, a2, a3, a4, _, _ = buffers(kind, g)
            for j in range(1, depth_z):
                step_3(kind, g, j).wait()
            total = a2[z].astype(f32)
            for j in range(1, depth_z):
                total = total + a3[j - 1].astype(f32)
            a4[...] = total.astype(bf16)
            step_4(kind, g).start()

        def move_4(kind, g):
            _, _, _, a4, b4, _ = buffers(kind, g)
            step_4(kind, g).wait()
            total = a4[...].astype(f32) + b4[...].astype(f32)
            if kind == "o":
                g_outer[:, g * narrow : (g + 1) * narrow] = total
            elif kind == "s" and g < OUT:
                g_inner[:, g * width : (g + 1) * width] = total
            elif kind == "s":
                g_out[...] = total
            else:
                group, begins = g // 2, (g % 2) * half
                for i, ref in enumerate((g_query, g_key, g_value)):
                    low, high = max(i * column, begins), min((i + 1) * column, begins + half)
                    if low < high:
                        to = group * column - i * column
                        ref[:, to + low : to + high] = total[:, low - begins : high - begins]

        def exchange(s):
            return remote(out_in.at[s, theirs], received.at[s], beside, o_send.at[s], o_recv.at[s])

        moves = {1: move_1, 2: move_2, 3: move_3, 4: move_4}

        def take(steps):
            for name, *what in steps:
                if name == "out":
                    exchange(*what).start()
                else:
                    moves[name](*what)

        def at_slot(slot):
            take(SCATTER_PLAN.get(slot, ()))

        def at_slots(first_slot, stride, index, bound):
            for value in range(bound):
                if first_slot + stride * value in SCATTER_PLAN:
                    @pl.when(index == value)
                    def _():
                        at_slot(first_slot + stride * value)

        def whole(i):
            return big[i].reshape(tokens_all, width)

        def keep(g, value):
            own_s[g % SLOTS] = value.astype(bf16).reshape(depth_z, depth_y, cores, part, width)

        pl.semaphore_wait(barrier, len(partners))

        first_loads[0].wait()
        for j in range(chunks):
            wide_load(2 + j % 2, gu_in, j).wait()
            at_slot(j)
            keep(j, mul(whole(0), whole(2 + j % 2), TN))
            step_1("s", j).start()
            following = j + 2 - chunks
            if following < 0:
                wide_load(2 + j % 2, gu_in, j + 2).start()
            else:
                wide_load(2 + j % 2, h_in, following).start()
            if j == 0:
                for s in range(2):
                    for copy in pool_load(s, s):
                        copy.start()
            if j == 1:
                for g in range(GROUPS):
                    for i in range(3):
                        w_load(i, g).start()
        load(0, ga_in).start()
        first_loads[2].wait()
        for j in range(chunks):
            wide_load(2 + j % 2, h_in, j).wait()
            at_slot(chunks + j)
            product = mul(whole(2 + j % 2), whole(1), TN).astype(bf16)
            for g in range(GROUPS):
                own_o[g, j] = product[:, g * narrow : (g + 1) * narrow].reshape(depth_y, cores, outer_part, narrow)
            if j + 2 < chunks:
                wide_load(2 + j % 2, h_in, j + 2).start()
            elif j + 2 == chunks:
                load(2 + j % 2, cb_in).start()
            else:
                load(2 + j % 2, x_in).start()
        for g in range(GROUPS):
            step_1("o", g).start()
        at_slot(2 * chunks)
        load(0, ga_in).wait()
        load(2 + chunks % 2, cb_in).wait()
        keep(OUT, mul(whole(2 + chunks % 2), whole(0), TN))
        step_1("s", OUT).start()
        for copy in pool_load(2, 2):
            copy.start()
        for g in range(GROUPS):
            for i in range(3):
                w_load(i, g).wait()
        load(2 + (chunks + 1) % 2, x_in).wait()
        x_at = 2 + (chunks + 1) % 2
        v_own[0] = sums_ref[...]

        cells = GROUPS * count
        def gx_copies(s):
            away = remote(gx_s.at[theirs], grad_tokens.at[k * count + s], beside, g_send.at[s], g_recv.at[s])
            stay = pltpu.make_async_copy(gx_s.at[mine], grad_tokens.at[k * count + s], keep_sem.at[1])
            return away, stay

        ga_load = [pltpu.make_async_copy(ga_in.at[s], ga_s, ga_sem.at[0]) for s in range(count)]
        ga_load[0].start()

        def cell(i, carry):
            s, g = i // GROUPS, i % GROUPS
            slot = s % 3

            @pl.when(g == 0)
            def _():
                for copy in pool_load(s, slot):
                    copy.wait()

            attend_back(
                pool.at[slot, 0], pool.at[slot, 1], pool.at[slot, 2], pool.at[slot, 3], l_ref.at[s], d_ref.at[s],
                big.at[g, s], kt, gqt, g * pairs, pairs,
            )
            span = pl.ds(pl.multiple_of(g * column, column), column)
            v_own[0, B_QUERY : B_QUERY + 1, span] += column_sum(big[g, s, :, :column])
            v_own[0, B_VALUE : B_VALUE + 1, span] += column_sum(big[g, s, :, 2 * column :])

            @pl.when(i == GROUPS - 1)
            def _():
                for copy in pool_load(3, 0):
                    copy.start()

            base = 2 * chunks + 1
            last_base = base + (GROUPS + 1) * (count - 1)
            for group in range(GROUPS):
                @pl.when(g == group)
                def _():
                    at_slots(base + group, GROUPS + 1, s, count - 1)

            @pl.when(s == count - 1)
            def _():
                at_slots(last_base, 2, g, GROUPS)
                keep(QKV + g, mul(whole(x_at), big[g].reshape(tokens_all, width), TN))
                step_1("p", g, 0).start()
                step_1("p", g, 1).start()
                at_slots(last_base + 1, 2, g, GROUPS)

            @pl.when(g == GROUPS - 1)
            def _():
                ga_load[0].wait()

                @pl.when(s > 0)
                def _():
                    away, stay = gx_copies(s - 1)
                    away.wait_send()
                    stay.wait()

                grad = ga_s[...].astype(f32)
                for group in range(GROUPS):
                    grad = grad + mul(big[group, s], w_cat[group], NT)
                gx_s[...] = grad.astype(bf16)
                away, stay = gx_copies(s)
                away.start()
                stay.start()

                @pl.when(s < count - 1)
                def _():
                    pltpu.make_async_copy(ga_in.at[s + 1], ga_s, ga_sem.at[0]).start()

                at_slots(base + GROUPS, GROUPS + 1, s, count - 1)

                @pl.when(s == count - 1)
                def _():
                    at_slot(last_base + 2 * GROUPS)

            return carry

        lax.fori_loop(0, cells, cell, 0)

        towards = [other_core, other_y, (at(z + 1 - 2 * (z % 2), y, c), k), (at((z + 2) % 4, y, c), k), beside]

        def v_copy(i):
            return remote(v_own.at[i], v_got.at[i], towards[i], v_send.at[i], v_recv.at[i])

        def v_move(i):
            v_copy(i).wait()
            v_own[i + 1] = v_own[i] + v_got[i]
            if i + 1 < STEPS:
                v_copy(i + 1).start()

        v_copy(0).start()
        rest = SCATTER_PLAN[2 * chunks + 1 + (GROUPS + 1) * (count - 1) + 2 * GROUPS + 1]
        for i in range(STEPS):
            take(rest[2 * i : 2 * i + 2])
            v_move(i)
        total = v_own[STEPS]
        inner_row = v_own[STEPS, pl.ds(B_INNER + b // (devices // chunks), 1), :]
        rolled = pltpu.roll(total, (width - b * part) % width, 1)
        wide = pltpu.roll(inner_row, (width - (b % (devices // chunks)) * outer_part) % width, 1)
        line = lax.broadcasted_iota(jnp.int32, total.shape, 0)
        vectors[...] = jnp.where(line == B_INNER, wide, rolled)
        take(rest[2 * STEPS :])
        away, stay = gx_copies(count - 1)
        away.wait_send()
        stay.wait()
        for s in range(count):
            exchange(s).wait_send()
            exchange(s).wait_recv()
            remote(gx_s.at[theirs], grad_tokens.at[(1 - k) * count + s], beside, g_send.at[s], g_recv.at[s]).wait_recv()

    hbm = pl.BlockSpec(memory_space=pl.ANY)
    dma = pltpu.SemaphoreType.DMA

    def vmem(*shape):
        return pltpu.VMEM(shape, bf16)

    def result(*shape):
        return jax.ShapeDtypeStruct(shape, f32)

    back = jax.ShapeDtypeStruct((rows, stretch, width), bf16)
    from_beside = jax.ShapeDtypeStruct((count, stretch, width), bf16)
    return pl.pallas_call(
        kernel,
        in_specs=[hbm] * 13 + [whole_vmem()] * 3,
        out_specs=[hbm] * 2 + [whole_vmem()] * 7,
        out_shape=[
            from_beside, back, result(part, width), result(part, width), result(part, width), result(part, width),
            result(part, inner), result(outer_part, width), result(16, width),
        ],
        scratch_shapes=[
            vmem(4, count, length, width),
            vmem(3, 4, length, width),
            vmem(GROUPS, width, 3 * column),
            vmem(length, width), vmem(length, width),
            vmem(column, length), vmem(column, length),
            vmem(SLOTS, depth_z, depth_y, cores, part, width),
            vmem(GROUPS, depth_z, depth_y, cores, outer_part, narrow),
            vmem(SQUARES, depth_z, depth_y, part, width), vmem(SQUARES, depth_z, part, width),
            vmem(SQUARES, depth_z - 1, part, width), vmem(SQUARES, part, width), vmem(SQUARES, part, width),
            vmem(GROUPS, depth_z, depth_y, outer_part, narrow), vmem(GROUPS, depth_z, outer_part, narrow),
            vmem(GROUPS, depth_z - 1, outer_part, narrow), vmem(GROUPS, outer_part, narrow), vmem(GROUPS, outer_part, narrow),
            vmem(PARTS, depth_z, depth_y, part, half), vmem(PARTS, depth_z, part, half),
            vmem(PARTS, depth_z - 1, part, half), vmem(PARTS, part, half), vmem(PARTS, part, half),
            pltpu.VMEM((STEPS + 1, 16, width), f32), pltpu.VMEM((STEPS, 16, width), f32),
            dma((every,)), dma((every,)), dma((every,)), dma((every,)),
            dma((every, depth_z - 1)), dma((every, depth_z - 1)), dma((every,)), dma((every,)),
            dma((STEPS,)), dma((STEPS,)), dma((count,)), dma((count,)), dma((count,)), dma((count,)),
            dma((4,)), dma((3, 4)), dma((3, GROUPS)), dma((1,)), dma((2,)),
        ],
        compiler_params=pltpu.CompilerParams(collective_id=2, has_side_effects=True, vmem_limit_bytes=63 * 2**20),
        name="backward",
    )(x, q, k, v, cb, mid, gf, ga, gc, hidden, gu, out, w_qkv, stat_l, stat_d, sums)


def settle_call(side, out, received, grad_tokens, grads):
    rows, stretch, width = grad_tokens.shape
    count = rows // 2

    def kernel(side_ref, out_ref, received_ref, tokens_ref, *refs):
        sources, (output_ref, grad_ref), results = refs[: len(grads)], refs[len(grads) : len(grads) + 2], refs[len(grads) + 2 :]
        step = pl.program_id(0)
        here = step // count == side_ref[0]

        @pl.when(here)
        def _():
            output_ref[...] = out_ref[...]

        @pl.when(jnp.logical_not(here))
        def _():
            output_ref[...] = received_ref[...]

        grad_ref[...] = tokens_ref[...]

        @pl.when(step == 0)
        def _():
            for source, result in zip(sources, results):
                result[...] = source[...]

    block = (None, stretch, width)
    straight = pl.BlockSpec(block, lambda i, side: (i, 0, 0))
    return pl.pallas_call(
        kernel,
        grid_spec=pltpu.PrefetchScalarGridSpec(
            num_scalar_prefetch=1,
            grid=(rows,),
            in_specs=[
                pl.BlockSpec(block, lambda i, side: (i % count, side[0], 0)),
                pl.BlockSpec(block, lambda i, side: (i % count, 0, 0)),
                straight,
            ]
            + [pl.BlockSpec(grad.shape, lambda i, side: (0, 0)) for grad in grads],
            out_specs=[straight] * 2 + [pl.BlockSpec(grad.shape, lambda i, side: (0, 0)) for grad in grads],
        ),
        out_shape=[jax.ShapeDtypeStruct(grad_tokens.shape, bf16)] * 2
        + [jax.ShapeDtypeStruct(grad.shape, f32) for grad in grads],
        compiler_params=params(),
        name="settle",
    )(side, out, received, grad_tokens, *grads)


def pack_shard(w_query, w_key, w_value, w_out, w_inner, w_outer, vectors):
    width = w_query.shape[1]
    inner_parts = [w_inner[:, i : i + width] for i in range(0, w_inner.shape[1], width)]
    small = jnp.concatenate(vectors)
    body_rows = sum(part.shape[0] for part in (w_query, w_key, w_value, w_out, w_outer, *inner_parts))
    rows = -(-(body_rows + 1) // 16) * 16
    tail = jnp.zeros(((rows - body_rows) * width,), small.dtype).at[: small.shape[0]].set(small)
    return jnp.concatenate(
        [w_query, w_key, w_value, w_out, *inner_parts, w_outer, tail.reshape(-1, width)]
    )


def vec_table(small, vec_names_sizes):
    rows, at = [], 0
    for size in vec_names_sizes:
        rows.append(small[:, at : at + size].reshape(-1))
        at += size
    return rows


def gather_weights(w_query, w_key, w_value, w_out, w_inner, w_outer, vectors):
    part, width = w_query.shape
    outer_part = w_outer.shape[0]
    chunks = w_inner.shape[1] // width
    sizes = [vector.shape[0] for vector in vectors]
    packed = pack_shard(w_query, w_key, w_value, w_out, w_inner, w_outer, vectors)
    gathered = lax.all_gather(packed, "batch", axis=0)

    def weight(at, count):
        return gathered[:, at : at + count].reshape(-1, width)

    squares = [weight(i * part, part) for i in range(4 + chunks)]
    outer_at = (4 + chunks) * part
    w_outer_all = weight(outer_at, outer_part)
    small = gathered[:, outer_at + outer_part :].reshape(gathered.shape[0], -1)
    vec = jnp.concatenate(vec_table(small, sizes)).reshape(-1, width).astype(f32)
    vec = jnp.concatenate([vec, jnp.zeros((16 - vec.shape[0], width), f32)])
    return jnp.concatenate(squares[:3], 1), squares[3], jnp.concatenate(squares[4:], 1), w_outer_all, vec


def body(
    tokens,
    span_mask,
    cotangent,
    w_query,
    b_query,
    w_key,
    w_value,
    b_value,
    w_out,
    b_out,
    gain_first,
    bias_first,
    w_inner,
    b_inner,
    w_outer,
    b_outer,
    gain_second,
    bias_second,
):
    rows, stretch, width = tokens.shape
    inner = w_inner.shape[1]
    part = w_query.shape[0]
    outer_part = w_outer.shape[0]
    vectors = (b_query, b_value, b_out, gain_first, bias_first, b_outer, gain_second, bias_second, b_inner)
    sizes = [vector.shape[0] for vector in vectors]

    devices = lax.axis_size("batch")
    chunks = inner // width
    swap = functools.partial(lax.all_to_all, axis_name="blk", tiled=True)
    outer_at = (4 + chunks) * part
    shard_rows = -(-(outer_at + outer_part + 1) // 16) * 16
    if (devices, lax.axis_size("blk")) == (16, 2):
        table = sum(
            lax.pad(
                vector.astype(f32).reshape(1, -1), f32(0), ((i, 15 - i, 0), (0, width - vector.shape[0], 0))
            )
            for i, vector in enumerate(vectors)
        )
        x, q, k, v, cb, stat_l, out, mid, gf, ga, gc, stat_d, hidden, gu, sums_ffn, w_qkv = forward_call(
            tokens, span_mask, cotangent, w_query, w_key, w_value, w_out, w_inner, w_outer, table, (4, 2, 2)
        )
        results = backward_call(
            x, q, k, v, cb, mid, gf, ga, gc, hidden, gu, out, stat_l, stat_d, w_qkv, sums_ffn, (4, 2, 2)
        )
        side = lax.axis_index("blk").astype(jnp.int32).reshape(1)
        settled = settle_call(side, out, results[0], results[1], results[2:-1])
        output, grad_tokens, g_query, g_key, g_value, g_out, g_inner, g_outer = settled
        totals = results[-1]
        small = [totals[i, :size] for i, size in enumerate(sizes)]
        return (
            output, grad_tokens, g_query, small[0], g_key, g_value, small[1], g_out, small[2], small[3], small[4], g_inner,
            small[8], g_outer, small[5], small[6], small[7],
        )
    w_qkv, w_out_all, w_inner_all, w_outer_all, vec = gather_weights(
        w_query, w_key, w_value, w_out, w_inner, w_outer, vectors
    )
    masked = cotangent * span_mask[..., None].astype(bf16)
    x = swap(tokens, split_axis=0, concat_axis=1)
    cot = swap(masked, split_axis=0, concat_axis=1)
    q, k, v, cb, stat_l = attention_call(x, w_qkv, vec)
    out, mid, gf, ga, gc, stat_d, hidden, gu, sums_ffn = feed_forward_call(
        x, cb, cot, w_out_all, w_inner_all, w_outer_all, vec
    )
    gx, gw_qkv, sums_att = attention_back_call(x, q, k, v, gc, ga, stat_l, stat_d, w_qkv)
    output = swap(out, split_axis=1, concat_axis=0)
    grad_tokens = swap(gx, split_axis=1, concat_axis=0)

    def flat(values):
        return values.reshape(-1, values.shape[-1])

    gw_out = weight_grad_call(flat(cb), flat(ga), False)
    gw_inner = weight_grad_call(flat(mid), flat(gu), False)
    gw_outer = weight_grad_call(flat(hidden), flat(gf), True)

    sums = sums_ffn + sums_att
    small_sums = [sums[i].reshape(devices, -1) for i in range(B_INNER)]
    small_sums.append(sums[B_INNER : B_INNER + chunks].reshape(devices, -1))
    tail = jnp.concatenate(small_sums, 1).astype(bf16)
    tail = jnp.pad(tail, ((0, 0), (0, (shard_rows - outer_at - outer_part) * width - tail.shape[1])))
    pieces = [gw_qkv[:, i * width : (i + 1) * width].reshape(devices, part, width) for i in range(3)]
    pieces.append(gw_out.reshape(devices, part, width))
    pieces += [gw_inner[:, i * width : (i + 1) * width].reshape(devices, part, width) for i in range(chunks)]
    pieces.append(gw_outer.reshape(devices, outer_part, width))
    pieces.append(tail.reshape(devices, -1, width))
    grads = jnp.concatenate(pieces, 1)
    share = lax.psum_scatter(grads, "batch", scatter_dimension=0, tiled=False)
    share = lax.psum(share, "blk").astype(f32)
    square = [share[i * part : (i + 1) * part] for i in range(4 + chunks)]
    share_small = share[outer_at + outer_part :].reshape(-1)
    small_out, at = [], 0
    for size in sizes:
        small_out.append(share_small[at : at + size])
        at += size
    (g_b_query, g_b_value, g_b_out, g_gain_1, g_bias_1, g_b_outer, g_gain_2, g_bias_2, g_b_inner) = small_out
    return (
        output,
        grad_tokens,
        square[0],
        g_b_query,
        square[1],
        square[2],
        g_b_value,
        square[3],
        g_b_out,
        g_gain_1,
        g_bias_1,
        jnp.concatenate(square[4:], 1),
        g_b_inner,
        share[outer_at : outer_at + outer_part],
        g_b_outer,
        g_gain_2,
        g_bias_2,
    )


def solution(mesh):
    block = P("batch", "blk", None)
    matrix, vector = P("batch", None), P("batch")
    weights = (
        matrix, vector, matrix, matrix, vector, matrix, vector, vector, vector, matrix, vector, matrix, vector, vector, vector,
    )
    return jax.shard_map(
        body,
        mesh=mesh,
        in_specs=(block, P("batch", "blk"), block) + weights,
        out_specs=(block, block) + weights,
        check_vma=False,
    )
```

```python
import functools

import jax
import jax.numpy as jnp
from jax import lax
from jax.experimental import pallas as pl
from jax.experimental.pallas import tpu as pltpu
from jax.sharding import PartitionSpec as P

HEADS = 12
HEAD_DIM = 64
PAIR = 2 * HEAD_DIM
STAT_ROWS = 16
VMEM_BYTES = 60 * 2**20

epsilon = 1e-06
bf16 = jnp.bfloat16
f32 = jnp.float32

NN = (((1,), (0,)), ((), ()))
NT = (((1,), (1,)), ((), ()))
TN = (((0,), (0,)), ((), ()))

B_QUERY, B_VALUE, B_OUT, GAIN_1, BIAS_1, B_OUTER, GAIN_2, BIAS_2, B_INNER = range(9)


def mul(left, right, dims=NN):
    return lax.dot_general(left, right, dims, preferred_element_type=f32)


def row(ref, index):
    return ref[index : index + 1, :]


def halves(block):
    lane = lax.broadcasted_iota(jnp.int32, block.shape, 1)
    zero = jnp.zeros_like(block)
    return jnp.where(lane < HEAD_DIM, block, zero), jnp.where(lane < HEAD_DIM, zero, block)


def pair_at(p):
    return pl.ds(pl.multiple_of(p * PAIR, PAIR), PAIR)


def normalize(values):
    center = values - jnp.mean(values, -1, keepdims=True)
    inverse = lax.rsqrt(jnp.mean(center * center, -1, keepdims=True) + epsilon)
    return center * inverse, inverse


def norm_back(grad, normed, inverse, gain):
    scaled = grad * gain
    return inverse * (
        scaled
        - jnp.mean(scaled, -1, keepdims=True)
        - normed * jnp.mean(scaled * normed, -1, keepdims=True)
    )


def column_sum(values):
    return jnp.sum(values.astype(f32), 0, keepdims=True)


def project(x, w_ref, vec_ref, q_ref, k_ref, v_ref):
    width = x.shape[-1]
    q = (mul(x, w_ref[:, :width]) + row(vec_ref, B_QUERY)).astype(bf16)
    q_ref[...] = q * bf16(HEAD_DIM**-0.5)
    k_ref[...] = mul(x, w_ref[:, width : 2 * width]).astype(bf16)
    v_ref[...] = (mul(x, w_ref[:, 2 * width :]) + row(vec_ref, B_VALUE)).astype(bf16)


def attend_pairs(q_ref, k_ref, v_ref, c_ref, stat, first, end):
    lane = lax.broadcasted_iota(jnp.int32, stat.shape, 1)

    def pair(p, carry):
        at = pair_at(p)
        q2, k2, v2 = q_ref[:, at], k_ref[:, at], v_ref[:, at]
        context = None
        for h, (k_one, v_one) in enumerate(zip(halves(k2), halves(v2))):
            scores = mul(q2, k_one, NT)
            best = jnp.max(scores, 1, keepdims=True)
            weights = jnp.exp(scores - best)
            total = jnp.sum(weights, 1, keepdims=True)
            part = mul(weights.astype(bf16), v_one) * (1.0 / total)
            context = part if context is None else context + part
            stat[...] = jnp.where(lane == 2 * p + h, best + jnp.log(total), stat[...])
        c_ref[:, at] = context.astype(bf16)
        return carry

    lax.fori_loop(first, end, pair, 0, unroll=3)


def attend(q_ref, k_ref, v_ref, c_ref, l_ref, stat):
    stat[...] = jnp.zeros_like(stat)
    attend_pairs(q_ref, k_ref, v_ref, c_ref, stat, 0, HEADS // 2)
    l_ref[...] = stat[...].T[:STAT_ROWS]


def attend_back(q_ref, k_ref, v_ref, g_ref, l_ref, d_ref, out_ref, kt, gqt, first, pairs):
    part = pairs * PAIR
    columns = pl.ds(pl.multiple_of(first * PAIR, PAIR), part)
    kt[...] = (k_ref[:, columns] * bf16(HEAD_DIM**-0.5)).T
    for p in range(pairs):
        at = pair_at(first + p)
        q2, g2 = q_ref[:, at], g_ref[:, at]
        ks, vs = halves(k_ref[:, at]), halves(v_ref[:, at])
        qs, gs = halves(q2), halves(g2)
        gk = gv = None
        for h in range(2):
            head = 2 * (first + p) + h
            probs = jnp.exp(mul(ks[h], q2, NT) - l_ref[pl.ds(head, 1), :])
            grad_probs = mul(vs[h], g2, NT)
            grad_scores = (probs * (grad_probs - d_ref[pl.ds(head, 1), :])).astype(bf16)
            gk_one = mul(grad_scores, qs[h])
            gv_one = mul(probs.astype(bf16), gs[h])
            gk = gk_one if gk is None else gk + gk_one
            gv = gv_one if gv is None else gv + gv_one
            rows = slice((2 * p + h) * HEAD_DIM, (2 * p + h + 1) * HEAD_DIM)
            gqt[rows, :] = mul(kt[rows, :], grad_scores).astype(bf16)
        out_ref[:, part + p * PAIR : part + (p + 1) * PAIR] = gk.astype(bf16)
        out_ref[:, 2 * part + p * PAIR : 2 * part + (p + 1) * PAIR] = gv.astype(bf16)
    out_ref[:, :part] = gqt[...].T


def to_hidden(x, cb, wo_ref, wi_ref, vec_ref, mid_ref, h_ref, slope_ref):
    width = x.shape[-1]
    normed, inverse = normalize(x.astype(f32) + (mul(cb, wo_ref[...]) + row(vec_ref, B_OUT)))
    mid = (normed * row(vec_ref, GAIN_1) + row(vec_ref, BIAS_1)).astype(bf16)
    mid_ref[...] = mid
    for c in range(wi_ref.shape[1] // width):
        at = slice(c * width, (c + 1) * width)
        inner = mul(mid, wi_ref[:, at]) + row(vec_ref, B_INNER + c)
        cdf = 0.5 + 0.5 * lax.erf(inner * (0.5**0.5))
        h_ref[:, at] = (inner * cdf).astype(bf16)
        slope = cdf + inner * (jnp.exp(inner * inner * -0.5) * ((0.5 / jnp.pi) ** 0.5))
        slope_ref[:, at] = slope.astype(bf16)
    return normed, inverse


def to_output(normed_1, cot, wu_ref, vec_ref, h_ref, out_ref, gf_ref, sums_ref):
    width = normed_1.shape[-1]
    total = normed_1 * row(vec_ref, GAIN_1) + (row(vec_ref, BIAS_1) + row(vec_ref, B_OUTER))
    for c in range(h_ref.shape[1] // width):
        at = slice(c * width, (c + 1) * width)
        total = total + mul(h_ref[:, at], wu_ref[at, :])
    normed, inverse = normalize(total)
    gain = row(vec_ref, GAIN_2)
    out_ref[...] = (normed * gain + row(vec_ref, BIAS_2)).astype(bf16)
    grad = cot.astype(f32)
    sums_ref[GAIN_2 : GAIN_2 + 1, :] += column_sum(grad * normed)
    sums_ref[BIAS_2 : BIAS_2 + 1, :] += column_sum(grad)
    grad_2 = norm_back(grad, normed, inverse, gain)
    gf = grad_2.astype(bf16)
    gf_ref[...] = gf
    sums_ref[B_OUTER : B_OUTER + 1, :] += column_sum(gf)
    return grad_2


def to_context_grad(
    grad_2, normed_1, inverse_1, cb, wo_ref, wi_ref, wu_ref, vec_ref, gf_ref, ga_ref, gc_ref, d_ref, gu_ref, sums_ref,
    hidden_done=None,
):
    width = grad_2.shape[-1]
    gf = gf_ref[...]
    grad_mid = grad_2
    for c in range(wi_ref.shape[1] // width):
        at = slice(c * width, (c + 1) * width)
        gu = (mul(gf, wu_ref[at, :], NT) * gu_ref[:, at].astype(f32)).astype(bf16)
        gu_ref[:, at] = gu
        sums_ref[B_INNER + c : B_INNER + c + 1, :] += column_sum(gu)
        grad_mid = grad_mid + mul(gu, wi_ref[:, at], NT)
    if hidden_done is not None:
        hidden_done()
    sums_ref[GAIN_1 : GAIN_1 + 1, :] += column_sum(grad_mid * normed_1)
    sums_ref[BIAS_1 : BIAS_1 + 1, :] += column_sum(grad_mid)
    ga = norm_back(grad_mid, normed_1, inverse_1, row(vec_ref, GAIN_1)).astype(bf16)
    ga_ref[...] = ga
    sums_ref[B_OUT : B_OUT + 1, :] += column_sum(ga)
    gc = mul(ga, wo_ref[...], NT).astype(bf16)
    gc_ref[...] = gc
    product = gc.astype(f32) * cb.astype(f32)
    high = product.astype(bf16)
    low = (product - high.astype(f32)).astype(bf16)
    head = lax.broadcasted_iota(jnp.int32, (STAT_ROWS, width), 0)
    column = lax.broadcasted_iota(jnp.int32, (STAT_ROWS, width), 1)
    pick = jnp.where(column // HEAD_DIM == head, 1.0, 0.0).astype(bf16)
    d_ref[...] = mul(pick, high, NT) + mul(pick, low, NT)


def spec(shape, pipelined=True):
    zeros = (0,) * (len(shape) - 1)
    if pipelined:
        return pl.BlockSpec(shape, lambda i: (i,) + zeros)
    return pl.BlockSpec(shape, lambda i: (0,) + zeros)


def whole_vmem():
    return pl.BlockSpec(memory_space=pltpu.VMEM)


def params():
    return pltpu.CompilerParams(vmem_limit_bytes=VMEM_BYTES, dimension_semantics=("arbitrary",))


def attention_call(x, w_qkv, vec):
    count, length, width = x.shape
    block = (None, length, width)

    def kernel(x_ref, w_ref, vec_ref, q_ref, k_ref, v_ref, c_ref, l_ref, stat):
        project(x_ref[...], w_ref, vec_ref, q_ref, k_ref, v_ref)
        attend(q_ref, k_ref, v_ref, c_ref, l_ref, stat)

    seq = jax.ShapeDtypeStruct(x.shape, bf16)
    return pl.pallas_call(
        kernel,
        grid=(count,),
        in_specs=[spec(block), whole_vmem(), whole_vmem()],
        out_specs=[spec(block)] * 4 + [spec((None, STAT_ROWS, length))],
        out_shape=[seq] * 4 + [jax.ShapeDtypeStruct((count, STAT_ROWS, length), f32)],
        scratch_shapes=[pltpu.VMEM((length, 128), f32)],
        compiler_params=params(),
        name="attention",
    )(x, w_qkv, vec)


def feed_forward_call(x, cb, cot, w_out, w_inner, w_outer, vec):
    count, length, width = x.shape
    inner = w_inner.shape[1]
    block, wide = (None, length, width), (None, length, inner)

    def kernel(x_ref, cb_ref, cot_ref, wo, wi, wu, vec_ref, out, mid, gf, ga, gc, d, h, gu, sums):
        @pl.when(pl.program_id(0) == 0)
        def _():
            sums[...] = jnp.zeros_like(sums)

        cb = cb_ref[...]
        normed, inverse = to_hidden(x_ref[...], cb, wo, wi, vec_ref, mid, h, gu)
        grad_2 = to_output(normed, cot_ref[...], wu, vec_ref, h, out, gf, sums)
        to_context_grad(grad_2, normed, inverse, cb, wo, wi, wu, vec_ref, gf, ga, gc, d, gu, sums)

    seq = jax.ShapeDtypeStruct(x.shape, bf16)
    seq_wide = jax.ShapeDtypeStruct((count, length, inner), bf16)
    return pl.pallas_call(
        kernel,
        grid=(count,),
        in_specs=[spec(block)] * 3 + [whole_vmem()] * 4,
        out_specs=[spec(block)] * 5
        + [spec((None, STAT_ROWS, length)), spec(wide), spec(wide), spec((16, width), False)],
        out_shape=[seq] * 5
        + [
            jax.ShapeDtypeStruct((count, STAT_ROWS, length), f32),
            seq_wide,
            seq_wide,
            jax.ShapeDtypeStruct((16, width), f32),
        ],
        compiler_params=params(),
        name="feed_forward",
    )(x, cb, cot, w_out, w_inner, w_outer, vec)


def weight_grad_call(left, right, over_left):
    tokens, rows = left.shape
    columns = right.shape[1]
    step = min(rows, columns)

    def kernel(left_ref, right_ref, out_ref):
        out_ref[...] = mul(left_ref[...], right_ref[...], TN).astype(bf16)

    if over_left:
        grid, left_map, right_map, out_map = rows // step, lambda i: (0, i), lambda i: (0, 0), lambda i: (i, 0)
    else:
        grid, left_map, right_map, out_map = columns // step, lambda i: (0, 0), lambda i: (0, i), lambda i: (0, i)
    return pl.pallas_call(
        kernel,
        grid=(grid,),
        in_specs=[pl.BlockSpec((tokens, step), left_map), pl.BlockSpec((tokens, step), right_map)],
        out_specs=pl.BlockSpec((step, step), out_map),
        out_shape=jax.ShapeDtypeStruct((rows, columns), bf16),
        compiler_params=params(),
        name="weight_grad",
    )(left, right)


def attention_back_call(x, q, k, v, gc, ga, stat_l, stat_d, w_qkv):
    count, length, width = x.shape
    block = (None, length, width)
    pairs = HEADS // 2

    def kernel(x_ref, q_ref, k_ref, v_ref, gc_ref, ga_ref, l_ref, d_ref, w_ref, gx_ref, gw_ref, sums_ref, kt, gqt, g, total):
        step = pl.program_id(0)

        @pl.when(step == 0)
        def _():
            sums_ref[...] = jnp.zeros_like(sums_ref)
            total[...] = jnp.zeros_like(total)

        attend_back(q_ref, k_ref, v_ref, gc_ref, l_ref, d_ref, g, kt, gqt, 0, pairs)
        sums_ref[B_QUERY : B_QUERY + 1, :] += column_sum(g[:, :width])
        sums_ref[B_VALUE : B_VALUE + 1, :] += column_sum(g[:, 2 * width :])
        grad = ga_ref[...].astype(f32)
        x = x_ref[...]
        for i in range(3):
            at = slice(i * width, (i + 1) * width)
            grad = grad + mul(g[:, at], w_ref[:, at], NT)
            total[:, at] += mul(x, g[:, at], TN)
        gx_ref[...] = grad.astype(bf16)

        @pl.when(step == count - 1)
        def _():
            gw_ref[...] = total[...].astype(bf16)

    return pl.pallas_call(
        kernel,
        grid=(count,),
        in_specs=[spec(block)] * 6 + [spec((None, STAT_ROWS, length))] * 2 + [whole_vmem()],
        out_specs=[spec(block), spec((width, 3 * width), False), spec((16, width), False)],
        out_shape=[
            jax.ShapeDtypeStruct(x.shape, bf16),
            jax.ShapeDtypeStruct((width, 3 * width), bf16),
            jax.ShapeDtypeStruct((16, width), f32),
        ],
        scratch_shapes=[pltpu.VMEM((width, length), bf16)] * 2
        + [pltpu.VMEM((length, 3 * width), bf16), pltpu.VMEM((width, 3 * width), f32)],
        compiler_params=params(),
        name="attention_back",
    )(x, q, k, v, gc, ga, stat_l, stat_d, w_qkv)


W1, W2, TABLE, M1, M2, UP = range(6)
GATHER_PLAN = {
    1: (("tokens", 1), ("own_z", M2),),
    2: (("own", M2), ("own_z", UP), ("tokens", 2),),
    3: (("hop", UP, 1),),
    4: (("hop", UP, 2), ("own_z", M1),),
    5: (("hop", UP, 3),),
    6: (("hop", M2, 1),),
    7: (("own", M1), ("hop", M2, 2), ("relay", M2, 0),),
    8: (("hop", M2, 3),),
    9: (("tokens", 3), ("hop", M1, 1), ("relay", M2, 1),),
    11: (("hop", M1, 2), ("relay", M2, 2), ("relay", M2, 3), ("swap", M2, 2, 0),),
    12: (("relay", UP, 2), ("own", UP),),
    13: (("swap", UP, 3, 0), ("swap", M2, 3, 0), ("relay", M1, 1), ("hop", M1, 3), ("swap", M2, 0, 1),),
    14: (("relay", M1, 0),),
    15: (("relay", M1, 2), ("relay", UP, 1), ("swap", M2, 1, 1), ("swap", M2, 2, 1),),
    16: (("swap", UP, 1, 0), ("swap", M2, 3, 1),),
    17: (("swap", M2, 1, 0), ("relay", M1, 3), ("relay", UP, 3), ("relay", UP, 0),),
    18: (("cotangent", 2),),
    19: (("swap", UP, 3, 1), ("cotangent", 3),),
    20: (("swap", UP, 2, 1), ("swap", UP, 2, 0), ("swap", UP, 1, 1), ("swap", UP, 0, 1),),
    21: (("cotangent", 0), ("cotangent", 1),),
}


def forward_call(tokens, span_mask, cotangent, w_query, w_key, w_value, w_out, w_inner, w_outer, table, sizes):
    depth_z, depth_y, cores = sizes
    rows, stretch, width = tokens.shape
    inner = w_inner.shape[1]
    part, outer_part = w_query.shape[0], w_outer.shape[0]
    devices = depth_z * depth_y * cores
    count, length = rows // 2, 2 * stretch
    chunks = inner // width
    qkv_width, mid_width = 3 * width, width + inner
    last = depth_z - 1
    ARRAYS = 6
    early = (TABLE, W1, W2)
    shared = (M2, UP)
    places = depth_z * depth_y
    half = width // 2
    m2_half = mid_width // 512 * 128
    m1_width = mid_width - 2 * m2_half

    def kernel(
        tokens_ref, mask_ref, cot_ref, wq_in, wk_in, wv_in, wo_in, wi_in, wu_in, table_in,
        x_out, q_out, k_out, v_out, cb_out, l_out, o_out, mid_out, gf_out, ga_out, gc_out, d_out, h_out, gu_out,
        sums_out, w_qkv_out,
        w_qkv, w_mid, w_up, tables, vec, x_all, cot_all, cot_away, cb_all, t_mid, t_3, t_4, t_5, l_s, stat, inv, d_s,
        normed_all, h_s, gu_s,
        up_send, down_send, z_recv, y_send, y_recv, c_send, c_recv, x_send, x_recv, t_send, t_recv, g_send, g_recv,
        in_sem, out_sem,
    ):
        b, k = lax.axis_index("batch"), lax.axis_index("blk")
        z, y, c = b // (depth_y * cores), (b // cores) % depth_y, b % cores

        def at(z_, y_, c_):
            return (z_ * depth_y + y_) * cores + c_

        barrier = pltpu.get_barrier_semaphore()

        def greet(device):
            pl.semaphore_signal(barrier, inc=1, device_id=device, device_id_type=pl.DeviceIdType.MESH)

        greet((b, 1 - k))
        greet((at(z, 1 - y, c), k))
        greet((at(z, y, 1 - c), k))

        @pl.when(z < last)
        def _():
            greet((at(z + 1, y, c), k))

        @pl.when(z > 0)
        def _():
            greet((at(z - 1, y, c), k))

        shard = pl.ds(b * part, part)
        mine = pl.ds(pl.multiple_of(k * stretch, stretch), stretch)
        theirs = pl.ds(pl.multiple_of((1 - k) * stretch, stretch), stretch)
        loads = [
            pltpu.make_async_copy(wq_in, w_qkv.at[shard, 0:width], in_sem.at[0]),
            pltpu.make_async_copy(wk_in, w_qkv.at[shard, width : 2 * width], in_sem.at[1]),
            pltpu.make_async_copy(wv_in, w_qkv.at[shard, 2 * width : 3 * width], in_sem.at[2]),
            pltpu.make_async_copy(wu_in, w_up.at[pl.ds(b * outer_part, outer_part)], in_sem.at[5]),
            pltpu.make_async_copy(wo_in, w_mid.at[shard, 0:width], in_sem.at[3]),
            pltpu.make_async_copy(wi_in, w_mid.at[shard, width:mid_width], in_sem.at[4]),
            pltpu.make_async_copy(cot_ref.at[pl.ds(k * count, count)], cot_all.at[:, mine], in_sem.at[6]),
            pltpu.make_async_copy(cot_ref.at[pl.ds((1 - k) * count, count)], cot_away, in_sem.at[7]),
            pltpu.make_async_copy(tokens_ref.at[pl.ds(k * count, count)], x_all.at[:, mine], in_sem.at[8]),
        ]
        for copy in loads:
            copy.start()

        raw = table_in[...]
        rolled = pltpu.roll(raw, b * part, 1)
        wide = pltpu.roll(raw[B_INNER : B_INNER + 1, :], (b % (devices // chunks)) * outer_part, 1)
        line = lax.broadcasted_iota(jnp.int32, raw.shape, 0)
        own_table = jnp.where(line < B_INNER, rolled, 0.0)
        own_table = jnp.where(line == B_INNER + b // (devices // chunks), wide, own_table)
        tables[b] = own_table.astype(bf16)

        t_1, t_2 = t_mid.at[0], t_mid.at[1]

        def piece(a, z_, y_, c_, side):
            d = at(z_, y_, c_)
            rows = pl.ds(d * part, part)
            if a == W1:
                return w_qkv.at[rows, : qkv_width // 2]
            if a == W2:
                return w_qkv.at[rows, qkv_width // 2 :]
            if a == TABLE:
                return tables.at[d]
            if a == M1:
                return w_mid.at[rows, :m1_width]
            if a == M2:
                return w_mid.at[rows, pl.ds(pl.multiple_of(m1_width + side * m2_half, 128), m2_half)]
            return w_up.at[pl.ds(d * outer_part, outer_part), pl.ds(pl.multiple_of(side * half, half), half)]

        def remote(ref, device, send, recv):
            return pltpu.make_async_remote_copy(
                src_ref=ref, dst_ref=ref, send_sem=send, recv_sem=recv, device_id=device, device_id_type=pl.DeviceIdType.MESH
            )

        def up(a, zs):
            return remote(piece(a, zs, y, c, k), (at(z + 1, y, c), k), up_send.at[a, zs], z_recv.at[a, zs])

        def down(a, zs):
            return remote(piece(a, zs, y, c, k), (at(z - 1, y, c), k), down_send.at[a, zs], z_recv.at[a, zs])

        def across(a, zs):
            return remote(piece(a, zs, y, c, k), (at(z, 1 - y, c), k), y_send.at[a, zs], y_recv.at[a, zs])

        def core(a, zs, ys, side):
            i = (zs * depth_y + ys) * 2 + (side if a in shared else 0)
            return remote(piece(a, zs, ys, c, side), (at(z, y, 1 - c), k), c_send.at[a, i], c_recv.at[a, i])

        def plane(a, zs, ys):
            i = zs * depth_y + ys
            return remote(piece(a, zs, ys, c, k), (b, 1 - k), x_send.at[a, i], x_recv.at[a, i])

        def arrived(ref, sem):
            remote(ref, (b, 1 - k), sem, sem).wait_recv()

        def begin_z(a):
            @pl.when(z < last)
            def _():
                up(a, z).start()

            @pl.when(z > 0)
            def _():
                down(a, z).start()

        def begin_y(a):
            across(a, z).start()

        def begin_core(a):
            core(a, z, y, k).start()
            if a in shared:
                core(a, z, y, 1 - k).start()

        def levels(step, do):
            if step == 0:
                do(z, 0)
                return

            @pl.when(z >= step)
            def _():
                do(z - step, 1)

            @pl.when(z + step <= last)
            def _():
                do(z + step, -1)

        def hop(a, step):
            def one(zs, way):
                arrived(piece(a, zs, y, c, k), z_recv.at[a, zs])
                if way > 0:
                    @pl.when(z < last)
                    def _():
                        up(a, zs).start()
                else:
                    @pl.when(z > 0)
                    def _():
                        down(a, zs).start()
                across(a, zs).start()
                if a in shared:
                    plane(a, zs, y).start()
                core(a, zs, y, k).start()

            levels(step, one)

        def relay(a, step):
            def one(zs, way):
                arrived(piece(a, zs, 1 - y, c, k), y_recv.at[a, zs])
                if a in shared:
                    plane(a, zs, 1 - y).start()
                core(a, zs, 1 - y, k).start()

            levels(step, one)

        def swap(a, step, ys):
            def one(zs, way):
                arrived(piece(a, zs, ys, c, 1 - k), x_recv.at[a, zs * depth_y + ys])
                core(a, zs, ys, 1 - k).start()

            levels(step, one)

        def complete(a):
            for zs in range(depth_z):
                for ys in range(depth_y):
                    for side in range(2 if a in shared else 1):
                        arrived(piece(a, zs, ys, 1 - c, side), c_recv.at[a, (zs * depth_y + ys) * 2 + side])

        def sent(a):
            for zs in range(depth_z):
                @pl.when((z < last) & (zs <= z))
                def _():
                    up(a, zs).wait_send()

                @pl.when((z > 0) & (zs >= z))
                def _():
                    down(a, zs).wait_send()

                across(a, zs).wait_send()
                for ys in range(depth_y):
                    for side in range(2 if a in shared else 1):
                        core(a, zs, ys, side).wait_send()
                    if a in shared:
                        @pl.when((zs != z) | (ys != y))
                        def _():
                            plane(a, zs, ys).wait_send()

        def token_copy(s):
            return pltpu.make_async_remote_copy(
                src_ref=tokens_ref.at[(1 - k) * count + s],
                dst_ref=x_all.at[s, mine],
                send_sem=t_send.at[s],
                recv_sem=t_recv.at[s],
                device_id=(b, 1 - k),
                device_id_type=pl.DeviceIdType.MESH,
            )

        def grad_copy(s):
            return pltpu.make_async_remote_copy(
                src_ref=cot_away.at[s],
                dst_ref=cot_all.at[s, mine],
                send_sem=g_send.at[s],
                recv_sem=g_recv.at[s],
                device_id=(b, 1 - k),
                device_id_type=pl.DeviceIdType.MESH,
            )

        def put(i, src, dst):
            return pltpu.make_async_copy(src, dst, out_sem.at[i])

        partners = 3 + (z < last).astype(jnp.int32) + (z > 0).astype(jnp.int32)
        pl.semaphore_wait(barrier, partners)
        for a in early:
            if a == W1:
                for i in range(3):
                    loads[i].wait()
            begin_z(a)
            begin_y(a)
            begin_core(a)
        token_copy(0).start()
        for i in (3, 4, 5):
            loads[i].wait()

        def begin_own(a):
            begin_y(a)
            begin_core(a)

        actions = {
            "hop": hop, "relay": relay, "swap": lambda a, step, far: swap(a, step, (1 - y) if far else y),
            "own": begin_own, "own_z": begin_z,
            "tokens": lambda s: token_copy(s).start(), "cotangent": lambda s: grad_copy(s).start(),
        }

        def at_slot(slot):
            for name, *what in GATHER_PLAN.get(slot, ()):
                actions[name](*what)

        def at_slots(first_slot, stride, index, bound):
            for value in range(bound):
                if first_slot + stride * value in GATHER_PLAN:
                    @pl.when(index == value)
                    def _():
                        at_slot(first_slot + stride * value)

        at_slot(0)

        for i in (6, 7):
            loads[i].wait()
        mask = mask_ref[...].astype(f32)
        own, away = jnp.where(k == 0, mask[:count], mask[count:]), jnp.where(k == 0, mask[count:], mask[:count])
        columns = jnp.concatenate([own, away], 0).T
        for s in range(count):
            cot_all[s, mine, :] = (cot_all[s, mine, :].astype(f32) * columns[:, s : s + 1]).astype(bf16)
            cot_away[s] = (cot_away[s].astype(f32) * columns[:, count + s : count + s + 1]).astype(bf16)

        loads[8].wait()
        for step in range(1, depth_z):
            for a in early:
                hop(a, step)
            at_slot(step)
            for a in early:
                relay(a, step - 1)
        for a in early:
            relay(a, last)
        at_slot(4)
        for a in early:
            complete(a)
        vec[...] = jnp.sum(tables[...].astype(f32), 0)
        save_w = put(0, w_qkv, w_qkv_out)
        save_w.start()

        def first(s, carry):
            arrived(x_all.at[s, theirs], t_recv.at[s])
            saves = [
                put(1, x_all.at[s], x_out.at[s]),
                put(2, t_1, q_out.at[s]),
                put(3, t_2, k_out.at[s]),
                put(4, t_3, v_out.at[s]),
                put(5, cb_all.at[s], cb_out.at[s]),
                put(6, l_s, l_out.at[s]),
            ]

            @pl.when(s > 0)
            def _():
                for save in saves[:4]:
                    save.wait()

            project(x_all[s], w_qkv, vec, t_1, t_2, t_3)
            for save in saves[:4]:
                save.start()
            at_slots(5, 3, s, count)
            stat[...] = jnp.zeros_like(stat)
            attend_pairs(t_1, t_2, t_3, cb_all.at[s], stat, 0, HEADS // 4)
            at_slots(6, 3, s, count)
            attend_pairs(t_1, t_2, t_3, cb_all.at[s], stat, HEADS // 4, HEADS // 2)

            @pl.when(s > 0)
            def _():
                for save in saves[4:]:
                    save.wait()

            l_s[...] = stat[...].T[:STAT_ROWS]
            for save in saves[4:]:
                save.start()
            at_slots(7, 3, s, count)
            return carry

        lax.fori_loop(0, count, first, 0)
        at_slot(17)
        for a in (M1, M2):
            complete(a)
        for i, (src, dst) in enumerate(((x_all.at[0], x_out.at[0]), (t_1, q_out.at[0]), (t_2, k_out.at[0]), (t_3, v_out.at[0]), (cb_all.at[0], cb_out.at[0]), (l_s, l_out.at[0]))):
            put(i + 1, src, dst).wait()
        save_w.wait()
        sums_out[...] = jnp.zeros_like(sums_out)
        w_o, w_i = w_mid.at[:, 0:width], w_mid.at[:, width:mid_width]
        O, GF, GA, GC, DELTA, H, GU, H_IN, GU_IN, MID = 8, 9, 10, 11, 12, 13, 15, 17, 19, 21

        lane = lax.broadcasted_iota(jnp.int32, inv.shape, 1)
        inv[...] = jnp.zeros_like(inv)

        def second(s, carry):
            slot = s % 2

            mid_s = t_mid.at[slot]

            @pl.when(s >= 2)
            def _():
                put(MID + slot, mid_s, mid_out.at[s]).wait()
                put(H + slot, h_s.at[slot], h_out.at[s]).wait()
                put(GU + slot, gu_s.at[slot], gu_out.at[s]).wait()

            normed, inverse = to_hidden(x_all[s], cb_all[s], w_o, w_i, vec, mid_s, h_s.at[slot], gu_s.at[slot])
            normed_all[s] = normed
            inv[...] = jnp.where(lane == s, inverse, inv[...])
            put(MID + slot, mid_s, mid_out.at[s]).start()
            put(H + slot, h_s.at[slot], h_out.at[s]).start()

            @pl.when(s < 2)
            def _():
                put(GU + slot, gu_s.at[slot], gu_out.at[s]).start()

            at_slots(18, 1, s, count)
            return carry

        lax.fori_loop(0, count, second, 0)
        for slot in range(2):
            put(MID + slot, t_mid.at[slot], mid_out.at[0]).wait()
        complete(UP)

        def third(i, carry):
            s = (i + count // 2) % count
            slot = i % 2
            at_slots(22, 1, i, count)
            arrived(cot_all.at[s, theirs], g_recv.at[s])
            saves = [
                put(O, t_1, o_out.at[s]),
                put(GF, t_3, gf_out.at[s]),
                put(GA, t_4, ga_out.at[s]),
                put(GC, t_5, gc_out.at[s]),
                put(DELTA, d_s, d_out.at[s]),
            ]

            @pl.when(i >= 2)
            def _():
                put(H_IN + slot, h_out.at[s], h_s.at[slot]).wait()
                put(GU_IN + slot, gu_out.at[s], gu_s.at[slot]).wait()

            @pl.when(i > 0)
            def _():
                for save in saves[:2]:
                    save.wait()

            grad_2 = to_output(normed_all[s], cot_all[s], w_up, vec, h_s.at[slot], t_1, t_3, sums_out)
            for save in saves[:2]:
                save.start()

            @pl.when(i > 0)
            def _():
                for save in saves[2:]:
                    save.wait()

            @pl.when((i > 0) & (i + 1 < count))
            def _():
                put(GU + 1 - slot, gu_s.at[1 - slot], gu_out.at[s]).wait()
                put(GU_IN + 1 - slot, gu_out.at[(s + 1) % count], gu_s.at[1 - slot]).start()

            inverse = jnp.sum(jnp.where(lane == s, inv[...], 0.0), 1, keepdims=True)
            to_context_grad(
                grad_2, normed_all[s], inverse, cb_all[s], w_o, w_i, w_up, vec, t_3, t_4, t_5, d_s, gu_s.at[slot], sums_out,
                put(GU + slot, gu_s.at[slot], gu_out.at[s]).start,
            )
            for save in saves[2:]:
                save.start()

            @pl.when(i + 2 < count)
            def _():
                put(H + slot, h_s.at[slot], h_out.at[s]).wait()
                put(H_IN + slot, h_out.at[(s + 2) % count], h_s.at[slot]).start()

            return carry

        lax.fori_loop(0, count, third, 0)
        for i, src, dst in ((O, t_1, o_out), (GF, t_3, gf_out), (GA, t_4, ga_out), (GC, t_5, gc_out), (DELTA, d_s, d_out)):
            put(i, src, dst.at[0]).wait()
        for slot in range(2):
            put(GU + slot, gu_s.at[slot], gu_out.at[0]).wait()
        for s in range(count):
            token_copy(s).wait_send()
            grad_copy(s).wait_send()
        for a in range(ARRAYS):
            sent(a)

    seq = jax.ShapeDtypeStruct((count, length, width), bf16)
    seq_wide = jax.ShapeDtypeStruct((count, length, inner), bf16)
    stat_shape = jax.ShapeDtypeStruct((count, STAT_ROWS, length), f32)
    hbm = pl.BlockSpec(memory_space=pl.ANY)
    one = pltpu.VMEM((length, width), bf16)
    two_wide = pltpu.VMEM((2, length, inner), bf16)
    all_seq = pltpu.VMEM((count, length, width), bf16)
    stat_one = pltpu.VMEM((STAT_ROWS, length), f32)
    lanes = pltpu.VMEM((length, 128), f32)
    dma = pltpu.SemaphoreType.DMA
    return pl.pallas_call(
        kernel,
        in_specs=[hbm, whole_vmem()] + [hbm] * 7 + [whole_vmem()],
        out_specs=[hbm] * 14 + [whole_vmem(), hbm],
        out_shape=[seq] * 5 + [stat_shape] + [seq] * 5 + [stat_shape, seq_wide, seq_wide]
        + [jax.ShapeDtypeStruct((16, width), f32), jax.ShapeDtypeStruct((width, qkv_width), bf16)],
        scratch_shapes=[
            pltpu.VMEM((width, qkv_width), bf16),
            pltpu.VMEM((width, mid_width), bf16),
            pltpu.VMEM((inner, width), bf16),
            pltpu.VMEM((devices, 16, width), bf16),
            pltpu.VMEM((16, width), f32),
            all_seq, all_seq,
            pltpu.VMEM((count, stretch, width), bf16),
            all_seq,
            pltpu.VMEM((2, length, width), bf16), one, one, one, stat_one, lanes, lanes, stat_one,
            pltpu.VMEM((count, length, width), f32),
            two_wide, two_wide,
            dma((ARRAYS, depth_z)), dma((ARRAYS, depth_z)), dma((ARRAYS, depth_z)),
            dma((ARRAYS, depth_z)), dma((ARRAYS, depth_z)),
            dma((ARRAYS, 2 * places)), dma((ARRAYS, 2 * places)), dma((ARRAYS, places)), dma((ARRAYS, places)),
            dma((count,)), dma((count,)), dma((count,)), dma((count,)), dma((9,)), dma((23,)),
        ],
        compiler_params=pltpu.CompilerParams(collective_id=1, has_side_effects=True, vmem_limit_bytes=63 * 2**20),
        name="forward",
    )(tokens, span_mask, cotangent, w_query, w_key, w_value, w_out, w_inner, w_outer, table)


SCATTER_PLAN = {
    2: (("out", 2), (1, "s", 0),),
    3: ((1, "s", 1),),
    4: (("out", 1), ("out", 3),),
    6: ((1, "s", 3), (2, "s", 0), ("out", 0),),
    7: ((1, "s", 2),),
    8: ((2, "s", 1),),
    9: ((1, "o", 0), (2, "s", 3),),
    10: ((1, "s", 4),),
    11: ((2, "s", 2),),
    14: ((2, "o", 0), (1, "o", 1),),
    16: ((3, "s", 0),),
    17: ((2, "s", 4),),
    18: ((1, "o", 2), (3, "o", 0),),
    19: ((2, "o", 1),),
    21: ((3, "s", 1),),
    22: ((2, "o", 2),),
    23: ((1, "p", 0), (1, "p", 1),),
    25: ((1, "p", 3), (3, "s", 4), (2, "p", 0), (3, "o", 1),),
    26: ((2, "p", 1), (1, "p", 2), (3, "o", 2),),
    27: ((2, "p", 3), (1, "p", 5), (4, "s", 4),),
    28: (
        (3, "p", 0),
        (4, "s", 0),
        (1, "p", 4),
        (3, "s", 3),
        (2, "p", 2),
        (4, "o", 2),
        (2, "p", 5),
        (4, "o", 0),
        (3, "p", 3),
        (3, "s", 2),
        (4, "o", 1),
        (4, "s", 1),
        (2, "p", 4),
        (4, "p", 0),
        (3, "p", 2),
        (3, "p", 1),
        (3, "p", 5),
        (3, "p", 4),
        (4, "s", 2),
        (4, "p", 5),
        (4, "p", 2),
        (4, "p", 1),
        (4, "s", 3),
        (4, "p", 3),
        (4, "p", 4),
    ),
}


def backward_call(x, q, k, v, cb, mid, gf, ga, gc, hidden, gu, out, stat_l, stat_d, w_qkv, sums, sizes):
    depth_z, depth_y, cores = sizes
    count, length, width = x.shape
    inner = hidden.shape[2]
    devices = depth_z * depth_y * cores
    part, outer_part = width // devices, inner // devices
    stretch, rows = length // 2, 2 * count
    chunks = inner // width
    GROUPS = 3
    pairs = HEADS // 2 // GROUPS
    column = pairs * PAIR
    narrow = width // GROUPS
    OUT = chunks
    QKV = chunks + 1
    SQUARES, PARTS = QKV, 2 * GROUPS
    first_of = {"s": 0, "o": SQUARES, "p": SQUARES + GROUPS}
    every = SQUARES + GROUPS + PARTS
    half = width // 2
    SLOTS = 2
    STEPS = 5
    tokens_all = count * length

    def kernel(
        x_in, q_in, k_in, v_in, cb_in, mid_in, gf_in, ga_in, gc_in, h_in, gu_in, out_in, w_in, l_ref, d_ref, sums_ref,
        received, grad_tokens, g_query, g_key, g_value, g_out, g_inner, g_outer, vectors,
        big, pool, w_cat, ga_s, gx_s, kt, gqt, own_s, own_o, r1, r2, r3, s4, r4, r1o, r2o, r3o, s4o, r4o, r1p, r2p, r3p, s4p, r4p, v_own, v_got,
        s1_send, s1_recv, s2_send, s2_recv, s3_send, s3_recv, s4_send, s4_recv,
        v_send, v_recv, o_send, o_recv, g_send, g_recv, big_sem, pool_sem, w_sem, ga_sem, keep_sem,
    ):
        b, k = lax.axis_index("batch"), lax.axis_index("blk")
        z, y, c = b // (depth_y * cores), (b // cores) % depth_y, b % cores

        def at(z_, y_, c_):
            return (z_ * depth_y + y_) * cores + c_

        beside = (b, 1 - k)
        other_core = (at(z, y, 1 - c), k)
        other_y = (at(z, 1 - y, c), k)

        def level(j):
            return (z + j) % depth_z

        barrier = pltpu.get_barrier_semaphore()
        partners = [beside, other_core, other_y] + [(at(level(j), y, c), k) for j in range(1, depth_z)]
        for device in partners:
            pl.semaphore_signal(barrier, inc=1, device_id=device, device_id_type=pl.DeviceIdType.MESH)

        def remote(src, dst, device, send, recv):
            return pltpu.make_async_remote_copy(
                src_ref=src, dst_ref=dst, send_sem=send, recv_sem=recv, device_id=device, device_id_type=pl.DeviceIdType.MESH
            )

        def load(i, src):
            return pltpu.make_async_copy(src, big.at[i], big_sem.at[i])

        def wide_load(i, src, j):
            return pltpu.make_async_copy(src.at[:, :, j * width : (j + 1) * width], big.at[i], big_sem.at[i])

        def pool_load(s, slot):
            return [
                pltpu.make_async_copy(src.at[s], pool.at[slot, i], pool_sem.at[slot, i])
                for i, src in enumerate((q_in, k_in, v_in, gc_in))
            ]

        def w_load(i, g):
            return pltpu.make_async_copy(
                w_in.at[:, i * width + g * column : i * width + (g + 1) * column],
                w_cat.at[g, :, i * column : (i + 1) * column],
                w_sem.at[i, g],
            )

        first_loads = [load(0, mid_in), wide_load(2, gu_in, 0), load(1, gf_in), wide_load(3, gu_in, 1)]
        for copy in first_loads:
            copy.start()
        mine = pl.ds(pl.multiple_of(k * stretch, stretch), stretch)
        theirs = pl.ds(pl.multiple_of((1 - k) * stretch, stretch), stretch)

        sums_of = {"s": (r1, r2, r3, s4, r4), "o": (r1o, r2o, r3o, s4o, r4o), "p": (r1p, r2p, r3p, s4p, r4p)}

        def buffers(kind, g):
            return [ref.at[g] for ref in sums_of[kind]] + [first_of[kind] + g]

        def own_part(kind, g, half_of, z_, y_, c_):
            if kind == "o":
                return own_o.at[g, z_, y_, c_]
            if kind == "s":
                return own_s.at[g % SLOTS, z_, y_, c_]
            return own_s.at[(QKV + g) % SLOTS, z_, y_, c_, :, half_of * half : (half_of + 1) * half]

        def step_1(kind, g, half_of=0):
            a1, _, _, _, _, i = buffers(kind, 2 * g + half_of if kind == "p" else g)
            own = own_part(kind, g, half_of, slice(None), slice(None), 1 - c)
            return remote(own, a1, other_core, s1_send.at[i], s1_recv.at[i])

        def step_2(kind, g):
            a1, a2, _, _, _, i = buffers(kind, g)
            return remote(a1.at[:, 1 - y], a2, other_y, s2_send.at[i], s2_recv.at[i])

        def step_3(kind, g, j):
            _, a2, a3, _, _, i = buffers(kind, g)
            return remote(
                a2.at[level(j)], a3.at[j - 1], (at(level(j), y, c), k), s3_send.at[i, j - 1], s3_recv.at[i, j - 1]
            )

        def step_4(kind, g):
            _, _, _, a4, b4, i = buffers(kind, g)
            return remote(a4, b4, beside, s4_send.at[i], s4_recv.at[i])

        def move_1(kind, g):
            a1, _, _, _, _, _ = buffers(kind, g)
            source = (g // 2, g % 2) if kind == "p" else (g, 0)
            step_1(kind, *source).wait()

            def add(i, carry):
                zi, yi = i // depth_y, i % depth_y
                a1[zi, yi] = a1[zi, yi] + own_part(kind, *source, zi, yi, c)[...]
                return carry

            lax.fori_loop(0, depth_z * depth_y, add, 0, unroll=True)
            step_2(kind, g).start()

        def move_2(kind, g):
            a1, a2, _, _, _, _ = buffers(kind, g)
            step_2(kind, g).wait()

            def add(zi, carry):
                a2[zi] = a2[zi] + a1[zi, y]
                return carry

            lax.fori_loop(0, depth_z, add, 0, unroll=True)
            for j in range(1, depth_z):
                step_3(kind, g, j).start()

        def move_3(kind, g):
            _, a2, a3, a4, _, _ = buffers(kind, g)
            for j in range(1, depth_z):
                step_3(kind, g, j).wait()
            total = a2[z].astype(f32)
            for j in range(1, depth_z):
                total = total + a3[j - 1].astype(f32)
            a4[...] = total.astype(bf16)
            step_4(kind, g).start()

        def move_4(kind, g):
            _, _, _, a4, b4, _ = buffers(kind, g)
            step_4(kind, g).wait()
            total = a4[...].astype(f32) + b4[...].astype(f32)
            if kind == "o":
                g_outer[:, g * narrow : (g + 1) * narrow] = total
            elif kind == "s" and g < OUT:
                g_inner[:, g * width : (g + 1) * width] = total
            elif kind == "s":
                g_out[...] = total
            else:
                group, begins = g // 2, (g % 2) * half
                for i, ref in enumerate((g_query, g_key, g_value)):
                    low, high = max(i * column, begins), min((i + 1) * column, begins + half)
                    if low < high:
                        to = group * column - i * column
                        ref[:, to + low : to + high] = total[:, low - begins : high - begins]

        def exchange(s):
            return remote(out_in.at[s, theirs], received.at[s], beside, o_send.at[s], o_recv.at[s])

        moves = {1: move_1, 2: move_2, 3: move_3, 4: move_4}

        def take(steps):
            for name, *what in steps:
                if name == "out":
                    exchange(*what).start()
                else:
                    moves[name](*what)

        def at_slot(slot):
            take(SCATTER_PLAN.get(slot, ()))

        def at_slots(first_slot, stride, index, bound):
            for value in range(bound):
                if first_slot + stride * value in SCATTER_PLAN:
                    @pl.when(index == value)
                    def _():
                        at_slot(first_slot + stride * value)

        def whole(i):
            return big[i].reshape(tokens_all, width)

        def keep(g, value):
            own_s[g % SLOTS] = value.astype(bf16).reshape(depth_z, depth_y, cores, part, width)

        pl.semaphore_wait(barrier, len(partners))

        first_loads[0].wait()
        for j in range(chunks):
            wide_load(2 + j % 2, gu_in, j).wait()
            at_slot(j)
            keep(j, mul(whole(0), whole(2 + j % 2), TN))
            step_1("s", j).start()
            following = j + 2 - chunks
            if following < 0:
                wide_load(2 + j % 2, gu_in, j + 2).start()
            else:
                wide_load(2 + j % 2, h_in, following).start()
            if j == 0:
                for s in range(2):
                    for copy in pool_load(s, s):
                        copy.start()
            if j == 1:
                for g in range(GROUPS):
                    for i in range(3):
                        w_load(i, g).start()
        load(0, ga_in).start()
        first_loads[2].wait()
        for j in range(chunks):
            wide_load(2 + j % 2, h_in, j).wait()
            at_slot(chunks + j)
            product = mul(whole(2 + j % 2), whole(1), TN).astype(bf16)
            for g in range(GROUPS):
                own_o[g, j] = product[:, g * narrow : (g + 1) * narrow].reshape(depth_y, cores, outer_part, narrow)
            if j + 2 < chunks:
                wide_load(2 + j % 2, h_in, j + 2).start()
            elif j + 2 == chunks:
                load(2 + j % 2, cb_in).start()
            else:
                load(2 + j % 2, x_in).start()
        for g in range(GROUPS):
            step_1("o", g).start()
        at_slot(2 * chunks)
        load(0, ga_in).wait()
        load(2 + chunks % 2, cb_in).wait()
        keep(OUT, mul(whole(2 + chunks % 2), whole(0), TN))
        step_1("s", OUT).start()
        for copy in pool_load(2, 2):
            copy.start()
        for g in range(GROUPS):
            for i in range(3):
                w_load(i, g).wait()
        load(2 + (chunks + 1) % 2, x_in).wait()
        x_at = 2 + (chunks + 1) % 2
        v_own[0] = sums_ref[...]

        cells = GROUPS * count
        def gx_copies(s):
            away = remote(gx_s.at[theirs], grad_tokens.at[k * count + s], beside, g_send.at[s], g_recv.at[s])
            stay = pltpu.make_async_copy(gx_s.at[mine], grad_tokens.at[k * count + s], keep_sem.at[1])
            return away, stay

        ga_load = [pltpu.make_async_copy(ga_in.at[s], ga_s, ga_sem.at[0]) for s in range(count)]
        ga_load[0].start()

        def cell(i, carry):
            s, g = i // GROUPS, i % GROUPS
            slot = s % 3

            @pl.when(g == 0)
            def _():
                for copy in pool_load(s, slot):
                    copy.wait()

            attend_back(
                pool.at[slot, 0], pool.at[slot, 1], pool.at[slot, 2], pool.at[slot, 3], l_ref.at[s], d_ref.at[s],
                big.at[g, s], kt, gqt, g * pairs, pairs,
            )
            span = pl.ds(pl.multiple_of(g * column, column), column)
            v_own[0, B_QUERY : B_QUERY + 1, span] += column_sum(big[g, s, :, :column])
            v_own[0, B_VALUE : B_VALUE + 1, span] += column_sum(big[g, s, :, 2 * column :])

            @pl.when(i == GROUPS - 1)
            def _():
                for copy in pool_load(3, 0):
                    copy.start()

            base = 2 * chunks + 1
            last_base = base + (GROUPS + 1) * (count - 1)
            for group in range(GROUPS):
                @pl.when(g == group)
                def _():
                    at_slots(base + group, GROUPS + 1, s, count - 1)

            @pl.when(s == count - 1)
            def _():
                at_slots(last_base, 2, g, GROUPS)
                keep(QKV + g, mul(whole(x_at), big[g].reshape(tokens_all, width), TN))
                step_1("p", g, 0).start()
                step_1("p", g, 1).start()
                at_slots(last_base + 1, 2, g, GROUPS)

            @pl.when(g == GROUPS - 1)
            def _():
                ga_load[0].wait()

                @pl.when(s > 0)
                def _():
                    away, stay = gx_copies(s - 1)
                    away.wait_send()
                    stay.wait()

                grad = ga_s[...].astype(f32)
                for group in range(GROUPS):
                    grad = grad + mul(big[group, s], w_cat[group], NT)
                gx_s[...] = grad.astype(bf16)
                away, stay = gx_copies(s)
                away.start()
                stay.start()

                @pl.when(s < count - 1)
                def _():
                    pltpu.make_async_copy(ga_in.at[s + 1], ga_s, ga_sem.at[0]).start()

                at_slots(base + GROUPS, GROUPS + 1, s, count - 1)

                @pl.when(s == count - 1)
                def _():
                    at_slot(last_base + 2 * GROUPS)

            return carry

        lax.fori_loop(0, cells, cell, 0)

        towards = [other_core, other_y, (at(z + 1 - 2 * (z % 2), y, c), k), (at((z + 2) % 4, y, c), k), beside]

        def v_copy(i):
            return remote(v_own.at[i], v_got.at[i], towards[i], v_send.at[i], v_recv.at[i])

        def v_move(i):
            v_copy(i).wait()
            v_own[i + 1] = v_own[i] + v_got[i]
            if i + 1 < STEPS:
                v_copy(i + 1).start()

        v_copy(0).start()
        rest = SCATTER_PLAN[2 * chunks + 1 + (GROUPS + 1) * (count - 1) + 2 * GROUPS + 1]
        for i in range(STEPS):
            take(rest[2 * i : 2 * i + 2])
            v_move(i)
        total = v_own[STEPS]
        inner_row = v_own[STEPS, pl.ds(B_INNER + b // (devices // chunks), 1), :]
        rolled = pltpu.roll(total, (width - b * part) % width, 1)
        wide = pltpu.roll(inner_row, (width - (b % (devices // chunks)) * outer_part) % width, 1)
        line = lax.broadcasted_iota(jnp.int32, total.shape, 0)
        vectors[...] = jnp.where(line == B_INNER, wide, rolled)
        take(rest[2 * STEPS :])
        away, stay = gx_copies(count - 1)
        away.wait_send()
        stay.wait()
        for s in range(count):
            exchange(s).wait_send()
            exchange(s).wait_recv()
            remote(gx_s.at[theirs], grad_tokens.at[(1 - k) * count + s], beside, g_send.at[s], g_recv.at[s]).wait_recv()

    hbm = pl.BlockSpec(memory_space=pl.ANY)
    dma = pltpu.SemaphoreType.DMA

    def vmem(*shape):
        return pltpu.VMEM(shape, bf16)

    def result(*shape):
        return jax.ShapeDtypeStruct(shape, f32)

    back = jax.ShapeDtypeStruct((rows, stretch, width), bf16)
    from_beside = jax.ShapeDtypeStruct((count, stretch, width), bf16)
    return pl.pallas_call(
        kernel,
        in_specs=[hbm] * 13 + [whole_vmem()] * 3,
        out_specs=[hbm] * 2 + [whole_vmem()] * 7,
        out_shape=[
            from_beside, back, result(part, width), result(part, width), result(part, width), result(part, width),
            result(part, inner), result(outer_part, width), result(16, width),
        ],
        scratch_shapes=[
            vmem(4, count, length, width),
            vmem(3, 4, length, width),
            vmem(GROUPS, width, 3 * column),
            vmem(length, width), vmem(length, width),
            vmem(column, length), vmem(column, length),
            vmem(SLOTS, depth_z, depth_y, cores, part, width),
            vmem(GROUPS, depth_z, depth_y, cores, outer_part, narrow),
            vmem(SQUARES, depth_z, depth_y, part, width), vmem(SQUARES, depth_z, part, width),
            vmem(SQUARES, depth_z - 1, part, width), vmem(SQUARES, part, width), vmem(SQUARES, part, width),
            vmem(GROUPS, depth_z, depth_y, outer_part, narrow), vmem(GROUPS, depth_z, outer_part, narrow),
            vmem(GROUPS, depth_z - 1, outer_part, narrow), vmem(GROUPS, outer_part, narrow), vmem(GROUPS, outer_part, narrow),
            vmem(PARTS, depth_z, depth_y, part, half), vmem(PARTS, depth_z, part, half),
            vmem(PARTS, depth_z - 1, part, half), vmem(PARTS, part, half), vmem(PARTS, part, half),
            pltpu.VMEM((STEPS + 1, 16, width), f32), pltpu.VMEM((STEPS, 16, width), f32),
            dma((every,)), dma((every,)), dma((every,)), dma((every,)),
            dma((every, depth_z - 1)), dma((every, depth_z - 1)), dma((every,)), dma((every,)),
            dma((STEPS,)), dma((STEPS,)), dma((count,)), dma((count,)), dma((count,)), dma((count,)),
            dma((4,)), dma((3, 4)), dma((3, GROUPS)), dma((1,)), dma((2,)),
        ],
        compiler_params=pltpu.CompilerParams(collective_id=2, has_side_effects=True, vmem_limit_bytes=63 * 2**20),
        name="backward",
    )(x, q, k, v, cb, mid, gf, ga, gc, hidden, gu, out, w_qkv, stat_l, stat_d, sums)


def settle_call(side, out, received, grad_tokens, grads, totals, sizes):
    rows, stretch, width = grad_tokens.shape
    count = rows // 2
    n = len(grads)

    def kernel(side_ref, out_ref, received_ref, tokens_ref, *refs):
        sources, totals_ref, (output_ref, grad_ref) = refs[:n], refs[n], refs[n + 1 : n + 3]
        results, vectors = refs[n + 3 : 2 * n + 3], refs[2 * n + 3 :]
        step = pl.program_id(0)
        here = step // count == side_ref[0]

        @pl.when(here)
        def _():
            output_ref[...] = out_ref[...]

        @pl.when(jnp.logical_not(here))
        def _():
            output_ref[...] = received_ref[...]

        grad_ref[...] = tokens_ref[...]

        @pl.when(step == 0)
        def _():
            for source, result in zip(sources, results):
                result[...] = source[...]
            for i, vector in enumerate(vectors):
                vector[...] = totals_ref[i : i + 1, : sizes[i]]

    block = (None, stretch, width)
    straight = pl.BlockSpec(block, lambda i, side: (i, 0, 0))

    def fixed(shape):
        return pl.BlockSpec(shape, lambda i, side: (0, 0))

    shapes = [grad.shape for grad in grads] + [(1, size) for size in sizes]
    return pl.pallas_call(
        kernel,
        grid_spec=pltpu.PrefetchScalarGridSpec(
            num_scalar_prefetch=1,
            grid=(rows,),
            in_specs=[
                pl.BlockSpec(block, lambda i, side: (jnp.clip(i - side[0] * count, 0, count - 1), side[0], 0)),
                pl.BlockSpec(block, lambda i, side: (jnp.clip(i - (1 - side[0]) * count, 0, count - 1), 0, 0)),
                straight,
            ]
            + [fixed(grad.shape) for grad in grads]
            + [fixed(totals.shape)],
            out_specs=[straight] * 2 + [fixed(shape) for shape in shapes],
        ),
        out_shape=[jax.ShapeDtypeStruct(grad_tokens.shape, bf16)] * 2
        + [jax.ShapeDtypeStruct(shape, f32) for shape in shapes],
        compiler_params=params(),
        name="settle",
    )(side, out, received, grad_tokens, *grads, totals)


def pack_shard(w_query, w_key, w_value, w_out, w_inner, w_outer, vectors):
    width = w_query.shape[1]
    inner_parts = [w_inner[:, i : i + width] for i in range(0, w_inner.shape[1], width)]
    small = jnp.concatenate(vectors)
    body_rows = sum(part.shape[0] for part in (w_query, w_key, w_value, w_out, w_outer, *inner_parts))
    rows = -(-(body_rows + 1) // 16) * 16
    tail = jnp.zeros(((rows - body_rows) * width,), small.dtype).at[: small.shape[0]].set(small)
    return jnp.concatenate(
        [w_query, w_key, w_value, w_out, *inner_parts, w_outer, tail.reshape(-1, width)]
    )


def vec_table(small, vec_names_sizes):
    rows, at = [], 0
    for size in vec_names_sizes:
        rows.append(small[:, at : at + size].reshape(-1))
        at += size
    return rows


def gather_weights(w_query, w_key, w_value, w_out, w_inner, w_outer, vectors):
    part, width = w_query.shape
    outer_part = w_outer.shape[0]
    chunks = w_inner.shape[1] // width
    sizes = [vector.shape[0] for vector in vectors]
    packed = pack_shard(w_query, w_key, w_value, w_out, w_inner, w_outer, vectors)
    gathered = lax.all_gather(packed, "batch", axis=0)

    def weight(at, count):
        return gathered[:, at : at + count].reshape(-1, width)

    squares = [weight(i * part, part) for i in range(4 + chunks)]
    outer_at = (4 + chunks) * part
    w_outer_all = weight(outer_at, outer_part)
    small = gathered[:, outer_at + outer_part :].reshape(gathered.shape[0], -1)
    vec = jnp.concatenate(vec_table(small, sizes)).reshape(-1, width).astype(f32)
    vec = jnp.concatenate([vec, jnp.zeros((16 - vec.shape[0], width), f32)])
    return jnp.concatenate(squares[:3], 1), squares[3], jnp.concatenate(squares[4:], 1), w_outer_all, vec


def body(
    tokens,
    span_mask,
    cotangent,
    w_query,
    b_query,
    w_key,
    w_value,
    b_value,
    w_out,
    b_out,
    gain_first,
    bias_first,
    w_inner,
    b_inner,
    w_outer,
    b_outer,
    gain_second,
    bias_second,
):
    rows, stretch, width = tokens.shape
    inner = w_inner.shape[1]
    part = w_query.shape[0]
    outer_part = w_outer.shape[0]
    vectors = (b_query, b_value, b_out, gain_first, bias_first, b_outer, gain_second, bias_second, b_inner)
    sizes = [vector.shape[0] for vector in vectors]

    devices = lax.axis_size("batch")
    chunks = inner // width
    swap = functools.partial(lax.all_to_all, axis_name="blk", tiled=True)
    outer_at = (4 + chunks) * part
    shard_rows = -(-(outer_at + outer_part + 1) // 16) * 16
    if (devices, lax.axis_size("blk")) == (16, 2):
        table = sum(
            lax.pad(
                vector.astype(f32).reshape(1, -1), f32(0), ((i, 15 - i, 0), (0, width - vector.shape[0], 0))
            )
            for i, vector in enumerate(vectors)
        )
        x, q, k, v, cb, stat_l, out, mid, gf, ga, gc, stat_d, hidden, gu, sums_ffn, w_qkv = forward_call(
            tokens, span_mask, cotangent, w_query, w_key, w_value, w_out, w_inner, w_outer, table, (4, 2, 2)
        )
        results = backward_call(
            x, q, k, v, cb, mid, gf, ga, gc, hidden, gu, out, stat_l, stat_d, w_qkv, sums_ffn, (4, 2, 2)
        )
        side = lax.axis_index("blk").astype(jnp.int32).reshape(1)
        settled = settle_call(side, out, results[0], results[1], results[2:-1], results[-1], sizes)
        output, grad_tokens, g_query, g_key, g_value, g_out, g_inner, g_outer = settled[:8]
        small = [vector.reshape(-1) for vector in settled[8:]]
        return (
            output, grad_tokens, g_query, small[0], g_key, g_value, small[1], g_out, small[2], small[3], small[4], g_inner,
            small[8], g_outer, small[5], small[6], small[7],
        )
    w_qkv, w_out_all, w_inner_all, w_outer_all, vec = gather_weights(
        w_query, w_key, w_value, w_out, w_inner, w_outer, vectors
    )
    masked = cotangent * span_mask[..., None].astype(bf16)
    x = swap(tokens, split_axis=0, concat_axis=1)
    cot = swap(masked, split_axis=0, concat_axis=1)
    q, k, v, cb, stat_l = attention_call(x, w_qkv, vec)
    out, mid, gf, ga, gc, stat_d, hidden, gu, sums_ffn = feed_forward_call(
        x, cb, cot, w_out_all, w_inner_all, w_outer_all, vec
    )
    gx, gw_qkv, sums_att = attention_back_call(x, q, k, v, gc, ga, stat_l, stat_d, w_qkv)
    output = swap(out, split_axis=1, concat_axis=0)
    grad_tokens = swap(gx, split_axis=1, concat_axis=0)

    def flat(values):
        return values.reshape(-1, values.shape[-1])

    gw_out = weight_grad_call(flat(cb), flat(ga), False)
    gw_inner = weight_grad_call(flat(mid), flat(gu), False)
    gw_outer = weight_grad_call(flat(hidden), flat(gf), True)

    sums = sums_ffn + sums_att
    small_sums = [sums[i].reshape(devices, -1) for i in range(B_INNER)]
    small_sums.append(sums[B_INNER : B_INNER + chunks].reshape(devices, -1))
    tail = jnp.concatenate(small_sums, 1).astype(bf16)
    tail = jnp.pad(tail, ((0, 0), (0, (shard_rows - outer_at - outer_part) * width - tail.shape[1])))
    pieces = [gw_qkv[:, i * width : (i + 1) * width].reshape(devices, part, width) for i in range(3)]
    pieces.append(gw_out.reshape(devices, part, width))
    pieces += [gw_inner[:, i * width : (i + 1) * width].reshape(devices, part, width) for i in range(chunks)]
    pieces.append(gw_outer.reshape(devices, outer_part, width))
    pieces.append(tail.reshape(devices, -1, width))
    grads = jnp.concatenate(pieces, 1)
    share = lax.psum_scatter(grads, "batch", scatter_dimension=0, tiled=False)
    share = lax.psum(share, "blk").astype(f32)
    square = [share[i * part : (i + 1) * part] for i in range(4 + chunks)]
    share_small = share[outer_at + outer_part :].reshape(-1)
    small_out, at = [], 0
    for size in sizes:
        small_out.append(share_small[at : at + size])
        at += size
    (g_b_query, g_b_value, g_b_out, g_gain_1, g_bias_1, g_b_outer, g_gain_2, g_bias_2, g_b_inner) = small_out
    return (
        output,
        grad_tokens,
        square[0],
        g_b_query,
        square[1],
        square[2],
        g_b_value,
        square[3],
        g_b_out,
        g_gain_1,
        g_bias_1,
        jnp.concatenate(square[4:], 1),
        g_b_inner,
        share[outer_at : outer_at + outer_part],
        g_b_outer,
        g_gain_2,
        g_bias_2,
    )


def solution(mesh):
    block = P("batch", "blk", None)
    matrix, vector = P("batch", None), P("batch")
    weights = (
        matrix, vector, matrix, matrix, vector, matrix, vector, vector, vector, matrix, vector, matrix, vector, vector, vector,
    )
    return jax.shard_map(
        body,
        mesh=mesh,
        in_specs=(block, P("batch", "blk"), block) + weights,
        out_specs=(block, block) + weights,
        check_vma=False,
    )
```

```python
import functools

import jax
import jax.numpy as jnp
from jax import lax
from jax.experimental import pallas as pl
from jax.experimental.pallas import tpu as pltpu
from jax.sharding import PartitionSpec as P

HEADS = 12
HEAD_DIM = 64
PAIR = 2 * HEAD_DIM
STAT_ROWS = 16
VMEM_BYTES = 60 * 2**20

epsilon = 1e-06
bf16 = jnp.bfloat16
f32 = jnp.float32

NN = (((1,), (0,)), ((), ()))
NT = (((1,), (1,)), ((), ()))
TN = (((0,), (0,)), ((), ()))

B_QUERY, B_VALUE, B_OUT, GAIN_1, BIAS_1, B_OUTER, GAIN_2, BIAS_2, B_INNER = range(9)


def mul(left, right, dims=NN):
    return lax.dot_general(left, right, dims, preferred_element_type=f32)


def row(ref, index):
    return ref[index : index + 1, :]


def halves(block):
    lane = lax.broadcasted_iota(jnp.int32, block.shape, 1)
    zero = jnp.zeros_like(block)
    return jnp.where(lane < HEAD_DIM, block, zero), jnp.where(lane < HEAD_DIM, zero, block)


def pair_at(p):
    return pl.ds(pl.multiple_of(p * PAIR, PAIR), PAIR)


def normalize(values):
    center = values - jnp.mean(values, -1, keepdims=True)
    inverse = lax.rsqrt(jnp.mean(center * center, -1, keepdims=True) + epsilon)
    return center * inverse, inverse


def norm_back(grad, normed, inverse, gain):
    scaled = grad * gain
    return inverse * (
        scaled
        - jnp.mean(scaled, -1, keepdims=True)
        - normed * jnp.mean(scaled * normed, -1, keepdims=True)
    )


def column_sum(values):
    return jnp.sum(values.astype(f32), 0, keepdims=True)


def project(x, w_ref, vec_ref, q_ref, k_ref, v_ref):
    width = x.shape[-1]
    q = (mul(x, w_ref[:, :width]) + row(vec_ref, B_QUERY)).astype(bf16)
    q_ref[...] = q * bf16(HEAD_DIM**-0.5)
    k_ref[...] = mul(x, w_ref[:, width : 2 * width]).astype(bf16)
    v_ref[...] = (mul(x, w_ref[:, 2 * width :]) + row(vec_ref, B_VALUE)).astype(bf16)


def attend_pairs(q_ref, k_ref, v_ref, c_ref, stat, first, end):
    lane = lax.broadcasted_iota(jnp.int32, stat.shape, 1)

    def pair(p, carry):
        at = pair_at(p)
        q2, k2, v2 = q_ref[:, at], k_ref[:, at], v_ref[:, at]
        context = None
        for h, (k_one, v_one) in enumerate(zip(halves(k2), halves(v2))):
            scores = mul(q2, k_one, NT)
            best = jnp.max(scores, 1, keepdims=True)
            weights = jnp.exp(scores - best)
            total = jnp.sum(weights, 1, keepdims=True)
            part = mul(weights.astype(bf16), v_one) * (1.0 / total)
            context = part if context is None else context + part
            stat[...] = jnp.where(lane == 2 * p + h, best + jnp.log(total), stat[...])
        c_ref[:, at] = context.astype(bf16)
        return carry

    lax.fori_loop(first, end, pair, 0, unroll=3)


def attend(q_ref, k_ref, v_ref, c_ref, l_ref, stat):
    stat[...] = jnp.zeros_like(stat)
    attend_pairs(q_ref, k_ref, v_ref, c_ref, stat, 0, HEADS // 2)
    l_ref[...] = stat[...].T[:STAT_ROWS]


def attend_back(q_ref, k_ref, v_ref, g_ref, l_ref, d_ref, out_ref, kt, gqt, first, pairs):
    part = pairs * PAIR
    columns = pl.ds(pl.multiple_of(first * PAIR, PAIR), part)
    kt[...] = (k_ref[:, columns] * bf16(HEAD_DIM**-0.5)).T
    for p in range(pairs):
        at = pair_at(first + p)
        q2, g2 = q_ref[:, at], g_ref[:, at]
        ks, vs = halves(k_ref[:, at]), halves(v_ref[:, at])
        qs, gs = halves(q2), halves(g2)
        gk = gv = None
        for h in range(2):
            head = 2 * (first + p) + h
            probs = jnp.exp(mul(ks[h], q2, NT) - l_ref[pl.ds(head, 1), :])
            grad_probs = mul(vs[h], g2, NT)
            grad_scores = (probs * (grad_probs - d_ref[pl.ds(head, 1), :])).astype(bf16)
            gk_one = mul(grad_scores, qs[h])
            gv_one = mul(probs.astype(bf16), gs[h])
            gk = gk_one if gk is None else gk + gk_one
            gv = gv_one if gv is None else gv + gv_one
            rows = slice((2 * p + h) * HEAD_DIM, (2 * p + h + 1) * HEAD_DIM)
            gqt[rows, :] = mul(kt[rows, :], grad_scores).astype(bf16)
        out_ref[:, part + p * PAIR : part + (p + 1) * PAIR] = gk.astype(bf16)
        out_ref[:, 2 * part + p * PAIR : 2 * part + (p + 1) * PAIR] = gv.astype(bf16)
    out_ref[:, :part] = gqt[...].T


def to_hidden(x, cb, wo_ref, wi_ref, vec_ref, mid_ref, h_ref, slope_ref):
    width = x.shape[-1]
    normed, inverse = normalize(x.astype(f32) + (mul(cb, wo_ref[...]) + row(vec_ref, B_OUT)))
    mid = (normed * row(vec_ref, GAIN_1) + row(vec_ref, BIAS_1)).astype(bf16)
    mid_ref[...] = mid
    for c in range(wi_ref.shape[1] // width):
        at = slice(c * width, (c + 1) * width)
        inner = mul(mid, wi_ref[:, at]) + row(vec_ref, B_INNER + c)
        cdf = 0.5 + 0.5 * lax.erf(inner * (0.5**0.5))
        h_ref[:, at] = (inner * cdf).astype(bf16)
        slope = cdf + inner * (jnp.exp(inner * inner * -0.5) * ((0.5 / jnp.pi) ** 0.5))
        slope_ref[:, at] = slope.astype(bf16)
    return normed, inverse


def to_output(normed_1, cot, wu_ref, vec_ref, h_ref, out_ref, gf_ref, sums_ref):
    width = normed_1.shape[-1]
    total = normed_1 * row(vec_ref, GAIN_1) + (row(vec_ref, BIAS_1) + row(vec_ref, B_OUTER))
    for c in range(h_ref.shape[1] // width):
        at = slice(c * width, (c + 1) * width)
        total = total + mul(h_ref[:, at], wu_ref[at, :])
    normed, inverse = normalize(total)
    gain = row(vec_ref, GAIN_2)
    out_ref[...] = (normed * gain + row(vec_ref, BIAS_2)).astype(bf16)
    grad = cot.astype(f32)
    sums_ref[GAIN_2 : GAIN_2 + 1, :] += column_sum(grad * normed)
    sums_ref[BIAS_2 : BIAS_2 + 1, :] += column_sum(grad)
    grad_2 = norm_back(grad, normed, inverse, gain)
    gf = grad_2.astype(bf16)
    gf_ref[...] = gf
    sums_ref[B_OUTER : B_OUTER + 1, :] += column_sum(gf)
    return grad_2


def to_context_grad(
    grad_2, normed_1, inverse_1, cb, wo_ref, wi_ref, wu_ref, vec_ref, gf_ref, ga_ref, gc_ref, d_ref, gu_ref, sums_ref
):
    width = grad_2.shape[-1]
    gf = gf_ref[...]
    grad_mid = grad_2
    for c in range(wi_ref.shape[1] // width):
        at = slice(c * width, (c + 1) * width)
        gu = (mul(gf, wu_ref[at, :], NT) * gu_ref[:, at].astype(f32)).astype(bf16)
        gu_ref[:, at] = gu
        sums_ref[B_INNER + c : B_INNER + c + 1, :] += column_sum(gu)
        grad_mid = grad_mid + mul(gu, wi_ref[:, at], NT)
    sums_ref[GAIN_1 : GAIN_1 + 1, :] += column_sum(grad_mid * normed_1)
    sums_ref[BIAS_1 : BIAS_1 + 1, :] += column_sum(grad_mid)
    ga = norm_back(grad_mid, normed_1, inverse_1, row(vec_ref, GAIN_1)).astype(bf16)
    ga_ref[...] = ga
    sums_ref[B_OUT : B_OUT + 1, :] += column_sum(ga)
    gc = mul(ga, wo_ref[...], NT).astype(bf16)
    gc_ref[...] = gc
    product = gc.astype(f32) * cb.astype(f32)
    high = product.astype(bf16)
    low = (product - high.astype(f32)).astype(bf16)
    head = lax.broadcasted_iota(jnp.int32, (STAT_ROWS, width), 0)
    column = lax.broadcasted_iota(jnp.int32, (STAT_ROWS, width), 1)
    pick = jnp.where(column // HEAD_DIM == head, 1.0, 0.0).astype(bf16)
    d_ref[...] = mul(pick, high, NT) + mul(pick, low, NT)


def spec(shape, pipelined=True):
    zeros = (0,) * (len(shape) - 1)
    if pipelined:
        return pl.BlockSpec(shape, lambda i: (i,) + zeros)
    return pl.BlockSpec(shape, lambda i: (0,) + zeros)


def whole_vmem():
    return pl.BlockSpec(memory_space=pltpu.VMEM)


def params():
    return pltpu.CompilerParams(vmem_limit_bytes=VMEM_BYTES, dimension_semantics=("arbitrary",))


def attention_call(x, w_qkv, vec):
    count, length, width = x.shape
    block = (None, length, width)

    def kernel(x_ref, w_ref, vec_ref, q_ref, k_ref, v_ref, c_ref, l_ref, stat):
        project(x_ref[...], w_ref, vec_ref, q_ref, k_ref, v_ref)
        attend(q_ref, k_ref, v_ref, c_ref, l_ref, stat)

    seq = jax.ShapeDtypeStruct(x.shape, bf16)
    return pl.pallas_call(
        kernel,
        grid=(count,),
        in_specs=[spec(block), whole_vmem(), whole_vmem()],
        out_specs=[spec(block)] * 4 + [spec((None, STAT_ROWS, length))],
        out_shape=[seq] * 4 + [jax.ShapeDtypeStruct((count, STAT_ROWS, length), f32)],
        scratch_shapes=[pltpu.VMEM((length, 128), f32)],
        compiler_params=params(),
        name="attention",
    )(x, w_qkv, vec)


def feed_forward_call(x, cb, cot, w_out, w_inner, w_outer, vec):
    count, length, width = x.shape
    inner = w_inner.shape[1]
    block, wide = (None, length, width), (None, length, inner)

    def kernel(x_ref, cb_ref, cot_ref, wo, wi, wu, vec_ref, out, mid, gf, ga, gc, d, h, gu, sums):
        @pl.when(pl.program_id(0) == 0)
        def _():
            sums[...] = jnp.zeros_like(sums)

        cb = cb_ref[...]
        normed, inverse = to_hidden(x_ref[...], cb, wo, wi, vec_ref, mid, h, gu)
        grad_2 = to_output(normed, cot_ref[...], wu, vec_ref, h, out, gf, sums)
        to_context_grad(grad_2, normed, inverse, cb, wo, wi, wu, vec_ref, gf, ga, gc, d, gu, sums)

    seq = jax.ShapeDtypeStruct(x.shape, bf16)
    seq_wide = jax.ShapeDtypeStruct((count, length, inner), bf16)
    return pl.pallas_call(
        kernel,
        grid=(count,),
        in_specs=[spec(block)] * 3 + [whole_vmem()] * 4,
        out_specs=[spec(block)] * 5
        + [spec((None, STAT_ROWS, length)), spec(wide), spec(wide), spec((16, width), False)],
        out_shape=[seq] * 5
        + [
            jax.ShapeDtypeStruct((count, STAT_ROWS, length), f32),
            seq_wide,
            seq_wide,
            jax.ShapeDtypeStruct((16, width), f32),
        ],
        compiler_params=params(),
        name="feed_forward",
    )(x, cb, cot, w_out, w_inner, w_outer, vec)


def weight_grad_call(left, right, over_left):
    tokens, rows = left.shape
    columns = right.shape[1]
    step = min(rows, columns)

    def kernel(left_ref, right_ref, out_ref):
        out_ref[...] = mul(left_ref[...], right_ref[...], TN).astype(bf16)

    if over_left:
        grid, left_map, right_map, out_map = rows // step, lambda i: (0, i), lambda i: (0, 0), lambda i: (i, 0)
    else:
        grid, left_map, right_map, out_map = columns // step, lambda i: (0, 0), lambda i: (0, i), lambda i: (0, i)
    return pl.pallas_call(
        kernel,
        grid=(grid,),
        in_specs=[pl.BlockSpec((tokens, step), left_map), pl.BlockSpec((tokens, step), right_map)],
        out_specs=pl.BlockSpec((step, step), out_map),
        out_shape=jax.ShapeDtypeStruct((rows, columns), bf16),
        compiler_params=params(),
        name="weight_grad",
    )(left, right)


def attention_back_call(x, q, k, v, gc, ga, stat_l, stat_d, w_qkv):
    count, length, width = x.shape
    block = (None, length, width)
    pairs = HEADS // 2

    def kernel(x_ref, q_ref, k_ref, v_ref, gc_ref, ga_ref, l_ref, d_ref, w_ref, gx_ref, gw_ref, sums_ref, kt, gqt, g, total):
        step = pl.program_id(0)

        @pl.when(step == 0)
        def _():
            sums_ref[...] = jnp.zeros_like(sums_ref)
            total[...] = jnp.zeros_like(total)

        attend_back(q_ref, k_ref, v_ref, gc_ref, l_ref, d_ref, g, kt, gqt, 0, pairs)
        sums_ref[B_QUERY : B_QUERY + 1, :] += column_sum(g[:, :width])
        sums_ref[B_VALUE : B_VALUE + 1, :] += column_sum(g[:, 2 * width :])
        grad = ga_ref[...].astype(f32)
        x = x_ref[...]
        for i in range(3):
            at = slice(i * width, (i + 1) * width)
            grad = grad + mul(g[:, at], w_ref[:, at], NT)
            total[:, at] += mul(x, g[:, at], TN)
        gx_ref[...] = grad.astype(bf16)

        @pl.when(step == count - 1)
        def _():
            gw_ref[...] = total[...].astype(bf16)

    return pl.pallas_call(
        kernel,
        grid=(count,),
        in_specs=[spec(block)] * 6 + [spec((None, STAT_ROWS, length))] * 2 + [whole_vmem()],
        out_specs=[spec(block), spec((width, 3 * width), False), spec((16, width), False)],
        out_shape=[
            jax.ShapeDtypeStruct(x.shape, bf16),
            jax.ShapeDtypeStruct((width, 3 * width), bf16),
            jax.ShapeDtypeStruct((16, width), f32),
        ],
        scratch_shapes=[pltpu.VMEM((width, length), bf16)] * 2
        + [pltpu.VMEM((length, 3 * width), bf16), pltpu.VMEM((width, 3 * width), f32)],
        compiler_params=params(),
        name="attention_back",
    )(x, q, k, v, gc, ga, stat_l, stat_d, w_qkv)


W1, W2, TABLE, M1, M2, UP = range(6)
GATHER_PLAN = {
    1: (("tokens", 1), ("own_z", M2),),
    2: (("own", M2), ("own_z", UP), ("tokens", 2),),
    3: (("hop", UP, 1),),
    4: (("hop", UP, 2), ("own_z", M1),),
    5: (("hop", UP, 3),),
    6: (("hop", M2, 1),),
    7: (("own", M1), ("hop", M2, 2), ("relay", M2, 0),),
    8: (("hop", M2, 3),),
    9: (("tokens", 3), ("hop", M1, 1), ("relay", M2, 1),),
    11: (("hop", M1, 2), ("relay", M2, 2), ("relay", M2, 3), ("swap", M2, 2, 0),),
    12: (("relay", UP, 2), ("own", UP),),
    13: (("swap", UP, 3, 0), ("swap", M2, 3, 0), ("relay", M1, 1), ("hop", M1, 3), ("swap", M2, 0, 1),),
    14: (("relay", M1, 0),),
    15: (("relay", M1, 2), ("relay", UP, 1), ("swap", M2, 1, 1), ("swap", M2, 2, 1),),
    16: (("swap", UP, 1, 0), ("swap", M2, 3, 1),),
    17: (("swap", M2, 1, 0), ("relay", M1, 3), ("relay", UP, 3), ("relay", UP, 0),),
    18: (("cotangent", 2),),
    19: (("swap", UP, 3, 1), ("cotangent", 3),),
    20: (("swap", UP, 2, 1), ("swap", UP, 2, 0), ("swap", UP, 1, 1), ("swap", UP, 0, 1),),
    21: (("cotangent", 0), ("cotangent", 1),),
}


def forward_call(tokens, span_mask, cotangent, w_query, w_key, w_value, w_out, w_inner, w_outer, table, sizes):
    depth_z, depth_y, cores = sizes
    rows, stretch, width = tokens.shape
    inner = w_inner.shape[1]
    part, outer_part = w_query.shape[0], w_outer.shape[0]
    devices = depth_z * depth_y * cores
    count, length = rows // 2, 2 * stretch
    chunks = inner // width
    qkv_width, mid_width = 3 * width, width + inner
    last = depth_z - 1
    ARRAYS = 6
    early = (TABLE, W1, W2)
    shared = (M2, UP)
    places = depth_z * depth_y
    half = width // 2
    m2_half = mid_width // 512 * 128
    m1_width = mid_width - 2 * m2_half

    def kernel(
        tokens_ref, mask_ref, cot_ref, wq_in, wk_in, wv_in, wo_in, wi_in, wu_in, table_in,
        x_out, q_out, k_out, v_out, cb_out, l_out, o_out, mid_out, gf_out, ga_out, gc_out, d_out, h_out, gu_out,
        sums_out, w_qkv_out,
        w_qkv, w_mid, w_up, tables, vec, x_all, cot_all, cot_away, cb_all, t_mid, t_3, t_4, t_5, l_s, stat, inv, d_s,
        normed_all, h_s, gu_s,
        up_send, down_send, z_recv, y_send, y_recv, c_send, c_recv, x_send, x_recv, t_send, t_recv, g_send, g_recv,
        in_sem, out_sem,
    ):
        b, k = lax.axis_index("batch"), lax.axis_index("blk")
        z, y, c = b // (depth_y * cores), (b // cores) % depth_y, b % cores

        def at(z_, y_, c_):
            return (z_ * depth_y + y_) * cores + c_

        barrier = pltpu.get_barrier_semaphore()

        def greet(device):
            pl.semaphore_signal(barrier, inc=1, device_id=device, device_id_type=pl.DeviceIdType.MESH)

        greet((b, 1 - k))
        greet((at(z, 1 - y, c), k))
        greet((at(z, y, 1 - c), k))

        @pl.when(z < last)
        def _():
            greet((at(z + 1, y, c), k))

        @pl.when(z > 0)
        def _():
            greet((at(z - 1, y, c), k))

        shard = pl.ds(b * part, part)
        mine = pl.ds(pl.multiple_of(k * stretch, stretch), stretch)
        theirs = pl.ds(pl.multiple_of((1 - k) * stretch, stretch), stretch)
        loads = [
            pltpu.make_async_copy(wq_in, w_qkv.at[shard, 0:width], in_sem.at[0]),
            pltpu.make_async_copy(wk_in, w_qkv.at[shard, width : 2 * width], in_sem.at[1]),
            pltpu.make_async_copy(wv_in, w_qkv.at[shard, 2 * width : 3 * width], in_sem.at[2]),
            pltpu.make_async_copy(wu_in, w_up.at[pl.ds(b * outer_part, outer_part)], in_sem.at[5]),
            pltpu.make_async_copy(wo_in, w_mid.at[shard, 0:width], in_sem.at[3]),
            pltpu.make_async_copy(wi_in, w_mid.at[shard, width:mid_width], in_sem.at[4]),
            pltpu.make_async_copy(cot_ref.at[pl.ds(k * count, count)], cot_all.at[:, mine], in_sem.at[6]),
            pltpu.make_async_copy(cot_ref.at[pl.ds((1 - k) * count, count)], cot_away, in_sem.at[7]),
            pltpu.make_async_copy(tokens_ref.at[pl.ds(k * count, count)], x_all.at[:, mine], in_sem.at[8]),
        ]
        for copy in loads:
            copy.start()

        raw = table_in[...]
        rolled = pltpu.roll(raw, b * part, 1)
        wide = pltpu.roll(raw[B_INNER : B_INNER + 1, :], (b % (devices // chunks)) * outer_part, 1)
        line = lax.broadcasted_iota(jnp.int32, raw.shape, 0)
        own_table = jnp.where(line < B_INNER, rolled, 0.0)
        own_table = jnp.where(line == B_INNER + b // (devices // chunks), wide, own_table)
        tables[b] = own_table.astype(bf16)

        t_1, t_2 = t_mid.at[0], t_mid.at[1]

        def piece(a, z_, y_, c_, side):
            d = at(z_, y_, c_)
            rows = pl.ds(d * part, part)
            if a == W1:
                return w_qkv.at[rows, : qkv_width // 2]
            if a == W2:
                return w_qkv.at[rows, qkv_width // 2 :]
            if a == TABLE:
                return tables.at[d]
            if a == M1:
                return w_mid.at[rows, :m1_width]
            if a == M2:
                return w_mid.at[rows, pl.ds(pl.multiple_of(m1_width + side * m2_half, 128), m2_half)]
            return w_up.at[pl.ds(d * outer_part, outer_part), pl.ds(pl.multiple_of(side * half, half), half)]

        def remote(ref, device, send, recv):
            return pltpu.make_async_remote_copy(
                src_ref=ref, dst_ref=ref, send_sem=send, recv_sem=recv, device_id=device, device_id_type=pl.DeviceIdType.MESH
            )

        def up(a, zs):
            return remote(piece(a, zs, y, c, k), (at(z + 1, y, c), k), up_send.at[a, zs], z_recv.at[a, zs])

        def down(a, zs):
            return remote(piece(a, zs, y, c, k), (at(z - 1, y, c), k), down_send.at[a, zs], z_recv.at[a, zs])

        def across(a, zs):
            return remote(piece(a, zs, y, c, k), (at(z, 1 - y, c), k), y_send.at[a, zs], y_recv.at[a, zs])

        def core(a, zs, ys, side):
            i = (zs * depth_y + ys) * 2 + (side if a in shared else 0)
            return remote(piece(a, zs, ys, c, side), (at(z, y, 1 - c), k), c_send.at[a, i], c_recv.at[a, i])

        def plane(a, zs, ys):
            i = zs * depth_y + ys
            return remote(piece(a, zs, ys, c, k), (b, 1 - k), x_send.at[a, i], x_recv.at[a, i])

        def arrived(ref, sem):
            remote(ref, (b, 1 - k), sem, sem).wait_recv()

        def begin_z(a):
            @pl.when(z < last)
            def _():
                up(a, z).start()

            @pl.when(z > 0)
            def _():
                down(a, z).start()

        def begin_y(a):
            across(a, z).start()

        def begin_core(a):
            core(a, z, y, k).start()
            if a in shared:
                core(a, z, y, 1 - k).start()

        def levels(step, do):
            if step == 0:
                do(z, 0)
                return

            @pl.when(z >= step)
            def _():
                do(z - step, 1)

            @pl.when(z + step <= last)
            def _():
                do(z + step, -1)

        def hop(a, step):
            def one(zs, way):
                arrived(piece(a, zs, y, c, k), z_recv.at[a, zs])
                if way > 0:
                    @pl.when(z < last)
                    def _():
                        up(a, zs).start()
                else:
                    @pl.when(z > 0)
                    def _():
                        down(a, zs).start()
                across(a, zs).start()
                if a in shared:
                    plane(a, zs, y).start()
                core(a, zs, y, k).start()

            levels(step, one)

        def relay(a, step):
            def one(zs, way):
                arrived(piece(a, zs, 1 - y, c, k), y_recv.at[a, zs])
                if a in shared:
                    plane(a, zs, 1 - y).start()
                core(a, zs, 1 - y, k).start()

            levels(step, one)

        def swap(a, step, ys):
            def one(zs, way):
                arrived(piece(a, zs, ys, c, 1 - k), x_recv.at[a, zs * depth_y + ys])
                core(a, zs, ys, 1 - k).start()

            levels(step, one)

        def complete(a):
            for zs in range(depth_z):
                for ys in range(depth_y):
                    for side in range(2 if a in shared else 1):
                        arrived(piece(a, zs, ys, 1 - c, side), c_recv.at[a, (zs * depth_y + ys) * 2 + side])

        def sent(a):
            for zs in range(depth_z):
                @pl.when((z < last) & (zs <= z))
                def _():
                    up(a, zs).wait_send()

                @pl.when((z > 0) & (zs >= z))
                def _():
                    down(a, zs).wait_send()

                across(a, zs).wait_send()
                for ys in range(depth_y):
                    for side in range(2 if a in shared else 1):
                        core(a, zs, ys, side).wait_send()
                    if a in shared:
                        @pl.when((zs != z) | (ys != y))
                        def _():
                            plane(a, zs, ys).wait_send()

        def token_copy(s):
            return pltpu.make_async_remote_copy(
                src_ref=tokens_ref.at[(1 - k) * count + s],
                dst_ref=x_all.at[s, mine],
                send_sem=t_send.at[s],
                recv_sem=t_recv.at[s],
                device_id=(b, 1 - k),
                device_id_type=pl.DeviceIdType.MESH,
            )

        def grad_copy(s):
            return pltpu.make_async_remote_copy(
                src_ref=cot_away.at[s],
                dst_ref=cot_all.at[s, mine],
                send_sem=g_send.at[s],
                recv_sem=g_recv.at[s],
                device_id=(b, 1 - k),
                device_id_type=pl.DeviceIdType.MESH,
            )

        def put(i, src, dst):
            return pltpu.make_async_copy(src, dst, out_sem.at[i])

        partners = 3 + (z < last).astype(jnp.int32) + (z > 0).astype(jnp.int32)
        pl.semaphore_wait(barrier, partners)
        for a in early:
            if a == W1:
                for i in range(3):
                    loads[i].wait()
            begin_z(a)
            begin_y(a)
            begin_core(a)
        token_copy(0).start()
        for i in (3, 4, 5):
            loads[i].wait()

        def begin_own(a):
            begin_y(a)
            begin_core(a)

        actions = {
            "hop": hop, "relay": relay, "swap": lambda a, step, far: swap(a, step, (1 - y) if far else y),
            "own": begin_own, "own_z": begin_z,
            "tokens": lambda s: token_copy(s).start(), "cotangent": lambda s: grad_copy(s).start(),
        }

        def at_slot(slot):
            for name, *what in GATHER_PLAN.get(slot, ()):
                actions[name](*what)

        def at_slots(first_slot, stride, index, bound):
            for value in range(bound):
                if first_slot + stride * value in GATHER_PLAN:
                    @pl.when(index == value)
                    def _():
                        at_slot(first_slot + stride * value)

        at_slot(0)

        for i in (6, 7):
            loads[i].wait()
        mask = mask_ref[...].astype(f32)
        own, away = jnp.where(k == 0, mask[:count], mask[count:]), jnp.where(k == 0, mask[count:], mask[:count])
        columns = jnp.concatenate([own, away], 0).T
        for s in range(count):
            cot_all[s, mine, :] = (cot_all[s, mine, :].astype(f32) * columns[:, s : s + 1]).astype(bf16)
            cot_away[s] = (cot_away[s].astype(f32) * columns[:, count + s : count + s + 1]).astype(bf16)

        loads[8].wait()
        for step in range(1, depth_z):
            for a in early:
                hop(a, step)
            at_slot(step)
            for a in early:
                relay(a, step - 1)
        for a in early:
            relay(a, last)
        at_slot(4)
        for a in early:
            complete(a)
        vec[...] = jnp.sum(tables[...].astype(f32), 0)
        save_w = put(0, w_qkv, w_qkv_out)
        save_w.start()

        def first(s, carry):
            arrived(x_all.at[s, theirs], t_recv.at[s])
            saves = [
                put(1, x_all.at[s], x_out.at[s]),
                put(2, t_1, q_out.at[s]),
                put(3, t_2, k_out.at[s]),
                put(4, t_3, v_out.at[s]),
                put(5, cb_all.at[s], cb_out.at[s]),
                put(6, l_s, l_out.at[s]),
            ]

            @pl.when(s > 0)
            def _():
                for save in saves[:4]:
                    save.wait()

            project(x_all[s], w_qkv, vec, t_1, t_2, t_3)
            for save in saves[:4]:
                save.start()
            at_slots(5, 3, s, count)
            stat[...] = jnp.zeros_like(stat)
            attend_pairs(t_1, t_2, t_3, cb_all.at[s], stat, 0, HEADS // 4)
            at_slots(6, 3, s, count)
            attend_pairs(t_1, t_2, t_3, cb_all.at[s], stat, HEADS // 4, HEADS // 2)

            @pl.when(s > 0)
            def _():
                for save in saves[4:]:
                    save.wait()

            l_s[...] = stat[...].T[:STAT_ROWS]
            for save in saves[4:]:
                save.start()
            at_slots(7, 3, s, count)
            return carry

        lax.fori_loop(0, count, first, 0)
        at_slot(17)
        for a in (M1, M2):
            complete(a)
        for i, (src, dst) in enumerate(((x_all.at[0], x_out.at[0]), (t_1, q_out.at[0]), (t_2, k_out.at[0]), (t_3, v_out.at[0]), (cb_all.at[0], cb_out.at[0]), (l_s, l_out.at[0]))):
            put(i + 1, src, dst).wait()
        save_w.wait()
        sums_out[...] = jnp.zeros_like(sums_out)
        w_o, w_i = w_mid.at[:, 0:width], w_mid.at[:, width:mid_width]
        O, GF, GA, GC, DELTA, H, GU, H_IN, GU_IN, MID = 8, 9, 10, 11, 12, 13, 15, 17, 19, 21

        lane = lax.broadcasted_iota(jnp.int32, inv.shape, 1)
        inv[...] = jnp.zeros_like(inv)

        def second(s, carry):
            slot = s % 2

            mid_s = t_mid.at[slot]

            @pl.when(s >= 2)
            def _():
                put(MID + slot, mid_s, mid_out.at[s]).wait()
                put(H + slot, h_s.at[slot], h_out.at[s]).wait()
                put(GU + slot, gu_s.at[slot], gu_out.at[s]).wait()

            normed, inverse = to_hidden(x_all[s], cb_all[s], w_o, w_i, vec, mid_s, h_s.at[slot], gu_s.at[slot])
            normed_all[s] = normed
            inv[...] = jnp.where(lane == s, inverse, inv[...])
            put(MID + slot, mid_s, mid_out.at[s]).start()
            put(H + slot, h_s.at[slot], h_out.at[s]).start()

            @pl.when(s < 2)
            def _():
                put(GU + slot, gu_s.at[slot], gu_out.at[s]).start()

            at_slots(18, 1, s, count)
            return carry

        lax.fori_loop(0, count, second, 0)
        for slot in range(2):
            put(MID + slot, t_mid.at[slot], mid_out.at[0]).wait()
        complete(UP)

        def third(i, carry):
            s = (i + count // 2) % count
            slot = i % 2
            at_slots(22, 1, i, count)
            arrived(cot_all.at[s, theirs], g_recv.at[s])
            saves = [
                put(O, t_1, o_out.at[s]),
                put(GF, t_3, gf_out.at[s]),
                put(GA, t_4, ga_out.at[s]),
                put(GC, t_5, gc_out.at[s]),
                put(DELTA, d_s, d_out.at[s]),
            ]

            @pl.when(i >= 2)
            def _():
                put(H_IN + slot, h_out.at[s], h_s.at[slot]).wait()
                put(GU_IN + slot, gu_out.at[s], gu_s.at[slot]).wait()

            @pl.when(i > 0)
            def _():
                for save in saves[:2]:
                    save.wait()

            grad_2 = to_output(normed_all[s], cot_all[s], w_up, vec, h_s.at[slot], t_1, t_3, sums_out)
            for save in saves[:2]:
                save.start()

            @pl.when(i > 0)
            def _():
                for save in saves[2:]:
                    save.wait()

            @pl.when((i > 0) & (i + 1 < count))
            def _():
                put(GU + 1 - slot, gu_s.at[1 - slot], gu_out.at[s]).wait()
                put(GU_IN + 1 - slot, gu_out.at[(s + 1) % count], gu_s.at[1 - slot]).start()

            inverse = jnp.sum(jnp.where(lane == s, inv[...], 0.0), 1, keepdims=True)
            to_context_grad(
                grad_2, normed_all[s], inverse, cb_all[s], w_o, w_i, w_up, vec, t_3, t_4, t_5, d_s, gu_s.at[slot], sums_out
            )
            for save in saves[2:]:
                save.start()
            put(GU + slot, gu_s.at[slot], gu_out.at[s]).start()

            @pl.when(i + 2 < count)
            def _():
                put(H + slot, h_s.at[slot], h_out.at[s]).wait()
                put(H_IN + slot, h_out.at[(s + 2) % count], h_s.at[slot]).start()

            return carry

        lax.fori_loop(0, count, third, 0)
        for i, src, dst in ((O, t_1, o_out), (GF, t_3, gf_out), (GA, t_4, ga_out), (GC, t_5, gc_out), (DELTA, d_s, d_out)):
            put(i, src, dst.at[0]).wait()
        for slot in range(2):
            put(GU + slot, gu_s.at[slot], gu_out.at[0]).wait()
        for s in range(count):
            token_copy(s).wait_send()
            grad_copy(s).wait_send()
        for a in range(ARRAYS):
            sent(a)

    seq = jax.ShapeDtypeStruct((count, length, width), bf16)
    seq_wide = jax.ShapeDtypeStruct((count, length, inner), bf16)
    stat_shape = jax.ShapeDtypeStruct((count, STAT_ROWS, length), f32)
    hbm = pl.BlockSpec(memory_space=pl.ANY)
    one = pltpu.VMEM((length, width), bf16)
    two_wide = pltpu.VMEM((2, length, inner), bf16)
    all_seq = pltpu.VMEM((count, length, width), bf16)
    stat_one = pltpu.VMEM((STAT_ROWS, length), f32)
    lanes = pltpu.VMEM((length, 128), f32)
    dma = pltpu.SemaphoreType.DMA
    return pl.pallas_call(
        kernel,
        in_specs=[hbm, whole_vmem()] + [hbm] * 7 + [whole_vmem()],
        out_specs=[hbm] * 14 + [whole_vmem(), hbm],
        out_shape=[seq] * 5 + [stat_shape] + [seq] * 5 + [stat_shape, seq_wide, seq_wide]
        + [jax.ShapeDtypeStruct((16, width), f32), jax.ShapeDtypeStruct((width, qkv_width), bf16)],
        scratch_shapes=[
            pltpu.VMEM((width, qkv_width), bf16),
            pltpu.VMEM((width, mid_width), bf16),
            pltpu.VMEM((inner, width), bf16),
            pltpu.VMEM((devices, 16, width), bf16),
            pltpu.VMEM((16, width), f32),
            all_seq, all_seq,
            pltpu.VMEM((count, stretch, width), bf16),
            all_seq,
            pltpu.VMEM((2, length, width), bf16), one, one, one, stat_one, lanes, lanes, stat_one,
            pltpu.VMEM((count, length, width), f32),
            two_wide, two_wide,
            dma((ARRAYS, depth_z)), dma((ARRAYS, depth_z)), dma((ARRAYS, depth_z)),
            dma((ARRAYS, depth_z)), dma((ARRAYS, depth_z)),
            dma((ARRAYS, 2 * places)), dma((ARRAYS, 2 * places)), dma((ARRAYS, places)), dma((ARRAYS, places)),
            dma((count,)), dma((count,)), dma((count,)), dma((count,)), dma((9,)), dma((23,)),
        ],
        compiler_params=pltpu.CompilerParams(collective_id=1, has_side_effects=True, vmem_limit_bytes=63 * 2**20),
        name="forward",
    )(tokens, span_mask, cotangent, w_query, w_key, w_value, w_out, w_inner, w_outer, table)


SCATTER_PLAN = {
    2: (("out", 2), (1, "s", 0),),
    3: ((1, "s", 1),),
    4: (("out", 1), ("out", 3),),
    6: ((1, "s", 3), (2, "s", 0), ("out", 0),),
    7: ((1, "s", 2),),
    8: ((2, "s", 1),),
    9: ((1, "o", 0), (2, "s", 3),),
    10: ((1, "s", 4),),
    11: ((2, "s", 2),),
    14: ((2, "o", 0), (1, "o", 1),),
    16: ((3, "s", 0),),
    17: ((2, "s", 4),),
    18: ((1, "o", 2), (3, "o", 0),),
    19: ((2, "o", 1),),
    21: ((3, "s", 1),),
    22: ((2, "o", 2),),
    23: ((1, "p", 0), (1, "p", 1),),
    25: ((1, "p", 3), (3, "s", 4), (2, "p", 0), (3, "o", 1),),
    26: ((2, "p", 1), (1, "p", 2), (3, "o", 2),),
    27: ((2, "p", 3), (1, "p", 5), (4, "s", 4),),
    28: (
        (3, "p", 0),
        (4, "s", 0),
        (1, "p", 4),
        (3, "s", 3),
        (2, "p", 2),
        (4, "o", 2),
        (2, "p", 5),
        (4, "o", 0),
        (3, "p", 3),
        (3, "s", 2),
        (4, "o", 1),
        (4, "s", 1),
        (2, "p", 4),
        (4, "p", 0),
        (3, "p", 2),
        (3, "p", 1),
        (3, "p", 5),
        (3, "p", 4),
        (4, "s", 2),
        (4, "p", 5),
        (4, "p", 2),
        (4, "p", 1),
        (4, "s", 3),
        (4, "p", 3),
        (4, "p", 4),
    ),
}


def backward_call(x, q, k, v, cb, mid, gf, ga, gc, hidden, gu, out, stat_l, stat_d, w_qkv, sums, sizes):
    depth_z, depth_y, cores = sizes
    count, length, width = x.shape
    inner = hidden.shape[2]
    devices = depth_z * depth_y * cores
    part, outer_part = width // devices, inner // devices
    stretch, rows = length // 2, 2 * count
    chunks = inner // width
    GROUPS = 3
    pairs = HEADS // 2 // GROUPS
    column = pairs * PAIR
    narrow = width // GROUPS
    OUT = chunks
    QKV = chunks + 1
    SQUARES, PARTS = QKV, 2 * GROUPS
    first_of = {"s": 0, "o": SQUARES, "p": SQUARES + GROUPS}
    every = SQUARES + GROUPS + PARTS
    half = width // 2
    SLOTS = 2
    STEPS = 5
    tokens_all = count * length

    def kernel(
        x_in, q_in, k_in, v_in, cb_in, mid_in, gf_in, ga_in, gc_in, h_in, gu_in, out_in, w_in, l_ref, d_ref, sums_ref,
        received, grad_tokens, g_query, g_key, g_value, g_out, g_inner, g_outer, vectors,
        big, pool, w_cat, ga_s, gx_s, kt, gqt, own_s, own_o, r1, r2, r3, s4, r4, r1o, r2o, r3o, s4o, r4o, r1p, r2p, r3p, s4p, r4p, v_own, v_got,
        s1_send, s1_recv, s2_send, s2_recv, s3_send, s3_recv, s4_send, s4_recv,
        v_send, v_recv, o_send, o_recv, g_send, g_recv, big_sem, pool_sem, w_sem, ga_sem, keep_sem,
    ):
        b, k = lax.axis_index("batch"), lax.axis_index("blk")
        z, y, c = b // (depth_y * cores), (b // cores) % depth_y, b % cores

        def at(z_, y_, c_):
            return (z_ * depth_y + y_) * cores + c_

        beside = (b, 1 - k)
        other_core = (at(z, y, 1 - c), k)
        other_y = (at(z, 1 - y, c), k)

        def level(j):
            return (z + j) % depth_z

        barrier = pltpu.get_barrier_semaphore()
        partners = [beside, other_core, other_y] + [(at(level(j), y, c), k) for j in range(1, depth_z)]
        for device in partners:
            pl.semaphore_signal(barrier, inc=1, device_id=device, device_id_type=pl.DeviceIdType.MESH)

        def remote(src, dst, device, send, recv):
            return pltpu.make_async_remote_copy(
                src_ref=src, dst_ref=dst, send_sem=send, recv_sem=recv, device_id=device, device_id_type=pl.DeviceIdType.MESH
            )

        def load(i, src):
            return pltpu.make_async_copy(src, big.at[i], big_sem.at[i])

        def wide_load(i, src, j):
            return pltpu.make_async_copy(src.at[:, :, j * width : (j + 1) * width], big.at[i], big_sem.at[i])

        def pool_load(s, slot):
            return [
                pltpu.make_async_copy(src.at[s], pool.at[slot, i], pool_sem.at[slot, i])
                for i, src in enumerate((q_in, k_in, v_in, gc_in))
            ]

        def w_load(i, g):
            return pltpu.make_async_copy(
                w_in.at[:, i * width + g * column : i * width + (g + 1) * column],
                w_cat.at[g, :, i * column : (i + 1) * column],
                w_sem.at[i, g],
            )

        first_loads = [load(0, mid_in), wide_load(2, gu_in, 0), load(1, gf_in), wide_load(3, gu_in, 1)]
        for copy in first_loads:
            copy.start()
        mine = pl.ds(pl.multiple_of(k * stretch, stretch), stretch)
        theirs = pl.ds(pl.multiple_of((1 - k) * stretch, stretch), stretch)

        sums_of = {"s": (r1, r2, r3, s4, r4), "o": (r1o, r2o, r3o, s4o, r4o), "p": (r1p, r2p, r3p, s4p, r4p)}

        def buffers(kind, g):
            return [ref.at[g] for ref in sums_of[kind]] + [first_of[kind] + g]

        def own_part(kind, g, half_of, z_, y_, c_):
            if kind == "o":
                return own_o.at[g, z_, y_, c_]
            if kind == "s":
                return own_s.at[g % SLOTS, z_, y_, c_]
            return own_s.at[(QKV + g) % SLOTS, z_, y_, c_, :, half_of * half : (half_of + 1) * half]

        def step_1(kind, g, half_of=0):
            a1, _, _, _, _, i = buffers(kind, 2 * g + half_of if kind == "p" else g)
            own = own_part(kind, g, half_of, slice(None), slice(None), 1 - c)
            return remote(own, a1, other_core, s1_send.at[i], s1_recv.at[i])

        def step_2(kind, g):
            a1, a2, _, _, _, i = buffers(kind, g)
            return remote(a1.at[:, 1 - y], a2, other_y, s2_send.at[i], s2_recv.at[i])

        def step_3(kind, g, j):
            _, a2, a3, _, _, i = buffers(kind, g)
            return remote(
                a2.at[level(j)], a3.at[j - 1], (at(level(j), y, c), k), s3_send.at[i, j - 1], s3_recv.at[i, j - 1]
            )

        def step_4(kind, g):
            _, _, _, a4, b4, i = buffers(kind, g)
            return remote(a4, b4, beside, s4_send.at[i], s4_recv.at[i])

        def move_1(kind, g):
            a1, _, _, _, _, _ = buffers(kind, g)
            source = (g // 2, g % 2) if kind == "p" else (g, 0)
            step_1(kind, *source).wait()

            def add(i, carry):
                zi, yi = i // depth_y, i % depth_y
                a1[zi, yi] = a1[zi, yi] + own_part(kind, *source, zi, yi, c)[...]
                return carry

            lax.fori_loop(0, depth_z * depth_y, add, 0, unroll=True)
            step_2(kind, g).start()

        def move_2(kind, g):
            a1, a2, _, _, _, _ = buffers(kind, g)
            step_2(kind, g).wait()

            def add(zi, carry):
                a2[zi] = a2[zi] + a1[zi, y]
                return carry

            lax.fori_loop(0, depth_z, add, 0, unroll=True)
            for j in range(1, depth_z):
                step_3(kind, g, j).start()

        def move_3(kind, g):
            _, a2, a3, a4, _, _ = buffers(kind, g)
            for j in range(1, depth_z):
                step_3(kind, g, j).wait()
            total = a2[z].astype(f32)
            for j in range(1, depth_z):
                total = total + a3[j - 1].astype(f32)
            a4[...] = total.astype(bf16)
            step_4(kind, g).start()

        def move_4(kind, g):
            _, _, _, a4, b4, _ = buffers(kind, g)
            step_4(kind, g).wait()
            total = a4[...].astype(f32) + b4[...].astype(f32)
            if kind == "o":
                g_outer[:, g * narrow : (g + 1) * narrow] = total
            elif kind == "s" and g < OUT:
                g_inner[:, g * width : (g + 1) * width] = total
            elif kind == "s":
                g_out[...] = total
            else:
                group, begins = g // 2, (g % 2) * half
                for i, ref in enumerate((g_query, g_key, g_value)):
                    low, high = max(i * column, begins), min((i + 1) * column, begins + half)
                    if low < high:
                        to = group * column - i * column
                        ref[:, to + low : to + high] = total[:, low - begins : high - begins]

        def exchange(s):
            return remote(out_in.at[s, theirs], received.at[s], beside, o_send.at[s], o_recv.at[s])

        moves = {1: move_1, 2: move_2, 3: move_3, 4: move_4}

        def take(steps):
            for name, *what in steps:
                if name == "out":
                    exchange(*what).start()
                else:
                    moves[name](*what)

        def at_slot(slot):
            take(SCATTER_PLAN.get(slot, ()))

        def at_slots(first_slot, stride, index, bound):
            for value in range(bound):
                if first_slot + stride * value in SCATTER_PLAN:
                    @pl.when(index == value)
                    def _():
                        at_slot(first_slot + stride * value)

        def whole(i):
            return big[i].reshape(tokens_all, width)

        def keep(g, value):
            own_s[g % SLOTS] = value.astype(bf16).reshape(depth_z, depth_y, cores, part, width)

        pl.semaphore_wait(barrier, len(partners))

        first_loads[0].wait()
        for j in range(chunks):
            wide_load(2 + j % 2, gu_in, j).wait()
            at_slot(j)
            keep(j, mul(whole(0), whole(2 + j % 2), TN))
            step_1("s", j).start()
            following = j + 2 - chunks
            if following < 0:
                wide_load(2 + j % 2, gu_in, j + 2).start()
            else:
                wide_load(2 + j % 2, h_in, following).start()
            if j == 0:
                for s in range(2):
                    for copy in pool_load(s, s):
                        copy.start()
            if j == 1:
                for g in range(GROUPS):
                    for i in range(3):
                        w_load(i, g).start()
        load(0, ga_in).start()
        first_loads[2].wait()
        for j in range(chunks):
            wide_load(2 + j % 2, h_in, j).wait()
            at_slot(chunks + j)
            product = mul(whole(2 + j % 2), whole(1), TN).astype(bf16)
            for g in range(GROUPS):
                own_o[g, j] = product[:, g * narrow : (g + 1) * narrow].reshape(depth_y, cores, outer_part, narrow)
            if j + 2 < chunks:
                wide_load(2 + j % 2, h_in, j + 2).start()
            elif j + 2 == chunks:
                load(2 + j % 2, cb_in).start()
            else:
                load(2 + j % 2, x_in).start()
        for g in range(GROUPS):
            step_1("o", g).start()
        at_slot(2 * chunks)
        load(0, ga_in).wait()
        load(2 + chunks % 2, cb_in).wait()
        keep(OUT, mul(whole(2 + chunks % 2), whole(0), TN))
        step_1("s", OUT).start()
        for copy in pool_load(2, 2):
            copy.start()
        for g in range(GROUPS):
            for i in range(3):
                w_load(i, g).wait()
        load(2 + (chunks + 1) % 2, x_in).wait()
        x_at = 2 + (chunks + 1) % 2
        v_own[0] = sums_ref[...]

        cells = GROUPS * count
        def gx_copies(s):
            away = remote(gx_s.at[theirs], grad_tokens.at[k * count + s], beside, g_send.at[s], g_recv.at[s])
            stay = pltpu.make_async_copy(gx_s.at[mine], grad_tokens.at[k * count + s], keep_sem.at[1])
            return away, stay

        ga_load = [pltpu.make_async_copy(ga_in.at[s], ga_s, ga_sem.at[0]) for s in range(count)]
        ga_load[0].start()

        def cell(i, carry):
            s, g = i // GROUPS, i % GROUPS
            slot = s % 3

            @pl.when(g == 0)
            def _():
                for copy in pool_load(s, slot):
                    copy.wait()

            attend_back(
                pool.at[slot, 0], pool.at[slot, 1], pool.at[slot, 2], pool.at[slot, 3], l_ref.at[s], d_ref.at[s],
                big.at[g, s], kt, gqt, g * pairs, pairs,
            )
            span = pl.ds(pl.multiple_of(g * column, column), column)
            v_own[0, B_QUERY : B_QUERY + 1, span] += column_sum(big[g, s, :, :column])
            v_own[0, B_VALUE : B_VALUE + 1, span] += column_sum(big[g, s, :, 2 * column :])

            @pl.when(i == GROUPS - 1)
            def _():
                for copy in pool_load(3, 0):
                    copy.start()

            base = 2 * chunks + 1
            last_base = base + (GROUPS + 1) * (count - 1)
            for group in range(GROUPS):
                @pl.when(g == group)
                def _():
                    at_slots(base + group, GROUPS + 1, s, count - 1)

            @pl.when(s == count - 1)
            def _():
                at_slots(last_base, 2, g, GROUPS)
                keep(QKV + g, mul(whole(x_at), big[g].reshape(tokens_all, width), TN))
                step_1("p", g, 0).start()
                step_1("p", g, 1).start()
                at_slots(last_base + 1, 2, g, GROUPS)

            @pl.when(g == GROUPS - 1)
            def _():
                ga_load[0].wait()

                @pl.when(s > 0)
                def _():
                    away, stay = gx_copies(s - 1)
                    away.wait_send()
                    stay.wait()

                grad = ga_s[...].astype(f32)
                for group in range(GROUPS):
                    grad = grad + mul(big[group, s], w_cat[group], NT)
                gx_s[...] = grad.astype(bf16)
                away, stay = gx_copies(s)
                away.start()
                stay.start()

                @pl.when(s < count - 1)
                def _():
                    pltpu.make_async_copy(ga_in.at[s + 1], ga_s, ga_sem.at[0]).start()

                at_slots(base + GROUPS, GROUPS + 1, s, count - 1)

                @pl.when(s == count - 1)
                def _():
                    at_slot(last_base + 2 * GROUPS)

            return carry

        lax.fori_loop(0, cells, cell, 0)

        towards = [other_core, other_y, (at(z + 1 - 2 * (z % 2), y, c), k), (at((z + 2) % 4, y, c), k), beside]

        def v_copy(i):
            return remote(v_own.at[i], v_got.at[i], towards[i], v_send.at[i], v_recv.at[i])

        def v_move(i):
            v_copy(i).wait()
            v_own[i + 1] = v_own[i] + v_got[i]
            if i + 1 < STEPS:
                v_copy(i + 1).start()

        v_copy(0).start()
        rest = SCATTER_PLAN[2 * chunks + 1 + (GROUPS + 1) * (count - 1) + 2 * GROUPS + 1]
        for i in range(STEPS):
            take(rest[2 * i : 2 * i + 2])
            v_move(i)
        total = v_own[STEPS]
        inner_row = v_own[STEPS, pl.ds(B_INNER + b // (devices // chunks), 1), :]
        rolled = pltpu.roll(total, (width - b * part) % width, 1)
        wide = pltpu.roll(inner_row, (width - (b % (devices // chunks)) * outer_part) % width, 1)
        line = lax.broadcasted_iota(jnp.int32, total.shape, 0)
        vectors[...] = jnp.where(line == B_INNER, wide, rolled)
        take(rest[2 * STEPS :])
        away, stay = gx_copies(count - 1)
        away.wait_send()
        stay.wait()
        for s in range(count):
            exchange(s).wait_send()
            exchange(s).wait_recv()
            remote(gx_s.at[theirs], grad_tokens.at[(1 - k) * count + s], beside, g_send.at[s], g_recv.at[s]).wait_recv()

    hbm = pl.BlockSpec(memory_space=pl.ANY)
    dma = pltpu.SemaphoreType.DMA

    def vmem(*shape):
        return pltpu.VMEM(shape, bf16)

    def result(*shape):
        return jax.ShapeDtypeStruct(shape, f32)

    back = jax.ShapeDtypeStruct((rows, stretch, width), bf16)
    from_beside = jax.ShapeDtypeStruct((count, stretch, width), bf16)
    return pl.pallas_call(
        kernel,
        in_specs=[hbm] * 13 + [whole_vmem()] * 3,
        out_specs=[hbm] * 2 + [whole_vmem()] * 7,
        out_shape=[
            from_beside, back, result(part, width), result(part, width), result(part, width), result(part, width),
            result(part, inner), result(outer_part, width), result(16, width),
        ],
        scratch_shapes=[
            vmem(4, count, length, width),
            vmem(3, 4, length, width),
            vmem(GROUPS, width, 3 * column),
            vmem(length, width), vmem(length, width),
            vmem(column, length), vmem(column, length),
            vmem(SLOTS, depth_z, depth_y, cores, part, width),
            vmem(GROUPS, depth_z, depth_y, cores, outer_part, narrow),
            vmem(SQUARES, depth_z, depth_y, part, width), vmem(SQUARES, depth_z, part, width),
            vmem(SQUARES, depth_z - 1, part, width), vmem(SQUARES, part, width), vmem(SQUARES, part, width),
            vmem(GROUPS, depth_z, depth_y, outer_part, narrow), vmem(GROUPS, depth_z, outer_part, narrow),
            vmem(GROUPS, depth_z - 1, outer_part, narrow), vmem(GROUPS, outer_part, narrow), vmem(GROUPS, outer_part, narrow),
            vmem(PARTS, depth_z, depth_y, part, half), vmem(PARTS, depth_z, part, half),
            vmem(PARTS, depth_z - 1, part, half), vmem(PARTS, part, half), vmem(PARTS, part, half),
            pltpu.VMEM((STEPS + 1, 16, width), f32), pltpu.VMEM((STEPS, 16, width), f32),
            dma((every,)), dma((every,)), dma((every,)), dma((every,)),
            dma((every, depth_z - 1)), dma((every, depth_z - 1)), dma((every,)), dma((every,)),
            dma((STEPS,)), dma((STEPS,)), dma((count,)), dma((count,)), dma((count,)), dma((count,)),
            dma((4,)), dma((3, 4)), dma((3, GROUPS)), dma((1,)), dma((2,)),
        ],
        compiler_params=pltpu.CompilerParams(collective_id=2, has_side_effects=True, vmem_limit_bytes=63 * 2**20),
        name="backward",
    )(x, q, k, v, cb, mid, gf, ga, gc, hidden, gu, out, w_qkv, stat_l, stat_d, sums)


def settle_call(side, out, received, grad_tokens, grads, totals, sizes):
    rows, stretch, width = grad_tokens.shape
    count = rows // 2
    n = len(grads)

    def kernel(side_ref, out_ref, received_ref, tokens_ref, *refs):
        sources, totals_ref, (output_ref, grad_ref) = refs[:n], refs[n], refs[n + 1 : n + 3]
        results, vectors = refs[n + 3 : 2 * n + 3], refs[2 * n + 3 :]
        step = pl.program_id(0)
        here = step // count == side_ref[0]

        @pl.when(here)
        def _():
            output_ref[...] = out_ref[...]

        @pl.when(jnp.logical_not(here))
        def _():
            output_ref[...] = received_ref[...]

        grad_ref[...] = tokens_ref[...]

        @pl.when(step == 0)
        def _():
            for source, result in zip(sources, results):
                result[...] = source[...]
            for i, vector in enumerate(vectors):
                vector[...] = totals_ref[i : i + 1, : sizes[i]]

    block = (None, stretch, width)
    straight = pl.BlockSpec(block, lambda i, side: (i, 0, 0))

    def fixed(shape):
        return pl.BlockSpec(shape, lambda i, side: (0, 0))

    shapes = [grad.shape for grad in grads] + [(1, size) for size in sizes]
    return pl.pallas_call(
        kernel,
        grid_spec=pltpu.PrefetchScalarGridSpec(
            num_scalar_prefetch=1,
            grid=(rows,),
            in_specs=[
                pl.BlockSpec(block, lambda i, side: (jnp.clip(i - side[0] * count, 0, count - 1), side[0], 0)),
                pl.BlockSpec(block, lambda i, side: (jnp.clip(i - (1 - side[0]) * count, 0, count - 1), 0, 0)),
                straight,
            ]
            + [fixed(grad.shape) for grad in grads]
            + [fixed(totals.shape)],
            out_specs=[straight] * 2 + [fixed(shape) for shape in shapes],
        ),
        out_shape=[jax.ShapeDtypeStruct(grad_tokens.shape, bf16)] * 2
        + [jax.ShapeDtypeStruct(shape, f32) for shape in shapes],
        compiler_params=params(),
        name="settle",
    )(side, out, received, grad_tokens, *grads, totals)


def pack_shard(w_query, w_key, w_value, w_out, w_inner, w_outer, vectors):
    width = w_query.shape[1]
    inner_parts = [w_inner[:, i : i + width] for i in range(0, w_inner.shape[1], width)]
    small = jnp.concatenate(vectors)
    body_rows = sum(part.shape[0] for part in (w_query, w_key, w_value, w_out, w_outer, *inner_parts))
    rows = -(-(body_rows + 1) // 16) * 16
    tail = jnp.zeros(((rows - body_rows) * width,), small.dtype).at[: small.shape[0]].set(small)
    return jnp.concatenate(
        [w_query, w_key, w_value, w_out, *inner_parts, w_outer, tail.reshape(-1, width)]
    )


def vec_table(small, vec_names_sizes):
    rows, at = [], 0
    for size in vec_names_sizes:
        rows.append(small[:, at : at + size].reshape(-1))
        at += size
    return rows


def gather_weights(w_query, w_key, w_value, w_out, w_inner, w_outer, vectors):
    part, width = w_query.shape
    outer_part = w_outer.shape[0]
    chunks = w_inner.shape[1] // width
    sizes = [vector.shape[0] for vector in vectors]
    packed = pack_shard(w_query, w_key, w_value, w_out, w_inner, w_outer, vectors)
    gathered = lax.all_gather(packed, "batch", axis=0)

    def weight(at, count):
        return gathered[:, at : at + count].reshape(-1, width)

    squares = [weight(i * part, part) for i in range(4 + chunks)]
    outer_at = (4 + chunks) * part
    w_outer_all = weight(outer_at, outer_part)
    small = gathered[:, outer_at + outer_part :].reshape(gathered.shape[0], -1)
    vec = jnp.concatenate(vec_table(small, sizes)).reshape(-1, width).astype(f32)
    vec = jnp.concatenate([vec, jnp.zeros((16 - vec.shape[0], width), f32)])
    return jnp.concatenate(squares[:3], 1), squares[3], jnp.concatenate(squares[4:], 1), w_outer_all, vec


def body(
    tokens,
    span_mask,
    cotangent,
    w_query,
    b_query,
    w_key,
    w_value,
    b_value,
    w_out,
    b_out,
    gain_first,
    bias_first,
    w_inner,
    b_inner,
    w_outer,
    b_outer,
    gain_second,
    bias_second,
):
    rows, stretch, width = tokens.shape
    inner = w_inner.shape[1]
    part = w_query.shape[0]
    outer_part = w_outer.shape[0]
    vectors = (b_query, b_value, b_out, gain_first, bias_first, b_outer, gain_second, bias_second, b_inner)
    sizes = [vector.shape[0] for vector in vectors]

    devices = lax.axis_size("batch")
    chunks = inner // width
    swap = functools.partial(lax.all_to_all, axis_name="blk", tiled=True)
    outer_at = (4 + chunks) * part
    shard_rows = -(-(outer_at + outer_part + 1) // 16) * 16
    if (devices, lax.axis_size("blk")) == (16, 2):
        table = sum(
            lax.pad(
                vector.astype(f32).reshape(1, -1), f32(0), ((i, 15 - i, 0), (0, width - vector.shape[0], 0))
            )
            for i, vector in enumerate(vectors)
        )
        x, q, k, v, cb, stat_l, out, mid, gf, ga, gc, stat_d, hidden, gu, sums_ffn, w_qkv = forward_call(
            tokens, span_mask, cotangent, w_query, w_key, w_value, w_out, w_inner, w_outer, table, (4, 2, 2)
        )
        results = backward_call(
            x, q, k, v, cb, mid, gf, ga, gc, hidden, gu, out, stat_l, stat_d, w_qkv, sums_ffn, (4, 2, 2)
        )
        side = lax.axis_index("blk").astype(jnp.int32).reshape(1)
        settled = settle_call(side, out, results[0], results[1], results[2:-1], results[-1], sizes)
        output, grad_tokens, g_query, g_key, g_value, g_out, g_inner, g_outer = settled[:8]
        small = [vector.reshape(-1) for vector in settled[8:]]
        return (
            output, grad_tokens, g_query, small[0], g_key, g_value, small[1], g_out, small[2], small[3], small[4], g_inner,
            small[8], g_outer, small[5], small[6], small[7],
        )
    w_qkv, w_out_all, w_inner_all, w_outer_all, vec = gather_weights(
        w_query, w_key, w_value, w_out, w_inner, w_outer, vectors
    )
    masked = cotangent * span_mask[..., None].astype(bf16)
    x = swap(tokens, split_axis=0, concat_axis=1)
    cot = swap(masked, split_axis=0, concat_axis=1)
    q, k, v, cb, stat_l = attention_call(x, w_qkv, vec)
    out, mid, gf, ga, gc, stat_d, hidden, gu, sums_ffn = feed_forward_call(
        x, cb, cot, w_out_all, w_inner_all, w_outer_all, vec
    )
    gx, gw_qkv, sums_att = attention_back_call(x, q, k, v, gc, ga, stat_l, stat_d, w_qkv)
    output = swap(out, split_axis=1, concat_axis=0)
    grad_tokens = swap(gx, split_axis=1, concat_axis=0)

    def flat(values):
        return values.reshape(-1, values.shape[-1])

    gw_out = weight_grad_call(flat(cb), flat(ga), False)
    gw_inner = weight_grad_call(flat(mid), flat(gu), False)
    gw_outer = weight_grad_call(flat(hidden), flat(gf), True)

    sums = sums_ffn + sums_att
    small_sums = [sums[i].reshape(devices, -1) for i in range(B_INNER)]
    small_sums.append(sums[B_INNER : B_INNER + chunks].reshape(devices, -1))
    tail = jnp.concatenate(small_sums, 1).astype(bf16)
    tail = jnp.pad(tail, ((0, 0), (0, (shard_rows - outer_at - outer_part) * width - tail.shape[1])))
    pieces = [gw_qkv[:, i * width : (i + 1) * width].reshape(devices, part, width) for i in range(3)]
    pieces.append(gw_out.reshape(devices, part, width))
    pieces += [gw_inner[:, i * width : (i + 1) * width].reshape(devices, part, width) for i in range(chunks)]
    pieces.append(gw_outer.reshape(devices, outer_part, width))
    pieces.append(tail.reshape(devices, -1, width))
    grads = jnp.concatenate(pieces, 1)
    share = lax.psum_scatter(grads, "batch", scatter_dimension=0, tiled=False)
    share = lax.psum(share, "blk").astype(f32)
    square = [share[i * part : (i + 1) * part] for i in range(4 + chunks)]
    share_small = share[outer_at + outer_part :].reshape(-1)
    small_out, at = [], 0
    for size in sizes:
        small_out.append(share_small[at : at + size])
        at += size
    (g_b_query, g_b_value, g_b_out, g_gain_1, g_bias_1, g_b_outer, g_gain_2, g_bias_2, g_b_inner) = small_out
    return (
        output,
        grad_tokens,
        square[0],
        g_b_query,
        square[1],
        square[2],
        g_b_value,
        square[3],
        g_b_out,
        g_gain_1,
        g_bias_1,
        jnp.concatenate(square[4:], 1),
        g_b_inner,
        share[outer_at : outer_at + outer_part],
        g_b_outer,
        g_gain_2,
        g_bias_2,
    )


def solution(mesh):
    block = P("batch", "blk", None)
    matrix, vector = P("batch", None), P("batch")
    weights = (
        matrix, vector, matrix, matrix, vector, matrix, vector, vector, vector, matrix, vector, matrix, vector, vector, vector,
    )
    return jax.shard_map(
        body,
        mesh=mesh,
        in_specs=(block, P("batch", "blk"), block) + weights,
        out_specs=(block, block) + weights,
        check_vma=False,
    )
```

```python
import functools

import jax
import jax.numpy as jnp
from jax import lax
from jax.experimental import pallas as pl
from jax.experimental.pallas import tpu as pltpu
from jax.sharding import PartitionSpec as P

HEADS = 12
HEAD_DIM = 64
PAIR = 2 * HEAD_DIM
STAT_ROWS = 16
VMEM_BYTES = 60 * 2**20

epsilon = 1e-06
bf16 = jnp.bfloat16
f32 = jnp.float32

NN = (((1,), (0,)), ((), ()))
NT = (((1,), (1,)), ((), ()))
TN = (((0,), (0,)), ((), ()))

B_QUERY, B_VALUE, B_OUT, GAIN_1, BIAS_1, B_OUTER, GAIN_2, BIAS_2, B_INNER = range(9)


def mul(left, right, dims=NN):
    return lax.dot_general(left, right, dims, preferred_element_type=f32)


def row(ref, index):
    return ref[index : index + 1, :]


def halves(block):
    lane = lax.broadcasted_iota(jnp.int32, block.shape, 1)
    zero = jnp.zeros_like(block)
    return jnp.where(lane < HEAD_DIM, block, zero), jnp.where(lane < HEAD_DIM, zero, block)


def pair_at(p):
    return pl.ds(pl.multiple_of(p * PAIR, PAIR), PAIR)


def normalize(values):
    center = values - jnp.mean(values, -1, keepdims=True)
    inverse = lax.rsqrt(jnp.mean(center * center, -1, keepdims=True) + epsilon)
    return center * inverse, inverse


def norm_back(grad, normed, inverse, gain):
    scaled = grad * gain
    return inverse * (
        scaled
        - jnp.mean(scaled, -1, keepdims=True)
        - normed * jnp.mean(scaled * normed, -1, keepdims=True)
    )


def column_sum(values):
    return jnp.sum(values.astype(f32), 0, keepdims=True)


def project(x, w_ref, vec_ref, q_ref, k_ref, v_ref):
    width = x.shape[-1]
    q = (mul(x, w_ref[:, :width]) + row(vec_ref, B_QUERY)).astype(bf16)
    q_ref[...] = q * bf16(HEAD_DIM**-0.5)
    k_ref[...] = mul(x, w_ref[:, width : 2 * width]).astype(bf16)
    v_ref[...] = (mul(x, w_ref[:, 2 * width :]) + row(vec_ref, B_VALUE)).astype(bf16)


def attend_pairs(q_ref, k_ref, v_ref, c_ref, stat, first, end):
    lane = lax.broadcasted_iota(jnp.int32, stat.shape, 1)

    def pair(p, carry):
        at = pair_at(p)
        q2, k2, v2 = q_ref[:, at], k_ref[:, at], v_ref[:, at]
        context = None
        for h, (k_one, v_one) in enumerate(zip(halves(k2), halves(v2))):
            scores = mul(q2, k_one, NT)
            best = jnp.max(scores, 1, keepdims=True)
            weights = jnp.exp(scores - best)
            total = jnp.sum(weights, 1, keepdims=True)
            part = mul(weights.astype(bf16), v_one) * (1.0 / total)
            context = part if context is None else context + part
            stat[...] = jnp.where(lane == 2 * p + h, best + jnp.log(total), stat[...])
        c_ref[:, at] = context.astype(bf16)
        return carry

    lax.fori_loop(first, end, pair, 0, unroll=3)


def attend(q_ref, k_ref, v_ref, c_ref, l_ref, stat):
    stat[...] = jnp.zeros_like(stat)
    attend_pairs(q_ref, k_ref, v_ref, c_ref, stat, 0, HEADS // 2)
    l_ref[...] = stat[...].T[:STAT_ROWS]


def attend_back(q_ref, k_ref, v_ref, g_ref, l_ref, d_ref, out_ref, kt, gqt, first, pairs):
    part = pairs * PAIR
    columns = pl.ds(pl.multiple_of(first * PAIR, PAIR), part)
    kt[...] = (k_ref[:, columns] * bf16(HEAD_DIM**-0.5)).T
    for p in range(pairs):
        at = pair_at(first + p)
        q2, g2 = q_ref[:, at], g_ref[:, at]
        ks, vs = halves(k_ref[:, at]), halves(v_ref[:, at])
        qs, gs = halves(q2), halves(g2)
        gk = gv = None
        for h in range(2):
            head = 2 * (first + p) + h
            probs = jnp.exp(mul(ks[h], q2, NT) - l_ref[pl.ds(head, 1), :])
            grad_probs = mul(vs[h], g2, NT)
            grad_scores = (probs * (grad_probs - d_ref[pl.ds(head, 1), :])).astype(bf16)
            gk_one = mul(grad_scores, qs[h])
            gv_one = mul(probs.astype(bf16), gs[h])
            gk = gk_one if gk is None else gk + gk_one
            gv = gv_one if gv is None else gv + gv_one
            rows = slice((2 * p + h) * HEAD_DIM, (2 * p + h + 1) * HEAD_DIM)
            gqt[rows, :] = mul(kt[rows, :], grad_scores).astype(bf16)
        out_ref[:, part + p * PAIR : part + (p + 1) * PAIR] = gk.astype(bf16)
        out_ref[:, 2 * part + p * PAIR : 2 * part + (p + 1) * PAIR] = gv.astype(bf16)
    out_ref[:, :part] = gqt[...].T


def to_hidden(x, cb, wo_ref, wi_ref, vec_ref, mid_ref, h_ref, slope_ref):
    width = x.shape[-1]
    normed, inverse = normalize(x.astype(f32) + (mul(cb, wo_ref[...]) + row(vec_ref, B_OUT)))
    mid = (normed * row(vec_ref, GAIN_1) + row(vec_ref, BIAS_1)).astype(bf16)
    mid_ref[...] = mid
    for c in range(wi_ref.shape[1] // width):
        at = slice(c * width, (c + 1) * width)
        inner = mul(mid, wi_ref[:, at]) + row(vec_ref, B_INNER + c)
        cdf = 0.5 + 0.5 * lax.erf(inner * (0.5**0.5))
        h_ref[:, at] = (inner * cdf).astype(bf16)
        slope = cdf + inner * (jnp.exp(inner * inner * -0.5) * ((0.5 / jnp.pi) ** 0.5))
        slope_ref[:, at] = slope.astype(bf16)
    return normed, inverse


def to_output(normed_1, cot, wu_ref, vec_ref, h_ref, out_ref, gf_ref, sums_ref):
    width = normed_1.shape[-1]
    total = normed_1 * row(vec_ref, GAIN_1) + (row(vec_ref, BIAS_1) + row(vec_ref, B_OUTER))
    for c in range(h_ref.shape[1] // width):
        at = slice(c * width, (c + 1) * width)
        total = total + mul(h_ref[:, at], wu_ref[at, :])
    normed, inverse = normalize(total)
    gain = row(vec_ref, GAIN_2)
    out_ref[...] = (normed * gain + row(vec_ref, BIAS_2)).astype(bf16)
    grad = cot.astype(f32)
    sums_ref[GAIN_2 : GAIN_2 + 1, :] += column_sum(grad * normed)
    sums_ref[BIAS_2 : BIAS_2 + 1, :] += column_sum(grad)
    grad_2 = norm_back(grad, normed, inverse, gain)
    gf = grad_2.astype(bf16)
    gf_ref[...] = gf
    sums_ref[B_OUTER : B_OUTER + 1, :] += column_sum(gf)
    return grad_2


def to_context_grad(
    grad_2, normed_1, inverse_1, cb, wo_ref, wi_ref, wu_ref, vec_ref, gf_ref, ga_ref, gc_ref, d_ref, gu_ref, sums_ref
):
    width = grad_2.shape[-1]
    gf = gf_ref[...]
    grad_mid = grad_2
    for c in range(wi_ref.shape[1] // width):
        at = slice(c * width, (c + 1) * width)
        gu = (mul(gf, wu_ref[at, :], NT) * gu_ref[:, at].astype(f32)).astype(bf16)
        gu_ref[:, at] = gu
        sums_ref[B_INNER + c : B_INNER + c + 1, :] += column_sum(gu)
        grad_mid = grad_mid + mul(gu, wi_ref[:, at], NT)
    sums_ref[GAIN_1 : GAIN_1 + 1, :] += column_sum(grad_mid * normed_1)
    sums_ref[BIAS_1 : BIAS_1 + 1, :] += column_sum(grad_mid)
    ga = norm_back(grad_mid, normed_1, inverse_1, row(vec_ref, GAIN_1)).astype(bf16)
    ga_ref[...] = ga
    sums_ref[B_OUT : B_OUT + 1, :] += column_sum(ga)
    gc = mul(ga, wo_ref[...], NT).astype(bf16)
    gc_ref[...] = gc
    product = gc.astype(f32) * cb.astype(f32)
    high = product.astype(bf16)
    low = (product - high.astype(f32)).astype(bf16)
    head = lax.broadcasted_iota(jnp.int32, (STAT_ROWS, width), 0)
    column = lax.broadcasted_iota(jnp.int32, (STAT_ROWS, width), 1)
    pick = jnp.where(column // HEAD_DIM == head, 1.0, 0.0).astype(bf16)
    d_ref[...] = mul(pick, high, NT) + mul(pick, low, NT)


def spec(shape, pipelined=True):
    zeros = (0,) * (len(shape) - 1)
    if pipelined:
        return pl.BlockSpec(shape, lambda i: (i,) + zeros)
    return pl.BlockSpec(shape, lambda i: (0,) + zeros)


def whole_vmem():
    return pl.BlockSpec(memory_space=pltpu.VMEM)


def params():
    return pltpu.CompilerParams(vmem_limit_bytes=VMEM_BYTES, dimension_semantics=("arbitrary",))


def attention_call(x, w_qkv, vec):
    count, length, width = x.shape
    block = (None, length, width)

    def kernel(x_ref, w_ref, vec_ref, q_ref, k_ref, v_ref, c_ref, l_ref, stat):
        project(x_ref[...], w_ref, vec_ref, q_ref, k_ref, v_ref)
        attend(q_ref, k_ref, v_ref, c_ref, l_ref, stat)

    seq = jax.ShapeDtypeStruct(x.shape, bf16)
    return pl.pallas_call(
        kernel,
        grid=(count,),
        in_specs=[spec(block), whole_vmem(), whole_vmem()],
        out_specs=[spec(block)] * 4 + [spec((None, STAT_ROWS, length))],
        out_shape=[seq] * 4 + [jax.ShapeDtypeStruct((count, STAT_ROWS, length), f32)],
        scratch_shapes=[pltpu.VMEM((length, 128), f32)],
        compiler_params=params(),
        name="attention",
    )(x, w_qkv, vec)


def feed_forward_call(x, cb, cot, w_out, w_inner, w_outer, vec):
    count, length, width = x.shape
    inner = w_inner.shape[1]
    block, wide = (None, length, width), (None, length, inner)

    def kernel(x_ref, cb_ref, cot_ref, wo, wi, wu, vec_ref, out, mid, gf, ga, gc, d, h, gu, sums):
        @pl.when(pl.program_id(0) == 0)
        def _():
            sums[...] = jnp.zeros_like(sums)

        cb = cb_ref[...]
        normed, inverse = to_hidden(x_ref[...], cb, wo, wi, vec_ref, mid, h, gu)
        grad_2 = to_output(normed, cot_ref[...], wu, vec_ref, h, out, gf, sums)
        to_context_grad(grad_2, normed, inverse, cb, wo, wi, wu, vec_ref, gf, ga, gc, d, gu, sums)

    seq = jax.ShapeDtypeStruct(x.shape, bf16)
    seq_wide = jax.ShapeDtypeStruct((count, length, inner), bf16)
    return pl.pallas_call(
        kernel,
        grid=(count,),
        in_specs=[spec(block)] * 3 + [whole_vmem()] * 4,
        out_specs=[spec(block)] * 5
        + [spec((None, STAT_ROWS, length)), spec(wide), spec(wide), spec((16, width), False)],
        out_shape=[seq] * 5
        + [
            jax.ShapeDtypeStruct((count, STAT_ROWS, length), f32),
            seq_wide,
            seq_wide,
            jax.ShapeDtypeStruct((16, width), f32),
        ],
        compiler_params=params(),
        name="feed_forward",
    )(x, cb, cot, w_out, w_inner, w_outer, vec)


def weight_grad_call(left, right, over_left):
    tokens, rows = left.shape
    columns = right.shape[1]
    step = min(rows, columns)

    def kernel(left_ref, right_ref, out_ref):
        out_ref[...] = mul(left_ref[...], right_ref[...], TN).astype(bf16)

    if over_left:
        grid, left_map, right_map, out_map = rows // step, lambda i: (0, i), lambda i: (0, 0), lambda i: (i, 0)
    else:
        grid, left_map, right_map, out_map = columns // step, lambda i: (0, 0), lambda i: (0, i), lambda i: (0, i)
    return pl.pallas_call(
        kernel,
        grid=(grid,),
        in_specs=[pl.BlockSpec((tokens, step), left_map), pl.BlockSpec((tokens, step), right_map)],
        out_specs=pl.BlockSpec((step, step), out_map),
        out_shape=jax.ShapeDtypeStruct((rows, columns), bf16),
        compiler_params=params(),
        name="weight_grad",
    )(left, right)


def attention_back_call(x, q, k, v, gc, ga, stat_l, stat_d, w_qkv):
    count, length, width = x.shape
    block = (None, length, width)
    pairs = HEADS // 2

    def kernel(x_ref, q_ref, k_ref, v_ref, gc_ref, ga_ref, l_ref, d_ref, w_ref, gx_ref, gw_ref, sums_ref, kt, gqt, g, total):
        step = pl.program_id(0)

        @pl.when(step == 0)
        def _():
            sums_ref[...] = jnp.zeros_like(sums_ref)
            total[...] = jnp.zeros_like(total)

        attend_back(q_ref, k_ref, v_ref, gc_ref, l_ref, d_ref, g, kt, gqt, 0, pairs)
        sums_ref[B_QUERY : B_QUERY + 1, :] += column_sum(g[:, :width])
        sums_ref[B_VALUE : B_VALUE + 1, :] += column_sum(g[:, 2 * width :])
        grad = ga_ref[...].astype(f32)
        x = x_ref[...]
        for i in range(3):
            at = slice(i * width, (i + 1) * width)
            grad = grad + mul(g[:, at], w_ref[:, at], NT)
            total[:, at] += mul(x, g[:, at], TN)
        gx_ref[...] = grad.astype(bf16)

        @pl.when(step == count - 1)
        def _():
            gw_ref[...] = total[...].astype(bf16)

    return pl.pallas_call(
        kernel,
        grid=(count,),
        in_specs=[spec(block)] * 6 + [spec((None, STAT_ROWS, length))] * 2 + [whole_vmem()],
        out_specs=[spec(block), spec((width, 3 * width), False), spec((16, width), False)],
        out_shape=[
            jax.ShapeDtypeStruct(x.shape, bf16),
            jax.ShapeDtypeStruct((width, 3 * width), bf16),
            jax.ShapeDtypeStruct((16, width), f32),
        ],
        scratch_shapes=[pltpu.VMEM((width, length), bf16)] * 2
        + [pltpu.VMEM((length, 3 * width), bf16), pltpu.VMEM((width, 3 * width), f32)],
        compiler_params=params(),
        name="attention_back",
    )(x, q, k, v, gc, ga, stat_l, stat_d, w_qkv)


W1, W2, TABLE, M1, M2, UP = range(6)
GATHER_PLAN = {
    1: (("tokens", 1), ("own_z", M2),),
    2: (("own", M2), ("own_z", UP), ("tokens", 2),),
    3: (("hop", UP, 1),),
    4: (("hop", UP, 2), ("own_z", M1),),
    5: (("hop", UP, 3),),
    6: (("hop", M2, 1),),
    7: (("own", M1), ("hop", M2, 2), ("relay", M2, 0),),
    8: (("hop", M2, 3),),
    9: (("tokens", 3), ("hop", M1, 1), ("relay", M2, 1),),
    11: (("hop", M1, 2), ("relay", M2, 2), ("relay", M2, 3), ("swap", M2, 2, 0),),
    12: (("relay", UP, 2), ("own", UP),),
    13: (("swap", UP, 3, 0), ("swap", M2, 3, 0), ("relay", M1, 1), ("hop", M1, 3), ("swap", M2, 0, 1),),
    14: (("relay", M1, 0),),
    15: (("relay", M1, 2), ("relay", UP, 1), ("swap", M2, 1, 1), ("swap", M2, 2, 1),),
    16: (("swap", UP, 1, 0), ("swap", M2, 3, 1),),
    17: (("swap", M2, 1, 0), ("relay", M1, 3), ("relay", UP, 3), ("relay", UP, 0),),
    18: (("cotangent", 2),),
    19: (("swap", UP, 3, 1), ("cotangent", 3),),
    20: (("swap", UP, 2, 1), ("swap", UP, 2, 0), ("swap", UP, 1, 1), ("swap", UP, 0, 1),),
    21: (("cotangent", 0), ("cotangent", 1),),
}


def forward_call(tokens, span_mask, cotangent, w_query, w_key, w_value, w_out, w_inner, w_outer, table, sizes):
    depth_z, depth_y, cores = sizes
    rows, stretch, width = tokens.shape
    inner = w_inner.shape[1]
    part, outer_part = w_query.shape[0], w_outer.shape[0]
    devices = depth_z * depth_y * cores
    count, length = rows // 2, 2 * stretch
    chunks = inner // width
    qkv_width, mid_width = 3 * width, width + inner
    last = depth_z - 1
    ARRAYS = 6
    early = (TABLE, W1, W2)
    shared = (M2, UP)
    places = depth_z * depth_y
    half = width // 2
    m2_half = mid_width // 512 * 128
    m1_width = mid_width - 2 * m2_half

    def kernel(
        tokens_ref, mask_ref, cot_ref, wq_in, wk_in, wv_in, wo_in, wi_in, wu_in, table_in,
        x_out, q_out, k_out, v_out, cb_out, l_out, o_out, mid_out, gf_out, ga_out, gc_out, d_out, h_out, gu_out,
        sums_out, w_qkv_out,
        w_qkv, w_mid, w_up, tables, vec, x_all, cot_all, cot_away, cb_all, t_mid, t_3, t_4, t_5, l_s, stat, inv, d_s,
        normed_all, h_s, gu_s,
        up_send, down_send, z_recv, y_send, y_recv, c_send, c_recv, x_send, x_recv, t_send, t_recv, g_send, g_recv,
        in_sem, out_sem,
    ):
        b, k = lax.axis_index("batch"), lax.axis_index("blk")
        z, y, c = b // (depth_y * cores), (b // cores) % depth_y, b % cores

        def at(z_, y_, c_):
            return (z_ * depth_y + y_) * cores + c_

        barrier = pltpu.get_barrier_semaphore()

        def greet(device):
            pl.semaphore_signal(barrier, inc=1, device_id=device, device_id_type=pl.DeviceIdType.MESH)

        greet((b, 1 - k))
        greet((at(z, 1 - y, c), k))
        greet((at(z, y, 1 - c), k))

        @pl.when(z < last)
        def _():
            greet((at(z + 1, y, c), k))

        @pl.when(z > 0)
        def _():
            greet((at(z - 1, y, c), k))

        shard = pl.ds(b * part, part)
        mine = pl.ds(pl.multiple_of(k * stretch, stretch), stretch)
        theirs = pl.ds(pl.multiple_of((1 - k) * stretch, stretch), stretch)
        loads = [
            pltpu.make_async_copy(wq_in, w_qkv.at[shard, 0:width], in_sem.at[0]),
            pltpu.make_async_copy(wk_in, w_qkv.at[shard, width : 2 * width], in_sem.at[1]),
            pltpu.make_async_copy(wv_in, w_qkv.at[shard, 2 * width : 3 * width], in_sem.at[2]),
            pltpu.make_async_copy(wu_in, w_up.at[pl.ds(b * outer_part, outer_part)], in_sem.at[5]),
            pltpu.make_async_copy(wo_in, w_mid.at[shard, 0:width], in_sem.at[3]),
            pltpu.make_async_copy(wi_in, w_mid.at[shard, width:mid_width], in_sem.at[4]),
            pltpu.make_async_copy(cot_ref.at[pl.ds(k * count, count)], cot_all.at[:, mine], in_sem.at[6]),
            pltpu.make_async_copy(cot_ref.at[pl.ds((1 - k) * count, count)], cot_away, in_sem.at[7]),
            pltpu.make_async_copy(tokens_ref.at[pl.ds(k * count, count)], x_all.at[:, mine], in_sem.at[8]),
        ]
        for copy in loads:
            copy.start()

        raw = table_in[...]
        rolled = pltpu.roll(raw, b * part, 1)
        wide = pltpu.roll(raw[B_INNER : B_INNER + 1, :], (b % (devices // chunks)) * outer_part, 1)
        line = lax.broadcasted_iota(jnp.int32, raw.shape, 0)
        own_table = jnp.where(line < B_INNER, rolled, 0.0)
        own_table = jnp.where(line == B_INNER + b // (devices // chunks), wide, own_table)
        tables[b] = own_table.astype(bf16)

        t_1, t_2 = t_mid.at[0], t_mid.at[1]

        def piece(a, z_, y_, c_, side):
            d = at(z_, y_, c_)
            rows = pl.ds(d * part, part)
            if a == W1:
                return w_qkv.at[rows, : qkv_width // 2]
            if a == W2:
                return w_qkv.at[rows, qkv_width // 2 :]
            if a == TABLE:
                return tables.at[d]
            if a == M1:
                return w_mid.at[rows, :m1_width]
            if a == M2:
                return w_mid.at[rows, pl.ds(pl.multiple_of(m1_width + side * m2_half, 128), m2_half)]
            return w_up.at[pl.ds(d * outer_part, outer_part), pl.ds(pl.multiple_of(side * half, half), half)]

        def remote(ref, device, send, recv):
            return pltpu.make_async_remote_copy(
                src_ref=ref, dst_ref=ref, send_sem=send, recv_sem=recv, device_id=device, device_id_type=pl.DeviceIdType.MESH
            )

        def up(a, zs):
            return remote(piece(a, zs, y, c, k), (at(z + 1, y, c), k), up_send.at[a, zs], z_recv.at[a, zs])

        def down(a, zs):
            return remote(piece(a, zs, y, c, k), (at(z - 1, y, c), k), down_send.at[a, zs], z_recv.at[a, zs])

        def across(a, zs):
            return remote(piece(a, zs, y, c, k), (at(z, 1 - y, c), k), y_send.at[a, zs], y_recv.at[a, zs])

        def core(a, zs, ys, side):
            i = (zs * depth_y + ys) * 2 + (side if a in shared else 0)
            return remote(piece(a, zs, ys, c, side), (at(z, y, 1 - c), k), c_send.at[a, i], c_recv.at[a, i])

        def plane(a, zs, ys):
            i = zs * depth_y + ys
            return remote(piece(a, zs, ys, c, k), (b, 1 - k), x_send.at[a, i], x_recv.at[a, i])

        def arrived(ref, sem):
            remote(ref, (b, 1 - k), sem, sem).wait_recv()

        def begin_z(a):
            @pl.when(z < last)
            def _():
                up(a, z).start()

            @pl.when(z > 0)
            def _():
                down(a, z).start()

        def begin_y(a):
            across(a, z).start()

        def begin_core(a):
            core(a, z, y, k).start()
            if a in shared:
                core(a, z, y, 1 - k).start()

        def levels(step, do):
            if step == 0:
                do(z, 0)
                return

            @pl.when(z >= step)
            def _():
                do(z - step, 1)

            @pl.when(z + step <= last)
            def _():
                do(z + step, -1)

        def hop(a, step):
            def one(zs, way):
                arrived(piece(a, zs, y, c, k), z_recv.at[a, zs])
                if way > 0:
                    @pl.when(z < last)
                    def _():
                        up(a, zs).start()
                else:
                    @pl.when(z > 0)
                    def _():
                        down(a, zs).start()
                across(a, zs).start()
                if a in shared:
                    plane(a, zs, y).start()
                core(a, zs, y, k).start()

            levels(step, one)

        def relay(a, step):
            def one(zs, way):
                arrived(piece(a, zs, 1 - y, c, k), y_recv.at[a, zs])
                if a in shared:
                    plane(a, zs, 1 - y).start()
                core(a, zs, 1 - y, k).start()

            levels(step, one)

        def swap(a, step, ys):
            def one(zs, way):
                arrived(piece(a, zs, ys, c, 1 - k), x_recv.at[a, zs * depth_y + ys])
                core(a, zs, ys, 1 - k).start()

            levels(step, one)

        def complete(a):
            for zs in range(depth_z):
                for ys in range(depth_y):
                    for side in range(2 if a in shared else 1):
                        arrived(piece(a, zs, ys, 1 - c, side), c_recv.at[a, (zs * depth_y + ys) * 2 + side])

        def sent(a):
            for zs in range(depth_z):
                @pl.when((z < last) & (zs <= z))
                def _():
                    up(a, zs).wait_send()

                @pl.when((z > 0) & (zs >= z))
                def _():
                    down(a, zs).wait_send()

                across(a, zs).wait_send()
                for ys in range(depth_y):
                    for side in range(2 if a in shared else 1):
                        core(a, zs, ys, side).wait_send()
                    if a in shared:
                        @pl.when((zs != z) | (ys != y))
                        def _():
                            plane(a, zs, ys).wait_send()

        def token_copy(s):
            return pltpu.make_async_remote_copy(
                src_ref=tokens_ref.at[(1 - k) * count + s],
                dst_ref=x_all.at[s, mine],
                send_sem=t_send.at[s],
                recv_sem=t_recv.at[s],
                device_id=(b, 1 - k),
                device_id_type=pl.DeviceIdType.MESH,
            )

        def grad_copy(s):
            return pltpu.make_async_remote_copy(
                src_ref=cot_away.at[s],
                dst_ref=cot_all.at[s, mine],
                send_sem=g_send.at[s],
                recv_sem=g_recv.at[s],
                device_id=(b, 1 - k),
                device_id_type=pl.DeviceIdType.MESH,
            )

        def put(i, src, dst):
            return pltpu.make_async_copy(src, dst, out_sem.at[i])

        partners = 3 + (z < last).astype(jnp.int32) + (z > 0).astype(jnp.int32)
        pl.semaphore_wait(barrier, partners)
        for a in early:
            if a == W1:
                for i in range(3):
                    loads[i].wait()
            begin_z(a)
            begin_y(a)
            begin_core(a)
        token_copy(0).start()
        for i in (3, 4, 5):
            loads[i].wait()

        def begin_own(a):
            begin_y(a)
            begin_core(a)

        actions = {
            "hop": hop, "relay": relay, "swap": lambda a, step, far: swap(a, step, (1 - y) if far else y),
            "own": begin_own, "own_z": begin_z,
            "tokens": lambda s: token_copy(s).start(), "cotangent": lambda s: grad_copy(s).start(),
        }

        def at_slot(slot):
            for name, *what in GATHER_PLAN.get(slot, ()):
                actions[name](*what)

        def at_slots(first_slot, stride, index, bound):
            for value in range(bound):
                if first_slot + stride * value in GATHER_PLAN:
                    @pl.when(index == value)
                    def _():
                        at_slot(first_slot + stride * value)

        at_slot(0)

        for i in (6, 7):
            loads[i].wait()
        mask = mask_ref[...].astype(f32)
        own, away = jnp.where(k == 0, mask[:count], mask[count:]), jnp.where(k == 0, mask[count:], mask[:count])
        columns = jnp.concatenate([own, away], 0).T
        for s in range(count):
            cot_all[s, mine, :] = (cot_all[s, mine, :].astype(f32) * columns[:, s : s + 1]).astype(bf16)
            cot_away[s] = (cot_away[s].astype(f32) * columns[:, count + s : count + s + 1]).astype(bf16)

        loads[8].wait()
        for step in range(1, depth_z):
            for a in early:
                hop(a, step)
            at_slot(step)
            for a in early:
                relay(a, step - 1)
        for a in early:
            relay(a, last)
        at_slot(4)
        for a in early:
            complete(a)
        vec[...] = jnp.sum(tables[...].astype(f32), 0)
        save_w = put(0, w_qkv, w_qkv_out)
        save_w.start()

        def first(s, carry):
            arrived(x_all.at[s, theirs], t_recv.at[s])
            saves = [
                put(1, x_all.at[s], x_out.at[s]),
                put(2, t_1, q_out.at[s]),
                put(3, t_2, k_out.at[s]),
                put(4, t_3, v_out.at[s]),
                put(5, cb_all.at[s], cb_out.at[s]),
                put(6, l_s, l_out.at[s]),
            ]

            @pl.when(s > 0)
            def _():
                for save in saves[:4]:
                    save.wait()

            project(x_all[s], w_qkv, vec, t_1, t_2, t_3)
            for save in saves[:4]:
                save.start()
            at_slots(5, 3, s, count)
            stat[...] = jnp.zeros_like(stat)
            attend_pairs(t_1, t_2, t_3, cb_all.at[s], stat, 0, HEADS // 4)
            at_slots(6, 3, s, count)
            attend_pairs(t_1, t_2, t_3, cb_all.at[s], stat, HEADS // 4, HEADS // 2)

            @pl.when(s > 0)
            def _():
                for save in saves[4:]:
                    save.wait()

            l_s[...] = stat[...].T[:STAT_ROWS]
            for save in saves[4:]:
                save.start()
            at_slots(7, 3, s, count)
            return carry

        lax.fori_loop(0, count, first, 0)
        at_slot(17)
        for a in (M1, M2):
            complete(a)
        for i, (src, dst) in enumerate(((x_all.at[0], x_out.at[0]), (t_1, q_out.at[0]), (t_2, k_out.at[0]), (t_3, v_out.at[0]), (cb_all.at[0], cb_out.at[0]), (l_s, l_out.at[0]))):
            put(i + 1, src, dst).wait()
        save_w.wait()
        sums_out[...] = jnp.zeros_like(sums_out)
        w_o, w_i = w_mid.at[:, 0:width], w_mid.at[:, width:mid_width]
        O, GF, GA, GC, DELTA, H, GU, H_IN, GU_IN, MID = 8, 9, 10, 11, 12, 13, 15, 17, 19, 21

        lane = lax.broadcasted_iota(jnp.int32, inv.shape, 1)
        inv[...] = jnp.zeros_like(inv)

        def second(s, carry):
            slot = s % 2

            mid_s = t_mid.at[slot]

            @pl.when(s >= 2)
            def _():
                put(MID + slot, mid_s, mid_out.at[s]).wait()
                put(H + slot, h_s.at[slot], h_out.at[s]).wait()
                put(GU + slot, gu_s.at[slot], gu_out.at[s]).wait()

            normed, inverse = to_hidden(x_all[s], cb_all[s], w_o, w_i, vec, mid_s, h_s.at[slot], gu_s.at[slot])
            normed_all[s] = normed
            inv[...] = jnp.where(lane == s, inverse, inv[...])
            put(MID + slot, mid_s, mid_out.at[s]).start()
            put(H + slot, h_s.at[slot], h_out.at[s]).start()

            @pl.when(s < 2)
            def _():
                put(GU + slot, gu_s.at[slot], gu_out.at[s]).start()

            at_slots(18, 1, s, count)
            return carry

        lax.fori_loop(0, count, second, 0)
        for slot in range(2):
            put(MID + slot, t_mid.at[slot], mid_out.at[0]).wait()
        complete(UP)

        def third(i, carry):
            s = (i + count // 2) % count
            slot = i % 2
            at_slots(22, 1, i, count)
            arrived(cot_all.at[s, theirs], g_recv.at[s])
            saves = [
                put(O, t_1, o_out.at[s]),
                put(GF, t_3, gf_out.at[s]),
                put(GA, t_4, ga_out.at[s]),
                put(GC, t_5, gc_out.at[s]),
                put(DELTA, d_s, d_out.at[s]),
            ]

            @pl.when(i >= 2)
            def _():
                put(H_IN + slot, h_out.at[s], h_s.at[slot]).wait()
                put(GU_IN + slot, gu_out.at[s], gu_s.at[slot]).wait()

            @pl.when(i > 0)
            def _():
                for save in saves[:2]:
                    save.wait()

            grad_2 = to_output(normed_all[s], cot_all[s], w_up, vec, h_s.at[slot], t_1, t_3, sums_out)
            for save in saves[:2]:
                save.start()

            @pl.when(i > 0)
            def _():
                for save in saves[2:]:
                    save.wait()

            @pl.when((i > 0) & (i + 1 < count))
            def _():
                put(GU + 1 - slot, gu_s.at[1 - slot], gu_out.at[s]).wait()
                put(GU_IN + 1 - slot, gu_out.at[(s + 1) % count], gu_s.at[1 - slot]).start()

            inverse = jnp.sum(jnp.where(lane == s, inv[...], 0.0), 1, keepdims=True)
            to_context_grad(
                grad_2, normed_all[s], inverse, cb_all[s], w_o, w_i, w_up, vec, t_3, t_4, t_5, d_s, gu_s.at[slot], sums_out
            )
            for save in saves[2:]:
                save.start()
            put(GU + slot, gu_s.at[slot], gu_out.at[s]).start()

            @pl.when(i + 2 < count)
            def _():
                put(H + slot, h_s.at[slot], h_out.at[s]).wait()
                put(H_IN + slot, h_out.at[(s + 2) % count], h_s.at[slot]).start()

            return carry

        lax.fori_loop(0, count, third, 0)
        for i, src, dst in ((O, t_1, o_out), (GF, t_3, gf_out), (GA, t_4, ga_out), (GC, t_5, gc_out), (DELTA, d_s, d_out)):
            put(i, src, dst.at[0]).wait()
        for slot in range(2):
            put(GU + slot, gu_s.at[slot], gu_out.at[0]).wait()
        for s in range(count):
            token_copy(s).wait_send()
            grad_copy(s).wait_send()
        for a in range(ARRAYS):
            sent(a)

    seq = jax.ShapeDtypeStruct((count, length, width), bf16)
    seq_wide = jax.ShapeDtypeStruct((count, length, inner), bf16)
    stat_shape = jax.ShapeDtypeStruct((count, STAT_ROWS, length), f32)
    hbm = pl.BlockSpec(memory_space=pl.ANY)
    one = pltpu.VMEM((length, width), bf16)
    two_wide = pltpu.VMEM((2, length, inner), bf16)
    all_seq = pltpu.VMEM((count, length, width), bf16)
    stat_one = pltpu.VMEM((STAT_ROWS, length), f32)
    lanes = pltpu.VMEM((length, 128), f32)
    dma = pltpu.SemaphoreType.DMA
    return pl.pallas_call(
        kernel,
        in_specs=[hbm, whole_vmem()] + [hbm] * 7 + [whole_vmem()],
        out_specs=[hbm] * 14 + [whole_vmem(), hbm],
        out_shape=[seq] * 5 + [stat_shape] + [seq] * 5 + [stat_shape, seq_wide, seq_wide]
        + [jax.ShapeDtypeStruct((16, width), f32), jax.ShapeDtypeStruct((width, qkv_width), bf16)],
        scratch_shapes=[
            pltpu.VMEM((width, qkv_width), bf16),
            pltpu.VMEM((width, mid_width), bf16),
            pltpu.VMEM((inner, width), bf16),
            pltpu.VMEM((devices, 16, width), bf16),
            pltpu.VMEM((16, width), f32),
            all_seq, all_seq,
            pltpu.VMEM((count, stretch, width), bf16),
            all_seq,
            pltpu.VMEM((2, length, width), bf16), one, one, one, stat_one, lanes, lanes, stat_one,
            pltpu.VMEM((count, length, width), f32),
            two_wide, two_wide,
            dma((ARRAYS, depth_z)), dma((ARRAYS, depth_z)), dma((ARRAYS, depth_z)),
            dma((ARRAYS, depth_z)), dma((ARRAYS, depth_z)),
            dma((ARRAYS, 2 * places)), dma((ARRAYS, 2 * places)), dma((ARRAYS, places)), dma((ARRAYS, places)),
            dma((count,)), dma((count,)), dma((count,)), dma((count,)), dma((9,)), dma((23,)),
        ],
        compiler_params=pltpu.CompilerParams(collective_id=1, has_side_effects=True, vmem_limit_bytes=63 * 2**20),
        name="forward",
    )(tokens, span_mask, cotangent, w_query, w_key, w_value, w_out, w_inner, w_outer, table)


SCATTER_PLAN = {
    2: (("out", 2), (1, "s", 0),),
    3: ((1, "s", 1),),
    4: (("out", 1), ("out", 3),),
    6: ((1, "s", 3), (2, "s", 0), ("out", 0),),
    7: ((1, "s", 2),),
    8: ((2, "s", 1),),
    9: ((1, "o", 0), (2, "s", 3),),
    10: ((1, "s", 4),),
    11: ((2, "s", 2),),
    14: ((2, "o", 0), (1, "o", 1),),
    16: ((3, "s", 0),),
    17: ((2, "s", 4),),
    18: ((1, "o", 2), (3, "o", 0),),
    19: ((2, "o", 1),),
    21: ((3, "s", 1),),
    22: ((2, "o", 2),),
    23: ((1, "p", 0), (1, "p", 1),),
    25: ((1, "p", 3), (3, "s", 4), (2, "p", 0), (3, "o", 1),),
    26: ((2, "p", 1), (1, "p", 2), (3, "o", 2),),
    27: ((2, "p", 3), (1, "p", 5), (4, "s", 4),),
    28: (
        (3, "p", 0),
        (4, "s", 0),
        (1, "p", 4),
        (3, "s", 3),
        (2, "p", 2),
        (4, "o", 2),
        (2, "p", 5),
        (4, "o", 0),
        (3, "p", 3),
        (3, "s", 2),
        (4, "o", 1),
        (4, "s", 1),
        (2, "p", 4),
        (4, "p", 0),
        (3, "p", 2),
        (3, "p", 1),
        (3, "p", 5),
        (3, "p", 4),
        (4, "s", 2),
        (4, "p", 5),
        (4, "p", 2),
        (4, "p", 1),
        (4, "s", 3),
        (4, "p", 3),
        (4, "p", 4),
    ),
}


def backward_call(x, q, k, v, cb, mid, gf, ga, gc, hidden, gu, out, stat_l, stat_d, w_qkv, sums, sizes):
    depth_z, depth_y, cores = sizes
    count, length, width = x.shape
    inner = hidden.shape[2]
    devices = depth_z * depth_y * cores
    part, outer_part = width // devices, inner // devices
    stretch, rows = length // 2, 2 * count
    chunks = inner // width
    GROUPS = 3
    pairs = HEADS // 2 // GROUPS
    column = pairs * PAIR
    narrow = width // GROUPS
    OUT = chunks
    QKV = chunks + 1
    SQUARES, PARTS = QKV, 2 * GROUPS
    first_of = {"s": 0, "o": SQUARES, "p": SQUARES + GROUPS}
    every = SQUARES + GROUPS + PARTS
    half = width // 2
    SLOTS = 2
    STEPS = 5
    tokens_all = count * length

    def kernel(
        x_in, q_in, k_in, v_in, cb_in, mid_in, gf_in, ga_in, gc_in, h_in, gu_in, out_in, w_in, l_ref, d_ref, sums_ref,
        received, grad_tokens, g_query, g_key, g_value, g_out, g_inner, g_outer, vectors,
        big, pool, w_cat, ga_s, gx_s, kt, gqt, own_s, own_o, r1, r2, r3, s4, r4, r1o, r2o, r3o, s4o, r4o, r1p, r2p, r3p, s4p, r4p, v_own, v_got,
        s1_send, s1_recv, s2_send, s2_recv, s3_send, s3_recv, s4_send, s4_recv,
        v_send, v_recv, o_send, o_recv, g_send, g_recv, big_sem, pool_sem, w_sem, ga_sem, keep_sem,
    ):
        b, k = lax.axis_index("batch"), lax.axis_index("blk")
        z, y, c = b // (depth_y * cores), (b // cores) % depth_y, b % cores

        def at(z_, y_, c_):
            return (z_ * depth_y + y_) * cores + c_

        beside = (b, 1 - k)
        other_core = (at(z, y, 1 - c), k)
        other_y = (at(z, 1 - y, c), k)

        def level(j):
            return (z + j) % depth_z

        barrier = pltpu.get_barrier_semaphore()
        partners = [beside, other_core, other_y] + [(at(level(j), y, c), k) for j in range(1, depth_z)]
        for device in partners:
            pl.semaphore_signal(barrier, inc=1, device_id=device, device_id_type=pl.DeviceIdType.MESH)

        def remote(src, dst, device, send, recv):
            return pltpu.make_async_remote_copy(
                src_ref=src, dst_ref=dst, send_sem=send, recv_sem=recv, device_id=device, device_id_type=pl.DeviceIdType.MESH
            )

        def load(i, src):
            return pltpu.make_async_copy(src, big.at[i], big_sem.at[i])

        def wide_load(i, src, j):
            return pltpu.make_async_copy(src.at[:, :, j * width : (j + 1) * width], big.at[i], big_sem.at[i])

        def pool_load(s, slot):
            return [
                pltpu.make_async_copy(src.at[s], pool.at[slot, i], pool_sem.at[slot, i])
                for i, src in enumerate((q_in, k_in, v_in, gc_in))
            ]

        def w_load(i, g):
            return pltpu.make_async_copy(
                w_in.at[:, i * width + g * column : i * width + (g + 1) * column],
                w_cat.at[g, :, i * column : (i + 1) * column],
                w_sem.at[i, g],
            )

        first_loads = [load(0, mid_in), wide_load(2, gu_in, 0), load(1, gf_in), wide_load(3, gu_in, 1)]
        for copy in first_loads:
            copy.start()
        mine = pl.ds(pl.multiple_of(k * stretch, stretch), stretch)
        theirs = pl.ds(pl.multiple_of((1 - k) * stretch, stretch), stretch)

        sums_of = {"s": (r1, r2, r3, s4, r4), "o": (r1o, r2o, r3o, s4o, r4o), "p": (r1p, r2p, r3p, s4p, r4p)}

        def buffers(kind, g):
            return [ref.at[g] for ref in sums_of[kind]] + [first_of[kind] + g]

        def own_part(kind, g, half_of, z_, y_, c_):
            if kind == "o":
                return own_o.at[g, z_, y_, c_]
            if kind == "s":
                return own_s.at[g % SLOTS, z_, y_, c_]
            return own_s.at[(QKV + g) % SLOTS, z_, y_, c_, :, half_of * half : (half_of + 1) * half]

        def step_1(kind, g, half_of=0):
            a1, _, _, _, _, i = buffers(kind, 2 * g + half_of if kind == "p" else g)
            own = own_part(kind, g, half_of, slice(None), slice(None), 1 - c)
            return remote(own, a1, other_core, s1_send.at[i], s1_recv.at[i])

        def step_2(kind, g):
            a1, a2, _, _, _, i = buffers(kind, g)
            return remote(a1.at[:, 1 - y], a2, other_y, s2_send.at[i], s2_recv.at[i])

        def step_3(kind, g, j):
            _, a2, a3, _, _, i = buffers(kind, g)
            return remote(
                a2.at[level(j)], a3.at[j - 1], (at(level(j), y, c), k), s3_send.at[i, j - 1], s3_recv.at[i, j - 1]
            )

        def step_4(kind, g):
            _, _, _, a4, b4, i = buffers(kind, g)
            return remote(a4, b4, beside, s4_send.at[i], s4_recv.at[i])

        def move_1(kind, g):
            a1, _, _, _, _, _ = buffers(kind, g)
            source = (g // 2, g % 2) if kind == "p" else (g, 0)
            step_1(kind, *source).wait()

            def add(i, carry):
                zi, yi = i // depth_y, i % depth_y
                a1[zi, yi] = a1[zi, yi] + own_part(kind, *source, zi, yi, c)[...]
                return carry

            lax.fori_loop(0, depth_z * depth_y, add, 0)
            step_2(kind, g).start()

        def move_2(kind, g):
            a1, a2, _, _, _, _ = buffers(kind, g)
            step_2(kind, g).wait()

            def add(zi, carry):
                a2[zi] = a2[zi] + a1[zi, y]
                return carry

            lax.fori_loop(0, depth_z, add, 0)
            for j in range(1, depth_z):
                step_3(kind, g, j).start()

        def move_3(kind, g):
            _, a2, a3, a4, _, _ = buffers(kind, g)
            for j in range(1, depth_z):
                step_3(kind, g, j).wait()
            total = a2[z].astype(f32)
            for j in range(1, depth_z):
                total = total + a3[j - 1].astype(f32)
            a4[...] = total.astype(bf16)
            step_4(kind, g).start()

        def move_4(kind, g):
            _, _, _, a4, b4, _ = buffers(kind, g)
            step_4(kind, g).wait()
            total = a4[...].astype(f32) + b4[...].astype(f32)
            if kind == "o":
                g_outer[:, g * narrow : (g + 1) * narrow] = total
            elif kind == "s" and g < OUT:
                g_inner[:, g * width : (g + 1) * width] = total
            elif kind == "s":
                g_out[...] = total
            else:
                group, begins = g // 2, (g % 2) * half
                for i, ref in enumerate((g_query, g_key, g_value)):
                    low, high = max(i * column, begins), min((i + 1) * column, begins + half)
                    if low < high:
                        to = group * column - i * column
                        ref[:, to + low : to + high] = total[:, low - begins : high - begins]

        def exchange(s):
            return remote(out_in.at[s, theirs], received.at[s], beside, o_send.at[s], o_recv.at[s])

        moves = {1: move_1, 2: move_2, 3: move_3, 4: move_4}

        def take(steps):
            for name, *what in steps:
                if name == "out":
                    exchange(*what).start()
                else:
                    moves[name](*what)

        def at_slot(slot):
            take(SCATTER_PLAN.get(slot, ()))

        def at_slots(first_slot, stride, index, bound):
            for value in range(bound):
                if first_slot + stride * value in SCATTER_PLAN:
                    @pl.when(index == value)
                    def _():
                        at_slot(first_slot + stride * value)

        def whole(i):
            return big[i].reshape(tokens_all, width)

        def keep(g, value):
            own_s[g % SLOTS] = value.astype(bf16).reshape(depth_z, depth_y, cores, part, width)

        pl.semaphore_wait(barrier, len(partners))

        first_loads[0].wait()
        for j in range(chunks):
            wide_load(2 + j % 2, gu_in, j).wait()
            at_slot(j)
            keep(j, mul(whole(0), whole(2 + j % 2), TN))
            step_1("s", j).start()
            following = j + 2 - chunks
            if following < 0:
                wide_load(2 + j % 2, gu_in, j + 2).start()
            else:
                wide_load(2 + j % 2, h_in, following).start()
            if j == 0:
                for s in range(2):
                    for copy in pool_load(s, s):
                        copy.start()
            if j == 1:
                for g in range(GROUPS):
                    for i in range(3):
                        w_load(i, g).start()
        load(0, ga_in).start()
        first_loads[2].wait()
        for j in range(chunks):
            wide_load(2 + j % 2, h_in, j).wait()
            at_slot(chunks + j)
            product = mul(whole(2 + j % 2), whole(1), TN).astype(bf16)
            for g in range(GROUPS):
                own_o[g, j] = product[:, g * narrow : (g + 1) * narrow].reshape(depth_y, cores, outer_part, narrow)
            if j + 2 < chunks:
                wide_load(2 + j % 2, h_in, j + 2).start()
            elif j + 2 == chunks:
                load(2 + j % 2, cb_in).start()
            else:
                load(2 + j % 2, x_in).start()
        for g in range(GROUPS):
            step_1("o", g).start()
        at_slot(2 * chunks)
        load(0, ga_in).wait()
        load(2 + chunks % 2, cb_in).wait()
        keep(OUT, mul(whole(2 + chunks % 2), whole(0), TN))
        step_1("s", OUT).start()
        for copy in pool_load(2, 2):
            copy.start()
        for g in range(GROUPS):
            for i in range(3):
                w_load(i, g).wait()
        load(2 + (chunks + 1) % 2, x_in).wait()
        x_at = 2 + (chunks + 1) % 2
        v_own[0] = sums_ref[...]

        cells = GROUPS * count
        def gx_copies(s):
            away = remote(gx_s.at[theirs], grad_tokens.at[k * count + s], beside, g_send.at[s], g_recv.at[s])
            stay = pltpu.make_async_copy(gx_s.at[mine], grad_tokens.at[k * count + s], keep_sem.at[1])
            return away, stay

        ga_load = [pltpu.make_async_copy(ga_in.at[s], ga_s, ga_sem.at[0]) for s in range(count)]
        ga_load[0].start()

        def cell(i, carry):
            s, g = i // GROUPS, i % GROUPS
            slot = s % 3

            @pl.when(g == 0)
            def _():
                for copy in pool_load(s, slot):
                    copy.wait()

            attend_back(
                pool.at[slot, 0], pool.at[slot, 1], pool.at[slot, 2], pool.at[slot, 3], l_ref.at[s], d_ref.at[s],
                big.at[g, s], kt, gqt, g * pairs, pairs,
            )
            span = pl.ds(pl.multiple_of(g * column, column), column)
            v_own[0, B_QUERY : B_QUERY + 1, span] += column_sum(big[g, s, :, :column])
            v_own[0, B_VALUE : B_VALUE + 1, span] += column_sum(big[g, s, :, 2 * column :])

            @pl.when(i == GROUPS - 1)
            def _():
                for copy in pool_load(3, 0):
                    copy.start()

            base = 2 * chunks + 1
            last_base = base + (GROUPS + 1) * (count - 1)
            for group in range(GROUPS):
                @pl.when(g == group)
                def _():
                    at_slots(base + group, GROUPS + 1, s, count - 1)

            @pl.when(s == count - 1)
            def _():
                at_slots(last_base, 2, g, GROUPS)
                keep(QKV + g, mul(whole(x_at), big[g].reshape(tokens_all, width), TN))
                step_1("p", g, 0).start()
                step_1("p", g, 1).start()
                at_slots(last_base + 1, 2, g, GROUPS)

            @pl.when(g == GROUPS - 1)
            def _():
                ga_load[0].wait()

                @pl.when(s > 0)
                def _():
                    away, stay = gx_copies(s - 1)
                    away.wait_send()
                    stay.wait()

                grad = ga_s[...].astype(f32)
                for group in range(GROUPS):
                    grad = grad + mul(big[group, s], w_cat[group], NT)
                gx_s[...] = grad.astype(bf16)
                away, stay = gx_copies(s)
                away.start()
                stay.start()

                @pl.when(s < count - 1)
                def _():
                    pltpu.make_async_copy(ga_in.at[s + 1], ga_s, ga_sem.at[0]).start()

                at_slots(base + GROUPS, GROUPS + 1, s, count - 1)

                @pl.when(s == count - 1)
                def _():
                    at_slot(last_base + 2 * GROUPS)

            return carry

        lax.fori_loop(0, cells, cell, 0)

        towards = [other_core, other_y, (at(z + 1 - 2 * (z % 2), y, c), k), (at((z + 2) % 4, y, c), k), beside]

        def v_copy(i):
            return remote(v_own.at[i], v_got.at[i], towards[i], v_send.at[i], v_recv.at[i])

        def v_move(i):
            v_copy(i).wait()
            v_own[i + 1] = v_own[i] + v_got[i]
            if i + 1 < STEPS:
                v_copy(i + 1).start()

        v_copy(0).start()
        rest = SCATTER_PLAN[2 * chunks + 1 + (GROUPS + 1) * (count - 1) + 2 * GROUPS + 1]
        for i in range(STEPS):
            take(rest[2 * i : 2 * i + 2])
            v_move(i)
        total = v_own[STEPS]
        inner_row = v_own[STEPS, pl.ds(B_INNER + b // (devices // chunks), 1), :]
        rolled = pltpu.roll(total, (width - b * part) % width, 1)
        wide = pltpu.roll(inner_row, (width - (b % (devices // chunks)) * outer_part) % width, 1)
        line = lax.broadcasted_iota(jnp.int32, total.shape, 0)
        vectors[...] = jnp.where(line == B_INNER, wide, rolled)
        take(rest[2 * STEPS :])
        away, stay = gx_copies(count - 1)
        away.wait_send()
        stay.wait()
        for s in range(count):
            exchange(s).wait_send()
            exchange(s).wait_recv()
            remote(gx_s.at[theirs], grad_tokens.at[(1 - k) * count + s], beside, g_send.at[s], g_recv.at[s]).wait_recv()

    hbm = pl.BlockSpec(memory_space=pl.ANY)
    dma = pltpu.SemaphoreType.DMA

    def vmem(*shape):
        return pltpu.VMEM(shape, bf16)

    def result(*shape):
        return jax.ShapeDtypeStruct(shape, f32)

    back = jax.ShapeDtypeStruct((rows, stretch, width), bf16)
    from_beside = jax.ShapeDtypeStruct((count, stretch, width), bf16)
    return pl.pallas_call(
        kernel,
        in_specs=[hbm] * 13 + [whole_vmem()] * 3,
        out_specs=[hbm] * 2 + [whole_vmem()] * 7,
        out_shape=[
            from_beside, back, result(part, width), result(part, width), result(part, width), result(part, width),
            result(part, inner), result(outer_part, width), result(16, width),
        ],
        scratch_shapes=[
            vmem(4, count, length, width),
            vmem(3, 4, length, width),
            vmem(GROUPS, width, 3 * column),
            vmem(length, width), vmem(length, width),
            vmem(column, length), vmem(column, length),
            vmem(SLOTS, depth_z, depth_y, cores, part, width),
            vmem(GROUPS, depth_z, depth_y, cores, outer_part, narrow),
            vmem(SQUARES, depth_z, depth_y, part, width), vmem(SQUARES, depth_z, part, width),
            vmem(SQUARES, depth_z - 1, part, width), vmem(SQUARES, part, width), vmem(SQUARES, part, width),
            vmem(GROUPS, depth_z, depth_y, outer_part, narrow), vmem(GROUPS, depth_z, outer_part, narrow),
            vmem(GROUPS, depth_z - 1, outer_part, narrow), vmem(GROUPS, outer_part, narrow), vmem(GROUPS, outer_part, narrow),
            vmem(PARTS, depth_z, depth_y, part, half), vmem(PARTS, depth_z, part, half),
            vmem(PARTS, depth_z - 1, part, half), vmem(PARTS, part, half), vmem(PARTS, part, half),
            pltpu.VMEM((STEPS + 1, 16, width), f32), pltpu.VMEM((STEPS, 16, width), f32),
            dma((every,)), dma((every,)), dma((every,)), dma((every,)),
            dma((every, depth_z - 1)), dma((every, depth_z - 1)), dma((every,)), dma((every,)),
            dma((STEPS,)), dma((STEPS,)), dma((count,)), dma((count,)), dma((count,)), dma((count,)),
            dma((4,)), dma((3, 4)), dma((3, GROUPS)), dma((1,)), dma((2,)),
        ],
        compiler_params=pltpu.CompilerParams(collective_id=2, has_side_effects=True, vmem_limit_bytes=63 * 2**20),
        name="backward",
    )(x, q, k, v, cb, mid, gf, ga, gc, hidden, gu, out, w_qkv, stat_l, stat_d, sums)


def settle_call(side, out, received, grad_tokens, grads, totals, sizes):
    rows, stretch, width = grad_tokens.shape
    count = rows // 2
    n = len(grads)

    def kernel(side_ref, out_ref, received_ref, tokens_ref, *refs):
        sources, totals_ref, (output_ref, grad_ref) = refs[:n], refs[n], refs[n + 1 : n + 3]
        results, vectors = refs[n + 3 : 2 * n + 3], refs[2 * n + 3 :]
        step = pl.program_id(0)
        here = step // count == side_ref[0]

        @pl.when(here)
        def _():
            output_ref[...] = out_ref[...]

        @pl.when(jnp.logical_not(here))
        def _():
            output_ref[...] = received_ref[...]

        grad_ref[...] = tokens_ref[...]

        @pl.when(step == 0)
        def _():
            for source, result in zip(sources, results):
                result[...] = source[...]
            for i, vector in enumerate(vectors):
                vector[...] = totals_ref[i : i + 1, : sizes[i]]

    block = (None, stretch, width)
    straight = pl.BlockSpec(block, lambda i, side: (i, 0, 0))

    def fixed(shape):
        return pl.BlockSpec(shape, lambda i, side: (0, 0))

    shapes = [grad.shape for grad in grads] + [(1, size) for size in sizes]
    return pl.pallas_call(
        kernel,
        grid_spec=pltpu.PrefetchScalarGridSpec(
            num_scalar_prefetch=1,
            grid=(rows,),
            in_specs=[
                pl.BlockSpec(block, lambda i, side: (jnp.clip(i - side[0] * count, 0, count - 1), side[0], 0)),
                pl.BlockSpec(block, lambda i, side: (jnp.clip(i - (1 - side[0]) * count, 0, count - 1), 0, 0)),
                straight,
            ]
            + [fixed(grad.shape) for grad in grads]
            + [fixed(totals.shape)],
            out_specs=[straight] * 2 + [fixed(shape) for shape in shapes],
        ),
        out_shape=[jax.ShapeDtypeStruct(grad_tokens.shape, bf16)] * 2
        + [jax.ShapeDtypeStruct(shape, f32) for shape in shapes],
        compiler_params=params(),
        name="settle",
    )(side, out, received, grad_tokens, *grads, totals)


def pack_shard(w_query, w_key, w_value, w_out, w_inner, w_outer, vectors):
    width = w_query.shape[1]
    inner_parts = [w_inner[:, i : i + width] for i in range(0, w_inner.shape[1], width)]
    small = jnp.concatenate(vectors)
    body_rows = sum(part.shape[0] for part in (w_query, w_key, w_value, w_out, w_outer, *inner_parts))
    rows = -(-(body_rows + 1) // 16) * 16
    tail = jnp.zeros(((rows - body_rows) * width,), small.dtype).at[: small.shape[0]].set(small)
    return jnp.concatenate(
        [w_query, w_key, w_value, w_out, *inner_parts, w_outer, tail.reshape(-1, width)]
    )


def vec_table(small, vec_names_sizes):
    rows, at = [], 0
    for size in vec_names_sizes:
        rows.append(small[:, at : at + size].reshape(-1))
        at += size
    return rows


def gather_weights(w_query, w_key, w_value, w_out, w_inner, w_outer, vectors):
    part, width = w_query.shape
    outer_part = w_outer.shape[0]
    chunks = w_inner.shape[1] // width
    sizes = [vector.shape[0] for vector in vectors]
    packed = pack_shard(w_query, w_key, w_value, w_out, w_inner, w_outer, vectors)
    gathered = lax.all_gather(packed, "batch", axis=0)

    def weight(at, count):
        return gathered[:, at : at + count].reshape(-1, width)

    squares = [weight(i * part, part) for i in range(4 + chunks)]
    outer_at = (4 + chunks) * part
    w_outer_all = weight(outer_at, outer_part)
    small = gathered[:, outer_at + outer_part :].reshape(gathered.shape[0], -1)
    vec = jnp.concatenate(vec_table(small, sizes)).reshape(-1, width).astype(f32)
    vec = jnp.concatenate([vec, jnp.zeros((16 - vec.shape[0], width), f32)])
    return jnp.concatenate(squares[:3], 1), squares[3], jnp.concatenate(squares[4:], 1), w_outer_all, vec


def body(
    tokens,
    span_mask,
    cotangent,
    w_query,
    b_query,
    w_key,
    w_value,
    b_value,
    w_out,
    b_out,
    gain_first,
    bias_first,
    w_inner,
    b_inner,
    w_outer,
    b_outer,
    gain_second,
    bias_second,
):
    rows, stretch, width = tokens.shape
    inner = w_inner.shape[1]
    part = w_query.shape[0]
    outer_part = w_outer.shape[0]
    vectors = (b_query, b_value, b_out, gain_first, bias_first, b_outer, gain_second, bias_second, b_inner)
    sizes = [vector.shape[0] for vector in vectors]

    devices = lax.axis_size("batch")
    chunks = inner // width
    swap = functools.partial(lax.all_to_all, axis_name="blk", tiled=True)
    outer_at = (4 + chunks) * part
    shard_rows = -(-(outer_at + outer_part + 1) // 16) * 16
    if (devices, lax.axis_size("blk")) == (16, 2):
        table = sum(
            lax.pad(
                vector.astype(f32).reshape(1, -1), f32(0), ((i, 15 - i, 0), (0, width - vector.shape[0], 0))
            )
            for i, vector in enumerate(vectors)
        )
        x, q, k, v, cb, stat_l, out, mid, gf, ga, gc, stat_d, hidden, gu, sums_ffn, w_qkv = forward_call(
            tokens, span_mask, cotangent, w_query, w_key, w_value, w_out, w_inner, w_outer, table, (4, 2, 2)
        )
        results = backward_call(
            x, q, k, v, cb, mid, gf, ga, gc, hidden, gu, out, stat_l, stat_d, w_qkv, sums_ffn, (4, 2, 2)
        )
        side = lax.axis_index("blk").astype(jnp.int32).reshape(1)
        settled = settle_call(side, out, results[0], results[1], results[2:-1], results[-1], sizes)
        output, grad_tokens, g_query, g_key, g_value, g_out, g_inner, g_outer = settled[:8]
        small = [vector.reshape(-1) for vector in settled[8:]]
        return (
            output, grad_tokens, g_query, small[0], g_key, g_value, small[1], g_out, small[2], small[3], small[4], g_inner,
            small[8], g_outer, small[5], small[6], small[7],
        )
    w_qkv, w_out_all, w_inner_all, w_outer_all, vec = gather_weights(
        w_query, w_key, w_value, w_out, w_inner, w_outer, vectors
    )
    masked = cotangent * span_mask[..., None].astype(bf16)
    x = swap(tokens, split_axis=0, concat_axis=1)
    cot = swap(masked, split_axis=0, concat_axis=1)
    q, k, v, cb, stat_l = attention_call(x, w_qkv, vec)
    out, mid, gf, ga, gc, stat_d, hidden, gu, sums_ffn = feed_forward_call(
        x, cb, cot, w_out_all, w_inner_all, w_outer_all, vec
    )
    gx, gw_qkv, sums_att = attention_back_call(x, q, k, v, gc, ga, stat_l, stat_d, w_qkv)
    output = swap(out, split_axis=1, concat_axis=0)
    grad_tokens = swap(gx, split_axis=1, concat_axis=0)

    def flat(values):
        return values.reshape(-1, values.shape[-1])

    gw_out = weight_grad_call(flat(cb), flat(ga), False)
    gw_inner = weight_grad_call(flat(mid), flat(gu), False)
    gw_outer = weight_grad_call(flat(hidden), flat(gf), True)

    sums = sums_ffn + sums_att
    small_sums = [sums[i].reshape(devices, -1) for i in range(B_INNER)]
    small_sums.append(sums[B_INNER : B_INNER + chunks].reshape(devices, -1))
    tail = jnp.concatenate(small_sums, 1).astype(bf16)
    tail = jnp.pad(tail, ((0, 0), (0, (shard_rows - outer_at - outer_part) * width - tail.shape[1])))
    pieces = [gw_qkv[:, i * width : (i + 1) * width].reshape(devices, part, width) for i in range(3)]
    pieces.append(gw_out.reshape(devices, part, width))
    pieces += [gw_inner[:, i * width : (i + 1) * width].reshape(devices, part, width) for i in range(chunks)]
    pieces.append(gw_outer.reshape(devices, outer_part, width))
    pieces.append(tail.reshape(devices, -1, width))
    grads = jnp.concatenate(pieces, 1)
    share = lax.psum_scatter(grads, "batch", scatter_dimension=0, tiled=False)
    share = lax.psum(share, "blk").astype(f32)
    square = [share[i * part : (i + 1) * part] for i in range(4 + chunks)]
    share_small = share[outer_at + outer_part :].reshape(-1)
    small_out, at = [], 0
    for size in sizes:
        small_out.append(share_small[at : at + size])
        at += size
    (g_b_query, g_b_value, g_b_out, g_gain_1, g_bias_1, g_b_outer, g_gain_2, g_bias_2, g_b_inner) = small_out
    return (
        output,
        grad_tokens,
        square[0],
        g_b_query,
        square[1],
        square[2],
        g_b_value,
        square[3],
        g_b_out,
        g_gain_1,
        g_bias_1,
        jnp.concatenate(square[4:], 1),
        g_b_inner,
        share[outer_at : outer_at + outer_part],
        g_b_outer,
        g_gain_2,
        g_bias_2,
    )


def solution(mesh):
    block = P("batch", "blk", None)
    matrix, vector = P("batch", None), P("batch")
    weights = (
        matrix, vector, matrix, matrix, vector, matrix, vector, vector, vector, matrix, vector, matrix, vector, vector, vector,
    )
    return jax.shard_map(
        body,
        mesh=mesh,
        in_specs=(block, P("batch", "blk"), block) + weights,
        out_specs=(block, block) + weights,
        check_vma=False,
    )
```
